128 devices in a mesh: dp: 32 (over x, y, core), mp: 4 (over z).
Axes of the slice: x: 4, y: 4, z: 4, core: 2. Of those that a mesh axis runs over, the one named last changes fastest.
Arguments:
- tokens: bfloat16 [4096, 2048], P('dp'), may hold values from -6 to 6
- depths: int32 [4096], P('dp'), may hold values from 1 to 3
- second_slot: int32 [4096], P('dp'), may hold values from -1 to 95, as said below
- third_slot: int32 [4096], P('dp'), may hold values from -1 to 63, as said below
- w_query: bfloat16 [2048, 2048], P('dp', 'mp'), may hold values from -0.125 to 0.125
- w_key: bfloat16 [2048, 256], P('dp', 'mp'), may hold values from -0.125 to 0.125
- w_value: bfloat16 [2048, 256], P('dp', 'mp'), may hold values from -0.125 to 0.125
- w_out: bfloat16 [2048, 2048], P('mp', 'dp'), may hold values from -0.75 to 0.75
- w_gate: bfloat16 [2048, 5632], P('dp', 'mp'), may hold values from -0.125 to 0.125
- w_up: bfloat16 [2048, 5632], P('dp', 'mp'), may hold values from -0.125 to 0.125
- w_down: bfloat16 [5632, 2048], P('mp', 'dp'), may hold values from -0.078125 to 0.078125
- norm_first: bfloat16 [2048], P('dp'), may hold values from 0.5 to 1.5
- norm_second: bfloat16 [2048], P('dp'), may hold values from 0.5 to 1.5
- router: bfloat16 [2048], P('dp'), may hold values from -0.125 to 0.125
- cotangent: float32 [4096, 2048], P('dp'), may hold values from -6 to 6
Outputs:
- hidden_states: float32 [4096, 2048], P('dp')
- input_grad: float32 [4096, 2048], P('dp')
- query_grad: float32 [2048, 2048], P('dp', 'mp')
- key_grad: float32 [2048, 256], P('dp', 'mp')
- value_grad: float32 [2048, 256], P('dp', 'mp')
- out_grad: float32 [2048, 2048], P('mp', 'dp')
- gate_grad: float32 [2048, 5632], P('dp', 'mp')
- up_grad: float32 [2048, 5632], P('dp', 'mp')
- down_grad: float32 [5632, 2048], P('mp', 'dp')
- norm_first_grad: float32 [2048], P('dp')
- norm_second_grad: float32 [2048], P('dp')
- router_grad: float32 [2048], P('dp')
The draws below stay inside these ranges and needn't reach their ends.
Inputs may be any that keep to these rules, and one draw needn't show every extreme that they name: `second_slot`: among the 128 tokens of one device the values other than -1 are distinct; -1 marks tokens of depth 1 and tokens that the capacity drops; some device uses every value. `third_slot`: among the 128 tokens of one device the values other than -1 are distinct; a token has one only if it has depth 3 and a second_slot; some device uses every value.
All inputs are finite; a program needn't handle non-finite values.
Results may differ from the reference program's by a relative error of at most 0.035.
Values may be sent and summed in bfloat16 or wider, within the bound.
A program may use at most 192 MiB of HBM per device.

```python
import math
import jax
import jax.numpy as jnp
from jax import lax

D = 2048
H = 32
KV = 4
HD = 64
FF = 5632
TOK_DEV = 128
SECOND_SLOTS = 96
THIRD_SLOTS = 64
TOKENS = 4096


def routing_plan(key):
    blocks = TOKENS // TOK_DEV
    parts = jax.random.split(key, 6)
    second = jax.random.randint(parts[0], (blocks,), TOK_DEV // 3, TOK_DEV + 1)
    fullest = jax.random.randint(parts[1], (), 0, blocks)
    second = second.at[fullest].set(TOK_DEV)
    third = jax.random.randint(parts[2], (blocks,), TOK_DEV // 8, second + 1)
    third = third.at[fullest].set(TOK_DEV)
    order = jax.vmap(lambda item: jax.random.permutation(item, TOK_DEV))(jax.random.split(parts[3], blocks))
    ranks = jnp.argsort(order, axis=1).astype(jnp.int32)
    depths = 1 + (ranks < second[:, None]).astype(jnp.int32) + (ranks < third[:, None]).astype(jnp.int32)
    return (ranks, second, third, depths, parts)


def slot_table(ranks, limit, capacity, key):
    blocks = ranks.shape[0]
    table = jax.vmap(lambda item: jax.random.permutation(item, capacity))(jax.random.split(key, blocks))
    picked = jnp.take_along_axis(table, jnp.minimum(ranks, capacity - 1), axis=1)
    used = ranks < jnp.minimum(limit, capacity)[:, None]
    return jnp.where(used, picked, -1).reshape(-1).astype(jnp.int32)


def draw_depths(key, part):
    ranks, second, third, depths, parts = routing_plan(key)
    return depths.reshape(-1).astype(jnp.int32)


def draw_second_slot(key, part):
    ranks, second, third, depths, parts = routing_plan(key)
    return slot_table(ranks, second, SECOND_SLOTS, parts[4])


def draw_third_slot(key, part):
    ranks, second, third, depths, parts = routing_plan(key)
    return slot_table(ranks, third, THIRD_SLOTS, parts[5])


def steps_of(key, extent, cuts, low, top_value):
    factor_of = 1.0
    for dim, blocks in cuts:
        draws = jax.random.uniform(jax.random.fold_in(jax.random.fold_in(key, 6), dim), (blocks,), jnp.float32, low / len(cuts), top_value / len(cuts))
        factor_of = factor_of * jnp.repeat(jnp.exp(draws), extent[dim] // blocks).reshape((-1,) + (1,) * (len(extent) - 1 - dim))
    return factor_of


def centred(stream_key, dims, width, most, cuts=(), kind=jnp.bfloat16):
    loudness = steps_of(stream_key, dims, cuts, -0.22, 0.18) if cuts else 1.0
    values = jax.random.normal(stream_key, dims, jnp.float32) * width * loudness
    return jnp.minimum(jnp.maximum(values, -most), most).astype(kind)


def setup_inputs(seed: int = 0) -> dict:
    key_of = jax.random.split(jax.random.key(seed), 16)
    tokens = centred(key_of[0], (TOKENS, D), 1.0, 6.0, ((0, 32),))
    depths = draw_depths(jax.random.fold_in(key_of[15], 71), 0)
    second_slot = draw_second_slot(jax.random.fold_in(key_of[15], 71), 0)
    third_slot = draw_third_slot(jax.random.fold_in(key_of[15], 71), 0)
    w_query = centred(key_of[4], (D, H * HD), D ** -0.5, 0.125, ((0, 32), (1, 4)))
    w_key = centred(key_of[5], (D, KV * HD), D ** -0.5, 0.125, ((0, 32), (1, 4)))
    w_value = centred(key_of[6], (D, KV * HD), D ** -0.5, 0.125, ((0, 32), (1, 4)))
    w_out = centred(key_of[7], (H * HD, D), HD ** -0.5, 0.75, ((0, 4), (1, 32)))
    w_gate = centred(key_of[8], (D, FF), D ** -0.5, 0.125, ((0, 32), (1, 4)))
    w_up = centred(key_of[9], (D, FF), D ** -0.5, 0.125, ((0, 32), (1, 4)))
    w_down = centred(key_of[10], (FF, D), FF ** -0.5, 0.078125, ((0, 4), (1, 32)))
    norm_first = jnp.clip(1.0 + 0.1 * jax.random.normal(key_of[11], (D,), jnp.float32), 0.5, 1.5).astype(jnp.bfloat16)
    norm_second = jnp.clip(1.0 + 0.1 * jax.random.normal(key_of[12], (D,), jnp.float32), 0.5, 1.5).astype(jnp.bfloat16)
    router = centred(key_of[13], (D,), D ** -0.5, 0.125, ((0, 32),))
    cotangent = centred(key_of[14], (TOKENS, D), 1.0, 6.0, ((0, 32),), jnp.float32)
    return dict(tokens=tokens, depths=depths, second_slot=second_slot, third_slot=third_slot, w_query=w_query, w_key=w_key, w_value=w_value, w_out=w_out, w_gate=w_gate, w_up=w_up, w_down=w_down, norm_first=norm_first, norm_second=norm_second, router=router, cotangent=cotangent)


EPS = 1e-05
NEG = -1e+30
ROPE_BASE = 10000.0

@jax.custom_vjp
def low(v):
    return lax.optimization_barrier(v.astype(jnp.bfloat16)).astype(jnp.float32)

@jax.custom_vjp
def low_back(v):
    return v

def low_keep(v):
    return (low(v), None)

def low_pass(kept, grad):
    return (grad,)

def back_keep(v):
    return (v, None)

def back_low(kept, grad):
    return (low(grad),)
low.defvjp(low_keep, low_pass)
low_back.defvjp(back_keep, back_low)

def matmul(left, right):
    return jnp.dot(left, right, precision=lax.Precision.HIGHEST)

def norm_rows(values, gain):
    return values * lax.rsqrt(lax.optimization_barrier(jnp.mean(values * values, axis=-1, keepdims=True)) + EPS) * gain

def frequencies():
    return jnp.exp(jnp.arange(HD // 2, dtype=jnp.float32) * (-2.0 * math.log(ROPE_BASE) / HD))

def rotate(values, cosine, sine):
    half = values.shape[-1] // 2
    first = values[..., :half]
    second = values[..., half:]
    return jnp.concatenate([first * cosine - second * sine, second * cosine + first * sine], axis=-1)

def attend(query, keys, values, place, keep):
    count = query.shape[0]
    groups = H // KV
    block = math.gcd(count, 512)
    blocks = count // block
    scale = HD ** (-0.5)
    query_blocks = query.reshape(blocks, block, KV, groups, HD)
    place_blocks = place.reshape(blocks, block)

    def one_block(pair):
        part_query, part_place = pair
        scores = jnp.einsum('qkgd,tkd->kgqt', part_query, keys, precision=lax.Precision.HIGHEST)
        scores = low_back(scores * scale)
        allowed = (place[None, None, None, :] <= part_place[None, None, :, None]) & keep[None, None, None, :]
        scores = jnp.where(allowed, scores, NEG)
        weights = low(jax.nn.softmax(scores, axis=-1))
        return jnp.einsum('kgqt,tkd->qkgd', weights, values, precision=lax.Precision.HIGHEST)
    mixed = lax.map(jax.checkpoint(one_block), (query_blocks, place_blocks))
    return mixed.reshape(count, H * HD)

def reference(tokens, depths, second_slot, third_slot, w_query, w_key, w_value, w_out, w_gate, w_up, w_down, norm_first, norm_second, router, cotangent):
    place = jnp.arange(TOKENS, dtype=jnp.int32)
    angle = place.astype(jnp.float32)[:, None] * frequencies()[None, :]
    cosine = jnp.cos(angle)[:, None, :]
    sine = jnp.sin(angle)[:, None, :]
    actives = [jnp.ones((TOKENS,), dtype=bool), (depths >= 2) & (second_slot >= 0), (depths >= 3) & (third_slot >= 0)]

    def forward(state, wq_full, wk_full, wv_full, wo_full, wg_full, wu_full, wd_full, gain_first, gain_second, router_full):
        for keep in actives:
            rows = low_back(low(state))
            gate = jax.nn.sigmoid(matmul(rows, router_full))
            normed = low(norm_rows(rows, gain_first))
            query = low(rotate(low_back(matmul(normed, wq_full)).reshape(TOKENS, H, HD), cosine, sine))
            keys = low(rotate(low_back(matmul(normed, wk_full)).reshape(TOKENS, KV, HD), cosine, sine))
            values = low(low_back(matmul(normed, wv_full))).reshape(TOKENS, KV, HD)
            mixed = low_back(low(attend(query, keys, values, place, keep)))
            attn = low_back(matmul(mixed, wo_full))
            middle = rows + attn
            second = low(norm_rows(middle, gain_second))
            gate_part = low_back(matmul(second, wg_full))
            up_part = low_back(matmul(second, wu_full))
            hidden = low(jax.nn.silu(gate_part) * up_part)
            ffn = low_back(matmul(hidden, wd_full))
            update = low_back(low(gate[:, None] * (attn + ffn)))
            state = state + jnp.where(keep[:, None], update, 0.0)
        return state
    params = tuple((item.astype(jnp.float32) for item in (w_query, w_key, w_value, w_out, w_gate, w_up, w_down, norm_first, norm_second, router)))
    hidden_states, pullback = jax.vjp(forward, tokens.astype(jnp.float32), *params)
    grads = pullback(cotangent)
    return (hidden_states, grads[0], grads[1], grads[2], grads[3], grads[4], grads[5], grads[6], grads[7], grads[8], grads[9], grads[10])
```

```python
import math

import jax
import jax.numpy as jnp
from jax import lax
from jax.sharding import PartitionSpec as P

HD = 64
SECOND_SLOTS = 96
THIRD_SLOTS = 64
EPS = 1e-05
NEG = -1e30
ROPE_BASE = 10000.0
FAR = 1073741824
BF = jnp.bfloat16
F32 = jnp.float32


def dot_nn(left, right):
    return lax.dot_general(left, right, (((1,), (0,)), ((), ())), preferred_element_type=F32)


def dot_nt(left, right):
    return lax.dot_general(left, right, (((1,), (1,)), ((), ())), preferred_element_type=F32)


def dot_tn(left, right):
    return lax.dot_general(left, right, (((0,), (0,)), ((), ())), preferred_element_type=F32)


def unit_of(values):
    factor = lax.rsqrt(jnp.mean(values * values, axis=-1, keepdims=True) + EPS)
    return values * factor, factor


def unit_back(shaped, unit, factor):
    return factor * (shaped - unit * jnp.mean(shaped * unit, axis=-1, keepdims=True))


def rotary_tables(place):
    freq = jnp.exp(jnp.arange(HD // 2, dtype=F32) * (-2.0 * math.log(ROPE_BASE) / HD))
    angle = place.astype(F32)[:, None] * freq[None, :]
    cosine, sine = jnp.cos(angle), jnp.sin(angle)
    return cosine, sine


def wide_tables(cosine, sine, heads):
    one = jnp.concatenate([cosine, cosine], axis=1)
    two = jnp.concatenate([-sine, sine], axis=1)
    rest = one.shape
    return (
        jnp.concatenate([jnp.tile(one, (1, heads + 1)), jnp.ones(rest, F32)], axis=1),
        jnp.concatenate([jnp.tile(two, (1, heads + 1)), jnp.zeros(rest, F32)], axis=1),
    )


def swap_halves(values):
    rows, width = values.shape
    parts = values.reshape(rows, width // HD, 2, HD // 2)
    return parts[:, :, ::-1, :].reshape(rows, width)


def scores_of(query, query_place, key_part, place_part):
    scores = dot_nt(query, key_part)
    return jnp.where(place_part[None, :] <= query_place[:, None], scores, NEG)


def key_blocks(packed, key_place):
    block = 512
    blocks = packed.shape[0] // block
    return packed.reshape(blocks, block, 2 * HD), key_place.reshape(blocks, block)


def attend_forward(query, packed, key_place, query_place):
    width = query.shape[0]

    def one_block(carry, part):
        top, total, acc = carry
        scores = scores_of(query, query_place, part[0][:, :HD], part[1])
        peak = jnp.maximum(top, jnp.max(scores, axis=-1))
        weights = jnp.exp(scores - peak[:, None])
        fade = jnp.exp(top - peak)
        total = total * fade + jnp.sum(weights, axis=-1)
        acc = acc * fade[:, None] + dot_nn(weights.astype(BF), part[0][:, HD:])
        return (peak, total, acc), None

    start = (jnp.full((width,), NEG, F32), jnp.zeros((width,), F32), jnp.zeros((width, HD), F32))
    (top, total, acc), unused = lax.scan(one_block, start, key_blocks(packed, key_place))
    return acc / total[:, None], top + jnp.log(total)


def attend_backward(query, packed, key_place, query_place, log_total, grad_mixed, delta):
    def one_block(grad_query, part):
        keys, values = part[0][:, :HD], part[0][:, HD:]
        weights = jnp.exp(scores_of(query, query_place, keys, part[1]) - log_total[:, None])
        grad_weights = dot_nt(grad_mixed, values)
        grad_scores = (weights * (grad_weights - delta[:, None])).astype(BF)
        grad_query = grad_query + dot_nn(grad_scores, keys)
        grad_keys = dot_tn(grad_scores, query)
        grad_values = dot_tn(weights.astype(BF), grad_mixed)
        return grad_query, jnp.concatenate([grad_keys, grad_values], axis=1)

    grad_query, grad_packed = lax.scan(
        one_block, jnp.zeros(query.shape, F32), key_blocks(packed, key_place)
    )
    return grad_query, grad_packed.reshape(packed.shape)


def stack_heads(values):
    count = values.shape[0]
    return values.reshape(count, -1, HD).transpose(1, 0, 2).reshape(-1, HD)


def unstack_heads(values, count):
    return values.reshape(-1, count, HD).transpose(1, 0, 2).reshape(count, -1)


def sum_mp(values):
    return lax.psum(values.astype(BF), "mp").astype(F32)


def split_columns(heads, hidden):
    ends, total = [], 0
    for width in (heads * HD + 2 * HD, heads * HD, hidden, hidden, hidden, 128):
        ends.append((total, total + width))
        total += width
    return ends


def local(
    tokens, depths, second_slot, third_slot, w_query, w_key, w_value, w_out, w_gate, w_up,
    w_down, norm_first, norm_second, router, cotangent,
):
    me = lax.axis_index("dp")
    devices = lax.axis_size("dp")
    rows = tokens.shape[0]
    heads = w_query.shape[1] // HD
    hidden_width = w_gate.shape[1]
    depth = w_query.shape[0]
    spans = split_columns(heads, hidden_width)

    actives = (
        (depths >= 2) & (second_slot >= 0),
        (depths >= 3) & (third_slot >= 0),
    )
    picks, marks = [], []
    for active, slot, capacity in zip(actives, (second_slot, third_slot), (SECOND_SLOTS, THIRD_SLOTS)):
        pick = (jnp.arange(capacity)[:, None] == slot[None, :]) & active[None, :]
        picks.append(pick.astype(BF))
        mark = jnp.min(jnp.where(pick, jnp.arange(rows, dtype=jnp.int32)[None, :], rows), axis=1)
        marks.append(mark)

    column = lambda a: a.reshape(depth, 1).astype(BF)
    second_mark = jnp.pad(marks[0], (0, 2 * depth - SECOND_SLOTS), constant_values=rows)
    extras = jnp.concatenate(
        [
            column(norm_first),
            column(norm_second),
            column(router),
            column(second_mark[:depth]),
            column(second_mark[depth:]),
            column(marks[1]),
            jnp.zeros((depth, 122), BF),
        ],
        axis=1,
    )
    shard = jnp.concatenate(
        [w_query, w_key, w_value, w_out.T, w_gate, w_up, w_down.T, extras], axis=1
    )
    full = lax.all_gather(shard, "dp", axis=0, tiled=True)
    w_qkv, w_o, w_g, w_u, w_d, extra = [full[:, a:b] for a, b in spans]
    extra = extra[:, :8].astype(F32)
    gain_first, gain_second, gain_router = extra[:, 0], extra[:, 1], extra[:, 2]
    marks_all = extra[:, 3:6].astype(jnp.int32).reshape(devices, depth, 3)
    second_all = jnp.concatenate([marks_all[:, :, 0], marks_all[:, : SECOND_SLOTS - depth, 1]], axis=1)
    third_all = marks_all[:, :, 2]
    base = (jnp.arange(devices, dtype=jnp.int32) * rows)[:, None]

    def place_of(mark, offset):
        return jnp.where(mark < rows, mark + offset, FAR)

    own = jnp.arange(rows, dtype=jnp.int32)
    levels = (
        (rows, None, own + me * rows, (jnp.arange(devices * rows, dtype=jnp.int32))),
        (SECOND_SLOTS, picks[0], place_of(marks[0], me * rows), place_of(second_all, base).reshape(-1)),
        (THIRD_SLOTS, picks[1], place_of(marks[1], me * rows), place_of(third_all, base).reshape(-1)),
    )
    state = tokens.astype(F32)
    kept = []
    for count, pick, place, key_place in levels:
        rows_in = state.astype(BF)
        if pick is not None:
            rows_in = dot_nn(pick, rows_in).astype(BF)
        level = rows_in.astype(F32)
        unit, factor = unit_of(level)
        normed = (unit * gain_first).astype(BF)
        tables = wide_tables(*rotary_tables(jnp.where(place == FAR, 0, place)), heads)
        qkv = dot_nn(normed, w_qkv)
        qkv = (qkv * tables[0] + swap_halves(qkv) * tables[1]).astype(BF)
        query = stack_heads(qkv[:, : heads * HD]) * BF(HD**-0.5)
        packed = lax.all_gather(qkv[:, heads * HD :], "dp", axis=0, tiled=True)
        query_place = jnp.tile(place, heads)
        mixed, log_total = attend_forward(query, packed, key_place, query_place)
        mixed_rows = unstack_heads(mixed, count).astype(BF)
        attn = sum_mp(dot_nt(mixed_rows, w_o))
        middle = level + attn
        unit_mid, factor_mid = unit_of(middle)
        second = (unit_mid * gain_second).astype(BF)
        gate_part, up_part = dot_nn(second, w_g), dot_nn(second, w_u)
        hidden = (jax.nn.silu(gate_part) * up_part).astype(BF)
        ffn = sum_mp(dot_nt(hidden, w_d))
        gate = jax.nn.sigmoid(jnp.sum(level * gain_router, axis=-1, keepdims=True))
        update = (gate * (attn + ffn)).astype(BF)
        if pick is not None:
            update = dot_tn(pick, update)
        state = state + update.astype(F32)
        kept.append(
            (pick, level, unit, factor, normed, tables, query, packed, key_place, query_place,
             mixed, log_total, mixed_rows, attn, unit_mid, factor_mid, second, gate_part, up_part, hidden, ffn, gate)
        )

    flow = cotangent
    terms = []
    for items in reversed(kept):
        (pick, level, unit, factor, normed, tables, query, packed, key_place, query_place,
         mixed, log_total, mixed_rows, attn, unit_mid, factor_mid, second, gate_part, up_part, hidden, ffn, gate) = items
        count = level.shape[0]
        grad_update = flow.astype(BF)
        if pick is not None:
            grad_update = dot_nn(pick, grad_update)
        grad_update = grad_update.astype(F32)
        gate_logit = jnp.sum(grad_update * (attn + ffn), axis=-1, keepdims=True) * gate * (1.0 - gate)
        grad_ffn = (gate * grad_update).astype(BF)
        grad_hidden = dot_nn(grad_ffn, w_d)
        sigma = jax.nn.sigmoid(gate_part)
        grad_gate_part = (grad_hidden * up_part * sigma * (1.0 + gate_part * (1.0 - sigma))).astype(BF)
        grad_up_part = (grad_hidden * gate_part * sigma).astype(BF)
        grad_second = sum_mp(dot_nt(grad_gate_part, w_g) + dot_nt(grad_up_part, w_u))
        grad_middle = unit_back(grad_second * gain_second, unit_mid, factor_mid)
        grad_attn = (gate * grad_update + grad_middle).astype(BF)
        grad_mixed = dot_nn(grad_attn, w_o).astype(BF)
        grad_heads = stack_heads(grad_mixed)
        delta = jnp.sum(grad_heads.astype(F32) * mixed, axis=-1)
        grad_query, grad_packed = attend_backward(
            query, packed, key_place, query_place, log_total, grad_heads, delta
        )
        own_packed = lax.psum_scatter(
            grad_packed.astype(BF), "dp", scatter_dimension=0, tiled=True
        ).astype(F32)
        grad_qkv = jnp.concatenate(
            [unstack_heads(grad_query, count) * HD**-0.5, own_packed], axis=1
        )
        grad_qkv = (grad_qkv * tables[0] - swap_halves(grad_qkv) * tables[1]).astype(BF)
        grad_normed = sum_mp(dot_nt(grad_qkv, w_qkv))
        grad_rows = unit_back(grad_normed * gain_first, unit, factor) + grad_middle + gate_logit * gain_router
        grad_rows = grad_rows.astype(BF)
        if pick is not None:
            grad_rows = dot_tn(pick, grad_rows)
        flow = flow + grad_rows.astype(F32)
        terms.append(
            (normed, grad_qkv, grad_attn, mixed_rows, second,
             grad_gate_part, grad_up_part, grad_ffn, hidden,
             jnp.sum(grad_normed * unit, axis=0),
             jnp.sum(grad_second * unit_mid, axis=0),
             jnp.sum(level * gate_logit, axis=0))
        )
    joined = [jnp.concatenate(list(parts), axis=0) for parts in list(zip(*terms))[:9]]
    normed, grad_qkv, grad_attn, mixed_rows, second, grad_gate_part, grad_up_part, grad_ffn, hidden = joined
    vectors = [sum(parts) for parts in list(zip(*terms))[9:]]
    totals = jnp.concatenate(
        [
            dot_tn(normed, grad_qkv).astype(BF),
            dot_tn(grad_attn, mixed_rows).astype(BF),
            dot_tn(second, grad_gate_part).astype(BF),
            dot_tn(second, grad_up_part).astype(BF),
            dot_tn(grad_ffn, hidden).astype(BF),
            jnp.pad(jnp.stack(vectors, axis=1), ((0, 0), (0, 125))).astype(BF),
        ],
        axis=1,
    )
    reduced = lax.psum_scatter(totals, "dp", scatter_dimension=0, tiled=True).astype(F32)
    qkv, out_t, gate_g, up_g, down_t, vec = [reduced[:, a:b] for a, b in spans]
    q_width = heads * HD
    return (
        state, flow,
        qkv[:, :q_width], qkv[:, q_width : q_width + HD], qkv[:, q_width + HD :],
        out_t.T, gate_g, up_g, down_t.T, vec[:, 0], vec[:, 1], vec[:, 2],
    )


def solution(mesh):
    in_specs = (
        P("dp", None), P("dp"), P("dp"), P("dp"), P("dp", "mp"), P("dp", "mp"), P("dp", "mp"),
        P("mp", "dp"), P("dp", "mp"), P("dp", "mp"), P("mp", "dp"), P("dp"), P("dp"), P("dp"),
        P("dp", None),
    )
    out_specs = (
        P("dp", None), P("dp", None), P("dp", "mp"), P("dp", "mp"), P("dp", "mp"), P("mp", "dp"),
        P("dp", "mp"), P("dp", "mp"), P("mp", "dp"), P("dp"), P("dp"), P("dp"),
    )
    return jax.shard_map(local, mesh=mesh, in_specs=in_specs, out_specs=out_specs, check_vma=False)
```

```python
import functools
import math

import jax
import jax.numpy as jnp
from jax import lax
from jax.experimental import pallas as pl
from jax.experimental.pallas import tpu as pltpu
from jax.sharding import PartitionSpec as P

HD = 64
SECOND_SLOTS = 96
THIRD_SLOTS = 64
EPS = 1e-05
NEG = -1e30
ROPE_BASE = 10000.0
FAR = 1073741824
BF = jnp.bfloat16
F32 = jnp.float32
MESH = pl.DeviceIdType.MESH
LANES = 128
VMEM_LIMIT = 58 * 1024 * 1024


def dot_nn(left, right):
    return lax.dot_general(left, right, (((1,), (0,)), ((), ())), preferred_element_type=F32)


def dot_nt(left, right):
    return lax.dot_general(left, right, (((1,), (1,)), ((), ())), preferred_element_type=F32)


def dot_tn(left, right):
    return lax.dot_general(left, right, (((0,), (0,)), ((), ())), preferred_element_type=F32)


def unit_of(values):
    factor = lax.rsqrt(jnp.mean(values * values, axis=-1, keepdims=True) + EPS)
    return values * factor, factor


def unit_back(shaped, unit, factor):
    return factor * (shaped - unit * jnp.mean(shaped * unit, axis=-1, keepdims=True))


def sigmoid(values):
    return 1.0 / (1.0 + jnp.exp(-values))


def lanes_of(shape):
    return lax.broadcasted_iota(jnp.int32, shape, 1)


def swap_halves(tile):
    first = lax.rem(lanes_of(tile.shape), HD) < HD // 2
    return jnp.where(first, pltpu.roll(tile, LANES - HD // 2, 1), pltpu.roll(tile, HD // 2, 1))


def tile_of(values, index):
    return values[:, index * LANES : (index + 1) * LANES]


def signal_all(group, me, axis):
    barrier = pltpu.get_barrier_semaphore()
    for k in range(1, group):
        pl.semaphore_signal(
            barrier, inc=1, device_id={axis: lax.rem(me + k, group)}, device_id_type=MESH
        )
    pl.semaphore_wait(barrier, group - 1)


def sum_over_mp(group, me, make_chunk, send, recv, full, sems):
    order = (2, 1, 3)
    copies = []
    for k in order:
        peer = lax.rem(me + k, group)
        send[k - 1] = make_chunk(peer).astype(BF)
        copy = pltpu.make_async_remote_copy(
            src_ref=send.at[k - 1], dst_ref=recv.at[k - 1],
            send_sem=sems.at[0, k - 1], recv_sem=sems.at[1, k - 1],
            device_id={"mp": peer}, device_id_type=MESH,
        )
        copy.start()
        copies.append(copy)
    total = make_chunk(me).astype(BF).astype(F32)
    for k, copy in zip(order, copies):
        copy.wait_recv()
        total = total + recv[k - 1].astype(F32)
    full[me] = total.astype(BF)
    backs = []
    for k in order:
        peer = lax.rem(me + k, group)
        copy = pltpu.make_async_remote_copy(
            src_ref=full.at[me], dst_ref=full.at[me],
            send_sem=sems.at[2, k - 1], recv_sem=sems.at[3, k - 1],
            device_id={"mp": peer}, device_id_type=MESH,
        )
        copy.start()
        backs.append(copy)
    for copy in backs:
        copy.wait_recv()
    for copy in copies + backs:
        copy.wait_send()
    return jnp.concatenate([full[c] for c in range(group)], axis=1)


def attend_kernel(n, heads, devices, group, picked, *refs):
    refs = list(refs)
    source = refs.pop(0)
    pick = refs.pop(0) if picked else None
    key_place = refs.pop(0) if picked else None
    query_place, gains, cosine, sine, w_hbm = [refs.pop(0) for _ in range(5)]
    rows_out, normed_out, packed_out, query_out, mixed_t_out, log_out, mixed_out = [
        refs.pop(0) for _ in range(7)
    ]
    w_v, packed, query_t, top, total, acc, w_sem, out_sem, send_sems, recv_sems = refs
    me = lax.axis_index("dp")
    width = heads * n
    load_w = pltpu.make_async_copy(w_hbm, w_v, w_sem)
    load_w.start()

    barrier = pltpu.get_barrier_semaphore()

    def greet(e, carry):
        pl.semaphore_signal(barrier, inc=1, device_id={"dp": e}, device_id_type=MESH)
        return carry

    lax.fori_loop(0, me, greet, 0)

    if picked:
        rows = dot_nn(pick[...], source[...].astype(BF)).astype(BF)
    else:
        rows = source[...]
    rows_out[...] = rows
    unit, unused = unit_of(rows.astype(F32))
    normed = (unit * gains[0:1, :]).astype(BF)
    normed_out[...] = normed
    load_w.wait()
    tiles = []
    for t in range(heads // 2 + 1):
        if t % 2 == 0:
            last = min((t + 2) * LANES, (heads // 2 + 1) * LANES)
            both = dot_nn(normed, w_v[:, t * LANES : last])
        part = tile_of(both, t % 2)
        cut = slice(t * LANES, (t + 1) * LANES)
        tiles.append(part * cosine[:, cut] + swap_halves(part) * sine[:, cut])
    packed[me] = tiles[-1].astype(BF)

    @pl.when(me < devices - 1)
    def _():
        pl.semaphore_wait(barrier, devices - 1 - me)

    def send_copy(e, source_index):
        return pltpu.make_async_remote_copy(
            src_ref=packed.at[me], dst_ref=packed.at[me],
            send_sem=send_sems.at[e], recv_sem=recv_sems.at[source_index],
            device_id={"dp": e}, device_id_type=MESH,
        )

    def send(e, carry):
        send_copy(e, me).start()
        return carry

    lax.fori_loop(me + 1, devices, send, 0)

    def clear(e, carry):
        packed[e] = jnp.zeros((n, 2 * HD), BF)
        return carry

    lax.fori_loop(me + 1, devices, clear, 0)

    left = lanes_of((n, LANES)) < HD
    for t in range(heads // 2):
        scaled = tiles[t].astype(BF).astype(F32) * HD**-0.5
        query_out[2 * t * n : (2 * t + 1) * n, :] = jnp.where(left, scaled, 0.0).astype(BF)
        query_out[(2 * t + 1) * n : (2 * t + 2) * n, :] = jnp.where(
            left, pltpu.roll(scaled, HD, 1), 0.0
        ).astype(BF)
    query_t[...] = query_out[...].T
    top[...] = jnp.full((1, width), NEG, F32)
    total[...] = jnp.zeros((1, width), F32)
    acc[...] = jnp.zeros((2 * HD, width), F32)

    def one_block(b, carry):
        for g in range(group):
            e = b * group + g

            @pl.when(e < me)
            def _():
                send_copy(me, e).wait_recv()

        part = packed[pl.ds(b * group, group)].reshape(group * n, 2 * HD)
        scores = dot_nn(part, query_t[...])
        if picked:
            start = pl.multiple_of(b * (group * n), group * n)
            place = key_place[pl.ds(start, group * n), :]
        else:
            place = lax.broadcasted_iota(jnp.int32, (group * n, LANES), 0) + b * (group * n)
        place = jnp.concatenate([place] * (width // LANES), axis=1)
        scores = jnp.where(place <= query_place[...], scores, NEG)
        peak = jnp.maximum(top[...], jnp.max(scores, axis=0, keepdims=True))
        weights = jnp.exp(scores - peak)
        fade = jnp.exp(top[...] - peak)
        total[...] = total[...] * fade + jnp.sum(weights, axis=0, keepdims=True)
        acc[...] = acc[...] * fade + dot_tn(part, weights.astype(BF))
        top[...] = peak
        return carry

    lax.fori_loop(0, me // group + 1, one_block, 0)
    mixed_t = acc[...] / total[...]
    mixed_t_out[...] = mixed_t
    log_out[...] = top[...] + jnp.log(total[...])
    mixed = mixed_t.T
    for t in range(heads // 2):
        even = mixed[2 * t * n : (2 * t + 1) * n, :]
        odd = mixed[(2 * t + 1) * n : (2 * t + 2) * n, :]
        mixed_out[:, t * LANES : (t + 1) * LANES] = jnp.where(
            left, pltpu.roll(even, HD, 1), odd
        ).astype(BF)
    keep = pltpu.make_async_copy(packed, packed_out, out_sem)
    keep.start()

    def sent(e, carry):
        send_copy(e, me).wait_send()
        return carry

    lax.fori_loop(me + 1, devices, sent, 0)
    keep.wait()


def vmem(count):
    return [pl.BlockSpec(memory_space=pltpu.VMEM)] * count


def attend(source, pick, key_place, query_place, gains, tables, w_qkv, heads, devices, n, ident):
    picked = pick is not None
    group = 512 // n if 512 % n == 0 else 4
    width = heads * n
    qkv_width = (heads + 2) * HD
    args = [source] + ([pick, key_place] if picked else []) + [query_place, gains, *tables, w_qkv]
    model = source.shape[1]
    return pl.pallas_call(
        functools.partial(attend_kernel, n, heads, devices, group, picked),
        out_shape=(
            jax.ShapeDtypeStruct((n, model), BF),
            jax.ShapeDtypeStruct((n, model), BF),
            jax.ShapeDtypeStruct((devices, n, 2 * HD), BF),
            jax.ShapeDtypeStruct((width, 2 * HD), BF),
            jax.ShapeDtypeStruct((2 * HD, width), F32),
            jax.ShapeDtypeStruct((1, width), F32),
            jax.ShapeDtypeStruct((n, heads * HD), BF),
        ),
        in_specs=vmem(len(args) - 1) + [pl.BlockSpec(memory_space=pl.ANY)],
        out_specs=tuple(vmem(2) + [pl.BlockSpec(memory_space=pl.ANY)] + vmem(4)),
        scratch_shapes=[
            pltpu.VMEM((model, qkv_width), BF),
            pltpu.VMEM((devices, n, 2 * HD), BF),
            pltpu.VMEM((2 * HD, width), BF),
            pltpu.VMEM((1, width), F32),
            pltpu.VMEM((1, width), F32),
            pltpu.VMEM((2 * HD, width), F32),
            pltpu.SemaphoreType.DMA(()),
            pltpu.SemaphoreType.DMA(()),
            pltpu.SemaphoreType.DMA((devices,)),
            pltpu.SemaphoreType.DMA((devices,)),
        ],
        compiler_params=pltpu.CompilerParams(
            collective_id=ident, has_side_effects=True, vmem_limit_bytes=VMEM_LIMIT
        ),
        cost_estimate=pl.CostEstimate(flops=4 * 10**9, bytes_accessed=10**7, transcendentals=0),
        name=f"attend_{n}",
    )(*args)


def attend_back_kernel(n, heads, devices, group, picked, *refs):
    refs = list(refs)
    key_place = refs.pop(0) if picked else None
    query_place, query, packed, mixed_t, log_total, grad_mixed, cosine, sine = [
        refs.pop(0) for _ in range(8)
    ]
    grad_out = refs.pop(0)
    query_t, grad_rows, grad_t, acc, delta, send_buf, recv_buf, send_sems, recv_sems = refs
    me = lax.axis_index("dp")
    barrier = pltpu.get_barrier_semaphore()

    def greet(e, carry):
        pl.semaphore_signal(barrier, inc=1, device_id={"dp": e}, device_id_type=MESH)
        return carry

    lax.fori_loop(me + 1, devices, greet, 0)

    left = lanes_of((n, LANES)) < HD
    for t in range(heads // 2):
        part = grad_mixed[:, t * LANES : (t + 1) * LANES].astype(F32)
        grad_rows[2 * t * n : (2 * t + 1) * n, :] = jnp.where(
            left, 0.0, pltpu.roll(part, HD, 1)
        ).astype(BF)
        grad_rows[(2 * t + 1) * n : (2 * t + 2) * n, :] = jnp.where(left, 0.0, part).astype(BF)
    query_t[...] = query[...].T
    grad_t[...] = grad_rows[...].T
    delta[...] = jnp.sum(grad_t[...].astype(F32) * mixed_t[...], axis=0, keepdims=True)
    acc[...] = jnp.zeros(acc.shape, F32)
    width = heads * n

    @pl.when(me > 0)
    def _():
        pl.semaphore_wait(barrier, me)

    def send_copy(e, source_index):
        return pltpu.make_async_remote_copy(
            src_ref=send_buf.at[e], dst_ref=recv_buf.at[source_index],
            send_sem=send_sems.at[e], recv_sem=recv_sems.at[source_index],
            device_id={"dp": e}, device_id_type=MESH,
        )

    def one_block(b, carry):
        part = packed[pl.ds(b * group, group)].reshape(group * n, 2 * HD)
        scores = dot_nn(part, query_t[...])
        if picked:
            start = pl.multiple_of(b * (group * n), group * n)
            place = key_place[pl.ds(start, group * n), :]
        else:
            place = lax.broadcasted_iota(jnp.int32, (group * n, LANES), 0) + b * (group * n)
        place = jnp.concatenate([place] * (width // LANES), axis=1)
        scores = jnp.where(place <= query_place[...], scores, NEG)
        weights = jnp.exp(scores - log_total[...])
        grad_weights = dot_nn(part, grad_t[...])
        grad_scores = (weights * (grad_weights - delta[...])).astype(BF)
        grad_part = dot_nn(grad_scores, query[...]) + dot_nn(weights.astype(BF), grad_rows[...])
        send_buf[pl.ds(b * group, group)] = grad_part.astype(BF).reshape(group, n, 2 * HD)
        acc[...] += dot_tn(part, grad_scores)
        for g in range(group):
            e = b * group + g

            @pl.when(e < me)
            def _():
                send_copy(e, me).start()

        return carry

    lax.fori_loop(0, me // group + 1, one_block, 0)

    grad_query = acc[...].T * HD**-0.5
    outs = []
    for t in range(heads // 2):
        even = grad_query[2 * t * n : (2 * t + 1) * n, :]
        odd = grad_query[(2 * t + 1) * n : (2 * t + 2) * n, :]
        outs.append(jnp.where(left, even, pltpu.roll(odd, HD, 1)))

    def add(e, carry):
        send_copy(me, e).wait_recv()
        return carry + recv_buf[e].astype(F32)

    outs.append(lax.fori_loop(me + 1, devices, add, send_buf[me].astype(F32)))
    for t, part in enumerate(outs):
        cut = slice(t * LANES, (t + 1) * LANES)
        grad_out[:, cut] = (part * cosine[:, cut] - swap_halves(part) * sine[:, cut]).astype(BF)

    def sent(e, carry):
        send_copy(e, me).wait_send()
        return carry

    lax.fori_loop(0, me, sent, 0)


def attend_back(key_place, query_place, query, packed, mixed_t, log_total, grad_mixed, tables, heads, devices, n, ident):
    picked = key_place is not None
    group = 512 // n if 512 % n == 0 else 4
    width = heads * n
    args = ([key_place] if picked else []) + [
        query_place, query, packed, mixed_t, log_total, grad_mixed, *tables
    ]
    return pl.pallas_call(
        functools.partial(attend_back_kernel, n, heads, devices, group, picked),
        out_shape=jax.ShapeDtypeStruct((n, (heads + 2) * HD), BF),
        in_specs=vmem(len(args)),
        out_specs=pl.BlockSpec(memory_space=pltpu.VMEM),
        scratch_shapes=[
            pltpu.VMEM((2 * HD, width), BF),
            pltpu.VMEM((width, 2 * HD), BF),
            pltpu.VMEM((2 * HD, width), BF),
            pltpu.VMEM((2 * HD, width), F32),
            pltpu.VMEM((1, width), F32),
            pltpu.VMEM((devices, n, 2 * HD), BF),
            pltpu.VMEM((devices, n, 2 * HD), BF),
            pltpu.SemaphoreType.DMA((devices,)),
            pltpu.SemaphoreType.DMA((devices,)),
        ],
        compiler_params=pltpu.CompilerParams(
            collective_id=ident, has_side_effects=True, vmem_limit_bytes=VMEM_LIMIT
        ),
        cost_estimate=pl.CostEstimate(flops=10**10, bytes_accessed=10**7, transcendentals=0),
        name=f"attend_back_{n}",
    )(*args)


def feed_kernel(n, mp, picked, *refs):
    refs = list(refs)
    state, rows_in, mixed = [refs.pop(0) for _ in range(3)]
    pick = refs.pop(0) if picked else None
    gains, w_hbm = refs.pop(0), refs.pop(0)
    attn_out, ffn_out, second_out, parts_out, state_out = [refs.pop(0) for _ in range(5)]
    w_o, w_gu, w_d, hidden, w_sems, send_a, recv_a, full_a, sems_a, send_b, recv_b, full_b, sems_b = refs
    me = lax.axis_index("mp")
    wide_o, wide_gu, wide_d = w_o.shape[1], w_gu.shape[1], w_d.shape[1]
    loads = []
    start = 0
    for index, (ref, wide) in enumerate(((w_o, wide_o), (w_gu, wide_gu), (w_d, wide_d))):
        load = pltpu.make_async_copy(w_hbm.at[:, start : start + wide], ref, w_sems.at[index])
        load.start()
        loads.append(load)
        start += wide
    signal_all(mp, me, "mp")
    chunk = w_o.shape[0] // mp
    loads[0].wait()
    mixed_now = mixed[...]

    def out_chunk(c):
        return dot_nt(mixed_now, w_o[pl.ds(pl.multiple_of(c * chunk, chunk), chunk), :])

    attn = sum_over_mp(mp, me, out_chunk, send_a, recv_a, full_a, sems_a)
    attn_out[...] = attn
    level = rows_in[...].astype(F32)
    unit, unused = unit_of(level + attn.astype(F32))
    second = (unit * gains[1:2, :]).astype(BF)
    second_out[...] = second
    loads[1].wait()
    step = 256
    for t in range(wide_gu // step):
        parts_out[:, t * step : (t + 1) * step] = dot_nn(second, w_gu[:, t * step : (t + 1) * step])
    half = wide_gu // 2
    for t in range(half // LANES):
        cut = slice(t * LANES, (t + 1) * LANES)
        gate_part = parts_out[:, cut]
        up_part = parts_out[:, half + t * LANES : half + (t + 1) * LANES]
        hidden[:, cut] = (gate_part * sigmoid(gate_part) * up_part).astype(BF)
    loads[2].wait()
    hidden_now = hidden[...]

    def down_chunk(c):
        return dot_nt(hidden_now, w_d[pl.ds(pl.multiple_of(c * chunk, chunk), chunk), :])

    ffn = sum_over_mp(mp, me, down_chunk, send_b, recv_b, full_b, sems_b)
    ffn_out[...] = ffn
    gate = sigmoid(jnp.sum(level * gains[2:3, :], axis=-1, keepdims=True))
    update = (gate * (attn.astype(F32) + ffn.astype(F32))).astype(BF)
    if picked:
        state_out[...] = state[...].astype(F32) + dot_tn(pick[...], update)
    else:
        state_out[...] = state[...].astype(F32) + update.astype(F32)


def sum_scratch(mp, n, model):
    return [
        pltpu.VMEM((mp - 1, n, model // mp), BF),
        pltpu.VMEM((mp - 1, n, model // mp), BF),
        pltpu.VMEM((mp, n, model // mp), BF),
        pltpu.SemaphoreType.DMA((4, mp - 1)),
    ]


def feed(state, rows, mixed, pick, gains, w_rest, hidden_width, mp, n, ident):
    picked = pick is not None
    model = rows.shape[1]
    args = [state, rows, mixed] + ([pick] if picked else []) + [gains, w_rest]
    return pl.pallas_call(
        functools.partial(feed_kernel, n, mp, picked),
        out_shape=(
            jax.ShapeDtypeStruct((n, model), BF),
            jax.ShapeDtypeStruct((n, model), BF),
            jax.ShapeDtypeStruct((n, model), BF),
            jax.ShapeDtypeStruct((n, 2 * hidden_width), F32),
            jax.ShapeDtypeStruct(state.shape, F32),
        ),
        in_specs=vmem(len(args) - 1) + [pl.BlockSpec(memory_space=pl.ANY)],
        out_specs=tuple(vmem(5)),
        scratch_shapes=[
            pltpu.VMEM((model, mixed.shape[1]), BF),
            pltpu.VMEM((model, 2 * hidden_width), BF),
            pltpu.VMEM((model, hidden_width), BF),
            pltpu.VMEM((n, hidden_width), BF),
            pltpu.SemaphoreType.DMA((3,)),
            *sum_scratch(mp, n, model),
            *sum_scratch(mp, n, model),
        ],
        compiler_params=pltpu.CompilerParams(
            collective_id=ident, has_side_effects=True, vmem_limit_bytes=VMEM_LIMIT
        ),
        cost_estimate=pl.CostEstimate(flops=5 * 10**9, bytes_accessed=10**8, transcendentals=0),
        name=f"feed_{n}",
    )(*args)


def feed_back_kernel(tail_n, head_n, mp, tail_picked, head_picked, *refs):
    refs = list(refs)
    flow, gains = refs.pop(0), refs.pop(0)
    if tail_n:
        grad_qkv, tail_rows, tail_middle, tail_logit = [refs.pop(0) for _ in range(4)]
        tail_pick = refs.pop(0) if tail_picked else None
    if head_n:
        rows_in, attn, ffn, second, parts = [refs.pop(0) for _ in range(5)]
        head_pick = refs.pop(0) if head_picked else None
    if tail_n:
        w_first_hbm = refs.pop(0)
    if head_n:
        w_rest_hbm = refs.pop(0)
    if tail_n:
        flow_out, first_out, router_out = [refs.pop(0) for _ in range(3)]
    if head_n:
        attn_grad_out, middle_out, logit_out, mixed_out, parts_grad_out, hidden_out, ffn_grad_out, second_vec_out = [
            refs.pop(0) for _ in range(8)
        ]
    if tail_n:
        w_qkv, w_first_sem = refs.pop(0), refs.pop(0)
        send_a, recv_a, full_a, sems_a = [refs.pop(0) for _ in range(4)]
    if head_n:
        w_o, w_gu, w_d, w_sems = [refs.pop(0) for _ in range(4)]
        send_b, recv_b, full_b, sems_b = [refs.pop(0) for _ in range(4)]
    me = lax.axis_index("mp")
    if tail_n:
        load_first = pltpu.make_async_copy(w_first_hbm, w_qkv, w_first_sem)
        load_first.start()
    if head_n:
        loads = {}
        wide_o, wide_gu, wide_d = w_o.shape[1], w_gu.shape[1], w_d.shape[1]
        for index, (name, ref, start) in enumerate(
            (("d", w_d, wide_o + wide_gu), ("gu", w_gu, wide_o), ("o", w_o, 0))
        ):
            loads[name] = pltpu.make_async_copy(
                w_rest_hbm.at[:, start : start + ref.shape[1]], ref, w_sems.at[index]
            )
            loads[name].start()
    signal_all(mp, me, "mp")

    if tail_n:
        load_first.wait()
        grad_now = grad_qkv[...]
        chunk = w_qkv.shape[0] // mp

        def first_chunk(c):
            return dot_nt(grad_now, w_qkv[pl.ds(pl.multiple_of(c * chunk, chunk), chunk), :])

        grad_normed = sum_over_mp(mp, me, first_chunk, send_a, recv_a, full_a, sems_a).astype(F32)
        level = tail_rows[...].astype(F32)
        unit, factor = unit_of(level)
        first_out[...] = jnp.sum(grad_normed * unit, axis=0, keepdims=True)
        router_out[...] = jnp.sum(level * tail_logit[...], axis=0, keepdims=True)
        grad_rows = (
            unit_back(grad_normed * gains[0:1, :], unit, factor)
            + tail_middle[...]
            + tail_logit[...] * gains[2:3, :]
        ).astype(BF)
        if tail_picked:
            flow_now = flow[...] + dot_tn(tail_pick[...], grad_rows)
        else:
            flow_now = flow[...] + grad_rows.astype(F32)
        flow_out[...] = flow_now
    else:
        flow_now = flow[...]

    if head_n:
        grad_update = flow_now.astype(BF)
        if head_picked:
            grad_update = dot_nn(head_pick[...], grad_update)
        grad_update = grad_update.astype(F32)
        level = rows_in[...].astype(F32)
        attn_now = attn[...].astype(F32)
        gate = sigmoid(jnp.sum(level * gains[2:3, :], axis=-1, keepdims=True))
        logit = jnp.sum(grad_update * (attn_now + ffn[...].astype(F32)), axis=-1, keepdims=True)
        logit_out[...] = logit * gate * (1.0 - gate)
        grad_ffn = (gate * grad_update).astype(BF)
        ffn_grad_out[...] = grad_ffn
        half = wide_d
        loads["d"].wait()
        for t in range(half // LANES):
            cut = slice(t * LANES, (t + 1) * LANES)
            up_cut = slice(half + t * LANES, half + (t + 1) * LANES)
            if t % 2 == 0:
                both = dot_nn(grad_ffn, w_d[:, t * LANES : min((t + 2) * LANES, half)])
            grad_hidden = tile_of(both, t % 2)
            gate_part = parts[:, cut]
            up_part = parts[:, up_cut]
            sigma = sigmoid(gate_part)
            active = gate_part * sigma
            hidden_out[:, cut] = (active * up_part).astype(BF)
            parts_grad_out[:, cut] = (
                grad_hidden * up_part * sigma * (1.0 + gate_part * (1.0 - sigma))
            ).astype(BF)
            parts_grad_out[:, up_cut] = (grad_hidden * active).astype(BF)
        loads["gu"].wait()
        parts_now = parts_grad_out[...]
        chunk = w_gu.shape[0] // mp

        def second_chunk(c):
            return dot_nt(parts_now, w_gu[pl.ds(pl.multiple_of(c * chunk, chunk), chunk), :])

        grad_second = sum_over_mp(mp, me, second_chunk, send_b, recv_b, full_b, sems_b).astype(F32)
        unit, factor = unit_of(level + attn_now)
        second_vec_out[...] = jnp.sum(grad_second * unit, axis=0, keepdims=True)
        grad_middle = unit_back(grad_second * gains[1:2, :], unit, factor)
        middle_out[...] = grad_middle
        grad_attn = (gate * grad_update + grad_middle).astype(BF)
        attn_grad_out[...] = grad_attn
        loads["o"].wait()
        mixed_out[...] = dot_nn(grad_attn, w_o[...]).astype(BF)


def feed_back(flow, gains, tail, head, w_qkv, w_rest, hidden_width, mp, ident):
    model = flow.shape[1]
    mix = w_qkv.shape[1] - 2 * HD
    args, outs, scratch = [flow, gains], [], []
    tail_n = head_n = 0
    tail_picked = head_picked = False
    if tail is not None:
        *items, pick = tail
        tail_n, tail_picked = items[0].shape[0], pick is not None
        args += items + ([pick] if tail_picked else [])
    if head is not None:
        *items, pick = head
        head_n, head_picked = items[0].shape[0], pick is not None
        args += items + ([pick] if head_picked else [])
    in_vmem = len(args)
    if tail_n:
        args.append(w_qkv)
        outs += [
            jax.ShapeDtypeStruct(flow.shape, F32),
            jax.ShapeDtypeStruct((1, model), F32),
            jax.ShapeDtypeStruct((1, model), F32),
        ]
        scratch += [
            pltpu.VMEM(w_qkv.shape, BF),
            pltpu.SemaphoreType.DMA(()),
            *sum_scratch(mp, tail_n, model),
        ]
    if head_n:
        args.append(w_rest)
        outs += [
            jax.ShapeDtypeStruct((head_n, model), BF),
            jax.ShapeDtypeStruct((head_n, model), F32),
            jax.ShapeDtypeStruct((head_n, 1), F32),
            jax.ShapeDtypeStruct((head_n, mix), BF),
            jax.ShapeDtypeStruct((head_n, 2 * hidden_width), BF),
            jax.ShapeDtypeStruct((head_n, hidden_width), BF),
            jax.ShapeDtypeStruct((head_n, model), BF),
            jax.ShapeDtypeStruct((1, model), F32),
        ]
        scratch += [
            pltpu.VMEM((model, mix), BF),
            pltpu.VMEM((model, 2 * hidden_width), BF),
            pltpu.VMEM((model, hidden_width), BF),
            pltpu.SemaphoreType.DMA((3,)),
            *sum_scratch(mp, head_n, model),
        ]
    return pl.pallas_call(
        functools.partial(feed_back_kernel, tail_n, head_n, mp, tail_picked, head_picked),
        out_shape=tuple(outs),
        in_specs=vmem(in_vmem) + [pl.BlockSpec(memory_space=pl.ANY)] * (len(args) - in_vmem),
        out_specs=tuple(vmem(len(outs))),
        scratch_shapes=scratch,
        compiler_params=pltpu.CompilerParams(
            collective_id=ident, has_side_effects=True, vmem_limit_bytes=VMEM_LIMIT
        ),
        cost_estimate=pl.CostEstimate(flops=5 * 10**9, bytes_accessed=10**8, transcendentals=0),
        name=f"feed_back_{tail_n}_{head_n}",
    )(*args)


def rotary_tables(place, heads):
    freq = jnp.exp(jnp.arange(HD // 2, dtype=F32) * (-2.0 * math.log(ROPE_BASE) / HD))
    angle = place.astype(F32)[:, None] * freq[None, :]
    cosine, sine = jnp.cos(angle), jnp.sin(angle)
    one = jnp.concatenate([cosine, cosine], axis=1)
    two = jnp.concatenate([-sine, sine], axis=1)
    return (
        jnp.concatenate([jnp.tile(one, (1, heads + 1)), jnp.ones(one.shape, F32)], axis=1),
        jnp.concatenate([jnp.tile(two, (1, heads + 1)), jnp.zeros(one.shape, F32)], axis=1),
    )


def local(
    tokens, depths, second_slot, third_slot, w_query, w_key, w_value, w_out, w_gate, w_up,
    w_down, norm_first, norm_second, router, cotangent,
):
    me = lax.axis_index("dp")
    devices, mp = lax.axis_size("dp"), lax.axis_size("mp")
    rows = tokens.shape[0]
    heads = w_query.shape[1] // HD
    hidden_width = w_gate.shape[1]
    depth = w_query.shape[0]
    qkv_width = (heads + 2) * HD

    picks, marks = [], []
    for active, slot, capacity in (
        ((depths >= 2) & (second_slot >= 0), second_slot, SECOND_SLOTS),
        ((depths >= 3) & (third_slot >= 0), third_slot, THIRD_SLOTS),
    ):
        pick = (jnp.arange(capacity)[:, None] == slot[None, :]) & active[None, :]
        picks.append(pick.astype(BF))
        marks.append(
            jnp.min(jnp.where(pick, jnp.arange(rows, dtype=jnp.int32)[None, :], rows), axis=1)
        )

    def column(values):
        return values.reshape(depth, 1).astype(BF)

    second_mark = jnp.pad(marks[0], (0, 2 * depth - SECOND_SLOTS), constant_values=rows)
    first_shard = jnp.concatenate(
        [
            w_query, w_key, w_value,
            column(norm_first), column(norm_second), column(router),
            column(second_mark[:depth]), column(second_mark[depth:]), column(marks[1]),
            jnp.zeros((depth, LANES - 6), BF),
        ],
        axis=1,
    )
    rest_shard = jnp.concatenate([w_out.T, w_gate, w_up, w_down.T], axis=1)
    first = lax.all_gather(first_shard, "dp", axis=0, tiled=True)
    w_rest = lax.all_gather(rest_shard, "dp", axis=0, tiled=True)
    w_qkv = first[:, :qkv_width]
    extra = first[:, qkv_width : qkv_width + 8].astype(F32)
    gains = extra.T
    marks_all = extra[:, 3:6].astype(jnp.int32).reshape(devices, depth, 3)
    second_all = jnp.concatenate(
        [marks_all[:, :, 0], marks_all[:, : SECOND_SLOTS - depth, 1]], axis=1
    )
    base = (jnp.arange(devices, dtype=jnp.int32) * rows)[:, None]

    def place_of(mark, offset):
        return jnp.where(mark < rows, mark + offset, FAR)

    def key_column(mark):
        return jnp.broadcast_to(place_of(mark, base).reshape(-1, 1), (mark.size, LANES))

    levels = (
        (rows, None, jnp.arange(rows, dtype=jnp.int32) + me * rows, None),
        (SECOND_SLOTS, picks[0], place_of(marks[0], me * rows), key_column(second_all)),
        (THIRD_SLOTS, picks[1], place_of(marks[1], me * rows), key_column(marks_all[:, :, 2])),
    )
    state = tokens
    kept = []
    for index, (count, pick, place, key_place) in enumerate(levels):
        tables = rotary_tables(jnp.where(place == FAR, 0, place), heads)
        query_place = jnp.tile(place, heads)[None, :]
        rows_in, normed, packed, query, mixed_t, log_total, mixed = attend(
            state, pick, key_place, query_place, gains, tables, w_qkv, heads, devices, count, index
        )
        attn, ffn, second, parts, state = feed(
            state, rows_in, mixed, pick, gains, w_rest, hidden_width, mp, count, 3 + index
        )
        kept.append(
            (pick, key_place, query_place, tables, rows_in, normed, packed, query, mixed_t, log_total, mixed,
             attn, ffn, second, parts)
        )

    flow = cotangent
    tail = None
    terms, vectors = [], []
    for index in (2, 1, 0, None):
        head = None
        if index is not None:
            (pick, key_place, query_place, tables, rows_in, normed, packed, query, mixed_t, log_total, mixed,
             attn, ffn, second, parts) = kept[index]
            head = (rows_in, attn, ffn, second, parts, pick)
        outs = list(
            feed_back(flow, gains, tail, head, w_qkv, w_rest, hidden_width, mp, 6 + (3 if index is None else index))
        )
        if tail is not None:
            flow, first_vec, router_vec = outs[:3]
            outs = outs[3:]
            vectors.append((first_vec, None, router_vec))
        if head is not None:
            grad_attn, grad_middle, logit, grad_mixed, parts_grad, hidden, grad_ffn, second_vec = outs
            vectors.append((None, second_vec, None))
            grad_qkv = attend_back(
                key_place, query_place, query, packed, mixed_t, log_total, grad_mixed, tables,
                heads, devices, rows_in.shape[0], 10 + index,
            )
            tail = (grad_qkv, rows_in, grad_middle, logit, pick)
            terms.append((normed, grad_qkv, grad_attn, mixed, second, parts_grad, grad_ffn, hidden))
    normed, grad_qkv, grad_attn, mixed, second, parts_grad, grad_ffn, hidden = [
        jnp.concatenate(items, axis=0) for items in zip(*terms)
    ]
    vectors = [sum(item for item in items if item is not None) for items in zip(*vectors)]
    columns = jnp.concatenate(vectors + [jnp.zeros((LANES - 3, flow.shape[1]), F32)], axis=0).T

    def scatter(parts):
        return lax.psum_scatter(
            jnp.concatenate([part.astype(BF) for part in parts], axis=1),
            "dp", scatter_dimension=0, tiled=True,
        ).astype(F32)

    rest = scatter([dot_tn(second, parts_grad), dot_tn(grad_ffn, hidden)])
    some = scatter([dot_tn(grad_attn, mixed), dot_tn(normed, grad_qkv), columns])
    mix = heads * HD
    return (
        state, flow,
        some[:, mix : 2 * mix],
        some[:, 2 * mix : 2 * mix + HD],
        some[:, 2 * mix + HD : 2 * mix + 2 * HD],
        some[:, :mix].T,
        rest[:, :hidden_width],
        rest[:, hidden_width : 2 * hidden_width],
        rest[:, 2 * hidden_width :].T,
        some[:, 2 * mix + 2 * HD],
        some[:, 2 * mix + 2 * HD + 1],
        some[:, 2 * mix + 2 * HD + 2],
    )


def solution(mesh):
    in_specs = (
        P("dp", None), P("dp"), P("dp"), P("dp"), P("dp", "mp"), P("dp", "mp"), P("dp", "mp"),
        P("mp", "dp"), P("dp", "mp"), P("dp", "mp"), P("mp", "dp"), P("dp"), P("dp"), P("dp"),
        P("dp", None),
    )
    out_specs = (
        P("dp", None), P("dp", None), P("dp", "mp"), P("dp", "mp"), P("dp", "mp"), P("mp", "dp"),
        P("dp", "mp"), P("dp", "mp"), P("mp", "dp"), P("dp"), P("dp"), P("dp"),
    )
    return jax.shard_map(local, mesh=mesh, in_specs=in_specs, out_specs=out_specs, check_vma=False)
```

```python
import functools
import math

import jax
import jax.numpy as jnp
from jax import lax
from jax.experimental import pallas as pl
from jax.experimental.pallas import tpu as pltpu
from jax.sharding import PartitionSpec as P

HD = 64
SECOND_SLOTS = 96
THIRD_SLOTS = 64
EPS = 1e-05
NEG = -1e30
ROPE_BASE = 10000.0
FAR = 1073741824
BF = jnp.bfloat16
F32 = jnp.float32
MESH = pl.DeviceIdType.MESH
LANES = 128
VMEM_LIMIT = 58 * 1024 * 1024


def dot_nn(left, right):
    return lax.dot_general(left, right, (((1,), (0,)), ((), ())), preferred_element_type=F32)


def dot_nt(left, right):
    return lax.dot_general(left, right, (((1,), (1,)), ((), ())), preferred_element_type=F32)


def dot_tn(left, right):
    return lax.dot_general(left, right, (((0,), (0,)), ((), ())), preferred_element_type=F32)


def unit_of(values):
    factor = lax.rsqrt(jnp.mean(values * values, axis=-1, keepdims=True) + EPS)
    return values * factor, factor


def unit_back(shaped, unit, factor):
    return factor * (shaped - unit * jnp.mean(shaped * unit, axis=-1, keepdims=True))


def sigmoid(values):
    return 1.0 / (1.0 + jnp.exp(-values))


def lanes_of(shape):
    return lax.broadcasted_iota(jnp.int32, shape, 1)


def swap_halves(tile):
    first = lax.rem(lanes_of(tile.shape), HD) < HD // 2
    return jnp.where(first, pltpu.roll(tile, LANES - HD // 2, 1), pltpu.roll(tile, HD // 2, 1))


def tile_of(values, index):
    return values[:, index * LANES : (index + 1) * LANES]


def signal_all(group, me, axis):
    barrier = pltpu.get_barrier_semaphore()
    for k in range(1, group):
        pl.semaphore_signal(
            barrier, inc=1, device_id={axis: lax.rem(me + k, group)}, device_id_type=MESH
        )
    pl.semaphore_wait(barrier, group - 1)


def sum_over_mp(group, me, make_chunk, send, recv, full, sems):
    order = (2, 1, 3)
    copies = []
    for k in order:
        peer = lax.rem(me + k, group)
        send[k - 1] = make_chunk(peer).astype(BF)
        copy = pltpu.make_async_remote_copy(
            src_ref=send.at[k - 1], dst_ref=recv.at[k - 1],
            send_sem=sems.at[0, k - 1], recv_sem=sems.at[1, k - 1],
            device_id={"mp": peer}, device_id_type=MESH,
        )
        copy.start()
        copies.append(copy)
    total = make_chunk(me).astype(BF).astype(F32)
    for k, copy in zip(order, copies):
        copy.wait_recv()
        total = total + recv[k - 1].astype(F32)
    full[me] = total.astype(BF)
    backs = []
    for k in order:
        peer = lax.rem(me + k, group)
        copy = pltpu.make_async_remote_copy(
            src_ref=full.at[me], dst_ref=full.at[me],
            send_sem=sems.at[2, k - 1], recv_sem=sems.at[3, k - 1],
            device_id={"mp": peer}, device_id_type=MESH,
        )
        copy.start()
        backs.append(copy)
    for copy in backs:
        copy.wait_recv()
    for copy in copies + backs:
        copy.wait_send()
    return jnp.concatenate([full[c] for c in range(group)], axis=1)


def attend_kernel(n, heads, devices, group, picked, *refs):
    refs = list(refs)
    source = refs.pop(0)
    pick = refs.pop(0) if picked else None
    key_place = refs.pop(0) if picked else None
    query_place, gains, cosine, sine, w_hbm = [refs.pop(0) for _ in range(5)]
    rows_out, normed_out, packed_out, query_out, mixed_t_out, log_out, mixed_out = [
        refs.pop(0) for _ in range(7)
    ]
    w_v, packed, query_t, top, total, acc, w_sem, out_sem, send_sems, recv_sems = refs
    me = lax.axis_index("dp")
    width = heads * n
    load_w = pltpu.make_async_copy(w_hbm.at[:, : w_v.shape[1]], w_v, w_sem)
    load_w.start()

    barrier = pltpu.get_barrier_semaphore()

    def greet(e, carry):
        pl.semaphore_signal(barrier, inc=1, device_id={"dp": e}, device_id_type=MESH)
        return carry

    lax.fori_loop(0, me, greet, 0)

    if picked:
        rows = dot_nn(pick[...], source[...].astype(BF)).astype(BF)
    else:
        rows = source[...]
    rows_out[...] = rows
    unit, unused = unit_of(rows.astype(F32))
    normed = (unit * gains[0:1, :]).astype(BF)
    normed_out[...] = normed
    load_w.wait()
    tiles = []
    for t in range(heads // 2 + 1):
        if t % 2 == 0:
            last = min((t + 2) * LANES, (heads // 2 + 1) * LANES)
            both = dot_nn(normed, w_v[:, t * LANES : last])
        part = tile_of(both, t % 2)
        cut = slice(t * LANES, (t + 1) * LANES)
        tiles.append(part * cosine[:, cut] + swap_halves(part) * sine[:, cut])
    packed[me] = tiles[-1].astype(BF)

    @pl.when(me < devices - 1)
    def _():
        pl.semaphore_wait(barrier, devices - 1 - me)

    def send_copy(e, source_index):
        return pltpu.make_async_remote_copy(
            src_ref=packed.at[me], dst_ref=packed.at[me],
            send_sem=send_sems.at[e], recv_sem=recv_sems.at[source_index],
            device_id={"dp": e}, device_id_type=MESH,
        )

    def send(e, carry):
        send_copy(e, me).start()
        return carry

    lax.fori_loop(me + 1, devices, send, 0)

    def clear(e, carry):
        packed[e] = jnp.zeros((n, 2 * HD), BF)
        return carry

    lax.fori_loop(me + 1, devices, clear, 0)

    left = lanes_of((n, LANES)) < HD
    for t in range(heads // 2):
        scaled = tiles[t].astype(BF).astype(F32) * HD**-0.5
        query_out[2 * t * n : (2 * t + 1) * n, :] = jnp.where(left, scaled, 0.0).astype(BF)
        query_out[(2 * t + 1) * n : (2 * t + 2) * n, :] = jnp.where(
            left, pltpu.roll(scaled, HD, 1), 0.0
        ).astype(BF)
    query_t[...] = query_out[...].T
    top[...] = jnp.full((1, width), NEG, F32)
    total[...] = jnp.zeros((1, width), F32)
    acc[...] = jnp.zeros((2 * HD, width), F32)

    def one_block(b, carry):
        for g in range(group):
            e = b * group + g

            @pl.when(e < me)
            def _():
                send_copy(me, e).wait_recv()

        part = packed[pl.ds(b * group, group)].reshape(group * n, 2 * HD)
        scores = dot_nn(part, query_t[...])
        if picked:
            start = pl.multiple_of(b * (group * n), group * n)
            place = key_place[pl.ds(start, group * n), :]
        else:
            place = lax.broadcasted_iota(jnp.int32, (group * n, LANES), 0) + b * (group * n)
        place = jnp.concatenate([place] * (width // LANES), axis=1)
        scores = jnp.where(place <= query_place[...], scores, NEG)
        peak = jnp.maximum(top[...], jnp.max(scores, axis=0, keepdims=True))
        weights = jnp.exp(scores - peak)
        fade = jnp.exp(top[...] - peak)
        total[...] = total[...] * fade + jnp.sum(weights, axis=0, keepdims=True)
        acc[...] = acc[...] * fade + dot_tn(part, weights.astype(BF))
        top[...] = peak
        return carry

    lax.fori_loop(0, me // group + 1, one_block, 0)
    mixed_t = acc[...] / total[...]
    mixed_t_out[...] = mixed_t
    log_out[...] = top[...] + jnp.log(total[...])
    mixed = mixed_t.T
    for t in range(heads // 2):
        even = mixed[2 * t * n : (2 * t + 1) * n, :]
        odd = mixed[(2 * t + 1) * n : (2 * t + 2) * n, :]
        mixed_out[:, t * LANES : (t + 1) * LANES] = jnp.where(
            left, pltpu.roll(even, HD, 1), odd
        ).astype(BF)
    keep = pltpu.make_async_copy(packed, packed_out, out_sem)
    keep.start()

    def sent(e, carry):
        send_copy(e, me).wait_send()
        return carry

    lax.fori_loop(me + 1, devices, sent, 0)
    keep.wait()


def vmem(count):
    return [pl.BlockSpec(memory_space=pltpu.VMEM)] * count


def attend(source, pick, key_place, query_place, gains, tables, w_qkv, heads, devices, n, ident):
    picked = pick is not None
    group = 512 // n if 512 % n == 0 else 4
    width = heads * n
    qkv_width = (heads + 2) * HD
    args = [source] + ([pick, key_place] if picked else []) + [query_place, gains, *tables, w_qkv]
    model = source.shape[1]
    return pl.pallas_call(
        functools.partial(attend_kernel, n, heads, devices, group, picked),
        out_shape=(
            jax.ShapeDtypeStruct((n, model), BF),
            jax.ShapeDtypeStruct((n, model), BF),
            jax.ShapeDtypeStruct((devices, n, 2 * HD), BF),
            jax.ShapeDtypeStruct((width, 2 * HD), BF),
            jax.ShapeDtypeStruct((2 * HD, width), F32),
            jax.ShapeDtypeStruct((1, width), F32),
            jax.ShapeDtypeStruct((n, heads * HD), BF),
        ),
        in_specs=vmem(len(args) - 1) + [pl.BlockSpec(memory_space=pl.ANY)],
        out_specs=tuple(vmem(2) + [pl.BlockSpec(memory_space=pl.ANY)] + vmem(4)),
        scratch_shapes=[
            pltpu.VMEM((model, qkv_width), BF),
            pltpu.VMEM((devices, n, 2 * HD), BF),
            pltpu.VMEM((2 * HD, width), BF),
            pltpu.VMEM((1, width), F32),
            pltpu.VMEM((1, width), F32),
            pltpu.VMEM((2 * HD, width), F32),
            pltpu.SemaphoreType.DMA(()),
            pltpu.SemaphoreType.DMA(()),
            pltpu.SemaphoreType.DMA((devices,)),
            pltpu.SemaphoreType.DMA((devices,)),
        ],
        compiler_params=pltpu.CompilerParams(
            collective_id=ident, has_side_effects=True, vmem_limit_bytes=VMEM_LIMIT
        ),
        cost_estimate=pl.CostEstimate(flops=4 * 10**9, bytes_accessed=10**7, transcendentals=0),
        name=f"attend_{n}",
    )(*args)


def attend_back_kernel(n, heads, devices, group, picked, *refs):
    refs = list(refs)
    key_place = refs.pop(0) if picked else None
    query_place, query, packed, mixed_t, log_total, grad_mixed, cosine, sine = [
        refs.pop(0) for _ in range(8)
    ]
    grad_out = refs.pop(0)
    query_t, grad_rows, grad_t, acc, delta, send_buf, recv_buf, send_sems, recv_sems = refs
    me = lax.axis_index("dp")
    barrier = pltpu.get_barrier_semaphore()

    def greet(e, carry):
        pl.semaphore_signal(barrier, inc=1, device_id={"dp": e}, device_id_type=MESH)
        return carry

    lax.fori_loop(me + 1, devices, greet, 0)

    left = lanes_of((n, LANES)) < HD
    for t in range(heads // 2):
        part = grad_mixed[:, t * LANES : (t + 1) * LANES].astype(F32)
        grad_rows[2 * t * n : (2 * t + 1) * n, :] = jnp.where(
            left, 0.0, pltpu.roll(part, HD, 1)
        ).astype(BF)
        grad_rows[(2 * t + 1) * n : (2 * t + 2) * n, :] = jnp.where(left, 0.0, part).astype(BF)
    query_t[...] = query[...].T
    grad_t[...] = grad_rows[...].T
    delta[...] = jnp.sum(grad_t[...].astype(F32) * mixed_t[...], axis=0, keepdims=True)
    acc[...] = jnp.zeros(acc.shape, F32)
    width = heads * n

    @pl.when(me > 0)
    def _():
        pl.semaphore_wait(barrier, me)

    def send_copy(e, source_index):
        return pltpu.make_async_remote_copy(
            src_ref=send_buf.at[e], dst_ref=recv_buf.at[source_index],
            send_sem=send_sems.at[e], recv_sem=recv_sems.at[source_index],
            device_id={"dp": e}, device_id_type=MESH,
        )

    def one_block(b, carry):
        part = packed[pl.ds(b * group, group)].reshape(group * n, 2 * HD)
        scores = dot_nn(part, query_t[...])
        if picked:
            start = pl.multiple_of(b * (group * n), group * n)
            place = key_place[pl.ds(start, group * n), :]
        else:
            place = lax.broadcasted_iota(jnp.int32, (group * n, LANES), 0) + b * (group * n)
        place = jnp.concatenate([place] * (width // LANES), axis=1)
        scores = jnp.where(place <= query_place[...], scores, NEG)
        weights = jnp.exp(scores - log_total[...])
        grad_weights = dot_nn(part, grad_t[...])
        grad_scores = (weights * (grad_weights - delta[...])).astype(BF)
        grad_part = dot_nn(grad_scores, query[...]) + dot_nn(weights.astype(BF), grad_rows[...])
        send_buf[pl.ds(b * group, group)] = grad_part.astype(BF).reshape(group, n, 2 * HD)
        acc[...] += dot_tn(part, grad_scores)
        for g in range(group):
            e = b * group + g

            @pl.when(e < me)
            def _():
                send_copy(e, me).start()

        return carry

    lax.fori_loop(0, me // group + 1, one_block, 0)

    grad_query = acc[...].T * HD**-0.5
    outs = []
    for t in range(heads // 2):
        even = grad_query[2 * t * n : (2 * t + 1) * n, :]
        odd = grad_query[(2 * t + 1) * n : (2 * t + 2) * n, :]
        outs.append(jnp.where(left, even, pltpu.roll(odd, HD, 1)))

    def add(e, carry):
        send_copy(me, e).wait_recv()
        return carry + recv_buf[e].astype(F32)

    outs.append(lax.fori_loop(me + 1, devices, add, send_buf[me].astype(F32)))
    for t, part in enumerate(outs):
        cut = slice(t * LANES, (t + 1) * LANES)
        grad_out[:, cut] = (part * cosine[:, cut] - swap_halves(part) * sine[:, cut]).astype(BF)

    def sent(e, carry):
        send_copy(e, me).wait_send()
        return carry

    lax.fori_loop(0, me, sent, 0)


def attend_back(key_place, query_place, query, packed, mixed_t, log_total, grad_mixed, tables, heads, devices, n, ident):
    picked = key_place is not None
    group = 512 // n if 512 % n == 0 else 4
    width = heads * n
    args = ([key_place] if picked else []) + [
        query_place, query, packed, mixed_t, log_total, grad_mixed, *tables
    ]
    return pl.pallas_call(
        functools.partial(attend_back_kernel, n, heads, devices, group, picked),
        out_shape=jax.ShapeDtypeStruct((n, (heads + 2) * HD), BF),
        in_specs=vmem(len(args)),
        out_specs=pl.BlockSpec(memory_space=pltpu.VMEM),
        scratch_shapes=[
            pltpu.VMEM((2 * HD, width), BF),
            pltpu.VMEM((width, 2 * HD), BF),
            pltpu.VMEM((2 * HD, width), BF),
            pltpu.VMEM((2 * HD, width), F32),
            pltpu.VMEM((1, width), F32),
            pltpu.VMEM((devices, n, 2 * HD), BF),
            pltpu.VMEM((devices, n, 2 * HD), BF),
            pltpu.SemaphoreType.DMA((devices,)),
            pltpu.SemaphoreType.DMA((devices,)),
        ],
        compiler_params=pltpu.CompilerParams(
            collective_id=ident, has_side_effects=True, vmem_limit_bytes=VMEM_LIMIT
        ),
        cost_estimate=pl.CostEstimate(flops=10**10, bytes_accessed=10**7, transcendentals=0),
        name=f"attend_back_{n}",
    )(*args)


def feed_kernel(n, mp, picked, *refs):
    refs = list(refs)
    state, rows_in, mixed = [refs.pop(0) for _ in range(3)]
    pick = refs.pop(0) if picked else None
    gains, w_hbm = refs.pop(0), refs.pop(0)
    attn_out, ffn_out, second_out, parts_out, state_out = [refs.pop(0) for _ in range(5)]
    w_o, w_gu, w_d, hidden, w_sems, send_a, recv_a, full_a, sems_a, send_b, recv_b, full_b, sems_b = refs
    me = lax.axis_index("mp")
    wide_o, wide_gu, wide_d = w_o.shape[1], w_gu.shape[1], w_d.shape[1]
    loads = []
    start = wide_o + 2 * LANES
    for index, (ref, wide) in enumerate(((w_o, wide_o), (w_gu, wide_gu), (w_d, wide_d))):
        load = pltpu.make_async_copy(w_hbm.at[:, start : start + wide], ref, w_sems.at[index])
        load.start()
        loads.append(load)
        start += wide
    signal_all(mp, me, "mp")
    chunk = w_o.shape[0] // mp
    loads[0].wait()
    mixed_now = mixed[...]

    def out_chunk(c):
        return dot_nt(mixed_now, w_o[pl.ds(pl.multiple_of(c * chunk, chunk), chunk), :])

    attn = sum_over_mp(mp, me, out_chunk, send_a, recv_a, full_a, sems_a)
    attn_out[...] = attn
    level = rows_in[...].astype(F32)
    unit, unused = unit_of(level + attn.astype(F32))
    second = (unit * gains[1:2, :]).astype(BF)
    second_out[...] = second
    loads[1].wait()
    step = 256
    for t in range(wide_gu // step):
        parts_out[:, t * step : (t + 1) * step] = dot_nn(second, w_gu[:, t * step : (t + 1) * step])
    half = wide_gu // 2
    for t in range(half // LANES):
        cut = slice(t * LANES, (t + 1) * LANES)
        gate_part = parts_out[:, cut]
        up_part = parts_out[:, half + t * LANES : half + (t + 1) * LANES]
        hidden[:, cut] = (gate_part * sigmoid(gate_part) * up_part).astype(BF)
    loads[2].wait()
    hidden_now = hidden[...]

    def down_chunk(c):
        return dot_nt(hidden_now, w_d[pl.ds(pl.multiple_of(c * chunk, chunk), chunk), :])

    ffn = sum_over_mp(mp, me, down_chunk, send_b, recv_b, full_b, sems_b)
    ffn_out[...] = ffn
    gate = sigmoid(jnp.sum(level * gains[2:3, :], axis=-1, keepdims=True))
    update = (gate * (attn.astype(F32) + ffn.astype(F32))).astype(BF)
    if picked:
        state_out[...] = state[...].astype(F32) + dot_tn(pick[...], update)
    else:
        state_out[...] = state[...].astype(F32) + update.astype(F32)


def sum_scratch(mp, n, model):
    return [
        pltpu.VMEM((mp - 1, n, model // mp), BF),
        pltpu.VMEM((mp - 1, n, model // mp), BF),
        pltpu.VMEM((mp, n, model // mp), BF),
        pltpu.SemaphoreType.DMA((4, mp - 1)),
    ]


def feed(state, rows, mixed, pick, gains, w_rest, hidden_width, mp, n, ident):
    picked = pick is not None
    model = rows.shape[1]
    args = [state, rows, mixed] + ([pick] if picked else []) + [gains, w_rest]
    return pl.pallas_call(
        functools.partial(feed_kernel, n, mp, picked),
        out_shape=(
            jax.ShapeDtypeStruct((n, model), BF),
            jax.ShapeDtypeStruct((n, model), BF),
            jax.ShapeDtypeStruct((n, model), BF),
            jax.ShapeDtypeStruct((n, 2 * hidden_width), F32),
            jax.ShapeDtypeStruct(state.shape, F32),
        ),
        in_specs=vmem(len(args) - 1) + [pl.BlockSpec(memory_space=pl.ANY)],
        out_specs=tuple(vmem(5)),
        scratch_shapes=[
            pltpu.VMEM((model, mixed.shape[1]), BF),
            pltpu.VMEM((model, 2 * hidden_width), BF),
            pltpu.VMEM((model, hidden_width), BF),
            pltpu.VMEM((n, hidden_width), BF),
            pltpu.SemaphoreType.DMA((3,)),
            *sum_scratch(mp, n, model),
            *sum_scratch(mp, n, model),
        ],
        compiler_params=pltpu.CompilerParams(
            collective_id=ident, has_side_effects=True, vmem_limit_bytes=VMEM_LIMIT
        ),
        cost_estimate=pl.CostEstimate(flops=5 * 10**9, bytes_accessed=10**8, transcendentals=0),
        name=f"feed_{n}",
    )(*args)


def feed_back_kernel(tail_n, head_n, mp, tail_picked, head_picked, *refs):
    refs = list(refs)
    flow, gains = refs.pop(0), refs.pop(0)
    if tail_n:
        grad_qkv, tail_rows, tail_middle, tail_logit = [refs.pop(0) for _ in range(4)]
        tail_pick = refs.pop(0) if tail_picked else None
    if head_n:
        rows_in, attn, ffn, second, parts = [refs.pop(0) for _ in range(5)]
        head_pick = refs.pop(0) if head_picked else None
    if tail_n:
        w_first_hbm = refs.pop(0)
    if head_n:
        w_rest_hbm = refs.pop(0)
    if tail_n:
        flow_out, first_out, router_out = [refs.pop(0) for _ in range(3)]
    if head_n:
        attn_grad_out, middle_out, logit_out, mixed_out, parts_grad_out, hidden_out, ffn_grad_out, second_vec_out = [
            refs.pop(0) for _ in range(8)
        ]
    if tail_n:
        w_qkv, w_first_sem = refs.pop(0), refs.pop(0)
        send_a, recv_a, full_a, sems_a = [refs.pop(0) for _ in range(4)]
    if head_n:
        w_o, w_gu, w_d, w_sems = [refs.pop(0) for _ in range(4)]
        send_b, recv_b, full_b, sems_b = [refs.pop(0) for _ in range(4)]
    me = lax.axis_index("mp")
    if tail_n:
        load_first = pltpu.make_async_copy(w_first_hbm.at[:, : w_qkv.shape[1]], w_qkv, w_first_sem)
        load_first.start()
    if head_n:
        loads = {}
        wide_o, wide_gu, wide_d = w_o.shape[1], w_gu.shape[1], w_d.shape[1]
        for index, (name, ref, start) in enumerate(
            (("d", w_d, wide_o + wide_gu), ("gu", w_gu, wide_o), ("o", w_o, 0))
        ):
            start += wide_o + 2 * LANES
            loads[name] = pltpu.make_async_copy(
                w_rest_hbm.at[:, start : start + ref.shape[1]], ref, w_sems.at[index]
            )
            loads[name].start()
    signal_all(mp, me, "mp")

    if tail_n:
        load_first.wait()
        grad_now = grad_qkv[...]
        chunk = w_qkv.shape[0] // mp

        def first_chunk(c):
            return dot_nt(grad_now, w_qkv[pl.ds(pl.multiple_of(c * chunk, chunk), chunk), :])

        grad_normed = sum_over_mp(mp, me, first_chunk, send_a, recv_a, full_a, sems_a).astype(F32)
        level = tail_rows[...].astype(F32)
        unit, factor = unit_of(level)
        first_out[...] = jnp.sum(grad_normed * unit, axis=0, keepdims=True)
        router_out[...] = jnp.sum(level * tail_logit[...], axis=0, keepdims=True)
        grad_rows = (
            unit_back(grad_normed * gains[0:1, :], unit, factor)
            + tail_middle[...]
            + tail_logit[...] * gains[2:3, :]
        ).astype(BF)
        if tail_picked:
            flow_now = flow[...] + dot_tn(tail_pick[...], grad_rows)
        else:
            flow_now = flow[...] + grad_rows.astype(F32)
        flow_out[...] = flow_now
    else:
        flow_now = flow[...]

    if head_n:
        grad_update = flow_now.astype(BF)
        if head_picked:
            grad_update = dot_nn(head_pick[...], grad_update)
        grad_update = grad_update.astype(F32)
        level = rows_in[...].astype(F32)
        attn_now = attn[...].astype(F32)
        gate = sigmoid(jnp.sum(level * gains[2:3, :], axis=-1, keepdims=True))
        logit = jnp.sum(grad_update * (attn_now + ffn[...].astype(F32)), axis=-1, keepdims=True)
        logit_out[...] = logit * gate * (1.0 - gate)
        grad_ffn = (gate * grad_update).astype(BF)
        ffn_grad_out[...] = grad_ffn
        half = wide_d
        loads["d"].wait()
        for t in range(half // LANES):
            cut = slice(t * LANES, (t + 1) * LANES)
            up_cut = slice(half + t * LANES, half + (t + 1) * LANES)
            if t % 2 == 0:
                both = dot_nn(grad_ffn, w_d[:, t * LANES : min((t + 2) * LANES, half)])
            grad_hidden = tile_of(both, t % 2)
            gate_part = parts[:, cut]
            up_part = parts[:, up_cut]
            sigma = sigmoid(gate_part)
            active = gate_part * sigma
            hidden_out[:, cut] = (active * up_part).astype(BF)
            parts_grad_out[:, cut] = (
                grad_hidden * up_part * sigma * (1.0 + gate_part * (1.0 - sigma))
            ).astype(BF)
            parts_grad_out[:, up_cut] = (grad_hidden * active).astype(BF)
        loads["gu"].wait()
        parts_now = parts_grad_out[...]
        chunk = w_gu.shape[0] // mp

        def second_chunk(c):
            return dot_nt(parts_now, w_gu[pl.ds(pl.multiple_of(c * chunk, chunk), chunk), :])

        grad_second = sum_over_mp(mp, me, second_chunk, send_b, recv_b, full_b, sems_b).astype(F32)
        unit, factor = unit_of(level + attn_now)
        second_vec_out[...] = jnp.sum(grad_second * unit, axis=0, keepdims=True)
        grad_middle = unit_back(grad_second * gains[1:2, :], unit, factor)
        middle_out[...] = grad_middle
        grad_attn = (gate * grad_update + grad_middle).astype(BF)
        attn_grad_out[...] = grad_attn
        loads["o"].wait()
        mixed_out[...] = dot_nn(grad_attn, w_o[...]).astype(BF)


def feed_back(flow, gains, tail, head, weights, hidden_width, mix, mp, ident):
    model = flow.shape[1]
    args, outs, scratch = [flow, gains], [], []
    tail_n = head_n = 0
    tail_picked = head_picked = False
    if tail is not None:
        *items, pick = tail
        tail_n, tail_picked = items[0].shape[0], pick is not None
        args += items + ([pick] if tail_picked else [])
    if head is not None:
        *items, pick = head
        head_n, head_picked = items[0].shape[0], pick is not None
        args += items + ([pick] if head_picked else [])
    in_vmem = len(args)
    if tail_n:
        args.append(weights)
        outs += [
            jax.ShapeDtypeStruct(flow.shape, F32),
            jax.ShapeDtypeStruct((1, model), F32),
            jax.ShapeDtypeStruct((1, model), F32),
        ]
        scratch += [
            pltpu.VMEM((model, mix + 2 * HD), BF),
            pltpu.SemaphoreType.DMA(()),
            *sum_scratch(mp, tail_n, model),
        ]
    if head_n:
        args.append(weights)
        outs += [
            jax.ShapeDtypeStruct((head_n, model), BF),
            jax.ShapeDtypeStruct((head_n, model), F32),
            jax.ShapeDtypeStruct((head_n, 1), F32),
            jax.ShapeDtypeStruct((head_n, mix), BF),
            jax.ShapeDtypeStruct((head_n, 2 * hidden_width), BF),
            jax.ShapeDtypeStruct((head_n, hidden_width), BF),
            jax.ShapeDtypeStruct((head_n, model), BF),
            jax.ShapeDtypeStruct((1, model), F32),
        ]
        scratch += [
            pltpu.VMEM((model, mix), BF),
            pltpu.VMEM((model, 2 * hidden_width), BF),
            pltpu.VMEM((model, hidden_width), BF),
            pltpu.SemaphoreType.DMA((3,)),
            *sum_scratch(mp, head_n, model),
        ]
    return pl.pallas_call(
        functools.partial(feed_back_kernel, tail_n, head_n, mp, tail_picked, head_picked),
        out_shape=tuple(outs),
        in_specs=vmem(in_vmem) + [pl.BlockSpec(memory_space=pl.ANY)] * (len(args) - in_vmem),
        out_specs=tuple(vmem(len(outs))),
        scratch_shapes=scratch,
        compiler_params=pltpu.CompilerParams(
            collective_id=ident, has_side_effects=True, vmem_limit_bytes=VMEM_LIMIT
        ),
        cost_estimate=pl.CostEstimate(flops=5 * 10**9, bytes_accessed=10**8, transcendentals=0),
        name=f"feed_back_{tail_n}_{head_n}",
    )(*args)


def plane(me):
    return me // 8, lax.rem(me // 2, 4), lax.rem(me, 2)


def peer(x, y, core):
    return {"dp": (lax.rem(x, 4) * 4 + lax.rem(y, 4)) * 2 + core}


def shifted(x, y, core, axis, k):
    return peer(x + k, y, core) if axis == 0 else peer(x, y + k, core)


def meet(me, partners):
    barrier = pltpu.get_barrier_semaphore()
    for device in partners:
        pl.semaphore_signal(barrier, inc=1, device_id=device, device_id_type=MESH)
    pl.semaphore_wait(barrier, len(partners))


def plane_partners(x, y, core):
    return (
        [peer(x, y, 1 - core)]
        + [shifted(x, y, core, 0, k) for k in (1, 2, 3)]
        + [shifted(x, y, core, 1, k) for k in (1, 2, 3)]
    )


def spread_kernel(
    groups, w_query, w_key, w_value, w_out, w_gate, w_up, w_down, extras, full, gains,
    shard, columns, own_sem, column_sem, send_sems, recv_sems,
):
    me = lax.axis_index("dp")
    x, y, core = plane(me)
    start = 0
    pair = jnp.concatenate([w_key[...].astype(F32), w_value[...].astype(F32)], axis=1).astype(BF)
    for part in (
        w_query[...], pair, extras[...],
        w_out[...].T, w_gate[...], w_up[...], w_down[...].T,
    ):
        shard[:, start : start + part.shape[1]] = part
        start += part.shape[1]
    own = pltpu.make_async_copy(shard, full.at[x, y, core], own_sem)
    own.start()
    meet(me, plane_partners(x, y, core))
    started = []

    def remote(g, index, source, target, device):
        copy = pltpu.make_async_remote_copy(
            src_ref=source, dst_ref=target, send_sem=send_sems.at[g, index],
            recv_sem=recv_sems.at[g, index], device_id=device, device_id_type=MESH,
        )
        copy.start()
        started.append(copy)
        return copy

    def line(axis, at, first, count, cut):
        if axis == 0:
            return full.at[pl.ds(first, count), at, core, :, cut]
        return full.at[at, pl.ds(first, count), core, :, cut]

    waits = [{} for _ in groups]

    def one(g):
        low, high, axis = groups[g]
        cut = slice(low, high)
        waits[g][1] = [
            remote(
                g, k - 1, shard.at[:, cut], full.at[x, y, core, :, cut],
                shifted(x, y, core, axis, k),
            )
            for k in (2, 1, 3)
        ]

    def two(g):
        low, high, axis = groups[g]
        cut = slice(low, high)
        for copy in waits[g][1]:
            copy.wait_recv()
        mine = line(axis, y if axis == 0 else x, 0, 4, cut)
        waits[g][2] = [
            remote(g, 3 + i, mine, mine, shifted(x, y, core, 1 - axis, k))
            for i, k in enumerate((1, 3))
        ]

    def three(g):
        low, high, axis = groups[g]
        cut = slice(low, high)
        at = y if axis == 0 else x
        waits[g][3] = []
        for i, k in enumerate((1, 3)):
            waits[g][2][i].wait_recv()
            piece = line(axis, lax.rem(at + 4 - k, 4), 2 * i, 2, cut)
            waits[g][3].append(
                remote(g, 5 + i, piece, piece, shifted(x, y, core, 1 - axis, k))
            )

    def four(g):
        low, high, axis = groups[g]
        for copy in waits[g][3]:
            copy.wait_recv()
        mine = full.at[:, :, core, :, slice(low, high)]
        waits[g][4] = [remote(g, 7, mine, mine, peer(x, y, 1 - core))]

    def five(g):
        waits[g][4][0].wait_recv()

    count = len(groups)
    one(0)
    one(1)
    own.wait()
    for i in range(count + 3):
        if i < count:
            two(i)
        if i + 2 < count:
            one(i + 2)
        if 0 <= i - 1 < count:
            three(i - 1)
        if 0 <= i - 2 < count:
            four(i - 2)
        if 0 <= i - 3 < count:
            five(i - 3)
            if i == 3:
                low = w_query.shape[1] + LANES
                load = pltpu.make_async_copy(
                    full.at[:, :, :, :, low : low + LANES], columns, column_sem
                )
                load.start()
                load.wait()
                flat = columns[...].reshape(gains.shape[1], LANES).astype(F32)
                gains[...] = flat.T[: gains.shape[0], :]
    for copy in started:
        copy.wait_send()


def spread(w_query, w_key, w_value, w_out, w_gate, w_up, w_down, extras, ident):
    depth, mix = w_query.shape
    hidden = w_gate.shape[1]
    total = 2 * mix + 2 * LANES + 3 * hidden
    cuts = [0, mix + 2 * LANES]
    while cuts[-1] < total:
        cuts.append(min(cuts[-1] + 512, total))
    if cuts[-1] - cuts[-2] < 256:
        cuts.pop(-2)
    groups = [(a, b, i % 2) for i, (a, b) in enumerate(zip(cuts[:-1], cuts[1:]))]
    return pl.pallas_call(
        functools.partial(spread_kernel, groups),
        out_shape=(
            jax.ShapeDtypeStruct((4, 4, 2, depth, total), BF),
            jax.ShapeDtypeStruct((8, 32 * depth), F32),
        ),
        in_specs=vmem(8),
        out_specs=(pl.BlockSpec(memory_space=pl.ANY), pl.BlockSpec(memory_space=pltpu.VMEM)),
        scratch_shapes=[
            pltpu.VMEM((depth, total), BF),
            pltpu.VMEM((4, 4, 2, depth, LANES), BF),
            pltpu.SemaphoreType.DMA(()),
            pltpu.SemaphoreType.DMA(()),
            pltpu.SemaphoreType.DMA((len(groups), 8)),
            pltpu.SemaphoreType.DMA((len(groups), 8)),
        ],
        compiler_params=pltpu.CompilerParams(
            collective_id=ident, has_side_effects=True, vmem_limit_bytes=VMEM_LIMIT
        ),
        name="spread",
    )(w_query, w_key, w_value, w_out, w_gate, w_up, w_down, extras)


SLOTS = 4
GROUP = 512


def collect_kernel(levels, spans, groups, *refs):
    refs = list(refs)
    sources = [[refs.pop(0) for _ in range(8)] for _ in levels]
    vectors = refs.pop(0)
    q_out, k_out, v_out, out_out, gate_out, up_out, down_out, vec_out = [refs.pop(0) for _ in range(8)]
    lefts, turned, rights, final, slots, core_recv, relay_recv, first_recv, mid, last_recv, loads, send_sems, recv_sems = refs
    me = lax.axis_index("dp")
    x, y, core = plane(me)
    copies = []
    row = 0
    for level, count in enumerate(levels):
        for s in range(4):
            low, high = spans[s]
            for side, ref in enumerate((lefts.at[s, row : row + count], rights.at[row : row + count, low:high])):
                copy = pltpu.make_async_copy(sources[level][2 * s + side], ref, loads.at[level, 2 * s + side])
                copy.start()
                copies.append(copy)
        row += count
    meet(me, plane_partners(x, y, core))
    for copy in copies:
        copy.wait()
    started = []

    def remote(g, index, source, target, device):
        copy = pltpu.make_async_remote_copy(
            src_ref=source, dst_ref=target, send_sem=send_sems.at[g, index],
            recv_sem=recv_sems.at[g, index], device_id=device, device_id_type=MESH,
        )
        copy.start()
        return copy

    waits = [{} for _ in groups]
    done = set()

    def held(slot, axis, at, first, count):
        if axis == 0:
            return slots.at[slot, at, pl.ds(first, count), core]
        return slots.at[slot, pl.ds(first, count), at, core]

    def zero(g):
        slot = g % SLOTS
        if g >= SLOTS:
            for copy in waits[g - SLOTS][0] + waits[g - SLOTS][1] + waits[g - SLOTS][2]:
                copy.wait_send()
        column = 0
        for section, low, high in groups[g][1]:
            wide = high - low
            if section < 4:
                if section not in done:
                    done.add(section)
                    turned[section] = lefts[section].T
                base = spans[section][0]

            def rows_of(m, carry, section=section, low=low, high=high, column=column, wide=wide):
                start = pl.multiple_of(m * 256, 256)
                if section < 4:
                    value = dot_nn(turned[section, pl.ds(start, 256), :], rights[:, base + low : base + high])
                else:
                    value = vectors[:, pl.ds(start, 256)].T
                slots[slot, m // 2, pl.ds(lax.rem(m, 2) * 2, 2), :, :, column : column + wide] = (
                    value.astype(BF).reshape(2, 2, 64, wide)
                )
                return carry

            lax.fori_loop(0, 8, rows_of, 0)
            column += wide
        waits[g][0] = [
            remote(g, 0, slots.at[slot, :, :, 1 - core, :, :column], core_recv.at[g, :, :, :, :column], peer(x, y, 1 - core))
        ]

    def first(g):
        slot, (width, _, axis) = g % SLOTS, groups[g]
        waits[g][0][0].wait_recv()

        def add(i, carry):
            a, b = i // 4, lax.rem(i, 4)
            slots[slot, a, b, core, :, :width] = (
                slots[slot, a, b, core, :, :width].astype(F32) + core_recv[g, a, b, :, :width].astype(F32)
            ).astype(BF)
            return carry

        lax.fori_loop(0, 16, add, 0)
        at = x if axis == 0 else y
        waits[g][1] = [
            remote(
                g, 1 + i, held(slot, axis, lax.rem(at + 2, 4), 2 * i, 2).at[:, :, :width],
                relay_recv.at[g, i, :, :, :width], shifted(x, y, core, axis, k),
            )
            for i, k in enumerate((1, 3))
        ]

    def second(g):
        slot, (width, _, axis) = g % SLOTS, groups[g]
        at = x if axis == 0 else y
        waits[g][2] = []
        for i, k in enumerate((1, 3)):
            waits[g][1][i].wait_recv()
            there = lax.rem(at + k, 4)
            for j in range(2):
                b = 2 * i + j
                where = (slot, there, b, core) if axis == 0 else (slot, b, there, core)
                slots[where + (slice(None), slice(0, width))] = (
                    slots[where + (slice(None), slice(0, width))].astype(F32)
                    + relay_recv[g, i, j, :, :width].astype(F32)
                ).astype(BF)
            waits[g][2].append(
                remote(
                    g, 3 + i, held(slot, axis, there, 0, 4).at[:, :, :width],
                    first_recv.at[g, i, :, :, :width], shifted(x, y, core, axis, k),
                )
            )

    def third(g):
        slot, (width, _, axis) = g % SLOTS, groups[g]
        at, other = (x, y) if axis == 0 else (y, x)
        for copy in waits[g][2]:
            copy.wait_recv()
        for b in range(4):
            where = (slot, at, b, core) if axis == 0 else (slot, b, at, core)
            mid[g, b, :, :width] = (
                slots[where + (slice(None), slice(0, width))].astype(F32)
                + first_recv[g, 0, b, :, :width].astype(F32)
                + first_recv[g, 1, b, :, :width].astype(F32)
            ).astype(BF)
        waits[g][3] = [
            remote(
                g, 4 + k, mid.at[g, lax.rem(other + k, 4), :, :width], last_recv.at[g, k - 1, :, :width],
                shifted(x, y, core, 1 - axis, k),
            )
            for k in (2, 1, 3)
        ]

    def fourth(g):
        width, pieces, axis = groups[g]
        other = y if axis == 0 else x
        value = mid[g, other, :, :width].astype(F32)
        for i, copy in enumerate(waits[g][3]):
            copy.wait_recv()
        for k in range(3):
            value = value + last_recv[g, k, :, :width].astype(F32)
        column = 0
        for section, low, high in pieces:
            base = spans[section][0]
            final[:, base + low : base + high] = value[:, column : column + high - low]
            column += high - low

    count = len(groups)
    for i in range(count + 4):
        for stage, step in enumerate((zero, first, second, third, fourth)):
            if 0 <= i - stage < count:
                step(i - stage)
    hidden = gate_out.shape[1]
    mix = q_out.shape[1]
    gate_out[...] = final[:, :hidden]
    up_out[...] = final[:, hidden : 2 * hidden]
    down_out[...] = final[:, spans[1][0] : spans[1][1]].T
    out_out[...] = final[:, spans[2][0] : spans[2][1]].T
    low = spans[3][0]
    q_out[...] = final[:, low : low + mix]
    k_out[...] = final[:, low + mix : low + mix + HD]
    v_out[...] = final[:, low + mix + HD : low + mix + 2 * HD]
    vec_out[...] = final[:, spans[4][0] : spans[4][1]]
    for g in range(count):
        for stage in range(4):
            if stage == 3 or g >= count - SLOTS:
                for copy in waits[g][stage]:
                    copy.wait_send()


def collect(levels, vectors, depth, ident):
    widths = [levels[0][i].shape[1] for i in (1, 3, 5, 7)] + [LANES]
    spans, total = [], 0
    for width in widths:
        spans.append((total, total + width))
        total += width
    pieces = []
    for section, width in enumerate(widths):
        low = 0
        while low < width:
            pieces.append((section, low, low + LANES))
            low += LANES
    groups = []
    per = GROUP // LANES
    for index in range(0, len(pieces), per):
        merged = []
        for section, low, high in pieces[index : index + per]:
            if merged and merged[-1][0] == section:
                merged[-1] = (section, merged[-1][1], high)
            else:
                merged.append((section, low, high))
        width = sum(high - low for _, low, high in merged)
        groups.append((width, merged, (index // per) % 2))
    counts = [level[0].shape[0] for level in levels]
    rows = sum(counts)
    model = levels[0][0].shape[1]
    hidden, mix = widths[1], widths[2]
    many = len(groups)
    args = [item for level in levels for item in level] + [vectors]
    return pl.pallas_call(
        functools.partial(collect_kernel, counts, spans, groups),
        out_shape=(
            jax.ShapeDtypeStruct((depth, mix), F32),
            jax.ShapeDtypeStruct((depth, HD), F32),
            jax.ShapeDtypeStruct((depth, HD), F32),
            jax.ShapeDtypeStruct((mix, depth), F32),
            jax.ShapeDtypeStruct((depth, hidden), F32),
            jax.ShapeDtypeStruct((depth, hidden), F32),
            jax.ShapeDtypeStruct((hidden, depth), F32),
            jax.ShapeDtypeStruct((depth, LANES), F32),
        ),
        in_specs=[pl.BlockSpec(memory_space=pl.ANY)] * (len(args) - 1) + vmem(1),
        out_specs=tuple(vmem(8)),
        scratch_shapes=[
            pltpu.VMEM((4, rows, model), BF),
            pltpu.VMEM((4, model, rows), BF),
            pltpu.VMEM((rows, spans[3][1]), BF),
            pltpu.VMEM((depth, total), F32),
            pltpu.VMEM((SLOTS, 4, 4, 2, depth, GROUP), BF),
            pltpu.VMEM((many, 4, 4, depth, GROUP), BF),
            pltpu.VMEM((many, 2, 2, depth, GROUP), BF),
            pltpu.VMEM((many, 2, 4, depth, GROUP), BF),
            pltpu.VMEM((many, 4, depth, GROUP), BF),
            pltpu.VMEM((many, 3, depth, GROUP), BF),
            pltpu.SemaphoreType.DMA((len(levels), 8)),
            pltpu.SemaphoreType.DMA((many, 8)),
            pltpu.SemaphoreType.DMA((many, 8)),
        ],
        compiler_params=pltpu.CompilerParams(
            collective_id=ident, has_side_effects=True, vmem_limit_bytes=VMEM_LIMIT
        ),
        name="collect",
    )(*args)


def rotary_tables(place, heads):
    freq = jnp.exp(jnp.arange(HD // 2, dtype=F32) * (-2.0 * math.log(ROPE_BASE) / HD))
    angle = place.astype(F32)[:, None] * freq[None, :]
    cosine, sine = jnp.cos(angle), jnp.sin(angle)
    one = jnp.concatenate([cosine, cosine], axis=1)
    two = jnp.concatenate([-sine, sine], axis=1)
    return (
        jnp.concatenate([jnp.tile(one, (1, heads + 1)), jnp.ones(one.shape, F32)], axis=1),
        jnp.concatenate([jnp.tile(two, (1, heads + 1)), jnp.zeros(one.shape, F32)], axis=1),
    )


def local(
    tokens, depths, second_slot, third_slot, w_query, w_key, w_value, w_out, w_gate, w_up,
    w_down, norm_first, norm_second, router, cotangent,
):
    me = lax.axis_index("dp")
    devices, mp = lax.axis_size("dp"), lax.axis_size("mp")
    rows = tokens.shape[0]
    heads = w_query.shape[1] // HD
    hidden_width = w_gate.shape[1]
    depth = w_query.shape[0]

    picks, marks = [], []
    for active, slot, capacity in (
        ((depths >= 2) & (second_slot >= 0), second_slot, SECOND_SLOTS),
        ((depths >= 3) & (third_slot >= 0), third_slot, THIRD_SLOTS),
    ):
        pick = (jnp.arange(capacity)[:, None] == slot[None, :]) & active[None, :]
        picks.append(pick.astype(BF))
        marks.append(
            jnp.min(jnp.where(pick, jnp.arange(rows, dtype=jnp.int32)[None, :], rows), axis=1)
        )

    def column(values):
        return values.reshape(depth, 1).astype(BF)

    second_mark = jnp.pad(marks[0], (0, 2 * depth - SECOND_SLOTS), constant_values=rows)
    extras = jnp.concatenate(
        [
            column(norm_first), column(norm_second), column(router),
            column(second_mark[:depth]), column(second_mark[depth:]), column(marks[1]),
            jnp.zeros((depth, LANES - 6), BF),
        ],
        axis=1,
    )
    weights, gains = spread(w_query, w_key, w_value, w_out, w_gate, w_up, w_down, extras, 13)
    weights = weights.reshape(devices * depth, -1)
    marks_all = gains[3:6].astype(jnp.int32).reshape(3, devices, depth)
    second_all = jnp.concatenate(
        [marks_all[0], marks_all[1, :, : SECOND_SLOTS - depth]], axis=1
    )
    base = (jnp.arange(devices, dtype=jnp.int32) * rows)[:, None]

    def place_of(mark, offset):
        return jnp.where(mark < rows, mark + offset, FAR)

    def key_column(mark):
        return jnp.broadcast_to(place_of(mark, base).reshape(-1, 1), (mark.size, LANES))

    levels = (
        (rows, None, jnp.arange(rows, dtype=jnp.int32) + me * rows, None),
        (SECOND_SLOTS, picks[0], place_of(marks[0], me * rows), key_column(second_all)),
        (THIRD_SLOTS, picks[1], place_of(marks[1], me * rows), key_column(marks_all[2])),
    )
    state = tokens
    kept = []
    for index, (count, pick, place, key_place) in enumerate(levels):
        tables = rotary_tables(jnp.where(place == FAR, 0, place), heads)
        query_place = jnp.tile(place, heads)[None, :]
        rows_in, normed, packed, query, mixed_t, log_total, mixed = attend(
            state, pick, key_place, query_place, gains, tables, weights, heads, devices, count, index
        )
        attn, ffn, second, parts, state = feed(
            state, rows_in, mixed, pick, gains, weights, hidden_width, mp, count, 3 + index
        )
        kept.append(
            (pick, key_place, query_place, tables, rows_in, normed, packed, query, mixed_t, log_total, mixed,
             attn, ffn, second, parts)
        )

    flow = cotangent
    tail = None
    terms, vectors = [], []
    for index in (2, 1, 0, None):
        head = None
        if index is not None:
            (pick, key_place, query_place, tables, rows_in, normed, packed, query, mixed_t, log_total, mixed,
             attn, ffn, second, parts) = kept[index]
            head = (rows_in, attn, ffn, second, parts, pick)
        outs = list(
            feed_back(flow, gains, tail, head, weights, hidden_width, heads * HD, mp, 6 + (3 if index is None else index))
        )
        if tail is not None:
            flow, first_vec, router_vec = outs[:3]
            outs = outs[3:]
            vectors.append((first_vec, None, router_vec))
        if head is not None:
            grad_attn, grad_middle, logit, grad_mixed, parts_grad, hidden, grad_ffn, second_vec = outs
            vectors.append((None, second_vec, None))
            grad_qkv = attend_back(
                key_place, query_place, query, packed, mixed_t, log_total, grad_mixed, tables,
                heads, devices, rows_in.shape[0], 10 + index,
            )
            tail = (grad_qkv, rows_in, grad_middle, logit, pick)
            terms.append((second, parts_grad, grad_ffn, hidden, grad_attn, mixed, normed, grad_qkv))
    vectors = [sum(item for item in items if item is not None) for items in zip(*vectors)]
    vectors = jnp.concatenate(vectors + [jnp.zeros((LANES - 3, flow.shape[1]), F32)], axis=0)
    query_grad, key_grad, value_grad, out_grad, gate_grad, up_grad, down_grad, vec = collect(
        terms[::-1], vectors, depth, 14
    )
    return (
        state, flow, query_grad, key_grad, value_grad, out_grad, gate_grad, up_grad, down_grad,
        vec[:, 0], vec[:, 1], vec[:, 2],
    )


def solution(mesh):
    in_specs = (
        P("dp", None), P("dp"), P("dp"), P("dp"), P("dp", "mp"), P("dp", "mp"), P("dp", "mp"),
        P("mp", "dp"), P("dp", "mp"), P("dp", "mp"), P("mp", "dp"), P("dp"), P("dp"), P("dp"),
        P("dp", None),
    )
    out_specs = (
        P("dp", None), P("dp", None), P("dp", "mp"), P("dp", "mp"), P("dp", "mp"), P("mp", "dp"),
        P("dp", "mp"), P("dp", "mp"), P("mp", "dp"), P("dp"), P("dp"), P("dp"),
    )
    return jax.shard_map(local, mesh=mesh, in_specs=in_specs, out_specs=out_specs, check_vma=False)
```

```python
import functools
import math

import jax
import jax.numpy as jnp
from jax import lax
from jax.experimental import pallas as pl
from jax.experimental.pallas import tpu as pltpu
from jax.sharding import PartitionSpec as P

HD = 64
SECOND_SLOTS = 96
THIRD_SLOTS = 64
EPS = 1e-05
NEG = -1e30
ROPE_BASE = 10000.0
FAR = 1073741824
BF = jnp.bfloat16
F32 = jnp.float32
MESH = pl.DeviceIdType.MESH
LANES = 128
VMEM_LIMIT = 58 * 1024 * 1024


def dot_nn(left, right):
    return lax.dot_general(left, right, (((1,), (0,)), ((), ())), preferred_element_type=F32)


def dot_nt(left, right):
    return lax.dot_general(left, right, (((1,), (1,)), ((), ())), preferred_element_type=F32)


def dot_tn(left, right):
    return lax.dot_general(left, right, (((0,), (0,)), ((), ())), preferred_element_type=F32)


def unit_of(values):
    factor = lax.rsqrt(jnp.mean(values * values, axis=-1, keepdims=True) + EPS)
    return values * factor, factor


def unit_back(shaped, unit, factor):
    return factor * (shaped - unit * jnp.mean(shaped * unit, axis=-1, keepdims=True))


def sigmoid(values):
    return 1.0 / (1.0 + jnp.exp(-values))


def lanes_of(shape):
    return lax.broadcasted_iota(jnp.int32, shape, 1)


def swap_halves(tile):
    first = lax.rem(lanes_of(tile.shape), HD) < HD // 2
    return jnp.where(first, pltpu.roll(tile, LANES - HD // 2, 1), pltpu.roll(tile, HD // 2, 1))


def tile_of(values, index):
    return values[:, index * LANES : (index + 1) * LANES]


def signal_all(group, me, axis):
    barrier = pltpu.get_barrier_semaphore()
    for k in range(1, group):
        pl.semaphore_signal(
            barrier, inc=1, device_id={axis: lax.rem(me + k, group)}, device_id_type=MESH
        )
    pl.semaphore_wait(barrier, group - 1)


def sum_over_mp(group, me, make_chunk, send, recv, full, sems):
    order = (2, 1, 3)
    copies = []
    for k in order:
        peer = lax.rem(me + k, group)
        send[k - 1] = make_chunk(peer).astype(BF)
        copy = pltpu.make_async_remote_copy(
            src_ref=send.at[k - 1], dst_ref=recv.at[k - 1],
            send_sem=sems.at[0, k - 1], recv_sem=sems.at[1, k - 1],
            device_id={"mp": peer}, device_id_type=MESH,
        )
        copy.start()
        copies.append(copy)
    total = make_chunk(me).astype(BF).astype(F32)
    for k, copy in zip(order, copies):
        copy.wait_recv()
        total = total + recv[k - 1].astype(F32)
    full[me] = total.astype(BF)
    backs = []
    for k in order:
        peer = lax.rem(me + k, group)
        copy = pltpu.make_async_remote_copy(
            src_ref=full.at[me], dst_ref=full.at[me],
            send_sem=sems.at[2, k - 1], recv_sem=sems.at[3, k - 1],
            device_id={"mp": peer}, device_id_type=MESH,
        )
        copy.start()
        backs.append(copy)
    for copy in backs:
        copy.wait_recv()
    for copy in copies + backs:
        copy.wait_send()
    return jnp.concatenate([full[c] for c in range(group)], axis=1)


def attend_kernel(n, heads, devices, group, picked, *refs):
    refs = list(refs)
    source = refs.pop(0)
    pick = refs.pop(0) if picked else None
    key_place = refs.pop(0) if picked else None
    query_place, gains, cosine, sine, w_hbm = [refs.pop(0) for _ in range(5)]
    rows_out, normed_out, packed_out, query_out, mixed_t_out, log_out, mixed_out = [
        refs.pop(0) for _ in range(7)
    ]
    w_v, packed, query_t, top, total, acc, w_sem, out_sem, send_sems, recv_sems = refs
    me = lax.axis_index("dp")
    width = heads * n
    load_w = pltpu.make_async_copy(w_hbm.at[:, : w_v.shape[1]], w_v, w_sem)
    load_w.start()

    barrier = pltpu.get_barrier_semaphore()

    def greet(e, carry):
        pl.semaphore_signal(barrier, inc=1, device_id={"dp": e}, device_id_type=MESH)
        return carry

    lax.fori_loop(0, me, greet, 0)

    if picked:
        rows = dot_nn(pick[...], source[...].astype(BF)).astype(BF)
    else:
        rows = source[...]
    rows_out[...] = rows
    unit, unused = unit_of(rows.astype(F32))
    normed = (unit * gains[0:1, :]).astype(BF)
    normed_out[...] = normed
    load_w.wait()
    tiles = []
    for t in range(heads // 2 + 1):
        if t % 2 == 0:
            last = min((t + 2) * LANES, (heads // 2 + 1) * LANES)
            both = dot_nn(normed, w_v[:, t * LANES : last])
        part = tile_of(both, t % 2)
        cut = slice(t * LANES, (t + 1) * LANES)
        tiles.append(part * cosine[:, cut] + swap_halves(part) * sine[:, cut])
    packed[me] = tiles[-1].astype(BF)

    @pl.when(me < devices - 1)
    def _():
        pl.semaphore_wait(barrier, devices - 1 - me)

    def send_copy(e, source_index):
        return pltpu.make_async_remote_copy(
            src_ref=packed.at[me], dst_ref=packed.at[me],
            send_sem=send_sems.at[e], recv_sem=recv_sems.at[source_index],
            device_id={"dp": e}, device_id_type=MESH,
        )

    def send(e, carry):
        send_copy(e, me).start()
        return carry

    lax.fori_loop(me + 1, devices, send, 0)

    def clear(e, carry):
        packed[e] = jnp.zeros((n, 2 * HD), BF)
        return carry

    lax.fori_loop(me + 1, devices, clear, 0)

    left = lanes_of((n, LANES)) < HD
    for t in range(heads // 2):
        scaled = tiles[t].astype(BF).astype(F32) * HD**-0.5
        query_out[2 * t * n : (2 * t + 1) * n, :] = jnp.where(left, scaled, 0.0).astype(BF)
        query_out[(2 * t + 1) * n : (2 * t + 2) * n, :] = jnp.where(
            left, pltpu.roll(scaled, HD, 1), 0.0
        ).astype(BF)
    query_t[...] = query_out[...].T
    top[...] = jnp.full((1, width), NEG, F32)
    total[...] = jnp.zeros((1, width), F32)
    acc[...] = jnp.zeros((2 * HD, width), F32)

    def one_block(b, carry):
        for g in range(group):
            e = b * group + g

            @pl.when(e < me)
            def _():
                send_copy(me, e).wait_recv()

        part = packed[pl.ds(b * group, group)].reshape(group * n, 2 * HD)
        scores = dot_nn(part, query_t[...])
        if picked:
            start = pl.multiple_of(b * (group * n), group * n)
            place = key_place[pl.ds(start, group * n), :]
        else:
            place = lax.broadcasted_iota(jnp.int32, (group * n, LANES), 0) + b * (group * n)
        place = jnp.concatenate([place] * (width // LANES), axis=1)
        scores = jnp.where(place <= query_place[...], scores, NEG)
        peak = jnp.maximum(top[...], jnp.max(scores, axis=0, keepdims=True))
        weights = jnp.exp(scores - peak)
        fade = jnp.exp(top[...] - peak)
        total[...] = total[...] * fade + jnp.sum(weights, axis=0, keepdims=True)
        acc[...] = acc[...] * fade + dot_tn(part, weights.astype(BF))
        top[...] = peak
        return carry

    lax.fori_loop(0, me // group + 1, one_block, 0)
    mixed_t = acc[...] / total[...]
    mixed_t_out[...] = mixed_t
    log_out[...] = top[...] + jnp.log(total[...])
    mixed = mixed_t.T
    for t in range(heads // 2):
        even = mixed[2 * t * n : (2 * t + 1) * n, :]
        odd = mixed[(2 * t + 1) * n : (2 * t + 2) * n, :]
        mixed_out[:, t * LANES : (t + 1) * LANES] = jnp.where(
            left, pltpu.roll(even, HD, 1), odd
        ).astype(BF)
    keep = pltpu.make_async_copy(packed, packed_out, out_sem)
    keep.start()

    def sent(e, carry):
        send_copy(e, me).wait_send()
        return carry

    lax.fori_loop(me + 1, devices, sent, 0)
    keep.wait()


def vmem(count):
    return [pl.BlockSpec(memory_space=pltpu.VMEM)] * count


def attend(source, pick, key_place, query_place, gains, tables, w_qkv, heads, devices, n, ident):
    picked = pick is not None
    group = 512 // n if 512 % n == 0 else 4
    width = heads * n
    qkv_width = (heads + 2) * HD
    args = [source] + ([pick, key_place] if picked else []) + [query_place, gains, *tables, w_qkv]
    model = source.shape[1]
    return pl.pallas_call(
        functools.partial(attend_kernel, n, heads, devices, group, picked),
        out_shape=(
            jax.ShapeDtypeStruct((n, model), BF),
            jax.ShapeDtypeStruct((n, model), BF),
            jax.ShapeDtypeStruct((devices, n, 2 * HD), BF),
            jax.ShapeDtypeStruct((width, 2 * HD), BF),
            jax.ShapeDtypeStruct((2 * HD, width), F32),
            jax.ShapeDtypeStruct((1, width), F32),
            jax.ShapeDtypeStruct((n, heads * HD), BF),
        ),
        in_specs=vmem(len(args) - 1) + [pl.BlockSpec(memory_space=pl.ANY)],
        out_specs=tuple(vmem(2) + [pl.BlockSpec(memory_space=pl.ANY)] + vmem(4)),
        scratch_shapes=[
            pltpu.VMEM((model, qkv_width), BF),
            pltpu.VMEM((devices, n, 2 * HD), BF),
            pltpu.VMEM((2 * HD, width), BF),
            pltpu.VMEM((1, width), F32),
            pltpu.VMEM((1, width), F32),
            pltpu.VMEM((2 * HD, width), F32),
            pltpu.SemaphoreType.DMA(()),
            pltpu.SemaphoreType.DMA(()),
            pltpu.SemaphoreType.DMA((devices,)),
            pltpu.SemaphoreType.DMA((devices,)),
        ],
        compiler_params=pltpu.CompilerParams(
            collective_id=ident, has_side_effects=True, vmem_limit_bytes=VMEM_LIMIT
        ),
        cost_estimate=pl.CostEstimate(flops=4 * 10**9, bytes_accessed=10**7, transcendentals=0),
        name=f"attend_{n}",
    )(*args)


def attend_back_kernel(n, heads, devices, group, picked, *refs):
    refs = list(refs)
    key_place = refs.pop(0) if picked else None
    query_place, query, packed, mixed_t, log_total, grad_mixed, cosine, sine = [
        refs.pop(0) for _ in range(8)
    ]
    grad_out = refs.pop(0)
    query_t, grad_rows, grad_t, acc, delta, send_buf, recv_buf, send_sems, recv_sems = refs
    me = lax.axis_index("dp")
    barrier = pltpu.get_barrier_semaphore()

    def greet(e, carry):
        pl.semaphore_signal(barrier, inc=1, device_id={"dp": e}, device_id_type=MESH)
        return carry

    lax.fori_loop(me + 1, devices, greet, 0)

    left = lanes_of((n, LANES)) < HD
    for t in range(heads // 2):
        part = grad_mixed[:, t * LANES : (t + 1) * LANES].astype(F32)
        grad_rows[2 * t * n : (2 * t + 1) * n, :] = jnp.where(
            left, 0.0, pltpu.roll(part, HD, 1)
        ).astype(BF)
        grad_rows[(2 * t + 1) * n : (2 * t + 2) * n, :] = jnp.where(left, 0.0, part).astype(BF)
    query_t[...] = query[...].T
    grad_t[...] = grad_rows[...].T
    delta[...] = jnp.sum(grad_t[...].astype(F32) * mixed_t[...], axis=0, keepdims=True)
    acc[...] = jnp.zeros(acc.shape, F32)
    width = heads * n

    @pl.when(me > 0)
    def _():
        pl.semaphore_wait(barrier, me)

    def send_copy(e, source_index):
        return pltpu.make_async_remote_copy(
            src_ref=send_buf.at[e], dst_ref=recv_buf.at[source_index],
            send_sem=send_sems.at[e], recv_sem=recv_sems.at[source_index],
            device_id={"dp": e}, device_id_type=MESH,
        )

    def one_block(b, carry):
        part = packed[pl.ds(b * group, group)].reshape(group * n, 2 * HD)
        scores = dot_nn(part, query_t[...])
        if picked:
            start = pl.multiple_of(b * (group * n), group * n)
            place = key_place[pl.ds(start, group * n), :]
        else:
            place = lax.broadcasted_iota(jnp.int32, (group * n, LANES), 0) + b * (group * n)
        place = jnp.concatenate([place] * (width // LANES), axis=1)
        scores = jnp.where(place <= query_place[...], scores, NEG)
        weights = jnp.exp(scores - log_total[...])
        grad_weights = dot_nn(part, grad_t[...])
        grad_scores = (weights * (grad_weights - delta[...])).astype(BF)
        grad_part = dot_nn(grad_scores, query[...]) + dot_nn(weights.astype(BF), grad_rows[...])
        send_buf[pl.ds(b * group, group)] = grad_part.astype(BF).reshape(group, n, 2 * HD)
        acc[...] += dot_tn(part, grad_scores)
        for g in range(group):
            e = b * group + g

            @pl.when(e < me)
            def _():
                send_copy(e, me).start()

        return carry

    lax.fori_loop(0, me // group + 1, one_block, 0)

    grad_query = acc[...].T * HD**-0.5
    outs = []
    for t in range(heads // 2):
        even = grad_query[2 * t * n : (2 * t + 1) * n, :]
        odd = grad_query[(2 * t + 1) * n : (2 * t + 2) * n, :]
        outs.append(jnp.where(left, even, pltpu.roll(odd, HD, 1)))

    def add(e, carry):
        send_copy(me, e).wait_recv()
        return carry + recv_buf[e].astype(F32)

    outs.append(lax.fori_loop(me + 1, devices, add, send_buf[me].astype(F32)))
    for t, part in enumerate(outs):
        cut = slice(t * LANES, (t + 1) * LANES)
        grad_out[:, cut] = (part * cosine[:, cut] - swap_halves(part) * sine[:, cut]).astype(BF)

    def sent(e, carry):
        send_copy(e, me).wait_send()
        return carry

    lax.fori_loop(0, me, sent, 0)


def attend_back(key_place, query_place, query, packed, mixed_t, log_total, grad_mixed, tables, heads, devices, n, ident):
    picked = key_place is not None
    group = 512 // n if 512 % n == 0 else 4
    width = heads * n
    args = ([key_place] if picked else []) + [
        query_place, query, packed, mixed_t, log_total, grad_mixed, *tables
    ]
    return pl.pallas_call(
        functools.partial(attend_back_kernel, n, heads, devices, group, picked),
        out_shape=jax.ShapeDtypeStruct((n, (heads + 2) * HD), BF),
        in_specs=vmem(len(args)),
        out_specs=pl.BlockSpec(memory_space=pltpu.VMEM),
        scratch_shapes=[
            pltpu.VMEM((2 * HD, width), BF),
            pltpu.VMEM((width, 2 * HD), BF),
            pltpu.VMEM((2 * HD, width), BF),
            pltpu.VMEM((2 * HD, width), F32),
            pltpu.VMEM((1, width), F32),
            pltpu.VMEM((devices, n, 2 * HD), BF),
            pltpu.VMEM((devices, n, 2 * HD), BF),
            pltpu.SemaphoreType.DMA((devices,)),
            pltpu.SemaphoreType.DMA((devices,)),
        ],
        compiler_params=pltpu.CompilerParams(
            collective_id=ident, has_side_effects=True, vmem_limit_bytes=VMEM_LIMIT
        ),
        cost_estimate=pl.CostEstimate(flops=10**10, bytes_accessed=10**7, transcendentals=0),
        name=f"attend_back_{n}",
    )(*args)


def feed_kernel(n, mp, picked, *refs):
    refs = list(refs)
    state, rows_in, mixed = [refs.pop(0) for _ in range(3)]
    pick = refs.pop(0) if picked else None
    gains, w_hbm = refs.pop(0), refs.pop(0)
    attn_out, ffn_out, second_out, parts_out, state_out = [refs.pop(0) for _ in range(5)]
    w_o, w_gu, w_d, hidden, w_sems, send_a, recv_a, full_a, sems_a, send_b, recv_b, full_b, sems_b = refs
    me = lax.axis_index("mp")
    wide_o, wide_gu, wide_d = w_o.shape[1], w_gu.shape[1], w_d.shape[1]
    loads = []
    start = wide_o + 2 * LANES
    for index, (ref, wide) in enumerate(((w_o, wide_o), (w_gu, wide_gu), (w_d, wide_d))):
        load = pltpu.make_async_copy(w_hbm.at[:, start : start + wide], ref, w_sems.at[index])
        load.start()
        loads.append(load)
        start += wide
    signal_all(mp, me, "mp")
    chunk = w_o.shape[0] // mp
    loads[0].wait()
    mixed_now = mixed[...]

    def out_chunk(c):
        return dot_nt(mixed_now, w_o[pl.ds(pl.multiple_of(c * chunk, chunk), chunk), :])

    attn = sum_over_mp(mp, me, out_chunk, send_a, recv_a, full_a, sems_a)
    attn_out[...] = attn
    level = rows_in[...].astype(F32)
    unit, unused = unit_of(level + attn.astype(F32))
    second = (unit * gains[1:2, :]).astype(BF)
    second_out[...] = second
    loads[1].wait()
    step = 256
    for t in range(wide_gu // step):
        parts_out[:, t * step : (t + 1) * step] = dot_nn(second, w_gu[:, t * step : (t + 1) * step])
    half = wide_gu // 2
    for t in range(half // LANES):
        cut = slice(t * LANES, (t + 1) * LANES)
        gate_part = parts_out[:, cut]
        up_part = parts_out[:, half + t * LANES : half + (t + 1) * LANES]
        hidden[:, cut] = (gate_part * sigmoid(gate_part) * up_part).astype(BF)
    loads[2].wait()
    hidden_now = hidden[...]

    def down_chunk(c):
        return dot_nt(hidden_now, w_d[pl.ds(pl.multiple_of(c * chunk, chunk), chunk), :])

    ffn = sum_over_mp(mp, me, down_chunk, send_b, recv_b, full_b, sems_b)
    ffn_out[...] = ffn
    gate = sigmoid(jnp.sum(level * gains[2:3, :], axis=-1, keepdims=True))
    update = (gate * (attn.astype(F32) + ffn.astype(F32))).astype(BF)
    if picked:
        state_out[...] = state[...].astype(F32) + dot_tn(pick[...], update)
    else:
        state_out[...] = state[...].astype(F32) + update.astype(F32)


def sum_scratch(mp, n, model):
    return [
        pltpu.VMEM((mp - 1, n, model // mp), BF),
        pltpu.VMEM((mp - 1, n, model // mp), BF),
        pltpu.VMEM((mp, n, model // mp), BF),
        pltpu.SemaphoreType.DMA((4, mp - 1)),
    ]


def feed(state, rows, mixed, pick, gains, w_rest, hidden_width, mp, n, ident):
    picked = pick is not None
    model = rows.shape[1]
    args = [state, rows, mixed] + ([pick] if picked else []) + [gains, w_rest]
    return pl.pallas_call(
        functools.partial(feed_kernel, n, mp, picked),
        out_shape=(
            jax.ShapeDtypeStruct((n, model), BF),
            jax.ShapeDtypeStruct((n, model), BF),
            jax.ShapeDtypeStruct((n, model), BF),
            jax.ShapeDtypeStruct((n, 2 * hidden_width), F32),
            jax.ShapeDtypeStruct(state.shape, F32),
        ),
        in_specs=vmem(len(args) - 1) + [pl.BlockSpec(memory_space=pl.ANY)],
        out_specs=tuple(vmem(5)),
        scratch_shapes=[
            pltpu.VMEM((model, mixed.shape[1]), BF),
            pltpu.VMEM((model, 2 * hidden_width), BF),
            pltpu.VMEM((model, hidden_width), BF),
            pltpu.VMEM((n, hidden_width), BF),
            pltpu.SemaphoreType.DMA((3,)),
            *sum_scratch(mp, n, model),
            *sum_scratch(mp, n, model),
        ],
        compiler_params=pltpu.CompilerParams(
            collective_id=ident, has_side_effects=True, vmem_limit_bytes=VMEM_LIMIT
        ),
        cost_estimate=pl.CostEstimate(flops=5 * 10**9, bytes_accessed=10**8, transcendentals=0),
        name=f"feed_{n}",
    )(*args)


def feed_back_kernel(tail_n, head_n, mp, tail_picked, head_picked, *refs):
    refs = list(refs)
    flow, gains = refs.pop(0), refs.pop(0)
    if tail_n:
        grad_qkv, tail_rows, tail_middle, tail_logit = [refs.pop(0) for _ in range(4)]
        tail_pick = refs.pop(0) if tail_picked else None
    if head_n:
        rows_in, attn, ffn, second, parts = [refs.pop(0) for _ in range(5)]
        head_pick = refs.pop(0) if head_picked else None
    if tail_n:
        w_first_hbm = refs.pop(0)
    if head_n:
        w_rest_hbm = refs.pop(0)
    if tail_n:
        flow_out, first_out, router_out = [refs.pop(0) for _ in range(3)]
    if head_n:
        attn_grad_out, middle_out, logit_out, mixed_out, parts_grad_out, hidden_out, ffn_grad_out, second_vec_out = [
            refs.pop(0) for _ in range(8)
        ]
    if tail_n:
        w_qkv, w_first_sem = refs.pop(0), refs.pop(0)
        send_a, recv_a, full_a, sems_a = [refs.pop(0) for _ in range(4)]
    if head_n:
        w_o, w_gu, w_d, w_sems = [refs.pop(0) for _ in range(4)]
        send_b, recv_b, full_b, sems_b = [refs.pop(0) for _ in range(4)]
    me = lax.axis_index("mp")
    if tail_n:
        load_first = pltpu.make_async_copy(w_first_hbm.at[:, : w_qkv.shape[1]], w_qkv, w_first_sem)
        load_first.start()
    if head_n:
        loads = {}
        wide_o, wide_gu, wide_d = w_o.shape[1], w_gu.shape[1], w_d.shape[1]
        for index, (name, ref, start) in enumerate(
            (("d", w_d, wide_o + wide_gu), ("gu", w_gu, wide_o), ("o", w_o, 0))
        ):
            start += wide_o + 2 * LANES
            loads[name] = pltpu.make_async_copy(
                w_rest_hbm.at[:, start : start + ref.shape[1]], ref, w_sems.at[index]
            )
            loads[name].start()
    signal_all(mp, me, "mp")

    if tail_n:
        load_first.wait()
        grad_now = grad_qkv[...]
        chunk = w_qkv.shape[0] // mp

        def first_chunk(c):
            return dot_nt(grad_now, w_qkv[pl.ds(pl.multiple_of(c * chunk, chunk), chunk), :])

        grad_normed = sum_over_mp(mp, me, first_chunk, send_a, recv_a, full_a, sems_a).astype(F32)
        level = tail_rows[...].astype(F32)
        unit, factor = unit_of(level)
        first_out[...] = jnp.sum(grad_normed * unit, axis=0, keepdims=True)
        router_out[...] = jnp.sum(level * tail_logit[...], axis=0, keepdims=True)
        grad_rows = (
            unit_back(grad_normed * gains[0:1, :], unit, factor)
            + tail_middle[...]
            + tail_logit[...] * gains[2:3, :]
        ).astype(BF)
        if tail_picked:
            flow_now = flow[...] + dot_tn(tail_pick[...], grad_rows)
        else:
            flow_now = flow[...] + grad_rows.astype(F32)
        flow_out[...] = flow_now
    else:
        flow_now = flow[...]

    if head_n:
        grad_update = flow_now.astype(BF)
        if head_picked:
            grad_update = dot_nn(head_pick[...], grad_update)
        grad_update = grad_update.astype(F32)
        level = rows_in[...].astype(F32)
        attn_now = attn[...].astype(F32)
        gate = sigmoid(jnp.sum(level * gains[2:3, :], axis=-1, keepdims=True))
        logit = jnp.sum(grad_update * (attn_now + ffn[...].astype(F32)), axis=-1, keepdims=True)
        logit_out[...] = logit * gate * (1.0 - gate)
        grad_ffn = (gate * grad_update).astype(BF)
        ffn_grad_out[...] = grad_ffn
        half = wide_d
        loads["d"].wait()
        for t in range(half // LANES):
            cut = slice(t * LANES, (t + 1) * LANES)
            up_cut = slice(half + t * LANES, half + (t + 1) * LANES)
            if t % 2 == 0:
                both = dot_nn(grad_ffn, w_d[:, t * LANES : min((t + 2) * LANES, half)])
            grad_hidden = tile_of(both, t % 2)
            gate_part = parts[:, cut]
            up_part = parts[:, up_cut]
            sigma = sigmoid(gate_part)
            active = gate_part * sigma
            hidden_out[:, cut] = (active * up_part).astype(BF)
            parts_grad_out[:, cut] = (
                grad_hidden * up_part * sigma * (1.0 + gate_part * (1.0 - sigma))
            ).astype(BF)
            parts_grad_out[:, up_cut] = (grad_hidden * active).astype(BF)
        loads["gu"].wait()
        parts_now = parts_grad_out[...]
        chunk = w_gu.shape[0] // mp

        def second_chunk(c):
            return dot_nt(parts_now, w_gu[pl.ds(pl.multiple_of(c * chunk, chunk), chunk), :])

        grad_second = sum_over_mp(mp, me, second_chunk, send_b, recv_b, full_b, sems_b).astype(F32)
        unit, factor = unit_of(level + attn_now)
        second_vec_out[...] = jnp.sum(grad_second * unit, axis=0, keepdims=True)
        grad_middle = unit_back(grad_second * gains[1:2, :], unit, factor)
        middle_out[...] = grad_middle
        grad_attn = (gate * grad_update + grad_middle).astype(BF)
        attn_grad_out[...] = grad_attn
        loads["o"].wait()
        mixed_out[...] = dot_nn(grad_attn, w_o[...]).astype(BF)


def feed_back(flow, gains, tail, head, weights, hidden_width, mix, mp, ident):
    model = flow.shape[1]
    args, outs, scratch = [flow, gains], [], []
    tail_n = head_n = 0
    tail_picked = head_picked = False
    if tail is not None:
        *items, pick = tail
        tail_n, tail_picked = items[0].shape[0], pick is not None
        args += items + ([pick] if tail_picked else [])
    if head is not None:
        *items, pick = head
        head_n, head_picked = items[0].shape[0], pick is not None
        args += items + ([pick] if head_picked else [])
    in_vmem = len(args)
    if tail_n:
        args.append(weights)
        outs += [
            jax.ShapeDtypeStruct(flow.shape, F32),
            jax.ShapeDtypeStruct((1, model), F32),
            jax.ShapeDtypeStruct((1, model), F32),
        ]
        scratch += [
            pltpu.VMEM((model, mix + 2 * HD), BF),
            pltpu.SemaphoreType.DMA(()),
            *sum_scratch(mp, tail_n, model),
        ]
    if head_n:
        args.append(weights)
        outs += [
            jax.ShapeDtypeStruct((head_n, model), BF),
            jax.ShapeDtypeStruct((head_n, model), F32),
            jax.ShapeDtypeStruct((head_n, 1), F32),
            jax.ShapeDtypeStruct((head_n, mix), BF),
            jax.ShapeDtypeStruct((head_n, 2 * hidden_width), BF),
            jax.ShapeDtypeStruct((head_n, hidden_width), BF),
            jax.ShapeDtypeStruct((head_n, model), BF),
            jax.ShapeDtypeStruct((1, model), F32),
        ]
        scratch += [
            pltpu.VMEM((model, mix), BF),
            pltpu.VMEM((model, 2 * hidden_width), BF),
            pltpu.VMEM((model, hidden_width), BF),
            pltpu.SemaphoreType.DMA((3,)),
            *sum_scratch(mp, head_n, model),
        ]
    return pl.pallas_call(
        functools.partial(feed_back_kernel, tail_n, head_n, mp, tail_picked, head_picked),
        out_shape=tuple(outs),
        in_specs=vmem(in_vmem) + [pl.BlockSpec(memory_space=pl.ANY)] * (len(args) - in_vmem),
        out_specs=tuple(vmem(len(outs))),
        scratch_shapes=scratch,
        compiler_params=pltpu.CompilerParams(
            collective_id=ident, has_side_effects=True, vmem_limit_bytes=VMEM_LIMIT
        ),
        cost_estimate=pl.CostEstimate(flops=5 * 10**9, bytes_accessed=10**8, transcendentals=0),
        name=f"feed_back_{tail_n}_{head_n}",
    )(*args)


def plane(me):
    return me // 8, lax.rem(me // 2, 4), lax.rem(me, 2)


def peer(x, y, core):
    return {"dp": (lax.rem(x, 4) * 4 + lax.rem(y, 4)) * 2 + core}


def shifted(x, y, core, axis, k):
    return peer(x + k, y, core) if axis == 0 else peer(x, y + k, core)


def meet(me, partners):
    barrier = pltpu.get_barrier_semaphore()
    for device in partners:
        pl.semaphore_signal(barrier, inc=1, device_id=device, device_id_type=MESH)
    pl.semaphore_wait(barrier, len(partners))


def plane_partners(x, y, core):
    return (
        [peer(x, y, 1 - core)]
        + [shifted(x, y, core, 0, k) for k in (1, 2, 3)]
        + [shifted(x, y, core, 1, k) for k in (1, 2, 3)]
    )


def spread_kernel(
    groups, w_query, w_key, w_value, w_out, w_gate, w_up, w_down, extras, full, gains,
    shard, columns, own_sem, column_sem, send_sems, recv_sems,
):
    me = lax.axis_index("dp")
    x, y, core = plane(me)
    start = 0
    pair = jnp.concatenate([w_key[...].astype(F32), w_value[...].astype(F32)], axis=1).astype(BF)
    for part in (
        w_query[...], pair, extras[...],
        w_out[...].T, w_gate[...], w_up[...], w_down[...].T,
    ):
        shard[:, start : start + part.shape[1]] = part
        start += part.shape[1]
    own = pltpu.make_async_copy(shard, full.at[x, y, core], own_sem)
    own.start()
    meet(me, plane_partners(x, y, core))
    started = []

    def remote(g, index, source, target, device):
        copy = pltpu.make_async_remote_copy(
            src_ref=source, dst_ref=target, send_sem=send_sems.at[g, index],
            recv_sem=recv_sems.at[g, index], device_id=device, device_id_type=MESH,
        )
        copy.start()
        started.append(copy)
        return copy

    def line(axis, at, first, count, cut):
        if axis == 0:
            return full.at[pl.ds(first, count), at, core, :, cut]
        return full.at[at, pl.ds(first, count), core, :, cut]

    waits = [{} for _ in groups]

    def one(g):
        low, high, axis = groups[g]
        cut = slice(low, high)
        waits[g][1] = [
            remote(
                g, k - 1, shard.at[:, cut], full.at[x, y, core, :, cut],
                shifted(x, y, core, axis, k),
            )
            for k in (2, 1, 3)
        ]

    def two(g):
        low, high, axis = groups[g]
        cut = slice(low, high)
        for copy in waits[g][1]:
            copy.wait_recv()
        mine = line(axis, y if axis == 0 else x, 0, 4, cut)
        waits[g][2] = [
            remote(g, 3 + i, mine, mine, shifted(x, y, core, 1 - axis, k))
            for i, k in enumerate((1, 3))
        ]

    def three(g):
        low, high, axis = groups[g]
        cut = slice(low, high)
        at = y if axis == 0 else x
        waits[g][3] = []
        for i, k in enumerate((1, 3)):
            waits[g][2][i].wait_recv()
            piece = line(axis, lax.rem(at + 4 - k, 4), 2 * i, 2, cut)
            waits[g][3].append(
                remote(g, 5 + i, piece, piece, shifted(x, y, core, 1 - axis, k))
            )

    def four(g):
        low, high, axis = groups[g]
        for copy in waits[g][3]:
            copy.wait_recv()
        mine = full.at[:, :, core, :, slice(low, high)]
        waits[g][4] = [remote(g, 7, mine, mine, peer(x, y, 1 - core))]

    def five(g):
        waits[g][4][0].wait_recv()

    count = len(groups)
    one(0)
    one(1)
    own.wait()
    for i in range(count + 3):
        if i < count:
            two(i)
        if i + 2 < count:
            one(i + 2)
        if 0 <= i - 1 < count:
            three(i - 1)
        if 0 <= i - 2 < count:
            four(i - 2)
        if 0 <= i - 3 < count:
            five(i - 3)
            if i == 3:
                low = w_query.shape[1] + LANES
                load = pltpu.make_async_copy(
                    full.at[:, :, :, :, low : low + LANES], columns, column_sem
                )
                load.start()
                load.wait()
                flat = columns[...].reshape(gains.shape[1], LANES).astype(F32)
                gains[...] = flat.T[: gains.shape[0], :]
    for copy in started:
        copy.wait_send()


def spread(w_query, w_key, w_value, w_out, w_gate, w_up, w_down, extras, ident):
    depth, mix = w_query.shape
    hidden = w_gate.shape[1]
    total = 2 * mix + 2 * LANES + 3 * hidden
    cuts = [0, mix + 2 * LANES]
    while cuts[-1] < total:
        cuts.append(min(cuts[-1] + 512, total))
    if cuts[-1] - cuts[-2] < 256:
        cuts.pop(-2)
    groups = [(a, b, i % 2) for i, (a, b) in enumerate(zip(cuts[:-1], cuts[1:]))]
    return pl.pallas_call(
        functools.partial(spread_kernel, groups),
        out_shape=(
            jax.ShapeDtypeStruct((4, 4, 2, depth, total), BF),
            jax.ShapeDtypeStruct((8, 32 * depth), F32),
        ),
        in_specs=vmem(8),
        out_specs=(pl.BlockSpec(memory_space=pl.ANY), pl.BlockSpec(memory_space=pltpu.VMEM)),
        scratch_shapes=[
            pltpu.VMEM((depth, total), BF),
            pltpu.VMEM((4, 4, 2, depth, LANES), BF),
            pltpu.SemaphoreType.DMA(()),
            pltpu.SemaphoreType.DMA(()),
            pltpu.SemaphoreType.DMA((len(groups), 8)),
            pltpu.SemaphoreType.DMA((len(groups), 8)),
        ],
        compiler_params=pltpu.CompilerParams(
            collective_id=ident, has_side_effects=True, vmem_limit_bytes=VMEM_LIMIT
        ),
        name="spread",
    )(w_query, w_key, w_value, w_out, w_gate, w_up, w_down, extras)


SLOTS = 6
GROUP = 512


class Collect:
    def __init__(self, spans, groups, x, y, core, turned, rights, vectors, store, slots, core_recv, relay_recv, first_recv, last_recv, send_sems, recv_sems, turn):
        self.spans, self.groups = spans, groups
        self.x, self.y, self.core = x, y, core
        self.turned, self.rights, self.vectors, self.store, self.slots = turned, rights, vectors, store, slots
        self.core_recv, self.relay_recv, self.first_recv = core_recv, relay_recv, first_recv
        self.last_recv = last_recv
        self.send_sems, self.recv_sems = send_sems, recv_sems
        self.turn = turn
        self.waits = [{} for _ in groups]
        self.done = set()

    def remote(self, g, index, source, target, device):
        copy = pltpu.make_async_remote_copy(
            src_ref=source, dst_ref=target, send_sem=self.send_sems.at[g, index],
            recv_sem=self.recv_sems.at[g, index], device_id=device, device_id_type=MESH,
        )
        copy.start()
        return copy

    def held(self, slot, axis, at, first, count):
        if axis == 0:
            return self.slots.at[slot, at, pl.ds(first, count), self.core]
        return self.slots.at[slot, pl.ds(first, count), at, self.core]

    def zero(self, g):
        slot, waits = g % SLOTS, self.waits
        if g >= SLOTS:
            for stage in range(3):
                for copy in waits[g - SLOTS][stage]:
                    copy.wait_send()
        column = 0
        for section, low, high in self.groups[g][1]:
            wide = high - low
            if section < 4:
                if section not in self.done:
                    self.done.add(section)
                    self.turn(section)
                base = self.spans[section][0]

            def rows_of(m, carry, section=section, low=low, high=high, column=column, wide=wide):
                start = pl.multiple_of(m * 1024, 1024)
                if section < 4:
                    value = dot_nn(
                        self.turned[section % 2, pl.ds(start, 1024), :], self.rights[:, base + low : base + high]
                    )
                else:
                    value = self.vectors[:, pl.ds(start, 1024)].T
                self.slots[slot, pl.ds(m * 2, 2), :, :, :, column : column + wide] = (
                    value.astype(BF).reshape(2, 4, 2, 64, wide)
                )
                return carry

            lax.fori_loop(0, 2, rows_of, 0)
            column += wide
        waits[g][0] = [
            self.remote(
                g, 0, self.slots.at[slot, :, :, 1 - self.core, :, :column],
                self.core_recv.at[g, :, :, :, :column], peer(self.x, self.y, 1 - self.core),
            )
        ]

    def first(self, g):
        slot, (width, _, axis) = g % SLOTS, self.groups[g]
        waits, slots = self.waits, self.slots
        waits[g][0][0].wait_recv()

        def add(i, carry):
            slots[slot, i, :, self.core, :, :width] = (
                slots[slot, i, :, self.core, :, :width] + self.core_recv[g, i, :, :, :width]
            )
            return carry

        lax.fori_loop(0, 4, add, 0)
        at = self.x if axis == 0 else self.y
        waits[g][1] = [
            self.remote(
                g, 1 + i, self.held(slot, axis, lax.rem(at + 2, 4), 2 * i, 2).at[:, :, :width],
                self.relay_recv.at[g, i, :, :, :width], shifted(self.x, self.y, self.core, axis, k),
            )
            for i, k in enumerate((1, 3))
        ]

    def second(self, g):
        slot, (width, _, axis) = g % SLOTS, self.groups[g]
        waits, slots = self.waits, self.slots
        at = self.x if axis == 0 else self.y
        waits[g][2] = []
        for i, k in enumerate((1, 3)):
            waits[g][1][i].wait_recv()
            there = lax.rem(at + k, 4)
            for j in range(2):
                b = 2 * i + j
                where = (slot, there, b, self.core) if axis == 0 else (slot, b, there, self.core)
                where = where + (slice(None), slice(0, width))
                slots[where] = slots[where] + self.relay_recv[g, i, j, :, :width]
            waits[g][2].append(
                self.remote(
                    g, 3 + i, self.held(slot, axis, there, 0, 4).at[:, :, :width],
                    self.first_recv.at[g, i, :, :, :width], shifted(self.x, self.y, self.core, axis, k),
                )
            )

    def third(self, g):
        slot, (width, _, axis) = g % SLOTS, self.groups[g]
        waits, slots = self.waits, self.slots
        at, other = (self.x, self.y) if axis == 0 else (self.y, self.x)
        for copy in waits[g][2]:
            copy.wait_recv()
        for b in range(4):
            where = (slot, at, b, self.core) if axis == 0 else (slot, b, at, self.core)
            self.core_recv[g, 0, b, :, :width] = (
                slots[where + (slice(None), slice(0, width))].astype(F32)
                + self.first_recv[g, 0, b, :, :width].astype(F32)
                + self.first_recv[g, 1, b, :, :width].astype(F32)
            ).astype(BF)
        waits[g][3] = [
            self.remote(
                g, 4 + k, self.core_recv.at[g, 0, lax.rem(other + k, 4), :, :width],
                self.last_recv.at[g, k - 1, :, :width],
                shifted(self.x, self.y, self.core, 1 - axis, k),
            )
            for k in (2, 1, 3)
        ]

    def fourth(self, g):
        width, pieces, axis = self.groups[g]
        other = self.y if axis == 0 else self.x
        value = self.core_recv[g, 0, other, :, :width].astype(F32)
        for copy in self.waits[g][3]:
            copy.wait_recv()
        for k in range(3):
            value = value + self.last_recv[g, k, :, :width].astype(F32)
        column = 0
        for section, low, high in pieces:
            self.store(section, low, value[:, column : column + high - low])
            column += high - low

    def step(self, i):
        for back, work in ((0, self.zero), (1, self.first), (3, self.second), (5, self.third), (6, self.fourth)):
            if 0 <= i - back < len(self.groups):
                work(i - back)

    def drain(self):
        count = len(self.groups)
        for g in range(count):
            for stage in range(4):
                if stage == 3 or g >= count - SLOTS:
                    for copy in self.waits[g][stage]:
                        copy.wait_send()


def finish_kernel(n, heads, devices, mp, group, levels, spans, groups, *refs):
    refs = list(refs)
    flow, gains, query_place, query, packed, mixed_t, log_total, grad_mixed, cosine, sine = [refs.pop(0) for _ in range(10)]
    rows_in, middle, logit, second_vecs, first_vecs, router_vecs = [refs.pop(0) for _ in range(6)]
    w_hbm = refs.pop(0)
    sources = [[refs.pop(0) for _ in range(8 if level else 7)] for level in range(len(levels))]
    flow_out, q_out, k_out, v_out, out_out, gate_out, up_out, down_out, vec_out = [refs.pop(0) for _ in range(9)]
    query_t, grad_rows, grad_t, acc, delta, send_buf, recv_buf, kv_send, kv_recv = [refs.pop(0) for _ in range(9)]
    w_qkv, w_sem, send_a, recv_a, full_a, sems_a = [refs.pop(0) for _ in range(6)]
    (lefts, turned, rights, vectors, slots, core_recv, relay_recv, first_recv, last_recv,
     loads, send_sems, recv_sems) = refs
    me, mp_me = lax.axis_index("dp"), lax.axis_index("mp")
    x, y, core = plane(me)
    load_w = pltpu.make_async_copy(w_hbm.at[:, : w_qkv.shape[1]], w_qkv, w_sem)
    load_w.start()
    fetches = [[] for _ in range(4)]

    def fetch(s, side):
        row = 0
        for level, count in enumerate(levels):
            low, high = spans[s]
            target = (lefts.at[s % 2, row : row + count], rights.at[row : row + count, low:high])[side]
            if 2 * s + side < len(sources[level]):
                copy = pltpu.make_async_copy(
                    sources[level][2 * s + side], target, loads.at[level, 2 * s + side]
                )
                copy.start()
                fetches[s].append(copy)
            row += count

    for s in range(4):
        if s < 2:
            fetch(s, 0)
        fetch(s, 1)

    barrier = pltpu.get_barrier_semaphore()

    def greet(k, carry):
        pl.semaphore_signal(
            barrier, inc=1, device_id={"dp": lax.rem(me + k, devices)}, device_id_type=MESH
        )
        return carry

    lax.fori_loop(1, devices, greet, 0)
    for k in range(1, mp):
        pl.semaphore_signal(
            barrier, inc=1, device_id={"mp": lax.rem(mp_me + k, mp)}, device_id_type=MESH
        )

    def turn(section):
        for copy in fetches[section]:
            copy.wait()
        turned[section % 2] = lefts[section % 2].T
        if section < 2:
            fetch(section + 2, 0)

    hidden = gate_out.shape[1]
    mix = q_out.shape[1]

    def store(section, low, value):
        high = low + value.shape[1]
        if section == 0:
            middle_cut = min(max(hidden - low, 0), high - low)
            if middle_cut:
                gate_out[:, low : low + middle_cut] = value[:, :middle_cut]
            if low + middle_cut < high:
                up_out[:, low + middle_cut - hidden : high - hidden] = value[:, middle_cut:]
        elif section == 1:
            down_out[low:high, :] = value.T
        elif section == 2:
            out_out[low:high, :] = value.T
        elif section == 3:
            if low < mix:
                q_out[:, low : min(high, mix)] = value[:, : min(high, mix) - low]
            if high > mix:
                k_out[...] = value[:, mix - low : mix - low + HD]
                v_out[...] = value[:, mix - low + HD :]
        else:
            vec_out[...] = value

    work = Collect(
        spans, groups, x, y, core, turned, rights, vectors, store, slots, core_recv, relay_recv,
        first_recv, last_recv, send_sems, recv_sems, turn,
    )
    left = lanes_of((n, LANES)) < HD
    for t in range(heads // 2):
        part = grad_mixed[:, t * LANES : (t + 1) * LANES].astype(F32)
        grad_rows[2 * t * n : (2 * t + 1) * n, :] = jnp.where(
            left, 0.0, pltpu.roll(part, HD, 1)
        ).astype(BF)
        grad_rows[(2 * t + 1) * n : (2 * t + 2) * n, :] = jnp.where(left, 0.0, part).astype(BF)
    query_t[...] = query[...].T
    grad_t[...] = grad_rows[...].T
    delta[...] = jnp.sum(grad_t[...].astype(F32) * mixed_t[...], axis=0, keepdims=True)
    acc[...] = jnp.zeros(acc.shape, F32)
    width = heads * n
    pl.semaphore_wait(barrier, devices - 1 + mp - 1)

    def send_copy(e, source_index):
        return pltpu.make_async_remote_copy(
            src_ref=send_buf.at[e], dst_ref=recv_buf.at[source_index],
            send_sem=kv_send.at[e], recv_sem=kv_recv.at[source_index],
            device_id={"dp": e}, device_id_type=MESH,
        )

    def one_block(b):
        part = packed[b * group : (b + 1) * group].reshape(group * n, 2 * HD)
        scores = dot_nn(part, query_t[...])
        place = lax.broadcasted_iota(jnp.int32, (group * n, LANES), 0) + b * (group * n)
        place = jnp.concatenate([place] * (width // LANES), axis=1)
        scores = jnp.where(place <= query_place[...], scores, NEG)
        weights = jnp.exp(scores - log_total[...])
        grad_weights = dot_nn(part, grad_t[...])
        grad_scores = (weights * (grad_weights - delta[...])).astype(BF)
        grad_part = dot_nn(grad_scores, query[...]) + dot_nn(weights.astype(BF), grad_rows[...])
        send_buf[b * group : (b + 1) * group] = grad_part.astype(BF).reshape(group, n, 2 * HD)
        acc[...] += dot_tn(part, grad_scores)
        for e in range(b * group, (b + 1) * group):

            @pl.when(e < me)
            def _(e=e):
                send_copy(e, me).start()

    blocks = devices // group
    for b in range(blocks):
        work.step(b)

        @pl.when(b * group <= me)
        def _(b=b):
            one_block(b)

    grad_query = acc[...].T * HD**-0.5
    outs = []
    for t in range(heads // 2):
        even = grad_query[2 * t * n : (2 * t + 1) * n, :]
        odd = grad_query[(2 * t + 1) * n : (2 * t + 2) * n, :]
        outs.append(jnp.where(left, even, pltpu.roll(odd, HD, 1)))

    def add(e, carry):
        send_copy(me, e).wait_recv()
        return carry + recv_buf[e].astype(F32)

    outs.append(lax.fori_loop(me + 1, devices, add, send_buf[me].astype(F32)))
    low = spans[3][0]
    for t, part in enumerate(outs):
        cut = slice(t * LANES, (t + 1) * LANES)
        rights[0:n, low + t * LANES : low + (t + 1) * LANES] = (
            part * cosine[:, cut] - swap_halves(part) * sine[:, cut]
        ).astype(BF)
    load_w.wait()
    grad_now = rights[0:n, low : spans[3][1]]
    chunk = w_qkv.shape[0] // mp

    def first_chunk(c):
        return dot_nt(grad_now, w_qkv[pl.ds(pl.multiple_of(c * chunk, chunk), chunk), :])

    total = Sum(mp, mp_me, send_a, recv_a, full_a, sems_a)
    total.start(first_chunk)
    work.step(blocks)
    total.middle()
    work.step(blocks + 1)
    grad_normed = total.finish().astype(F32)
    level = rows_in[...].astype(F32)
    unit, factor = unit_of(level)
    vectors[...] = jnp.zeros(vectors.shape, F32)
    vectors[0:1, :] = jnp.sum(grad_normed * unit, axis=0, keepdims=True) + first_vecs[0:1, :] + first_vecs[1:2, :]
    vectors[1:2, :] = second_vecs[0:1, :] + second_vecs[1:2, :] + second_vecs[2:3, :]
    vectors[2:3, :] = jnp.sum(level * logit[...], axis=0, keepdims=True) + router_vecs[0:1, :] + router_vecs[1:2, :]
    flow_out[...] = flow[...] + (
        unit_back(grad_normed * gains[0:1, :], unit, factor) + middle[...] + logit[...] * gains[2:3, :]
    ).astype(BF).astype(F32)
    for i in range(blocks + 2, len(groups) + 6):
        work.step(i)
    work.drain()
    total.drain()

    def sent(e, carry):
        send_copy(e, me).wait_send()
        return carry

    lax.fori_loop(0, me, sent, 0)


class Sum:
    order = (2, 1, 3)

    def __init__(self, group, me, send, recv, full, sems):
        self.group, self.me, self.send, self.recv, self.full, self.sems = group, me, send, recv, full, sems

    def remote(self, source, target, stage, k):
        copy = pltpu.make_async_remote_copy(
            src_ref=source, dst_ref=target, send_sem=self.sems.at[stage, k - 1],
            recv_sem=self.sems.at[stage + 1, k - 1],
            device_id={"mp": lax.rem(self.me + k, self.group)}, device_id_type=MESH,
        )
        copy.start()
        return copy

    def start(self, make_chunk):
        self.out = []
        for k in self.order:
            self.send[k - 1] = make_chunk(lax.rem(self.me + k, self.group)).astype(BF)
            self.out.append(self.remote(self.send.at[k - 1], self.recv.at[k - 1], 0, k))
        self.own = make_chunk(self.me).astype(BF).astype(F32)

    def middle(self):
        total = self.own
        for k, copy in zip(self.order, self.out):
            copy.wait_recv()
            total = total + self.recv[k - 1].astype(F32)
        self.full[self.me] = total.astype(BF)
        self.back = [self.remote(self.full.at[self.me], self.full.at[self.me], 2, k) for k in self.order]

    def finish(self):
        for copy in self.back:
            copy.wait_recv()
        return jnp.concatenate([self.full[c] for c in range(self.group)], axis=1)

    def drain(self):
        for copy in self.out + self.back:
            copy.wait_send()


def finish(flow, gains, attention, tail, vecs, weights, levels, heads, devices, mp, depth, ident):
    n, model = levels[0][0].shape
    width = heads * n
    group = 512 // n
    mix = heads * HD
    widths = [levels[1][i].shape[1] for i in (1, 3, 5, 7)] + [LANES]
    spans, total = [], 0
    for wide in widths:
        spans.append((total, total + wide))
        total += wide
    pieces = []
    for section, wide in enumerate(widths):
        pieces += [(section, low, low + LANES) for low in range(0, wide, LANES)]
    groups = []
    per = GROUP // LANES
    for index in range(0, len(pieces), per):
        merged = []
        for section, low, high in pieces[index : index + per]:
            if merged and merged[-1][0] == section:
                merged[-1] = (section, merged[-1][1], high)
            else:
                merged.append((section, low, high))
        wide = sum(high - low for _, low, high in merged)
        groups.append((wide, merged, (index // per) % 2))
    counts = [level[0].shape[0] for level in levels]
    rows = sum(counts)
    hidden = widths[1]
    many = len(groups)
    whole = [flow, gains, *attention, *tail, *vecs]
    args = whole + [weights] + [item for level in levels for item in level]
    return pl.pallas_call(
        functools.partial(finish_kernel, n, heads, devices, mp, group, counts, spans, groups),
        out_shape=(
            jax.ShapeDtypeStruct(flow.shape, F32),
            jax.ShapeDtypeStruct((depth, mix), F32),
            jax.ShapeDtypeStruct((depth, HD), F32),
            jax.ShapeDtypeStruct((depth, HD), F32),
            jax.ShapeDtypeStruct((mix, depth), F32),
            jax.ShapeDtypeStruct((depth, hidden), F32),
            jax.ShapeDtypeStruct((depth, hidden), F32),
            jax.ShapeDtypeStruct((hidden, depth), F32),
            jax.ShapeDtypeStruct((depth, LANES), F32),
        ),
        in_specs=vmem(len(whole)) + [pl.BlockSpec(memory_space=pl.ANY)] * (len(args) - len(whole)),
        out_specs=tuple(vmem(9)),
        scratch_shapes=[
            pltpu.VMEM((2 * HD, width), BF),
            pltpu.VMEM((width, 2 * HD), BF),
            pltpu.VMEM((2 * HD, width), BF),
            pltpu.VMEM((2 * HD, width), F32),
            pltpu.VMEM((1, width), F32),
            pltpu.VMEM((devices, n, 2 * HD), BF),
            pltpu.VMEM((devices, n, 2 * HD), BF),
            pltpu.SemaphoreType.DMA((devices,)),
            pltpu.SemaphoreType.DMA((devices,)),
            pltpu.VMEM((model, mix + 2 * HD), BF),
            pltpu.SemaphoreType.DMA(()),
            *sum_scratch(mp, n, model),
            pltpu.VMEM((2, rows, model), BF),
            pltpu.VMEM((2, model, rows), BF),
            pltpu.VMEM((rows, spans[3][1]), BF),
            pltpu.VMEM((LANES, model), F32),
            pltpu.VMEM((SLOTS, 4, 4, 2, depth, GROUP), BF),
            pltpu.VMEM((many, 4, 4, depth, GROUP), BF),
            pltpu.VMEM((many, 2, 2, depth, GROUP), BF),
            pltpu.VMEM((many, 2, 4, depth, GROUP), BF),
            pltpu.VMEM((many, 3, depth, GROUP), BF),
            pltpu.SemaphoreType.DMA((len(levels), 8)),
            pltpu.SemaphoreType.DMA((many, 8)),
            pltpu.SemaphoreType.DMA((many, 8)),
        ],
        compiler_params=pltpu.CompilerParams(
            collective_id=ident, has_side_effects=True, vmem_limit_bytes=63 * 1024 * 1024
        ),
        name="finish",
    )(*args)


def rotary_tables(place, heads):
    freq = jnp.exp(jnp.arange(HD // 2, dtype=F32) * (-2.0 * math.log(ROPE_BASE) / HD))
    angle = place.astype(F32)[:, None] * freq[None, :]
    cosine, sine = jnp.cos(angle), jnp.sin(angle)
    one = jnp.concatenate([cosine, cosine], axis=1)
    two = jnp.concatenate([-sine, sine], axis=1)
    return (
        jnp.concatenate([jnp.tile(one, (1, heads + 1)), jnp.ones(one.shape, F32)], axis=1),
        jnp.concatenate([jnp.tile(two, (1, heads + 1)), jnp.zeros(one.shape, F32)], axis=1),
    )


def local(
    tokens, depths, second_slot, third_slot, w_query, w_key, w_value, w_out, w_gate, w_up,
    w_down, norm_first, norm_second, router, cotangent,
):
    me = lax.axis_index("dp")
    devices, mp = lax.axis_size("dp"), lax.axis_size("mp")
    rows = tokens.shape[0]
    heads = w_query.shape[1] // HD
    hidden_width = w_gate.shape[1]
    depth = w_query.shape[0]

    picks, marks = [], []
    for active, slot, capacity in (
        ((depths >= 2) & (second_slot >= 0), second_slot, SECOND_SLOTS),
        ((depths >= 3) & (third_slot >= 0), third_slot, THIRD_SLOTS),
    ):
        pick = (jnp.arange(capacity)[:, None] == slot[None, :]) & active[None, :]
        picks.append(pick.astype(BF))
        marks.append(
            jnp.min(jnp.where(pick, jnp.arange(rows, dtype=jnp.int32)[None, :], rows), axis=1)
        )

    def column(values):
        return values.reshape(depth, 1).astype(BF)

    second_mark = jnp.pad(marks[0], (0, 2 * depth - SECOND_SLOTS), constant_values=rows)
    extras = jnp.concatenate(
        [
            column(norm_first), column(norm_second), column(router),
            column(second_mark[:depth]), column(second_mark[depth:]), column(marks[1]),
            jnp.zeros((depth, LANES - 6), BF),
        ],
        axis=1,
    )
    weights, gains = spread(w_query, w_key, w_value, w_out, w_gate, w_up, w_down, extras, 13)
    weights = weights.reshape(devices * depth, -1)
    marks_all = gains[3:6].astype(jnp.int32).reshape(3, devices, depth)
    second_all = jnp.concatenate(
        [marks_all[0], marks_all[1, :, : SECOND_SLOTS - depth]], axis=1
    )
    base = (jnp.arange(devices, dtype=jnp.int32) * rows)[:, None]

    def place_of(mark, offset):
        return jnp.where(mark < rows, mark + offset, FAR)

    def key_column(mark):
        return jnp.broadcast_to(place_of(mark, base).reshape(-1, 1), (mark.size, LANES))

    levels = (
        (rows, None, jnp.arange(rows, dtype=jnp.int32) + me * rows, None),
        (SECOND_SLOTS, picks[0], place_of(marks[0], me * rows), key_column(second_all)),
        (THIRD_SLOTS, picks[1], place_of(marks[1], me * rows), key_column(marks_all[2])),
    )
    state = tokens
    kept = []
    for index, (count, pick, place, key_place) in enumerate(levels):
        tables = rotary_tables(jnp.where(place == FAR, 0, place), heads)
        query_place = jnp.tile(place, heads)[None, :]
        rows_in, normed, packed, query, mixed_t, log_total, mixed = attend(
            state, pick, key_place, query_place, gains, tables, weights, heads, devices, count, index
        )
        attn, ffn, second, parts, state = feed(
            state, rows_in, mixed, pick, gains, weights, hidden_width, mp, count, 3 + index
        )
        kept.append(
            (pick, key_place, query_place, tables, rows_in, normed, packed, query, mixed_t, log_total, mixed,
             attn, ffn, second, parts)
        )

    flow = cotangent
    tail = None
    terms, vectors, second_vecs = [], [], []
    for index in (2, 1, 0):
        (pick, key_place, query_place, tables, rows_in, normed, packed, query, mixed_t, log_total, mixed,
         attn, ffn, second, parts) = kept[index]
        head = (rows_in, attn, ffn, second, parts, pick)
        outs = list(
            feed_back(flow, gains, tail, head, weights, hidden_width, heads * HD, mp, 6 + index)
        )
        if tail is not None:
            flow, first_vec, router_vec = outs[:3]
            outs = outs[3:]
            vectors.append((first_vec, router_vec))
        grad_attn, grad_middle, logit, grad_mixed, parts_grad, hidden, grad_ffn, second_vec = outs
        second_vecs.append(second_vec)
        items = (second, parts_grad, grad_ffn, hidden, grad_attn, mixed, normed)
        if index:
            grad_qkv = attend_back(
                key_place, query_place, query, packed, mixed_t, log_total, grad_mixed, tables,
                heads, devices, rows_in.shape[0], 10 + index,
            )
            tail = (grad_qkv, rows_in, grad_middle, logit, pick)
            items = items + (grad_qkv,)
        terms.append(items)
    attention = (query_place, query, packed, mixed_t, log_total, grad_mixed, *tables)
    vecs = [jnp.concatenate(list(part), axis=0) for part in (second_vecs, *zip(*vectors))]
    flow, query_grad, key_grad, value_grad, out_grad, gate_grad, up_grad, down_grad, vec = finish(
        flow, gains, attention, (rows_in, grad_middle, logit), vecs, weights, terms[::-1],
        heads, devices, mp, depth, 14,
    )
    return (
        state, flow, query_grad, key_grad, value_grad, out_grad, gate_grad, up_grad, down_grad,
        vec[:, 0], vec[:, 1], vec[:, 2],
    )


def solution(mesh):
    in_specs = (
        P("dp", None), P("dp"), P("dp"), P("dp"), P("dp", "mp"), P("dp", "mp"), P("dp", "mp"),
        P("mp", "dp"), P("dp", "mp"), P("dp", "mp"), P("mp", "dp"), P("dp"), P("dp"), P("dp"),
        P("dp", None),
    )
    out_specs = (
        P("dp", None), P("dp", None), P("dp", "mp"), P("dp", "mp"), P("dp", "mp"), P("mp", "dp"),
        P("dp", "mp"), P("dp", "mp"), P("mp", "dp"), P("dp"), P("dp"), P("dp"),
    )
    return jax.shard_map(local, mesh=mesh, in_specs=in_specs, out_specs=out_specs, check_vma=False)
```

```python
import functools
import math

import jax
import jax.numpy as jnp
from jax import lax
from jax.experimental import pallas as pl
from jax.experimental.pallas import tpu as pltpu
from jax.sharding import PartitionSpec as P

HD = 64
SECOND_SLOTS = 96
THIRD_SLOTS = 64
EPS = 1e-05
NEG = -1e30
ROPE_BASE = 10000.0
FAR = 1e9
BF = jnp.bfloat16
F32 = jnp.float32
MESH = pl.DeviceIdType.MESH
LANES = 128
VMEM_LIMIT = 63 * 1024 * 1024


def dot_nn(left, right):
    return lax.dot_general(left, right, (((1,), (0,)), ((), ())), preferred_element_type=F32)


def dot_nt(left, right):
    return lax.dot_general(left, right, (((1,), (1,)), ((), ())), preferred_element_type=F32)


def dot_tn(left, right):
    return lax.dot_general(left, right, (((0,), (0,)), ((), ())), preferred_element_type=F32)


def unit_of(values):
    factor = lax.rsqrt(jnp.mean(values * values, axis=-1, keepdims=True) + EPS)
    return values * factor, factor


def unit_back(shaped, unit, factor):
    return factor * (shaped - unit * jnp.mean(shaped * unit, axis=-1, keepdims=True))


def sigmoid(values):
    return 1.0 / (1.0 + jnp.exp(-values))


def lanes_of(shape):
    return lax.broadcasted_iota(jnp.int32, shape, 1)


def swap_halves(tile):
    first = lax.rem(lanes_of(tile.shape), HD) < HD // 2
    return jnp.where(first, pltpu.roll(tile, LANES - HD // 2, 1), pltpu.roll(tile, HD // 2, 1))


def turn_back(part, cosine, sine, packed):
    if packed:
        left = lanes_of(part.shape) < HD
        cosine, sine = jnp.where(left, cosine, 1.0), jnp.where(left, sine, 0.0)
    return (part * cosine - swap_halves(part) * sine).astype(BF)


def tile_of(values, index):
    return values[:, index * LANES : (index + 1) * LANES]


def signal_all(group, me, axis):
    barrier = pltpu.get_barrier_semaphore()
    for k in range(1, group):
        pl.semaphore_signal(
            barrier, inc=1, device_id={axis: lax.rem(me + k, group)}, device_id_type=MESH
        )
    pl.semaphore_wait(barrier, group - 1)


def sum_over_mp(group, me, make_chunk, send, recv, full, sems):
    order = (2, 1, 3)
    copies = []
    for k in order:
        peer = lax.rem(me + k, group)
        send[k - 1] = make_chunk(peer).astype(BF)
        copy = pltpu.make_async_remote_copy(
            src_ref=send.at[k - 1], dst_ref=recv.at[k - 1],
            send_sem=sems.at[0, k - 1], recv_sem=sems.at[1, k - 1],
            device_id={"mp": peer}, device_id_type=MESH,
        )
        copy.start()
        copies.append(copy)
    total = make_chunk(me).astype(BF).astype(F32)
    for k, copy in zip(order, copies):
        copy.wait_recv()
        total = total + recv[k - 1].astype(F32)
    full[me] = total.astype(BF)
    backs = []
    for k in order:
        peer = lax.rem(me + k, group)
        copy = pltpu.make_async_remote_copy(
            src_ref=full.at[me], dst_ref=full.at[me],
            send_sem=sems.at[2, k - 1], recv_sem=sems.at[3, k - 1],
            device_id={"mp": peer}, device_id_type=MESH,
        )
        copy.start()
        backs.append(copy)
    for copy in backs:
        copy.wait_recv()
    for copy in copies + backs:
        copy.wait_send()
    return jnp.concatenate([full[c] for c in range(group)], axis=1)


def vmem(count):
    return [pl.BlockSpec(memory_space=pltpu.VMEM)] * count


def attend_back_kernel(n, heads, devices, group, picked, *refs):
    refs = list(refs)
    key_place = refs.pop(0) if picked else None
    query_place, query, packed, mixed_t, log_total, grad_mixed, cosine, sine = [
        refs.pop(0) for _ in range(8)
    ]
    grad_out = refs.pop(0)
    query_t, grad_rows, grad_t, acc, delta, send_buf, recv_buf, send_sems, recv_sems = refs
    me = lax.axis_index("dp")
    barrier = pltpu.get_barrier_semaphore()

    def greet(e, carry):
        pl.semaphore_signal(barrier, inc=1, device_id={"dp": e}, device_id_type=MESH)
        return carry

    lax.fori_loop(me + 1, devices, greet, 0)

    left = lanes_of((n, LANES)) < HD
    for t in range(heads // 2):
        part = grad_mixed[:, t * LANES : (t + 1) * LANES].astype(F32)
        grad_rows[2 * t * n : (2 * t + 1) * n, :] = jnp.where(
            left, 0.0, pltpu.roll(part, HD, 1)
        ).astype(BF)
        grad_rows[(2 * t + 1) * n : (2 * t + 2) * n, :] = jnp.where(left, 0.0, part).astype(BF)
    query_t[...] = query[...].T
    grad_t[...] = grad_rows[...].T
    delta[...] = jnp.sum(grad_t[...].astype(F32) * mixed_t[...], axis=0, keepdims=True)
    acc[...] = jnp.zeros(acc.shape, F32)
    width = heads * n

    @pl.when(me > 0)
    def _():
        pl.semaphore_wait(barrier, me)

    def send_copy(e, source_index):
        return pltpu.make_async_remote_copy(
            src_ref=send_buf.at[e], dst_ref=recv_buf.at[source_index],
            send_sem=send_sems.at[e], recv_sem=recv_sems.at[source_index],
            device_id={"dp": e}, device_id_type=MESH,
        )

    def one_block(b, carry):
        part = packed[pl.ds(b * group, group)].reshape(group * n, 2 * HD)
        scores = dot_nn(part, query_t[...])
        if picked:
            start = pl.multiple_of(b * (group * n), group * n)
            place = key_place[pl.ds(start, group * n), :]
        else:
            place = (lax.broadcasted_iota(jnp.int32, (group * n, LANES), 0) + b * (group * n)).astype(F32)
        place = jnp.concatenate([place] * (width // LANES), axis=1)
        scores = jnp.where(place <= query_place[...], scores, NEG)
        weights = jnp.exp(scores - log_total[...])
        grad_weights = dot_nn(part, grad_t[...])
        grad_scores = (weights * (grad_weights - delta[...])).astype(BF)
        grad_part = dot_nn(grad_scores, query[...]) + dot_nn(weights.astype(BF), grad_rows[...])
        send_buf[pl.ds(b * group, group)] = grad_part.astype(BF).reshape(group, n, 2 * HD)
        acc[...] += dot_tn(part, grad_scores)
        for g in range(group):
            e = b * group + g

            @pl.when(e < me)
            def _():
                send_copy(e, me).start()

        return carry

    lax.fori_loop(0, me // group + 1, one_block, 0)

    grad_query = acc[...].T * HD**-0.5
    outs = []
    for t in range(heads // 2):
        even = grad_query[2 * t * n : (2 * t + 1) * n, :]
        odd = grad_query[(2 * t + 1) * n : (2 * t + 2) * n, :]
        outs.append(jnp.where(left, even, pltpu.roll(odd, HD, 1)))

    def add(e, carry):
        send_copy(me, e).wait_recv()
        return carry + recv_buf[e].astype(F32)

    outs.append(lax.fori_loop(me + 1, devices, add, send_buf[me].astype(F32)))
    for t, part in enumerate(outs):
        grad_out[:, t * LANES : (t + 1) * LANES] = turn_back(
            part, cosine[...], sine[...], t == heads // 2
        )

    def sent(e, carry):
        send_copy(e, me).wait_send()
        return carry

    lax.fori_loop(0, me, sent, 0)


def attend_back(key_place, query_place, query, packed, mixed_t, log_total, grad_mixed, tables, heads, devices, n, ident):
    picked = key_place is not None
    group = 512 // n if 512 % n == 0 else 4
    width = heads * n
    args = ([key_place] if picked else []) + [
        query_place, query, packed, mixed_t, log_total, grad_mixed, *tables
    ]
    return pl.pallas_call(
        functools.partial(attend_back_kernel, n, heads, devices, group, picked),
        out_shape=jax.ShapeDtypeStruct((n, (heads + 2) * HD), BF),
        in_specs=vmem(len(args)),
        out_specs=pl.BlockSpec(memory_space=pltpu.VMEM),
        scratch_shapes=[
            pltpu.VMEM((2 * HD, width), BF),
            pltpu.VMEM((width, 2 * HD), BF),
            pltpu.VMEM((2 * HD, width), BF),
            pltpu.VMEM((2 * HD, width), F32),
            pltpu.VMEM((1, width), F32),
            pltpu.VMEM((devices, n, 2 * HD), BF),
            pltpu.VMEM((devices, n, 2 * HD), BF),
            pltpu.SemaphoreType.DMA((devices,)),
            pltpu.SemaphoreType.DMA((devices,)),
        ],
        compiler_params=pltpu.CompilerParams(
            collective_id=ident, has_side_effects=True, vmem_limit_bytes=VMEM_LIMIT
        ),
        cost_estimate=pl.CostEstimate(flops=10**10, bytes_accessed=10**7, transcendentals=0),
        name=f"attend_back_{n}",
    )(*args)


def sum_scratch(mp, n, model):
    return [
        pltpu.VMEM((mp - 1, n, model // mp), BF),
        pltpu.VMEM((mp - 1, n, model // mp), BF),
        pltpu.VMEM((mp, n, model // mp), BF),
        pltpu.SemaphoreType.DMA((4, mp - 1)),
    ]


def feed_back_kernel(tail_n, head_n, mp, tail_picked, head_picked, *refs):
    refs = list(refs)
    flow, gains = refs.pop(0), refs.pop(0)
    if tail_n:
        grad_qkv, tail_rows, tail_middle, tail_logit = [refs.pop(0) for _ in range(4)]
        tail_pick = refs.pop(0) if tail_picked else None
    if head_n:
        rows_in, attn, ffn, second, parts = [refs.pop(0) for _ in range(5)]
        head_pick = refs.pop(0) if head_picked else None
    if tail_n:
        w_first_hbm = refs.pop(0)
    if head_n:
        w_rest_hbm = refs.pop(0)
    if tail_n:
        flow_out, first_out, router_out = [refs.pop(0) for _ in range(3)]
    if head_n:
        attn_grad_out, middle_out, logit_out, mixed_out, parts_grad_out, hidden_out, ffn_grad_out, second_vec_out = [
            refs.pop(0) for _ in range(8)
        ]
    if tail_n:
        w_qkv, w_first_sem = refs.pop(0), refs.pop(0)
        send_a, recv_a, full_a, sems_a = [refs.pop(0) for _ in range(4)]
    if head_n:
        w_o, w_gu, w_d, w_sems = [refs.pop(0) for _ in range(4)]
        send_b, recv_b, full_b, sems_b = [refs.pop(0) for _ in range(4)]
    me = lax.axis_index("mp")
    if tail_n:
        load_first = pltpu.make_async_copy(w_first_hbm.at[:, : w_qkv.shape[1]], w_qkv, w_first_sem)
        load_first.start()
    if head_n:
        loads = {}
        wide_o, wide_gu, wide_d = w_o.shape[1], w_gu.shape[1], w_d.shape[1]
        for index, (name, ref, start) in enumerate(
            (("d", w_d, wide_o + wide_gu), ("gu", w_gu, wide_o), ("o", w_o, 0))
        ):
            start += wide_o + 2 * LANES
            loads[name] = pltpu.make_async_copy(
                w_rest_hbm.at[:, start : start + ref.shape[1]], ref, w_sems.at[index]
            )
            loads[name].start()
    signal_all(mp, me, "mp")

    if tail_n:
        load_first.wait()
        grad_now = grad_qkv[...]
        chunk = w_qkv.shape[0] // mp

        def first_chunk(c):
            return dot_nt(grad_now, w_qkv[pl.ds(pl.multiple_of(c * chunk, chunk), chunk), :])

        grad_normed = sum_over_mp(mp, me, first_chunk, send_a, recv_a, full_a, sems_a).astype(F32)
        level = tail_rows[...].astype(F32)
        unit, factor = unit_of(level)
        first_out[...] = jnp.sum(grad_normed * unit, axis=0, keepdims=True)
        router_out[...] = jnp.sum(level * tail_logit[...], axis=0, keepdims=True)
        grad_rows = (
            unit_back(grad_normed * gains[0:1, :], unit, factor)
            + tail_middle[...]
            + tail_logit[...] * gains[2:3, :]
        ).astype(BF)
        if tail_picked:
            flow_now = flow[...] + dot_tn(tail_pick[...], grad_rows)
        else:
            flow_now = flow[...] + grad_rows.astype(F32)
        flow_out[...] = flow_now
    else:
        flow_now = flow[...]

    if head_n:
        grad_update = flow_now.astype(BF)
        if head_picked:
            grad_update = dot_nn(head_pick[...], grad_update)
        grad_update = grad_update.astype(F32)
        level = rows_in[...].astype(F32)
        attn_now = attn[...].astype(F32)
        gate = sigmoid(jnp.sum(level * gains[2:3, :], axis=-1, keepdims=True))
        logit = jnp.sum(grad_update * (attn_now + ffn[...].astype(F32)), axis=-1, keepdims=True)
        logit_out[...] = logit * gate * (1.0 - gate)
        grad_ffn = (gate * grad_update).astype(BF)
        ffn_grad_out[...] = grad_ffn
        half = wide_d
        loads["d"].wait()
        for t in range(half // LANES):
            cut = slice(t * LANES, (t + 1) * LANES)
            up_cut = slice(half + t * LANES, half + (t + 1) * LANES)
            if t % 2 == 0:
                both = dot_nn(grad_ffn, w_d[:, t * LANES : min((t + 2) * LANES, half)])
            grad_hidden = tile_of(both, t % 2)
            gate_part = parts[:, cut]
            up_part = parts[:, up_cut]
            sigma = sigmoid(gate_part)
            active = gate_part * sigma
            hidden_out[:, cut] = (active * up_part).astype(BF)
            parts_grad_out[:, cut] = (
                grad_hidden * up_part * sigma * (1.0 + gate_part * (1.0 - sigma))
            ).astype(BF)
            parts_grad_out[:, up_cut] = (grad_hidden * active).astype(BF)
        loads["gu"].wait()
        parts_now = parts_grad_out[...]
        chunk = w_gu.shape[0] // mp

        def second_chunk(c):
            return dot_nt(parts_now, w_gu[pl.ds(pl.multiple_of(c * chunk, chunk), chunk), :])

        grad_second = sum_over_mp(mp, me, second_chunk, send_b, recv_b, full_b, sems_b).astype(F32)
        unit, factor = unit_of(level + attn_now)
        second_vec_out[...] = jnp.sum(grad_second * unit, axis=0, keepdims=True)
        grad_middle = unit_back(grad_second * gains[1:2, :], unit, factor)
        middle_out[...] = grad_middle
        grad_attn = (gate * grad_update + grad_middle).astype(BF)
        attn_grad_out[...] = grad_attn
        loads["o"].wait()
        mixed_out[...] = dot_nn(grad_attn, w_o[...]).astype(BF)


def feed_back(flow, gains, tail, head, weights, hidden_width, mix, mp, ident):
    model = flow.shape[1]
    args, outs, scratch = [flow, gains], [], []
    tail_n = head_n = 0
    tail_picked = head_picked = False
    if tail is not None:
        *items, pick = tail
        tail_n, tail_picked = items[0].shape[0], pick is not None
        args += items + ([pick] if tail_picked else [])
    if head is not None:
        *items, pick = head
        head_n, head_picked = items[0].shape[0], pick is not None
        args += items + ([pick] if head_picked else [])
    in_vmem = len(args)
    if tail_n:
        args.append(weights)
        outs += [
            jax.ShapeDtypeStruct(flow.shape, F32),
            jax.ShapeDtypeStruct((1, model), F32),
            jax.ShapeDtypeStruct((1, model), F32),
        ]
        scratch += [
            pltpu.VMEM((model, mix + 2 * HD), BF),
            pltpu.SemaphoreType.DMA(()),
            *sum_scratch(mp, tail_n, model),
        ]
    if head_n:
        args.append(weights)
        outs += [
            jax.ShapeDtypeStruct((head_n, model), BF),
            jax.ShapeDtypeStruct((head_n, model), F32),
            jax.ShapeDtypeStruct((head_n, 1), F32),
            jax.ShapeDtypeStruct((head_n, mix), BF),
            jax.ShapeDtypeStruct((head_n, 2 * hidden_width), BF),
            jax.ShapeDtypeStruct((head_n, hidden_width), BF),
            jax.ShapeDtypeStruct((head_n, model), BF),
            jax.ShapeDtypeStruct((1, model), F32),
        ]
        scratch += [
            pltpu.VMEM((model, mix), BF),
            pltpu.VMEM((model, 2 * hidden_width), BF),
            pltpu.VMEM((model, hidden_width), BF),
            pltpu.SemaphoreType.DMA((3,)),
            *sum_scratch(mp, head_n, model),
        ]
    return pl.pallas_call(
        functools.partial(feed_back_kernel, tail_n, head_n, mp, tail_picked, head_picked),
        out_shape=tuple(outs),
        in_specs=vmem(in_vmem) + [pl.BlockSpec(memory_space=pl.ANY)] * (len(args) - in_vmem),
        out_specs=tuple(vmem(len(outs))),
        scratch_shapes=scratch,
        compiler_params=pltpu.CompilerParams(
            collective_id=ident, has_side_effects=True, vmem_limit_bytes=VMEM_LIMIT
        ),
        cost_estimate=pl.CostEstimate(flops=5 * 10**9, bytes_accessed=10**8, transcendentals=0),
        name=f"feed_back_{tail_n}_{head_n}",
    )(*args)


def plane(me):
    return me // 8, lax.rem(me // 2, 4), lax.rem(me, 2)


def peer(x, y, core):
    return {"dp": (lax.rem(x, 4) * 4 + lax.rem(y, 4)) * 2 + core}


def shifted(x, y, core, axis, k):
    return peer(x + k, y, core) if axis == 0 else peer(x, y + k, core)


def meet(me, partners):
    barrier = pltpu.get_barrier_semaphore()
    for device in partners:
        pl.semaphore_signal(barrier, inc=1, device_id=device, device_id_type=MESH)
    pl.semaphore_wait(barrier, len(partners))


def plane_partners(x, y, core):
    return (
        [peer(x, y, 1 - core)]
        + [shifted(x, y, core, 0, k) for k in (1, 2, 3)]
        + [shifted(x, y, core, 1, k) for k in (1, 2, 3)]
    )


class Spread:
    def __init__(self, groups, x, y, core, shard, full, send_sems, recv_sems):
        self.groups, self.x, self.y, self.core = groups, x, y, core
        self.shard, self.full = shard, full
        self.send_sems, self.recv_sems = send_sems, recv_sems
        self.started = []
        self.waits = [{} for _ in groups]

    def remote(self, g, index, source, target, device):
        copy = pltpu.make_async_remote_copy(
            src_ref=source, dst_ref=target, send_sem=self.send_sems.at[g, index],
            recv_sem=self.recv_sems.at[g, index], device_id=device, device_id_type=MESH,
        )
        copy.start()
        self.started.append(copy)
        return copy

    def line(self, axis, at, first, count, cut):
        if axis == 0:
            return self.full.at[pl.ds(first, count), at, self.core, :, cut]
        return self.full.at[at, pl.ds(first, count), self.core, :, cut]

    def one(self, g):
        low, high, axis = self.groups[g]
        cut = slice(low, high)
        self.waits[g][1] = [
            self.remote(
                g, k - 1, self.shard.at[:, cut], self.full.at[self.x, self.y, self.core, :, cut],
                shifted(self.x, self.y, self.core, axis, k),
            )
            for k in (2, 1, 3)
        ]

    def two(self, g):
        low, high, axis = self.groups[g]
        for copy in self.waits[g][1]:
            copy.wait_recv()
        mine = self.line(axis, self.y if axis == 0 else self.x, 0, 4, slice(low, high))
        self.waits[g][2] = [
            self.remote(g, 3 + i, mine, mine, shifted(self.x, self.y, self.core, 1 - axis, k))
            for i, k in enumerate((1, 3))
        ]

    def three(self, g):
        low, high, axis = self.groups[g]
        at = self.y if axis == 0 else self.x
        self.waits[g][3] = []
        for i, k in enumerate((1, 3)):
            self.waits[g][2][i].wait_recv()
            piece = self.line(axis, lax.rem(at + 4 - k, 4), 2 * i, 2, slice(low, high))
            self.waits[g][3].append(
                self.remote(g, 5 + i, piece, piece, shifted(self.x, self.y, self.core, 1 - axis, k))
            )

    def four(self, g):
        low, high, axis = self.groups[g]
        for copy in self.waits[g][3]:
            copy.wait_recv()
        mine = self.full.at[:, :, self.core, :, slice(low, high)]
        self.waits[g][4] = [self.remote(g, 7, mine, mine, peer(self.x, self.y, 1 - self.core))]

    def five(self, g):
        self.waits[g][4][0].wait_recv()

    def step(self, i):
        for back, work in ((0, self.one), (2, self.two), (4, self.three), (5, self.four), (6, self.five)):
            if 1 <= i - back < len(self.groups):
                work(i - back)

    def drain(self):
        for copy in self.started:
            copy.wait_send()


def advance_kernel(counts, heads, devices, mp, hidden, groups, names, *refs):
    refs = list(refs)
    (tokens, depths, second_slot, third_slot, w_query, w_key, w_value, w_out, w_gate, w_up, w_down,
     norm_first, norm_second, router, cosine_in, sine_in) = [refs.pop(0) for _ in range(16)]
    outs = {name: refs.pop(0) for name in names}
    held = {name: refs.pop(0) for name in names}
    shard, own_sem, send_sems, recv_sems, query_t, top, total, acc, hidden_v, keep_sems, kv_send, kv_recv = [
        refs.pop(0) for _ in range(12)
    ]
    sum_refs = refs
    me, mp_me = lax.axis_index("dp"), lax.axis_index("mp")
    x, y, core = plane(me)
    weights = held["weights"]
    rows, model = tokens.shape
    mix = heads * HD
    lanes = lanes_of((rows, LANES))
    left = lanes < HD
    keeps = []

    def keep(name):
        copy = pltpu.make_async_copy(held[name], outs[name], keep_sems.at[len(keeps)])
        copy.start()
        keeps.append(copy)

    barrier = pltpu.get_barrier_semaphore()

    def greet(k, carry):
        pl.semaphore_signal(
            barrier, inc=1, device_id={"dp": lax.rem(me + k, devices)}, device_id_type=MESH
        )
        return carry

    lax.fori_loop(1, devices, greet, 0)
    for k in range(1, mp):
        pl.semaphore_signal(
            barrier, inc=1, device_id={"mp": lax.rem(mp_me + k, mp)}, device_id_type=MESH
        )

    token = lanes_of((1, rows)).astype(F32)
    picks, marks, query_places = [None], [None], []
    query_places.append(
        (lax.rem(lanes_of((1, heads * rows)), rows) + me * rows).astype(F32)
    )
    held["place_0"][...] = query_places[0]
    for level, slot, deep in ((1, second_slot, 2), (2, third_slot, 3)):
        count = counts[level]
        slots = lax.broadcasted_iota(jnp.int32, (count, rows), 0)
        active = (depths[...] >= deep) & (slot[...] >= 0)
        chosen = jnp.where(active, slot[...], -1) == slots
        pick = jnp.where(chosen, 1.0, 0.0).astype(BF)
        held[f"pick_{level}"][...] = pick
        picks.append(pick)
        marks.append(
            jnp.min(jnp.where(chosen, token, float(rows)), axis=1, keepdims=True)
        )
        sublane = lax.broadcasted_iota(jnp.int32, (16, rows), 0)
        probe = jnp.where(sublane == 0, token, 1.0).astype(BF)
        found = dot_nt(probe, jnp.concatenate([pick] * heads, axis=0))
        place = jnp.where(found[1:2, :] > 0.5, found[0:1, :] + (me * rows).astype(F32), FAR)
        held[f"place_{level}"][...] = place
        query_places.append(place)
        table = jnp.concatenate([cosine_in[...], sine_in[...]], axis=1)
        turned = lax.dot_general(
            pick.astype(F32), table, (((1,), (0,)), ((), ())),
            preferred_element_type=F32, precision=lax.Precision.HIGHEST,
        )
        held[f"cosine_{level}"][...] = turned[:, :LANES]
        held[f"sine_{level}"][...] = turned[:, LANES:]
    depth = w_query.shape[0]
    wide = jnp.zeros((1, LANES - depth), F32)
    gain_rows = jnp.concatenate(
        [jnp.concatenate([ref[...].astype(F32), wide], axis=1) for ref in (norm_first, norm_second, router)]
        + [jnp.zeros((LANES - 3, LANES), F32)],
        axis=0,
    )
    extra = gain_rows.T[:depth, :]
    rest = counts[1] - depth
    lane = lanes_of((depth, LANES))
    over = jnp.concatenate([marks[1][depth:, :], jnp.full((depth - rest, 1), float(rows), F32)], axis=0)
    extra = jnp.where(lane == 3, marks[1][:depth, :], extra)
    extra = jnp.where(lane == 4, over, extra)
    extra = jnp.where(lane == 5, marks[2], extra)
    pair = jnp.concatenate([w_key[...].astype(F32), w_value[...].astype(F32)], axis=1).astype(BF)
    start = 0
    for part in (
        w_query[...], pair, extra.astype(BF), w_out[...], w_gate[...], w_up[...], w_down[...],
    ):
        shard[:, start : start + part.shape[1]] = part
        start += part.shape[1]
    own = pltpu.make_async_copy(shard, weights.at[x, y, core], own_sem)
    own.start()
    spread = Spread(groups, x, y, core, shard, weights, send_sems, recv_sems)
    pl.semaphore_wait(barrier, devices - 1 + mp - 1)
    spread.one(0)
    own.wait()
    spread.step(1)
    spread.two(0)
    spread.step(2)
    spread.three(0)
    spread.four(0)
    spread.step(3)
    spread.five(0)
    upto = 4

    gains = held["gains"]
    columns = weights[:, :, :, :, mix + LANES : mix + 2 * LANES].reshape(model, LANES).astype(F32)
    gains[...] = columns.T[: gains.shape[0], :]
    keep("gains")

    def key_places(e, carry):
        for level, lanes_at in ((1, (3, 4)), (2, (5,))):
            tile = weights[e // 8, lax.rem(e // 2, 4), lax.rem(e, 2), :, mix + LANES : mix + 2 * LANES].astype(F32)
            value = jnp.concatenate(
                [jnp.broadcast_to(tile[:, at : at + 1], (depth, LANES)) for at in lanes_at], axis=0
            )[: counts[level], :]
            held[f"keys_{level}"][e] = jnp.where(
                value < rows, value + (e * rows).astype(F32), FAR
            )
        return carry

    lax.fori_loop(0, devices, key_places, 0)

    def kv_copy(level, e, source_index):
        packed = held[f"packed_{level}"]
        return pltpu.make_async_remote_copy(
            src_ref=packed.at[me], dst_ref=packed.at[me],
            send_sem=kv_send.at[level, e], recv_sem=kv_recv.at[level, source_index],
            device_id={"dp": e}, device_id_type=MESH,
        )

    def project(level, now):
        n = counts[level]
        name = lambda base: held[f"{base}_{level}"]
        name("rows")[...] = now
        unit, unused = unit_of(now.astype(F32))
        normed = (unit * gains[0:1, :]).astype(BF)
        name("normed")[...] = normed
        cosine, sine = (cosine_in[...], sine_in[...]) if level == 0 else (name("cosine")[...], name("sine")[...])
        here = left[:n]
        tiles = [None] * (heads // 2 + 1)
        for t in range(heads // 2, -1, -2):
            low = max(t - 1, 0)
            both = dot_nn(normed, weights[:, :, :, :, low * LANES : (t + 1) * LANES].reshape(model, (t + 1 - low) * LANES))
            for j in range(low, t + 1):
                part = tile_of(both, j - low)
                if j == heads // 2:
                    part = part * jnp.where(here, cosine, 1.0) + swap_halves(part) * jnp.where(here, sine, 0.0)
                    name("packed")[me] = part.astype(BF)

                    def send(e, carry):
                        kv_copy(level, e, me).start()
                        return carry

                    lax.fori_loop(me + 1, devices, send, 0)
                else:
                    tiles[j] = part * cosine + swap_halves(part) * sine

        def clear(e, carry):
            name("packed")[e] = jnp.zeros((n, 2 * HD), BF)
            return carry

        lax.fori_loop(me + 1, devices, clear, 0)
        for t in range(heads // 2):
            scaled = tiles[t].astype(BF).astype(F32) * HD**-0.5
            name("query")[2 * t * n : (2 * t + 1) * n, :] = jnp.where(here, scaled, 0.0).astype(BF)
            name("query")[(2 * t + 1) * n : (2 * t + 2) * n, :] = jnp.where(
                here, pltpu.roll(scaled, HD, 1), 0.0
            ).astype(BF)
        width = heads * n
        query_t[:, :width] = name("query")[...].T
        top[:, :width] = jnp.full((1, width), NEG, F32)
        total[:, :width] = jnp.zeros((1, width), F32)
        acc[:, :width] = jnp.zeros((2 * HD, width), F32)
        for base in ("rows", "normed", "query"):
            keep(f"{base}_{level}")

    def group_of(level):
        return 512 // counts[level] if 512 % counts[level] == 0 else 4

    def block(level, b):
        n, group = counts[level], group_of(level)
        width = heads * n
        for g in range(group):
            e = b * group + g

            @pl.when(e < me)
            def _(e=e):
                kv_copy(level, me, e).wait_recv()

        part = held[f"packed_{level}"][pl.ds(b * group, group)].reshape(group * n, 2 * HD)
        scores = dot_nn(part, query_t[:, :width])
        if level:
            place = held[f"keys_{level}"][pl.ds(b * group, group)].reshape(group * n, LANES)
        else:
            place = (lax.broadcasted_iota(jnp.int32, (group * n, LANES), 0) + b * (group * n)).astype(F32)
        place = jnp.concatenate([place] * (width // LANES), axis=1)
        scores = jnp.where(place <= held[f"place_{level}"][...], scores, NEG)
        before = top[:, :width]
        peak = jnp.maximum(before, jnp.max(scores, axis=0, keepdims=True))
        soft = jnp.exp(scores - peak)
        fade = jnp.exp(before - peak)
        total[:, :width] = total[:, :width] * fade + jnp.sum(soft, axis=0, keepdims=True)
        acc[:, :width] = acc[:, :width] * fade + dot_tn(part, soft.astype(BF))
        top[:, :width] = peak

    def mix_heads(level):
        n = counts[level]
        width = heads * n
        mixed_t = acc[:, :width] / total[:, :width]
        held[f"mixed_t_{level}"][...] = mixed_t
        held[f"log_{level}"][...] = top[:, :width] + jnp.log(total[:, :width])
        mixed = mixed_t.T
        for t in range(heads // 2):
            even = mixed[2 * t * n : (2 * t + 1) * n, :]
            odd = mixed[(2 * t + 1) * n : (2 * t + 2) * n, :]
            held[f"mixed_{level}"][:, t * LANES : (t + 1) * LANES] = jnp.where(
                left[:n], pltpu.roll(even, HD, 1), odd
            ).astype(BF)
        for base in ("mixed_t", "log", "mixed", "packed"):
            keep(f"{base}_{level}")

    sums = [Sum(mp, mp_me, *sum_refs[4 * i : 4 * i + 4]) for i in range(2 * len(counts))]
    chunk = model // mp
    base_o = mix + 2 * LANES
    base_gu = base_o + mix
    base_d = base_gu + 2 * hidden

    def chunk_of(c, low, high):
        return weights[c, :, :, :, low:high].reshape(chunk, high - low)

    def feed(level, beside):
        name = lambda base: held[f"{base}_{level}"]
        mixed_now = name("mixed")[...]
        first, last = sums[2 * level], sums[2 * level + 1]
        first.start(lambda c: dot_nt(mixed_now, chunk_of(c, base_o, base_gu)))
        beside(1)
        first.middle()
        beside(1)
        attn = first.finish()
        name("attn")[...] = attn
        level_rows = name("rows")[...].astype(F32)
        unit, unused = unit_of(level_rows + attn.astype(F32))
        second = (unit * gains[1:2, :]).astype(BF)
        name("second")[...] = second
        beside(100)
        parts = name("parts")
        for t in range(2 * hidden // 256):
            low = base_gu + t * 256
            parts[:, t * 256 : (t + 1) * 256] = dot_nn(
                second, weights[:, :, :, :, low : low + 256].reshape(model, 256)
            )
        n = counts[level]
        for t in range(hidden // LANES):
            cut = slice(t * LANES, (t + 1) * LANES)
            gate_part = parts[:, cut]
            up_part = parts[:, hidden + t * LANES : hidden + (t + 1) * LANES]
            hidden_v[:n, cut] = (gate_part * sigmoid(gate_part) * up_part).astype(BF)
        hidden_now = hidden_v[:n, :]
        last.start(lambda c: dot_nt(hidden_now, chunk_of(c, base_d, base_d + hidden)))
        for base in ("attn", "second", "parts"):
            keep(f"{base}_{level}")
        gate = sigmoid(jnp.sum(level_rows * gains[2:3, :], axis=-1, keepdims=True))
        last.middle()
        ffn = last.finish()
        name("ffn")[...] = ffn
        keep(f"ffn_{level}")
        update = (gate * (attn.astype(F32) + ffn.astype(F32))).astype(BF)
        if level:
            update = dot_tn(held[f"pick_{level}"][...], update)
        held["state"][...] = held["state"][...] + update.astype(F32)

    steps = len(groups) + 6
    done = [upto]

    def beside(count):
        for _ in range(count):
            if done[0] < steps:
                spread.step(done[0])
                done[0] += 1

    project(0, tokens[...])
    held["state"][...] = tokens[...].astype(F32)
    for name in ("place_0", "pick_1", "pick_2", "place_1", "place_2", "cosine_1", "sine_1", "cosine_2", "sine_2", "keys_1", "keys_2"):
        keep(name)
    for b in range(devices // group_of(0)):
        beside(1)

        @pl.when(b * group_of(0) <= me)
        def _(b=b):
            block(0, b)

    mix_heads(0)
    feed(0, beside)
    keep("weights")
    for level in range(1, len(counts)):
        now = dot_nn(held[f"pick_{level}"][...], held["state"][...].astype(BF)).astype(BF)
        project(level, now)

        def one_block(b, carry, level=level):
            block(level, b)
            return carry

        lax.fori_loop(0, me // group_of(level) + 1, one_block, 0)
        mix_heads(level)
        feed(level, lambda count: None)
    keep("state")
    spread.drain()
    for item in sums:
        item.drain()
    for level in range(len(counts)):

        def sent(e, carry, level=level):
            kv_copy(level, e, me).wait_send()
            return carry

        lax.fori_loop(me + 1, devices, sent, 0)
    for copy in keeps:
        copy.wait()


def advance(tokens, depths, second_slot, third_slot, matrices, vectors, tables, heads, devices, mp, ident):
    counts = (tokens.shape[0], SECOND_SLOTS, THIRD_SLOTS)
    rows, model = tokens.shape
    depth, mix = matrices[0].shape
    hidden = matrices[4].shape[1]
    total = 2 * mix + 2 * LANES + 3 * hidden
    cuts = [0, mix + 2 * LANES]
    while cuts[-1] < total:
        cuts.append(min(cuts[-1] + 512, total))
    if cuts[-1] - cuts[-2] < 256:
        cuts.pop(-2)
    groups = [(a, b, i % 2) for i, (a, b) in enumerate(zip(cuts[:-1], cuts[1:]))]
    shapes = {
        "state": ((rows, model), F32),
        "weights": ((4, 4, 2, depth, total), BF),
        "gains": ((8, model), F32),
    }
    for level, n in enumerate(counts):
        width = heads * n
        shapes[f"place_{level}"] = ((1, width), F32)
        if level:
            shapes[f"pick_{level}"] = ((n, rows), BF)
            shapes[f"cosine_{level}"] = ((n, LANES), F32)
            shapes[f"sine_{level}"] = ((n, LANES), F32)
            shapes[f"keys_{level}"] = ((devices, n, LANES), F32)
        for base in ("rows", "normed", "attn", "ffn", "second"):
            shapes[f"{base}_{level}"] = ((n, model), BF)
        shapes[f"parts_{level}"] = ((n, 2 * hidden), F32)
        shapes[f"packed_{level}"] = ((devices, n, 2 * HD), BF)
        shapes[f"query_{level}"] = ((width, 2 * HD), BF)
        shapes[f"mixed_t_{level}"] = ((2 * HD, width), F32)
        shapes[f"log_{level}"] = ((1, width), F32)
        shapes[f"mixed_{level}"] = ((n, mix), BF)
    names = tuple(shapes)
    args = (tokens, depths, second_slot, third_slot, *matrices, *vectors, *tables)
    width = heads * rows
    outs = pl.pallas_call(
        functools.partial(advance_kernel, counts, heads, devices, mp, hidden, groups, names),
        out_shape=tuple(jax.ShapeDtypeStruct(*shapes[name]) for name in names),
        in_specs=vmem(len(args)),
        out_specs=tuple([pl.BlockSpec(memory_space=pl.ANY)] * len(names)),
        scratch_shapes=[pltpu.VMEM(*shapes[name]) for name in names]
        + [
            pltpu.VMEM((depth, total), BF),
            pltpu.SemaphoreType.DMA(()),
            pltpu.SemaphoreType.DMA((len(groups), 8)),
            pltpu.SemaphoreType.DMA((len(groups), 8)),
            pltpu.VMEM((2 * HD, width), BF),
            pltpu.VMEM((1, width), F32),
            pltpu.VMEM((1, width), F32),
            pltpu.VMEM((2 * HD, width), F32),
            pltpu.VMEM((rows, hidden), BF),
            pltpu.SemaphoreType.DMA((len(names),)),
            pltpu.SemaphoreType.DMA((len(counts), devices)),
            pltpu.SemaphoreType.DMA((len(counts), devices)),
        ]
        + [item for n in counts for _ in range(2) for item in sum_scratch(mp, n, model)],
        compiler_params=pltpu.CompilerParams(
            collective_id=ident, has_side_effects=True, vmem_limit_bytes=VMEM_LIMIT
        ),
        name="advance",
    )(*args)
    return dict(zip(names, outs))


SLOTS = 6
GROUP = 512


class Collect:
    def __init__(self, spans, groups, x, y, core, turned, rights, vectors, store, slots, core_recv, relay_recv, first_recv, last_recv, send_sems, recv_sems, turn):
        self.spans, self.groups = spans, groups
        self.x, self.y, self.core = x, y, core
        self.turned, self.rights, self.vectors, self.store, self.slots = turned, rights, vectors, store, slots
        self.core_recv, self.relay_recv, self.first_recv = core_recv, relay_recv, first_recv
        self.last_recv = last_recv
        self.send_sems, self.recv_sems = send_sems, recv_sems
        self.turn = turn
        self.waits = [{} for _ in groups]
        self.done = set()

    def remote(self, g, index, source, target, device):
        copy = pltpu.make_async_remote_copy(
            src_ref=source, dst_ref=target, send_sem=self.send_sems.at[g, index],
            recv_sem=self.recv_sems.at[g, index], device_id=device, device_id_type=MESH,
        )
        copy.start()
        return copy

    def held(self, slot, axis, at, first, count):
        if axis == 0:
            return self.slots.at[slot, at, pl.ds(first, count), self.core]
        return self.slots.at[slot, pl.ds(first, count), at, self.core]

    def zero(self, g):
        slot, waits = g % SLOTS, self.waits
        if g >= SLOTS:
            for stage in range(3):
                for copy in waits[g - SLOTS][stage]:
                    copy.wait_send()
        column = 0
        for section, low, high in self.groups[g][1]:
            wide = high - low
            if section < 4:
                if section not in self.done:
                    self.done.add(section)
                    self.turn(section)
                base = self.spans[section][0]

            def rows_of(m, carry, section=section, low=low, high=high, column=column, wide=wide):
                start = pl.multiple_of(m * 1024, 1024)
                if section < 4:
                    value = dot_nn(
                        self.turned[section % 2, pl.ds(start, 1024), :], self.rights[:, base + low : base + high]
                    )
                else:
                    value = self.vectors[:, pl.ds(start, 1024)].T
                self.slots[slot, pl.ds(m * 2, 2), :, :, :, column : column + wide] = (
                    value.astype(BF).reshape(2, 4, 2, 64, wide)
                )
                return carry

            lax.fori_loop(0, 2, rows_of, 0)
            column += wide
        waits[g][0] = [
            self.remote(
                g, 0, self.slots.at[slot, :, :, 1 - self.core, :, :column],
                self.core_recv.at[g, :, :, :, :column], peer(self.x, self.y, 1 - self.core),
            )
        ]

    def first(self, g):
        slot, (width, _, axis) = g % SLOTS, self.groups[g]
        waits, slots = self.waits, self.slots
        waits[g][0][0].wait_recv()

        def add(i, carry):
            slots[slot, i, :, self.core, :, :width] = (
                slots[slot, i, :, self.core, :, :width] + self.core_recv[g, i, :, :, :width]
            )
            return carry

        lax.fori_loop(0, 4, add, 0)
        at = self.x if axis == 0 else self.y
        waits[g][1] = [
            self.remote(
                g, 1 + i, self.held(slot, axis, lax.rem(at + 2, 4), 2 * i, 2).at[:, :, :width],
                self.relay_recv.at[g, i, :, :, :width], shifted(self.x, self.y, self.core, axis, k),
            )
            for i, k in enumerate((1, 3))
        ]

    def second(self, g):
        slot, (width, _, axis) = g % SLOTS, self.groups[g]
        waits, slots = self.waits, self.slots
        at = self.x if axis == 0 else self.y
        waits[g][2] = []
        for i, k in enumerate((1, 3)):
            waits[g][1][i].wait_recv()
            there = lax.rem(at + k, 4)
            for j in range(2):
                b = 2 * i + j
                where = (slot, there, b, self.core) if axis == 0 else (slot, b, there, self.core)
                where = where + (slice(None), slice(0, width))
                slots[where] = slots[where] + self.relay_recv[g, i, j, :, :width]
            waits[g][2].append(
                self.remote(
                    g, 3 + i, self.held(slot, axis, there, 0, 4).at[:, :, :width],
                    self.first_recv.at[g, i, :, :, :width], shifted(self.x, self.y, self.core, axis, k),
                )
            )

    def third(self, g):
        slot, (width, _, axis) = g % SLOTS, self.groups[g]
        waits, slots = self.waits, self.slots
        at, other = (self.x, self.y) if axis == 0 else (self.y, self.x)
        for copy in waits[g][2]:
            copy.wait_recv()
        for b in range(4):
            where = (slot, at, b, self.core) if axis == 0 else (slot, b, at, self.core)
            self.core_recv[g, 0, b, :, :width] = (
                slots[where + (slice(None), slice(0, width))].astype(F32)
                + self.first_recv[g, 0, b, :, :width].astype(F32)
                + self.first_recv[g, 1, b, :, :width].astype(F32)
            ).astype(BF)
        waits[g][3] = [
            self.remote(
                g, 4 + k, self.core_recv.at[g, 0, lax.rem(other + k, 4), :, :width],
                self.last_recv.at[g, k - 1, :, :width],
                shifted(self.x, self.y, self.core, 1 - axis, k),
            )
            for k in (2, 1, 3)
        ]

    def fourth(self, g):
        width, pieces, axis = self.groups[g]
        other = self.y if axis == 0 else self.x
        value = self.core_recv[g, 0, other, :, :width].astype(F32)
        for copy in self.waits[g][3]:
            copy.wait_recv()
        for k in range(3):
            value = value + self.last_recv[g, k, :, :width].astype(F32)
        column = 0
        for section, low, high in pieces:
            self.store(section, low, value[:, column : column + high - low])
            column += high - low

    def step(self, i):
        for back, work in ((0, self.zero), (1, self.first), (3, self.second), (5, self.third), (6, self.fourth)):
            if 0 <= i - back < len(self.groups):
                work(i - back)

    def drain(self):
        count = len(self.groups)
        for g in range(count):
            for stage in range(4):
                if stage == 3 or g >= count - SLOTS:
                    for copy in self.waits[g][stage]:
                        copy.wait_send()


def finish_kernel(n, heads, devices, mp, group, levels, spans, groups, *refs):
    refs = list(refs)
    flow, gains, query_place, query, packed, mixed_t, log_total, grad_mixed, cosine, sine = [refs.pop(0) for _ in range(10)]
    rows_in, middle, logit, second_vecs, first_vecs, router_vecs = [refs.pop(0) for _ in range(6)]
    w_hbm = refs.pop(0)
    sources = [[refs.pop(0) for _ in range(8 if level else 7)] for level in range(len(levels))]
    flow_out, q_out, k_out, v_out, out_out, gate_out, up_out, down_out, vec_out = [refs.pop(0) for _ in range(9)]
    query_t, grad_rows, grad_t, acc, delta, send_buf, recv_buf, kv_send, kv_recv = [refs.pop(0) for _ in range(9)]
    w_qkv, w_sem, send_a, recv_a, full_a, sems_a = [refs.pop(0) for _ in range(6)]
    (lefts, turned, rights, vectors, slots, core_recv, relay_recv, first_recv, last_recv,
     loads, send_sems, recv_sems) = refs
    me, mp_me = lax.axis_index("dp"), lax.axis_index("mp")
    x, y, core = plane(me)
    load_w = pltpu.make_async_copy(w_hbm.at[:, : w_qkv.shape[1]], w_qkv, w_sem)
    load_w.start()
    fetches = [[] for _ in range(4)]

    def fetch(s, side):
        row = 0
        for level, count in enumerate(levels):
            low, high = spans[s]
            target = (lefts.at[s % 2, row : row + count], rights.at[row : row + count, low:high])[side]
            if 2 * s + side < len(sources[level]):
                copy = pltpu.make_async_copy(
                    sources[level][2 * s + side], target, loads.at[level, 2 * s + side]
                )
                copy.start()
                fetches[s].append(copy)
            row += count

    for s in range(4):
        if s < 2:
            fetch(s, 0)
        fetch(s, 1)

    barrier = pltpu.get_barrier_semaphore()

    def greet(k, carry):
        pl.semaphore_signal(
            barrier, inc=1, device_id={"dp": lax.rem(me + k, devices)}, device_id_type=MESH
        )
        return carry

    lax.fori_loop(1, devices, greet, 0)
    for k in range(1, mp):
        pl.semaphore_signal(
            barrier, inc=1, device_id={"mp": lax.rem(mp_me + k, mp)}, device_id_type=MESH
        )

    def turn(section):
        for copy in fetches[section]:
            copy.wait()
        turned[section % 2] = lefts[section % 2].T
        if section < 2:
            fetch(section + 2, 0)

    hidden = gate_out.shape[1]
    mix = q_out.shape[1]

    def store(section, low, value):
        high = low + value.shape[1]
        if section == 0:
            middle_cut = min(max(hidden - low, 0), high - low)
            if middle_cut:
                gate_out[:, low : low + middle_cut] = value[:, :middle_cut]
            if low + middle_cut < high:
                up_out[:, low + middle_cut - hidden : high - hidden] = value[:, middle_cut:]
        elif section == 1:
            down_out[:, low:high] = value
        elif section == 2:
            out_out[:, low:high] = value
        elif section == 3:
            if low < mix:
                q_out[:, low : min(high, mix)] = value[:, : min(high, mix) - low]
            if high > mix:
                k_out[...] = value[:, mix - low : mix - low + HD]
                v_out[...] = value[:, mix - low + HD :]
        else:
            vec_out[...] = value

    work = Collect(
        spans, groups, x, y, core, turned, rights, vectors, store, slots, core_recv, relay_recv,
        first_recv, last_recv, send_sems, recv_sems, turn,
    )
    left = lanes_of((n, LANES)) < HD
    for t in range(heads // 2):
        part = grad_mixed[:, t * LANES : (t + 1) * LANES].astype(F32)
        grad_rows[2 * t * n : (2 * t + 1) * n, :] = jnp.where(
            left, 0.0, pltpu.roll(part, HD, 1)
        ).astype(BF)
        grad_rows[(2 * t + 1) * n : (2 * t + 2) * n, :] = jnp.where(left, 0.0, part).astype(BF)
    query_t[...] = query[...].T
    grad_t[...] = grad_rows[...].T
    delta[...] = jnp.sum(grad_t[...].astype(F32) * mixed_t[...], axis=0, keepdims=True)
    acc[...] = jnp.zeros(acc.shape, F32)
    width = heads * n
    pl.semaphore_wait(barrier, devices - 1 + mp - 1)

    def send_copy(e, source_index):
        return pltpu.make_async_remote_copy(
            src_ref=send_buf.at[e], dst_ref=recv_buf.at[source_index],
            send_sem=kv_send.at[e], recv_sem=kv_recv.at[source_index],
            device_id={"dp": e}, device_id_type=MESH,
        )

    def one_block(b):
        part = packed[b * group : (b + 1) * group].reshape(group * n, 2 * HD)
        scores = dot_nn(part, query_t[...])
        place = (lax.broadcasted_iota(jnp.int32, (group * n, LANES), 0) + b * (group * n)).astype(F32)
        place = jnp.concatenate([place] * (width // LANES), axis=1)
        scores = jnp.where(place <= query_place[...], scores, NEG)
        weights = jnp.exp(scores - log_total[...])
        grad_weights = dot_nn(part, grad_t[...])
        grad_scores = (weights * (grad_weights - delta[...])).astype(BF)
        grad_part = dot_nn(grad_scores, query[...]) + dot_nn(weights.astype(BF), grad_rows[...])
        send_buf[b * group : (b + 1) * group] = grad_part.astype(BF).reshape(group, n, 2 * HD)
        acc[...] += dot_tn(part, grad_scores)
        for e in range(b * group, (b + 1) * group):

            @pl.when(e < me)
            def _(e=e):
                send_copy(e, me).start()

    blocks = devices // group
    for b in range(blocks):
        work.step(b)

        @pl.when(b * group <= me)
        def _(b=b):
            one_block(b)

    grad_query = acc[...].T * HD**-0.5
    outs = []
    for t in range(heads // 2):
        even = grad_query[2 * t * n : (2 * t + 1) * n, :]
        odd = grad_query[(2 * t + 1) * n : (2 * t + 2) * n, :]
        outs.append(jnp.where(left, even, pltpu.roll(odd, HD, 1)))

    def add(e, carry):
        send_copy(me, e).wait_recv()
        return carry + recv_buf[e].astype(F32)

    outs.append(lax.fori_loop(me + 1, devices, add, send_buf[me].astype(F32)))
    low = spans[3][0]
    for t, part in enumerate(outs):
        rights[0:n, low + t * LANES : low + (t + 1) * LANES] = turn_back(
            part, cosine[...], sine[...], t == heads // 2
        )
    load_w.wait()
    grad_now = rights[0:n, low : spans[3][1]]
    chunk = w_qkv.shape[0] // mp

    def first_chunk(c):
        return dot_nt(grad_now, w_qkv[pl.ds(pl.multiple_of(c * chunk, chunk), chunk), :])

    total = Sum(mp, mp_me, send_a, recv_a, full_a, sems_a)
    total.start(first_chunk)
    work.step(blocks)
    total.middle()
    work.step(blocks + 1)
    grad_normed = total.finish().astype(F32)
    level = rows_in[...].astype(F32)
    unit, factor = unit_of(level)
    vectors[...] = jnp.zeros(vectors.shape, F32)
    vectors[0:1, :] = jnp.sum(grad_normed * unit, axis=0, keepdims=True) + first_vecs[0:1, :] + first_vecs[1:2, :]
    vectors[1:2, :] = second_vecs[0:1, :] + second_vecs[1:2, :] + second_vecs[2:3, :]
    vectors[2:3, :] = jnp.sum(level * logit[...], axis=0, keepdims=True) + router_vecs[0:1, :] + router_vecs[1:2, :]
    flow_out[...] = flow[...] + (
        unit_back(grad_normed * gains[0:1, :], unit, factor) + middle[...] + logit[...] * gains[2:3, :]
    ).astype(BF).astype(F32)
    for i in range(blocks + 2, len(groups) + 6):
        work.step(i)
    work.drain()
    total.drain()

    def sent(e, carry):
        send_copy(e, me).wait_send()
        return carry

    lax.fori_loop(0, me, sent, 0)


class Sum:
    order = (2, 1, 3)

    def __init__(self, group, me, send, recv, full, sems):
        self.group, self.me, self.send, self.recv, self.full, self.sems = group, me, send, recv, full, sems

    def remote(self, source, target, stage, k):
        copy = pltpu.make_async_remote_copy(
            src_ref=source, dst_ref=target, send_sem=self.sems.at[stage, k - 1],
            recv_sem=self.sems.at[stage + 1, k - 1],
            device_id={"mp": lax.rem(self.me + k, self.group)}, device_id_type=MESH,
        )
        copy.start()
        return copy

    def start(self, make_chunk):
        self.out = []
        for k in self.order:
            self.send[k - 1] = make_chunk(lax.rem(self.me + k, self.group)).astype(BF)
            self.out.append(self.remote(self.send.at[k - 1], self.recv.at[k - 1], 0, k))
        self.own = make_chunk(self.me).astype(BF).astype(F32)

    def middle(self):
        total = self.own
        for k, copy in zip(self.order, self.out):
            copy.wait_recv()
            total = total + self.recv[k - 1].astype(F32)
        self.full[self.me] = total.astype(BF)
        self.back = [self.remote(self.full.at[self.me], self.full.at[self.me], 2, k) for k in self.order]

    def finish(self):
        for copy in self.back:
            copy.wait_recv()
        return jnp.concatenate([self.full[c] for c in range(self.group)], axis=1)

    def drain(self):
        for copy in self.out + self.back:
            copy.wait_send()


def finish(flow, gains, attention, tail, vecs, weights, levels, heads, devices, mp, depth, ident):
    n, model = levels[0][0].shape
    width = heads * n
    group = 512 // n
    mix = heads * HD
    widths = [levels[1][i].shape[1] for i in (1, 3, 5, 7)] + [LANES]
    spans, total = [], 0
    for wide in widths:
        spans.append((total, total + wide))
        total += wide
    pieces = []
    for section, wide in enumerate(widths):
        pieces += [(section, low, low + LANES) for low in range(0, wide, LANES)]
    groups = []
    per = GROUP // LANES
    for index in range(0, len(pieces), per):
        merged = []
        for section, low, high in pieces[index : index + per]:
            if merged and merged[-1][0] == section:
                merged[-1] = (section, merged[-1][1], high)
            else:
                merged.append((section, low, high))
        wide = sum(high - low for _, low, high in merged)
        groups.append((wide, merged, (index // per) % 2))
    counts = [level[0].shape[0] for level in levels]
    rows = sum(counts)
    hidden = widths[1]
    many = len(groups)
    whole = [flow, gains, *attention, *tail, *vecs]
    args = whole + [weights] + [item for level in levels for item in level]
    return pl.pallas_call(
        functools.partial(finish_kernel, n, heads, devices, mp, group, counts, spans, groups),
        out_shape=(
            jax.ShapeDtypeStruct(flow.shape, F32),
            jax.ShapeDtypeStruct((depth, mix), F32),
            jax.ShapeDtypeStruct((depth, HD), F32),
            jax.ShapeDtypeStruct((depth, HD), F32),
            jax.ShapeDtypeStruct((depth, mix), F32),
            jax.ShapeDtypeStruct((depth, hidden), F32),
            jax.ShapeDtypeStruct((depth, hidden), F32),
            jax.ShapeDtypeStruct((depth, hidden), F32),
            jax.ShapeDtypeStruct((depth, LANES), F32),
        ),
        in_specs=vmem(len(whole)) + [pl.BlockSpec(memory_space=pl.ANY)] * (len(args) - len(whole)),
        out_specs=tuple(vmem(9)),
        scratch_shapes=[
            pltpu.VMEM((2 * HD, width), BF),
            pltpu.VMEM((width, 2 * HD), BF),
            pltpu.VMEM((2 * HD, width), BF),
            pltpu.VMEM((2 * HD, width), F32),
            pltpu.VMEM((1, width), F32),
            pltpu.VMEM((devices, n, 2 * HD), BF),
            pltpu.VMEM((devices, n, 2 * HD), BF),
            pltpu.SemaphoreType.DMA((devices,)),
            pltpu.SemaphoreType.DMA((devices,)),
            pltpu.VMEM((model, mix + 2 * HD), BF),
            pltpu.SemaphoreType.DMA(()),
            *sum_scratch(mp, n, model),
            pltpu.VMEM((2, rows, model), BF),
            pltpu.VMEM((2, model, rows), BF),
            pltpu.VMEM((rows, spans[3][1]), BF),
            pltpu.VMEM((LANES, model), F32),
            pltpu.VMEM((SLOTS, 4, 4, 2, depth, GROUP), BF),
            pltpu.VMEM((many, 4, 4, depth, GROUP), BF),
            pltpu.VMEM((many, 2, 2, depth, GROUP), BF),
            pltpu.VMEM((many, 2, 4, depth, GROUP), BF),
            pltpu.VMEM((many, 3, depth, GROUP), BF),
            pltpu.SemaphoreType.DMA((len(levels), 8)),
            pltpu.SemaphoreType.DMA((many, 8)),
            pltpu.SemaphoreType.DMA((many, 8)),
        ],
        compiler_params=pltpu.CompilerParams(
            collective_id=ident, has_side_effects=True, vmem_limit_bytes=63 * 1024 * 1024
        ),
        name="finish",
    )(*args)


def rotary_tables(place):
    freq = jnp.exp(jnp.arange(HD // 2, dtype=F32) * (-2.0 * math.log(ROPE_BASE) / HD))
    angle = place.astype(F32)[:, None] * freq[None, :]
    cosine, sine = jnp.cos(angle), jnp.sin(angle)
    return (
        jnp.concatenate([cosine] * 4, axis=1),
        jnp.concatenate([-sine, sine, -sine, sine], axis=1),
    )


def local(
    tokens, depths, second_slot, third_slot, w_query, w_key, w_value, w_out, w_gate, w_up,
    w_down, norm_first, norm_second, router, cotangent,
):
    me = lax.axis_index("dp")
    devices, mp = lax.axis_size("dp"), lax.axis_size("mp")
    rows = tokens.shape[0]
    heads = w_query.shape[1] // HD
    hidden_width = w_gate.shape[1]
    depth = w_query.shape[0]
    home = rotary_tables(jnp.arange(rows, dtype=jnp.int32) + me * rows)

    def row(values):
        return values.reshape(1, -1)

    kept = advance(
        tokens, row(depths), row(second_slot), row(third_slot),
        (w_query, w_key, w_value, w_out.T, w_gate, w_up, w_down.T),
        (row(norm_first), row(norm_second), row(router)), home, heads, devices, mp, 0,
    )
    weights = kept["weights"].reshape(devices * depth, -1)
    gains = kept["gains"]
    flow = cotangent
    tail = None
    terms, vectors, second_vecs = [], [], []
    for index in (2, 1, 0):
        query_place, rows_in, normed, packed, query, mixed_t, log_total, mixed, attn, ffn, second, parts = [
            kept[f"{base}_{index}"]
            for base in (
                "place", "rows", "normed", "packed", "query", "mixed_t", "log", "mixed", "attn", "ffn", "second", "parts"
            )
        ]
        pick = kept[f"pick_{index}"] if index else None
        head = (rows_in, attn, ffn, second, parts, pick)
        outs = list(
            feed_back(flow, gains, tail, head, weights, hidden_width, heads * HD, mp, 6 + index)
        )
        if tail is not None:
            flow, first_vec, router_vec = outs[:3]
            outs = outs[3:]
            vectors.append((first_vec, router_vec))
        grad_attn, grad_middle, logit, grad_mixed, parts_grad, hidden, grad_ffn, second_vec = outs
        second_vecs.append(second_vec)
        items = (second, parts_grad, grad_ffn, hidden, grad_attn, mixed, normed)
        if index:
            grad_qkv = attend_back(
                kept[f"keys_{index}"].reshape(-1, LANES), query_place, query, packed, mixed_t, log_total,
                grad_mixed, (kept[f"cosine_{index}"], kept[f"sine_{index}"]),
                heads, devices, rows_in.shape[0], 10 + index,
            )
            tail = (grad_qkv, rows_in, grad_middle, logit, pick)
            items = items + (grad_qkv,)
        terms.append(items)
    attention = (query_place, query, packed, mixed_t, log_total, grad_mixed, *home)
    vecs = [jnp.concatenate(list(part), axis=0) for part in (second_vecs, *zip(*vectors))]
    flow, query_grad, key_grad, value_grad, out_grad, gate_grad, up_grad, down_grad, vec = finish(
        flow, gains, attention, (rows_in, grad_middle, logit), vecs, weights, terms[::-1],
        heads, devices, mp, depth, 14,
    )
    return (
        kept["state"], flow, query_grad, key_grad, value_grad, out_grad.T, gate_grad, up_grad, down_grad.T,
        vec[:, 0], vec[:, 1], vec[:, 2],
    )


def solution(mesh):
    in_specs = (
        P("dp", None), P("dp"), P("dp"), P("dp"), P("dp", "mp"), P("dp", "mp"), P("dp", "mp"),
        P("mp", "dp"), P("dp", "mp"), P("dp", "mp"), P("mp", "dp"), P("dp"), P("dp"), P("dp"),
        P("dp", None),
    )
    out_specs = (
        P("dp", None), P("dp", None), P("dp", "mp"), P("dp", "mp"), P("dp", "mp"), P("mp", "dp"),
        P("dp", "mp"), P("dp", "mp"), P("mp", "dp"), P("dp"), P("dp"), P("dp"),
    )
    return jax.shard_map(local, mesh=mesh, in_specs=in_specs, out_specs=out_specs, check_vma=False)
```

```python
import functools
import math

import jax
import jax.numpy as jnp
from jax import lax
from jax.experimental import pallas as pl
from jax.experimental.pallas import tpu as pltpu
from jax.sharding import PartitionSpec as P

HD = 64
SECOND_SLOTS = 96
THIRD_SLOTS = 64
EPS = 1e-05
NEG = -1e30
ROPE_BASE = 10000.0
FAR = 1e9
BF = jnp.bfloat16
F32 = jnp.float32
MESH = pl.DeviceIdType.MESH
LANES = 128
VMEM_LIMIT = 63 * 1024 * 1024


def dot_nn(left, right):
    return lax.dot_general(left, right, (((1,), (0,)), ((), ())), preferred_element_type=F32)


def dot_nt(left, right):
    return lax.dot_general(left, right, (((1,), (1,)), ((), ())), preferred_element_type=F32)


def dot_tn(left, right):
    return lax.dot_general(left, right, (((0,), (0,)), ((), ())), preferred_element_type=F32)


def unit_of(values):
    factor = lax.rsqrt(jnp.mean(values * values, axis=-1, keepdims=True) + EPS)
    return values * factor, factor


def unit_back(shaped, unit, factor):
    return factor * (shaped - unit * jnp.mean(shaped * unit, axis=-1, keepdims=True))


def sigmoid(values):
    return 1.0 / (1.0 + jnp.exp(-values))


def lanes_of(shape):
    return lax.broadcasted_iota(jnp.int32, shape, 1)


def swap_halves(tile):
    first = lax.rem(lanes_of(tile.shape), HD) < HD // 2
    return jnp.where(first, pltpu.roll(tile, LANES - HD // 2, 1), pltpu.roll(tile, HD // 2, 1))


def turn_back(part, cosine, sine, packed):
    if packed:
        left = lanes_of(part.shape) < HD
        cosine, sine = jnp.where(left, cosine, 1.0), jnp.where(left, sine, 0.0)
    return (part * cosine - swap_halves(part) * sine).astype(BF)


def tile_of(values, index):
    return values[:, index * LANES : (index + 1) * LANES]


def signal_all(group, me, axis):
    barrier = pltpu.get_barrier_semaphore()
    for k in range(1, group):
        pl.semaphore_signal(
            barrier, inc=1, device_id={axis: lax.rem(me + k, group)}, device_id_type=MESH
        )
    pl.semaphore_wait(barrier, group - 1)


PIECES = 2


class Sum:
    order = (2, 1, 3)

    def __init__(self, group, me, send, recv, full, sems):
        self.group, self.me, self.send, self.recv, self.full, self.sems = group, me, send, recv, full, sems
        self.wide = send.shape[-1]

    def remote(self, source, target, stage, k, piece):
        copy = pltpu.make_async_remote_copy(
            src_ref=source, dst_ref=target, send_sem=self.sems.at[stage, k - 1, piece],
            recv_sem=self.sems.at[stage + 1, k - 1, piece],
            device_id={"mp": lax.rem(self.me + k, self.group)}, device_id_type=MESH,
        )
        copy.start()
        return copy

    def start(self, make_piece):
        self.make, self.out, self.back = make_piece, [], []
        for piece in range(PIECES):
            copies = []
            for k in self.order:
                at = (k - 1, piece)
                self.send[at] = self.part(lax.rem(self.me + k, self.group), piece).astype(BF)
                copies.append(self.remote(self.send.at[at], self.recv.at[at], 0, k, piece))
            self.out.append(copies)

    def part(self, c, piece):
        start = c * (PIECES * self.wide) + piece * self.wide
        return self.make(pl.multiple_of(start, self.wide), self.wide)

    def middle(self):
        for piece in range(PIECES):
            total = self.part(self.me, piece).astype(BF).astype(F32)
            for k, copy in zip(self.order, self.out[piece]):
                copy.wait_recv()
                total = total + self.recv[k - 1, piece].astype(F32)
            self.full[self.me, piece] = total.astype(BF)
            where = self.full.at[self.me, piece]
            self.back.append([self.remote(where, where, 2, k, piece) for k in self.order])

    def finish(self):
        for copies in self.back:
            for copy in copies:
                copy.wait_recv()
        return jnp.concatenate(
            [self.full[c, piece] for c in range(self.group) for piece in range(PIECES)], axis=1
        )

    def drain(self):
        for copies in self.out + self.back:
            for copy in copies:
                copy.wait_send()


def vmem(count):
    return [pl.BlockSpec(memory_space=pltpu.VMEM)] * count


def sum_scratch(mp, n, model):
    wide = model // mp // PIECES
    return [
        pltpu.VMEM((mp - 1, PIECES, n, wide), BF),
        pltpu.VMEM((mp - 1, PIECES, n, wide), BF),
        pltpu.VMEM((mp, PIECES, n, wide), BF),
        pltpu.SemaphoreType.DMA((4, mp - 1, PIECES)),
    ]


def retreat_kernel(counts, heads, devices, mp, hidden, ins, names, *refs):
    refs = list(refs)
    sources = {name: refs.pop(0) for name in ins}
    w_hbm = refs.pop(0)
    outs = {name: refs.pop(0) for name in names}
    held = {name: refs.pop(0) for name in ins}
    held.update({name: refs.pop(0) for name in names})
    w_qkv, w_o, w_gu, w_d, fetch_sems, w_sems, keep_sems = [refs.pop(0) for _ in range(7)]
    query_t, grad_rows, grad_t, acc, delta = [refs.pop(0) for _ in range(5)]
    buffers = {level: [refs.pop(0) for _ in range(4)] for level in (1, 2)}
    sum_refs = {key: [refs.pop(0) for _ in range(4)] for key in ("head_2", "tail_2", "head_1", "tail_1", "head_0")}
    me, mp_me = lax.axis_index("dp"), lax.axis_index("mp")
    model = w_o.shape[0]
    mix = heads * HD
    loads, keeps = {}, []

    def fetch(name):
        loads[name] = pltpu.make_async_copy(sources[name], held[name], fetch_sems.at[ins.index(name)])
        loads[name].start()

    def load(name, ref, start, index):
        loads[name] = pltpu.make_async_copy(w_hbm.at[:, start : start + ref.shape[1]], ref, w_sems.at[index])
        loads[name].start()

    def get(name):
        if name in loads:
            loads.pop(name).wait()
        return held[name]

    def need(name):
        if name in loads:
            loads.pop(name).wait()

    def keep(name):
        copy = pltpu.make_async_copy(held[name], outs[name], keep_sems.at[len(keeps)])
        copy.start()
        keeps.append(copy)

    base_o = mix + 2 * LANES
    for name in ("flow", "gains", "pick_2", "rows_2", "attn_2", "ffn_2", "parts_2"):
        fetch(name)
    load("d", w_d, base_o + mix + 2 * hidden, 0)
    load("gu", w_gu, base_o + mix, 1)
    load("o", w_o, base_o, 2)
    load("qkv", w_qkv, 0, 3)
    for name in ins:
        if name not in loads:
            fetch(name)

    barrier = pltpu.get_barrier_semaphore()

    def greet(k, carry):
        pl.semaphore_signal(
            barrier, inc=1, device_id={"dp": lax.rem(me + k, devices)}, device_id_type=MESH
        )
        return carry

    lax.fori_loop(1, devices, greet, 0)
    for k in range(1, mp):
        pl.semaphore_signal(
            barrier, inc=1, device_id={"mp": lax.rem(mp_me + k, mp)}, device_id_type=MESH
        )
    sums = {key: Sum(mp, mp_me, *items) for key, items in sum_refs.items()}
    vecs = held["vecs"]
    vecs[...] = jnp.zeros(vecs.shape, F32)
    gate_of = {}

    def head(level):
        n = counts[level]
        name = lambda base: held[f"{base}_{level}"]
        grad_update = get("flow")[...].astype(BF)
        if level:
            grad_update = dot_nn(get(f"pick_{level}")[...], grad_update)
        grad_update = grad_update.astype(F32)
        rows_now = get(f"rows_{level}")[...].astype(F32)
        attn_now = get(f"attn_{level}")[...].astype(F32)
        gains = get("gains")
        gate = sigmoid(jnp.sum(rows_now * gains[2:3, :], axis=-1, keepdims=True))
        logit = jnp.sum(
            grad_update * (attn_now + get(f"ffn_{level}")[...].astype(F32)), axis=-1, keepdims=True
        )
        name("logit")[...] = logit * gate * (1.0 - gate)
        grad_ffn = (gate * grad_update).astype(BF)
        name("grad_ffn")[...] = grad_ffn
        parts, parts_grad, hidden_out = get(f"parts_{level}"), name("parts_grad"), name("hidden")
        need("d")
        for t in range(hidden // LANES):
            cut = slice(t * LANES, (t + 1) * LANES)
            up_cut = slice(hidden + t * LANES, hidden + (t + 1) * LANES)
            if t % 2 == 0:
                both = dot_nn(grad_ffn, w_d[:, t * LANES : min((t + 2) * LANES, hidden)])
            grad_hidden = tile_of(both, t % 2)
            gate_part = parts[:, cut]
            up_part = parts[:, up_cut]
            sigma = sigmoid(gate_part)
            active = gate_part * sigma
            hidden_out[:, cut] = (active * up_part).astype(BF)
            parts_grad[:, cut] = (
                grad_hidden * up_part * sigma * (1.0 + gate_part * (1.0 - sigma))
            ).astype(BF)
            parts_grad[:, up_cut] = (grad_hidden * active).astype(BF)
        need("gu")
        if level == 2:
            pl.semaphore_wait(barrier, devices - 1 + mp - 1)
        parts_now = parts_grad[...]
        total = sums[f"head_{level}"]
        total.start(lambda start, wide: dot_nt(parts_now, w_gu[pl.ds(start, wide), :]))
        for base in ("grad_ffn", "hidden", "parts_grad", "logit"):
            keep(f"{base}_{level}")
        unit, factor = unit_of(rows_now + attn_now)
        total.middle()
        grad_second = total.finish().astype(F32)
        vecs[2 - level : 3 - level, :] = jnp.sum(grad_second * unit, axis=0, keepdims=True)
        grad_middle = unit_back(grad_second * gains[1:2, :], unit, factor)
        name("middle")[...] = grad_middle
        grad_attn = (gate * grad_update + grad_middle).astype(BF)
        name("grad_attn")[...] = grad_attn
        need("o")
        name("grad_mixed")[...] = dot_nn(grad_attn, w_o[...]).astype(BF)
        for base in ("grad_attn", "middle", "grad_mixed"):
            keep(f"{base}_{level}")

    def attention(level):
        n = counts[level]
        group = 512 // n if 512 % n == 0 else 4
        width = heads * n
        send_buf, recv_buf, send_sems, recv_sems = buffers[level]
        query, packed = get(f"query_{level}"), get(f"packed_{level}")
        mixed_t, log_total = get(f"mixed_t_{level}"), get(f"log_{level}")
        keys, query_place = get(f"keys_{level}"), get(f"place_{level}")
        cosine, sine = get(f"cosine_{level}"), get(f"sine_{level}")
        grad_mixed, grad_qkv = held[f"grad_mixed_{level}"], held[f"grad_qkv_{level}"]
        left = lanes_of((n, LANES)) < HD
        for t in range(heads // 2):
            part = grad_mixed[:, t * LANES : (t + 1) * LANES].astype(F32)
            grad_rows[2 * t * n : (2 * t + 1) * n, :] = jnp.where(
                left, 0.0, pltpu.roll(part, HD, 1)
            ).astype(BF)
            grad_rows[(2 * t + 1) * n : (2 * t + 2) * n, :] = jnp.where(left, 0.0, part).astype(BF)
        query_t[:, :width] = query[...].T
        grad_t[:, :width] = grad_rows[:width, :].T
        delta[:, :width] = jnp.sum(grad_t[:, :width].astype(F32) * mixed_t[...], axis=0, keepdims=True)
        acc[:, :width] = jnp.zeros((2 * HD, width), F32)

        def send_copy(e, source_index):
            return pltpu.make_async_remote_copy(
                src_ref=send_buf.at[e], dst_ref=recv_buf.at[source_index],
                send_sem=send_sems.at[e], recv_sem=recv_sems.at[source_index],
                device_id={"dp": e}, device_id_type=MESH,
            )

        def one_block(b, carry):
            part = packed[pl.ds(b * group, group)].reshape(group * n, 2 * HD)
            scores = dot_nn(part, query_t[:, :width])
            place = keys[pl.ds(b * group, group)].reshape(group * n, LANES)
            place = jnp.concatenate([place] * (width // LANES), axis=1)
            scores = jnp.where(place <= query_place[...], scores, NEG)
            soft = jnp.exp(scores - log_total[...])
            grad_soft = dot_nn(part, grad_t[:, :width])
            grad_scores = (soft * (grad_soft - delta[:, :width])).astype(BF)
            grad_part = dot_nn(grad_scores, query[...]) + dot_nn(soft.astype(BF), grad_rows[:width, :])
            send_buf[pl.ds(b * group, group)] = grad_part.astype(BF).reshape(group, n, 2 * HD)
            acc[:, :width] += dot_tn(part, grad_scores)
            for g in range(group):
                e = b * group + g

                @pl.when(e < me)
                def _(e=e):
                    send_copy(e, me).start()

            return carry

        lax.fori_loop(0, me // group + 1, one_block, 0)
        grad_query = acc[:, :width].T * HD**-0.5
        for t in range(heads // 2):
            even = grad_query[2 * t * n : (2 * t + 1) * n, :]
            odd = grad_query[(2 * t + 1) * n : (2 * t + 2) * n, :]
            part = jnp.where(left, even, pltpu.roll(odd, HD, 1))
            grad_qkv[:, t * LANES : (t + 1) * LANES] = turn_back(part, cosine[...], sine[...], False)

        def add(e, carry):
            send_copy(me, e).wait_recv()
            return carry + recv_buf[e].astype(F32)

        part = lax.fori_loop(me + 1, devices, add, send_buf[me].astype(F32))
        grad_qkv[:, mix:] = turn_back(part, cosine[...], sine[...], True)

        def drain():
            def sent(e, carry):
                send_copy(e, me).wait_send()
                return carry

            lax.fori_loop(0, me, sent, 0)

        return drain

    def tail(level):
        gains, flow = held["gains"], held["flow"]
        grad_now = held[f"grad_qkv_{level}"][...]
        need("qkv")
        total = sums[f"tail_{level}"]
        total.start(lambda start, wide: dot_nt(grad_now, w_qkv[pl.ds(start, wide), :]))
        keep(f"grad_qkv_{level}")
        rows_now = held[f"rows_{level}"][...].astype(F32)
        unit, factor = unit_of(rows_now)
        logit = held[f"logit_{level}"][...]
        vecs[7 - level : 8 - level, :] = jnp.sum(rows_now * logit, axis=0, keepdims=True)
        total.middle()
        grad_normed = total.finish().astype(F32)
        vecs[5 - level : 6 - level, :] = jnp.sum(grad_normed * unit, axis=0, keepdims=True)
        grad_rows_now = (
            unit_back(grad_normed * gains[0:1, :], unit, factor)
            + held[f"middle_{level}"][...]
            + logit * gains[2:3, :]
        ).astype(BF)
        flow[...] = flow[...] + dot_tn(held[f"pick_{level}"][...], grad_rows_now)

    drains = []
    for level in (2, 1):
        head(level)
        drains.append(attention(level))
        tail(level)
    held["flow_out"][...] = held["flow"][...]
    keep("flow_out")
    head(0)
    keep("vecs")
    for drain in drains:
        drain()
    for item in sums.values():
        item.drain()
    for copy in keeps:
        copy.wait()


def retreat(cotangent, kept, weights, heads, devices, mp, ident):
    counts = tuple(kept[f"rows_{level}"].shape[0] for level in range(3))
    model = cotangent.shape[1]
    mix = heads * HD
    hidden = kept["parts_0"].shape[1] // 2
    ins = {"flow": cotangent, "gains": kept["gains"]}
    shapes = {"flow_out": (cotangent.shape, F32), "vecs": ((8, model), F32)}
    for level, n in enumerate(counts):
        for base in ("rows", "attn", "ffn", "parts"):
            ins[f"{base}_{level}"] = kept[f"{base}_{level}"]
        if level:
            for base in ("pick", "query", "packed", "mixed_t", "log", "keys", "place", "cosine", "sine"):
                ins[f"{base}_{level}"] = kept[f"{base}_{level}"]
            shapes[f"grad_qkv_{level}"] = ((n, mix + 2 * HD), BF)
        shapes[f"grad_attn_{level}"] = ((n, model), BF)
        shapes[f"grad_ffn_{level}"] = ((n, model), BF)
        shapes[f"hidden_{level}"] = ((n, hidden), BF)
        shapes[f"parts_grad_{level}"] = ((n, 2 * hidden), BF)
        shapes[f"grad_mixed_{level}"] = ((n, mix), BF)
        shapes[f"middle_{level}"] = ((n, model), F32)
        shapes[f"logit_{level}"] = ((n, 1), F32)
    names = tuple(shapes)
    most = heads * max(counts[1:])
    anywhere = pl.BlockSpec(memory_space=pl.ANY)
    outs = pl.pallas_call(
        functools.partial(retreat_kernel, counts, heads, devices, mp, hidden, tuple(ins), names),
        out_shape=tuple(jax.ShapeDtypeStruct(*shapes[name]) for name in names),
        in_specs=[anywhere] * (len(ins) + 1),
        out_specs=tuple([anywhere] * len(names)),
        scratch_shapes=[pltpu.VMEM(item.shape, item.dtype) for item in ins.values()]
        + [pltpu.VMEM(*shapes[name]) for name in names]
        + [
            pltpu.VMEM((model, mix + 2 * HD), BF),
            pltpu.VMEM((model, mix), BF),
            pltpu.VMEM((model, 2 * hidden), BF),
            pltpu.VMEM((model, hidden), BF),
            pltpu.SemaphoreType.DMA((len(ins),)),
            pltpu.SemaphoreType.DMA((4,)),
            pltpu.SemaphoreType.DMA((len(names),)),
            pltpu.VMEM((2 * HD, most), BF),
            pltpu.VMEM((most, 2 * HD), BF),
            pltpu.VMEM((2 * HD, most), BF),
            pltpu.VMEM((2 * HD, most), F32),
            pltpu.VMEM((1, most), F32),
        ]
        + [
            item
            for level in (1, 2)
            for item in (
                pltpu.VMEM((devices, counts[level], 2 * HD), BF),
                pltpu.VMEM((devices, counts[level], 2 * HD), BF),
                pltpu.SemaphoreType.DMA((devices,)),
                pltpu.SemaphoreType.DMA((devices,)),
            )
        ]
        + [item for level in (2, 2, 1, 1, 0) for item in sum_scratch(mp, counts[level], model)],
        compiler_params=pltpu.CompilerParams(
            collective_id=ident, has_side_effects=True, vmem_limit_bytes=VMEM_LIMIT
        ),
        name="retreat",
    )(*ins.values(), weights)
    return dict(zip(names, outs))


def plane(me):
    return me // 8, lax.rem(me // 2, 4), lax.rem(me, 2)


def peer(x, y, core):
    return {"dp": (lax.rem(x, 4) * 4 + lax.rem(y, 4)) * 2 + core}


def shifted(x, y, core, axis, k):
    return peer(x + k, y, core) if axis == 0 else peer(x, y + k, core)


def meet(me, partners):
    barrier = pltpu.get_barrier_semaphore()
    for device in partners:
        pl.semaphore_signal(barrier, inc=1, device_id=device, device_id_type=MESH)
    pl.semaphore_wait(barrier, len(partners))


def plane_partners(x, y, core):
    return (
        [peer(x, y, 1 - core)]
        + [shifted(x, y, core, 0, k) for k in (1, 2, 3)]
        + [shifted(x, y, core, 1, k) for k in (1, 2, 3)]
    )


class Spread:
    def __init__(self, groups, x, y, core, shard, full, send_sems, recv_sems):
        self.groups, self.x, self.y, self.core = groups, x, y, core
        self.shard, self.full = shard, full
        self.send_sems, self.recv_sems = send_sems, recv_sems
        self.started = []
        self.waits = [{} for _ in groups]

    def remote(self, g, index, source, target, device):
        copy = pltpu.make_async_remote_copy(
            src_ref=source, dst_ref=target, send_sem=self.send_sems.at[g, index],
            recv_sem=self.recv_sems.at[g, index], device_id=device, device_id_type=MESH,
        )
        copy.start()
        self.started.append(copy)
        return copy

    def line(self, axis, at, first, count, cut):
        if axis == 0:
            return self.full.at[pl.ds(first, count), at, self.core, :, cut]
        return self.full.at[at, pl.ds(first, count), self.core, :, cut]

    def one(self, g):
        low, high, axis = self.groups[g]
        cut = slice(low, high)
        self.waits[g][1] = [
            self.remote(
                g, k - 1, self.shard.at[:, cut], self.full.at[self.x, self.y, self.core, :, cut],
                shifted(self.x, self.y, self.core, axis, k),
            )
            for k in (2, 1, 3)
        ]

    def two(self, g):
        low, high, axis = self.groups[g]
        for copy in self.waits[g][1]:
            copy.wait_recv()
        mine = self.line(axis, self.y if axis == 0 else self.x, 0, 4, slice(low, high))
        self.waits[g][2] = [
            self.remote(g, 3 + i, mine, mine, shifted(self.x, self.y, self.core, 1 - axis, k))
            for i, k in enumerate((1, 3))
        ]

    def three(self, g):
        low, high, axis = self.groups[g]
        at = self.y if axis == 0 else self.x
        self.waits[g][3] = []
        for i, k in enumerate((1, 3)):
            self.waits[g][2][i].wait_recv()
            piece = self.line(axis, lax.rem(at + 4 - k, 4), 2 * i, 2, slice(low, high))
            self.waits[g][3].append(
                self.remote(g, 5 + i, piece, piece, shifted(self.x, self.y, self.core, 1 - axis, k))
            )

    def four(self, g):
        low, high, axis = self.groups[g]
        for copy in self.waits[g][3]:
            copy.wait_recv()
        mine = self.full.at[:, :, self.core, :, slice(low, high)]
        self.waits[g][4] = [self.remote(g, 7, mine, mine, peer(self.x, self.y, 1 - self.core))]

    def five(self, g):
        self.waits[g][4][0].wait_recv()

    def step(self, i):
        for back, work in ((0, self.one), (2, self.two), (4, self.three), (5, self.four), (6, self.five)):
            if 1 <= i - back < len(self.groups):
                work(i - back)

    def drain(self):
        for copy in self.started:
            copy.wait_send()


def advance_kernel(counts, heads, devices, mp, hidden, groups, names, *refs):
    refs = list(refs)
    (tokens, depths, second_slot, third_slot, w_query, w_key, w_value, w_out, w_gate, w_up, w_down,
     norm_first, norm_second, router, cosine_in, sine_in) = [refs.pop(0) for _ in range(16)]
    outs = {name: refs.pop(0) for name in names}
    held = {name: refs.pop(0) for name in names}
    shard, own_sem, send_sems, recv_sems, query_t, top, total, acc, hidden_v, keep_sems, kv_send, kv_recv = [
        refs.pop(0) for _ in range(12)
    ]
    sum_refs = refs
    me, mp_me = lax.axis_index("dp"), lax.axis_index("mp")
    x, y, core = plane(me)
    weights = held["weights"]
    rows, model = tokens.shape
    mix = heads * HD
    lanes = lanes_of((rows, LANES))
    left = lanes < HD
    keeps = []

    def keep(name):
        copy = pltpu.make_async_copy(held[name], outs[name], keep_sems.at[len(keeps)])
        copy.start()
        keeps.append(copy)

    barrier = pltpu.get_barrier_semaphore()

    def greet(k, carry):
        pl.semaphore_signal(
            barrier, inc=1, device_id={"dp": lax.rem(me + k, devices)}, device_id_type=MESH
        )
        return carry

    lax.fori_loop(1, devices, greet, 0)
    for k in range(1, mp):
        pl.semaphore_signal(
            barrier, inc=1, device_id={"mp": lax.rem(mp_me + k, mp)}, device_id_type=MESH
        )

    token = lanes_of((1, rows)).astype(F32)
    picks, marks, query_places = [None], [None], []
    query_places.append(
        (lax.rem(lanes_of((1, heads * rows)), rows) + me * rows).astype(F32)
    )
    held["place_0"][...] = query_places[0]
    for level, slot, deep in ((1, second_slot, 2), (2, third_slot, 3)):
        count = counts[level]
        slots = lax.broadcasted_iota(jnp.int32, (count, rows), 0)
        active = (depths[...] >= deep) & (slot[...] >= 0)
        chosen = jnp.where(active, slot[...], -1) == slots
        pick = jnp.where(chosen, 1.0, 0.0).astype(BF)
        held[f"pick_{level}"][...] = pick
        picks.append(pick)
        marks.append(
            jnp.min(jnp.where(chosen, token, float(rows)), axis=1, keepdims=True)
        )
        sublane = lax.broadcasted_iota(jnp.int32, (16, rows), 0)
        probe = jnp.where(sublane == 0, token, 1.0).astype(BF)
        found = dot_nt(probe, jnp.concatenate([pick] * heads, axis=0))
        place = jnp.where(found[1:2, :] > 0.5, found[0:1, :] + (me * rows).astype(F32), FAR)
        held[f"place_{level}"][...] = place
        query_places.append(place)
        table = jnp.concatenate([cosine_in[...], sine_in[...]], axis=1)
        turned = lax.dot_general(
            pick.astype(F32), table, (((1,), (0,)), ((), ())),
            preferred_element_type=F32, precision=lax.Precision.HIGHEST,
        )
        held[f"cosine_{level}"][...] = turned[:, :LANES]
        held[f"sine_{level}"][...] = turned[:, LANES:]
    depth = w_query.shape[0]
    wide = jnp.zeros((1, LANES - depth), F32)
    gain_rows = jnp.concatenate(
        [jnp.concatenate([ref[...].astype(F32), wide], axis=1) for ref in (norm_first, norm_second, router)]
        + [jnp.zeros((LANES - 3, LANES), F32)],
        axis=0,
    )
    extra = gain_rows.T[:depth, :]
    rest = counts[1] - depth
    lane = lanes_of((depth, LANES))
    over = jnp.concatenate([marks[1][depth:, :], jnp.full((depth - rest, 1), float(rows), F32)], axis=0)
    extra = jnp.where(lane == 3, marks[1][:depth, :], extra)
    extra = jnp.where(lane == 4, over, extra)
    extra = jnp.where(lane == 5, marks[2], extra)
    pair = jnp.concatenate([w_key[...].astype(F32), w_value[...].astype(F32)], axis=1).astype(BF)
    start = 0
    for part in (
        w_query[...], pair, extra.astype(BF), w_out[...], w_gate[...], w_up[...], w_down[...],
    ):
        shard[:, start : start + part.shape[1]] = part
        start += part.shape[1]
    own = pltpu.make_async_copy(shard, weights.at[x, y, core], own_sem)
    own.start()
    spread = Spread(groups, x, y, core, shard, weights, send_sems, recv_sems)
    pl.semaphore_wait(barrier, devices - 1 + mp - 1)
    spread.one(0)
    own.wait()
    spread.step(1)
    spread.two(0)
    spread.step(2)
    spread.three(0)
    spread.four(0)
    spread.step(3)
    spread.five(0)
    upto = 4

    gains = held["gains"]
    columns = weights[:, :, :, :, mix + LANES : mix + 2 * LANES].reshape(model, LANES).astype(F32)
    gains[...] = columns.T[: gains.shape[0], :]
    keep("gains")

    def key_places(e, carry):
        for level, lanes_at in ((1, (3, 4)), (2, (5,))):
            tile = weights[e // 8, lax.rem(e // 2, 4), lax.rem(e, 2), :, mix + LANES : mix + 2 * LANES].astype(F32)
            value = jnp.concatenate(
                [jnp.broadcast_to(tile[:, at : at + 1], (depth, LANES)) for at in lanes_at], axis=0
            )[: counts[level], :]
            held[f"keys_{level}"][e] = jnp.where(
                value < rows, value + (e * rows).astype(F32), FAR
            )
        return carry

    lax.fori_loop(0, devices, key_places, 0)

    def kv_copy(level, e, source_index):
        packed = held[f"packed_{level}"]
        return pltpu.make_async_remote_copy(
            src_ref=packed.at[me], dst_ref=packed.at[me],
            send_sem=kv_send.at[level, e], recv_sem=kv_recv.at[level, source_index],
            device_id={"dp": e}, device_id_type=MESH,
        )

    def project(level, now):
        n = counts[level]
        name = lambda base: held[f"{base}_{level}"]
        name("rows")[...] = now
        unit, unused = unit_of(now.astype(F32))
        normed = (unit * gains[0:1, :]).astype(BF)
        name("normed")[...] = normed
        cosine, sine = (cosine_in[...], sine_in[...]) if level == 0 else (name("cosine")[...], name("sine")[...])
        here = left[:n]
        tiles = [None] * (heads // 2 + 1)
        for t in range(heads // 2, -1, -2):
            low = max(t - 1, 0)
            both = dot_nn(normed, weights[:, :, :, :, low * LANES : (t + 1) * LANES].reshape(model, (t + 1 - low) * LANES))
            for j in range(low, t + 1):
                part = tile_of(both, j - low)
                if j == heads // 2:
                    part = part * jnp.where(here, cosine, 1.0) + swap_halves(part) * jnp.where(here, sine, 0.0)
                    name("packed")[me] = part.astype(BF)

                    def send(e, carry):
                        kv_copy(level, e, me).start()
                        return carry

                    lax.fori_loop(me + 1, devices, send, 0)
                else:
                    tiles[j] = part * cosine + swap_halves(part) * sine

        def clear(e, carry):
            name("packed")[e] = jnp.zeros((n, 2 * HD), BF)
            return carry

        lax.fori_loop(me + 1, devices, clear, 0)
        for t in range(heads // 2):
            scaled = tiles[t].astype(BF).astype(F32) * HD**-0.5
            name("query")[2 * t * n : (2 * t + 1) * n, :] = jnp.where(here, scaled, 0.0).astype(BF)
            name("query")[(2 * t + 1) * n : (2 * t + 2) * n, :] = jnp.where(
                here, pltpu.roll(scaled, HD, 1), 0.0
            ).astype(BF)
        width = heads * n
        query_t[:, :width] = name("query")[...].T
        top[:, :width] = jnp.full((1, width), NEG, F32)
        total[:, :width] = jnp.zeros((1, width), F32)
        acc[:, :width] = jnp.zeros((2 * HD, width), F32)
        for base in ("rows", "normed", "query"):
            keep(f"{base}_{level}")

    def group_of(level):
        return 512 // counts[level] if 512 % counts[level] == 0 else 4

    def block(level, b):
        n, group = counts[level], group_of(level)
        width = heads * n
        for g in range(group):
            e = b * group + g

            @pl.when(e < me)
            def _(e=e):
                kv_copy(level, me, e).wait_recv()

        part = held[f"packed_{level}"][pl.ds(b * group, group)].reshape(group * n, 2 * HD)
        scores = dot_nn(part, query_t[:, :width])
        if level:
            place = held[f"keys_{level}"][pl.ds(b * group, group)].reshape(group * n, LANES)
        else:
            place = (lax.broadcasted_iota(jnp.int32, (group * n, LANES), 0) + b * (group * n)).astype(F32)
        place = jnp.concatenate([place] * (width // LANES), axis=1)
        scores = jnp.where(place <= held[f"place_{level}"][...], scores, NEG)
        before = top[:, :width]
        peak = jnp.maximum(before, jnp.max(scores, axis=0, keepdims=True))
        soft = jnp.exp(scores - peak)
        fade = jnp.exp(before - peak)
        total[:, :width] = total[:, :width] * fade + jnp.sum(soft, axis=0, keepdims=True)
        acc[:, :width] = acc[:, :width] * fade + dot_tn(part, soft.astype(BF))
        top[:, :width] = peak

    def mix_heads(level):
        n = counts[level]
        width = heads * n
        mixed_t = acc[:, :width] / total[:, :width]
        held[f"mixed_t_{level}"][...] = mixed_t
        held[f"log_{level}"][...] = top[:, :width] + jnp.log(total[:, :width])
        mixed = mixed_t.T
        for t in range(heads // 2):
            even = mixed[2 * t * n : (2 * t + 1) * n, :]
            odd = mixed[(2 * t + 1) * n : (2 * t + 2) * n, :]
            held[f"mixed_{level}"][:, t * LANES : (t + 1) * LANES] = jnp.where(
                left[:n], pltpu.roll(even, HD, 1), odd
            ).astype(BF)
        for base in ("mixed_t", "log", "mixed", "packed"):
            keep(f"{base}_{level}")

    sums = [Sum(mp, mp_me, *sum_refs[4 * i : 4 * i + 4]) for i in range(2 * len(counts))]
    chunk = model // mp
    base_o = mix + 2 * LANES
    base_gu = base_o + mix
    base_d = base_gu + 2 * hidden

    def rows_of(start, wide, low, high):
        return weights[start // chunk, pl.ds(lax.rem(start, chunk) // LANES, wide // LANES), :, :, low:high].reshape(
            wide, high - low
        )

    def feed(level, beside):
        name = lambda base: held[f"{base}_{level}"]
        mixed_now = name("mixed")[...]
        first, last = sums[2 * level], sums[2 * level + 1]
        first.start(lambda start, wide: dot_nt(mixed_now, rows_of(start, wide, base_o, base_gu)))
        beside(1)
        first.middle()
        beside(1)
        attn = first.finish()
        name("attn")[...] = attn
        level_rows = name("rows")[...].astype(F32)
        unit, unused = unit_of(level_rows + attn.astype(F32))
        second = (unit * gains[1:2, :]).astype(BF)
        name("second")[...] = second
        beside(100)
        parts = name("parts")
        for t in range(2 * hidden // 256):
            low = base_gu + t * 256
            parts[:, t * 256 : (t + 1) * 256] = dot_nn(
                second, weights[:, :, :, :, low : low + 256].reshape(model, 256)
            )
        n = counts[level]
        for t in range(hidden // LANES):
            cut = slice(t * LANES, (t + 1) * LANES)
            gate_part = parts[:, cut]
            up_part = parts[:, hidden + t * LANES : hidden + (t + 1) * LANES]
            hidden_v[:n, cut] = (gate_part * sigmoid(gate_part) * up_part).astype(BF)
        hidden_now = hidden_v[:n, :]
        last.start(lambda start, wide: dot_nt(hidden_now, rows_of(start, wide, base_d, base_d + hidden)))
        for base in ("attn", "second", "parts"):
            keep(f"{base}_{level}")
        gate = sigmoid(jnp.sum(level_rows * gains[2:3, :], axis=-1, keepdims=True))
        last.middle()
        ffn = last.finish()
        name("ffn")[...] = ffn
        keep(f"ffn_{level}")
        update = (gate * (attn.astype(F32) + ffn.astype(F32))).astype(BF)
        if level:
            update = dot_tn(held[f"pick_{level}"][...], update)
        held["state"][...] = held["state"][...] + update.astype(F32)

    steps = len(groups) + 6
    done = [upto]

    def beside(count):
        for _ in range(count):
            if done[0] < steps:
                spread.step(done[0])
                done[0] += 1

    project(0, tokens[...])
    held["state"][...] = tokens[...].astype(F32)
    for name in ("place_0", "pick_1", "pick_2", "place_1", "place_2", "cosine_1", "sine_1", "cosine_2", "sine_2", "keys_1", "keys_2"):
        keep(name)
    for b in range(devices // group_of(0)):
        beside(1)

        @pl.when(b * group_of(0) <= me)
        def _(b=b):
            block(0, b)

    mix_heads(0)
    feed(0, beside)
    keep("weights")
    for level in range(1, len(counts)):
        now = dot_nn(held[f"pick_{level}"][...], held["state"][...].astype(BF)).astype(BF)
        project(level, now)

        def one_block(b, carry, level=level):
            block(level, b)
            return carry

        lax.fori_loop(0, me // group_of(level) + 1, one_block, 0)
        mix_heads(level)
        feed(level, lambda count: None)
    keep("state")
    spread.drain()
    for item in sums:
        item.drain()
    for level in range(len(counts)):

        def sent(e, carry, level=level):
            kv_copy(level, e, me).wait_send()
            return carry

        lax.fori_loop(me + 1, devices, sent, 0)
    for copy in keeps:
        copy.wait()


def advance(tokens, depths, second_slot, third_slot, matrices, vectors, tables, heads, devices, mp, ident):
    counts = (tokens.shape[0], SECOND_SLOTS, THIRD_SLOTS)
    rows, model = tokens.shape
    depth, mix = matrices[0].shape
    hidden = matrices[4].shape[1]
    total = 2 * mix + 2 * LANES + 3 * hidden
    cuts = [0, mix + 2 * LANES]
    while cuts[-1] < total:
        cuts.append(min(cuts[-1] + 512, total))
    if cuts[-1] - cuts[-2] < 256:
        cuts.pop(-2)
    groups = [(a, b, i % 2) for i, (a, b) in enumerate(zip(cuts[:-1], cuts[1:]))]
    shapes = {
        "state": ((rows, model), F32),
        "weights": ((4, 4, 2, depth, total), BF),
        "gains": ((8, model), F32),
    }
    for level, n in enumerate(counts):
        width = heads * n
        shapes[f"place_{level}"] = ((1, width), F32)
        if level:
            shapes[f"pick_{level}"] = ((n, rows), BF)
            shapes[f"cosine_{level}"] = ((n, LANES), F32)
            shapes[f"sine_{level}"] = ((n, LANES), F32)
            shapes[f"keys_{level}"] = ((devices, n, LANES), F32)
        for base in ("rows", "normed", "attn", "ffn", "second"):
            shapes[f"{base}_{level}"] = ((n, model), BF)
        shapes[f"parts_{level}"] = ((n, 2 * hidden), F32)
        shapes[f"packed_{level}"] = ((devices, n, 2 * HD), BF)
        shapes[f"query_{level}"] = ((width, 2 * HD), BF)
        shapes[f"mixed_t_{level}"] = ((2 * HD, width), F32)
        shapes[f"log_{level}"] = ((1, width), F32)
        shapes[f"mixed_{level}"] = ((n, mix), BF)
    names = tuple(shapes)
    args = (tokens, depths, second_slot, third_slot, *matrices, *vectors, *tables)
    width = heads * rows
    outs = pl.pallas_call(
        functools.partial(advance_kernel, counts, heads, devices, mp, hidden, groups, names),
        out_shape=tuple(jax.ShapeDtypeStruct(*shapes[name]) for name in names),
        in_specs=vmem(len(args)),
        out_specs=tuple([pl.BlockSpec(memory_space=pl.ANY)] * len(names)),
        scratch_shapes=[pltpu.VMEM(*shapes[name]) for name in names]
        + [
            pltpu.VMEM((depth, total), BF),
            pltpu.SemaphoreType.DMA(()),
            pltpu.SemaphoreType.DMA((len(groups), 8)),
            pltpu.SemaphoreType.DMA((len(groups), 8)),
            pltpu.VMEM((2 * HD, width), BF),
            pltpu.VMEM((1, width), F32),
            pltpu.VMEM((1, width), F32),
            pltpu.VMEM((2 * HD, width), F32),
            pltpu.VMEM((rows, hidden), BF),
            pltpu.SemaphoreType.DMA((len(names),)),
            pltpu.SemaphoreType.DMA((len(counts), devices)),
            pltpu.SemaphoreType.DMA((len(counts), devices)),
        ]
        + [item for n in counts for _ in range(2) for item in sum_scratch(mp, n, model)],
        compiler_params=pltpu.CompilerParams(
            collective_id=ident, has_side_effects=True, vmem_limit_bytes=VMEM_LIMIT
        ),
        name="advance",
    )(*args)
    return dict(zip(names, outs))


SLOTS = 6
GROUP = 512


class Collect:
    def __init__(self, spans, groups, x, y, core, turned, rights, vectors, store, slots, core_recv, relay_recv, first_recv, last_recv, send_sems, recv_sems, turn):
        self.spans, self.groups = spans, groups
        self.x, self.y, self.core = x, y, core
        self.turned, self.rights, self.vectors, self.store, self.slots = turned, rights, vectors, store, slots
        self.core_recv, self.relay_recv, self.first_recv = core_recv, relay_recv, first_recv
        self.last_recv = last_recv
        self.send_sems, self.recv_sems = send_sems, recv_sems
        self.turn = turn
        self.waits = [{} for _ in groups]
        self.done = set()

    def remote(self, g, index, source, target, device):
        copy = pltpu.make_async_remote_copy(
            src_ref=source, dst_ref=target, send_sem=self.send_sems.at[g, index],
            recv_sem=self.recv_sems.at[g, index], device_id=device, device_id_type=MESH,
        )
        copy.start()
        return copy

    def held(self, slot, axis, at, first, count):
        if axis == 0:
            return self.slots.at[slot, at, pl.ds(first, count), self.core]
        return self.slots.at[slot, pl.ds(first, count), at, self.core]

    def zero(self, g):
        slot, waits = g % SLOTS, self.waits
        if g >= SLOTS:
            for stage in range(3):
                for copy in waits[g - SLOTS][stage]:
                    copy.wait_send()
        column = 0
        for section, low, high in self.groups[g][1]:
            wide = high - low
            if section < 4:
                if section not in self.done:
                    self.done.add(section)
                    self.turn(section)
                base = self.spans[section][0]

            def rows_of(m, carry, section=section, low=low, high=high, column=column, wide=wide):
                start = pl.multiple_of(m * 1024, 1024)
                if section < 4:
                    value = dot_nn(
                        self.turned[section % 2, pl.ds(start, 1024), :], self.rights[:, base + low : base + high]
                    )
                else:
                    value = self.vectors[:, pl.ds(start, 1024)].T
                self.slots[slot, pl.ds(m * 2, 2), :, :, :, column : column + wide] = (
                    value.astype(BF).reshape(2, 4, 2, 64, wide)
                )
                return carry

            lax.fori_loop(0, 2, rows_of, 0)
            column += wide
        waits[g][0] = [
            self.remote(
                g, 0, self.slots.at[slot, :, :, 1 - self.core, :, :column],
                self.core_recv.at[g, :, :, :, :column], peer(self.x, self.y, 1 - self.core),
            )
        ]

    def first(self, g):
        slot, (width, _, axis) = g % SLOTS, self.groups[g]
        waits, slots = self.waits, self.slots
        waits[g][0][0].wait_recv()

        def add(i, carry):
            slots[slot, i, :, self.core, :, :width] = (
                slots[slot, i, :, self.core, :, :width] + self.core_recv[g, i, :, :, :width]
            )
            return carry

        lax.fori_loop(0, 4, add, 0)
        at = self.x if axis == 0 else self.y
        waits[g][1] = [
            self.remote(
                g, 1 + i, self.held(slot, axis, lax.rem(at + 2, 4), 2 * i, 2).at[:, :, :width],
                self.relay_recv.at[g, i, :, :, :width], shifted(self.x, self.y, self.core, axis, k),
            )
            for i, k in enumerate((1, 3))
        ]

    def second(self, g):
        slot, (width, _, axis) = g % SLOTS, self.groups[g]
        waits, slots = self.waits, self.slots
        at = self.x if axis == 0 else self.y
        waits[g][2] = []
        for i, k in enumerate((1, 3)):
            waits[g][1][i].wait_recv()
            there = lax.rem(at + k, 4)
            for j in range(2):
                b = 2 * i + j
                where = (slot, there, b, self.core) if axis == 0 else (slot, b, there, self.core)
                where = where + (slice(None), slice(0, width))
                slots[where] = slots[where] + self.relay_recv[g, i, j, :, :width]
            waits[g][2].append(
                self.remote(
                    g, 3 + i, self.held(slot, axis, there, 0, 4).at[:, :, :width],
                    self.first_recv.at[g, i, :, :, :width], shifted(self.x, self.y, self.core, axis, k),
                )
            )

    def third(self, g):
        slot, (width, _, axis) = g % SLOTS, self.groups[g]
        waits, slots = self.waits, self.slots
        at, other = (self.x, self.y) if axis == 0 else (self.y, self.x)
        for copy in waits[g][2]:
            copy.wait_recv()
        for b in range(4):
            where = (slot, at, b, self.core) if axis == 0 else (slot, b, at, self.core)
            self.core_recv[g, 0, b, :, :width] = (
                slots[where + (slice(None), slice(0, width))].astype(F32)
                + self.first_recv[g, 0, b, :, :width].astype(F32)
                + self.first_recv[g, 1, b, :, :width].astype(F32)
            ).astype(BF)
        waits[g][3] = [
            self.remote(
                g, 4 + k, self.core_recv.at[g, 0, lax.rem(other + k, 4), :, :width],
                self.last_recv.at[g, k - 1, :, :width],
                shifted(self.x, self.y, self.core, 1 - axis, k),
            )
            for k in (2, 1, 3)
        ]

    def fourth(self, g):
        width, pieces, axis = self.groups[g]
        other = self.y if axis == 0 else self.x
        value = self.core_recv[g, 0, other, :, :width].astype(F32)
        for copy in self.waits[g][3]:
            copy.wait_recv()
        for k in range(3):
            value = value + self.last_recv[g, k, :, :width].astype(F32)
        column = 0
        for section, low, high in pieces:
            self.store(section, low, value[:, column : column + high - low])
            column += high - low

    def step(self, i):
        for back, work in ((0, self.zero), (1, self.first), (3, self.second), (5, self.third), (6, self.fourth)):
            if 0 <= i - back < len(self.groups):
                work(i - back)

    def drain(self):
        count = len(self.groups)
        for g in range(count):
            for stage in range(4):
                if stage == 3 or g >= count - SLOTS:
                    for copy in self.waits[g][stage]:
                        copy.wait_send()


def finish_kernel(n, heads, devices, mp, group, levels, spans, groups, *refs):
    refs = list(refs)
    flow, gains, query_place, query, packed, mixed_t, log_total, grad_mixed, cosine, sine = [refs.pop(0) for _ in range(10)]
    rows_in, middle, logit, vecs = [refs.pop(0) for _ in range(4)]
    w_hbm = refs.pop(0)
    sources = [[refs.pop(0) for _ in range(8 if level else 7)] for level in range(len(levels))]
    flow_out, q_out, k_out, v_out, out_out, gate_out, up_out, down_out, vec_out = [refs.pop(0) for _ in range(9)]
    query_t, grad_rows, grad_t, acc, delta, send_buf, recv_buf, kv_send, kv_recv = [refs.pop(0) for _ in range(9)]
    w_qkv, w_sem, send_a, recv_a, full_a, sems_a = [refs.pop(0) for _ in range(6)]
    (lefts, turned, rights, vectors, slots, core_recv, relay_recv, first_recv, last_recv,
     loads, send_sems, recv_sems) = refs
    me, mp_me = lax.axis_index("dp"), lax.axis_index("mp")
    x, y, core = plane(me)
    load_w = pltpu.make_async_copy(w_hbm.at[:, : w_qkv.shape[1]], w_qkv, w_sem)
    load_w.start()
    fetches = [[] for _ in range(4)]

    def fetch(s, side):
        row = 0
        for level, count in enumerate(levels):
            low, high = spans[s]
            target = (lefts.at[s % 2, row : row + count], rights.at[row : row + count, low:high])[side]
            if 2 * s + side < len(sources[level]):
                copy = pltpu.make_async_copy(
                    sources[level][2 * s + side], target, loads.at[level, 2 * s + side]
                )
                copy.start()
                fetches[s].append(copy)
            row += count

    for s in range(4):
        if s < 2:
            fetch(s, 0)
        fetch(s, 1)

    barrier = pltpu.get_barrier_semaphore()

    def greet(k, carry):
        pl.semaphore_signal(
            barrier, inc=1, device_id={"dp": lax.rem(me + k, devices)}, device_id_type=MESH
        )
        return carry

    lax.fori_loop(1, devices, greet, 0)
    for k in range(1, mp):
        pl.semaphore_signal(
            barrier, inc=1, device_id={"mp": lax.rem(mp_me + k, mp)}, device_id_type=MESH
        )

    def turn(section):
        for copy in fetches[section]:
            copy.wait()
        turned[section % 2] = lefts[section % 2].T
        if section < 2:
            fetch(section + 2, 0)

    hidden = gate_out.shape[1]
    mix = q_out.shape[1]

    def store(section, low, value):
        high = low + value.shape[1]
        if section == 0:
            middle_cut = min(max(hidden - low, 0), high - low)
            if middle_cut:
                gate_out[:, low : low + middle_cut] = value[:, :middle_cut]
            if low + middle_cut < high:
                up_out[:, low + middle_cut - hidden : high - hidden] = value[:, middle_cut:]
        elif section == 1:
            down_out[:, low:high] = value
        elif section == 2:
            out_out[:, low:high] = value
        elif section == 3:
            if low < mix:
                q_out[:, low : min(high, mix)] = value[:, : min(high, mix) - low]
            if high > mix:
                k_out[...] = value[:, mix - low : mix - low + HD]
                v_out[...] = value[:, mix - low + HD :]
        else:
            vec_out[...] = value

    work = Collect(
        spans, groups, x, y, core, turned, rights, vectors, store, slots, core_recv, relay_recv,
        first_recv, last_recv, send_sems, recv_sems, turn,
    )
    left = lanes_of((n, LANES)) < HD
    for t in range(heads // 2):
        part = grad_mixed[:, t * LANES : (t + 1) * LANES].astype(F32)
        grad_rows[2 * t * n : (2 * t + 1) * n, :] = jnp.where(
            left, 0.0, pltpu.roll(part, HD, 1)
        ).astype(BF)
        grad_rows[(2 * t + 1) * n : (2 * t + 2) * n, :] = jnp.where(left, 0.0, part).astype(BF)
    query_t[...] = query[...].T
    grad_t[...] = grad_rows[...].T
    delta[...] = jnp.sum(grad_t[...].astype(F32) * mixed_t[...], axis=0, keepdims=True)
    acc[...] = jnp.zeros(acc.shape, F32)
    width = heads * n
    pl.semaphore_wait(barrier, devices - 1 + mp - 1)

    def send_copy(e, source_index):
        return pltpu.make_async_remote_copy(
            src_ref=send_buf.at[e], dst_ref=recv_buf.at[source_index],
            send_sem=kv_send.at[e], recv_sem=kv_recv.at[source_index],
            device_id={"dp": e}, device_id_type=MESH,
        )

    def one_block(b):
        part = packed[b * group : (b + 1) * group].reshape(group * n, 2 * HD)
        scores = dot_nn(part, query_t[...])
        place = (lax.broadcasted_iota(jnp.int32, (group * n, LANES), 0) + b * (group * n)).astype(F32)
        place = jnp.concatenate([place] * (width // LANES), axis=1)
        scores = jnp.where(place <= query_place[...], scores, NEG)
        weights = jnp.exp(scores - log_total[...])
        grad_weights = dot_nn(part, grad_t[...])
        grad_scores = (weights * (grad_weights - delta[...])).astype(BF)
        grad_part = dot_nn(grad_scores, query[...]) + dot_nn(weights.astype(BF), grad_rows[...])
        send_buf[b * group : (b + 1) * group] = grad_part.astype(BF).reshape(group, n, 2 * HD)
        acc[...] += dot_tn(part, grad_scores)
        for e in range(b * group, (b + 1) * group):

            @pl.when(e < me)
            def _(e=e):
                send_copy(e, me).start()

    blocks = devices // group
    for b in range(blocks):
        work.step(b)

        @pl.when(b * group <= me)
        def _(b=b):
            one_block(b)

    grad_query = acc[...].T * HD**-0.5
    outs = []
    for t in range(heads // 2):
        even = grad_query[2 * t * n : (2 * t + 1) * n, :]
        odd = grad_query[(2 * t + 1) * n : (2 * t + 2) * n, :]
        outs.append(jnp.where(left, even, pltpu.roll(odd, HD, 1)))

    def add(e, carry):
        send_copy(me, e).wait_recv()
        return carry + recv_buf[e].astype(F32)

    outs.append(lax.fori_loop(me + 1, devices, add, send_buf[me].astype(F32)))
    low = spans[3][0]
    for t, part in enumerate(outs):
        rights[0:n, low + t * LANES : low + (t + 1) * LANES] = turn_back(
            part, cosine[...], sine[...], t == heads // 2
        )
    load_w.wait()
    grad_now = rights[0:n, low : spans[3][1]]

    def first_piece(start, wide):
        return dot_nt(grad_now, w_qkv[pl.ds(start, wide), :])

    total = Sum(mp, mp_me, send_a, recv_a, full_a, sems_a)
    total.start(first_piece)
    work.step(blocks)
    total.middle()
    work.step(blocks + 1)
    grad_normed = total.finish().astype(F32)
    level = rows_in[...].astype(F32)
    unit, factor = unit_of(level)
    vectors[...] = jnp.zeros(vectors.shape, F32)
    vectors[0:1, :] = jnp.sum(grad_normed * unit, axis=0, keepdims=True) + vecs[3:4, :] + vecs[4:5, :]
    vectors[1:2, :] = vecs[0:1, :] + vecs[1:2, :] + vecs[2:3, :]
    vectors[2:3, :] = jnp.sum(level * logit[...], axis=0, keepdims=True) + vecs[5:6, :] + vecs[6:7, :]
    flow_out[...] = flow[...] + (
        unit_back(grad_normed * gains[0:1, :], unit, factor) + middle[...] + logit[...] * gains[2:3, :]
    ).astype(BF).astype(F32)
    for i in range(blocks + 2, len(groups) + 6):
        work.step(i)
    work.drain()
    total.drain()

    def sent(e, carry):
        send_copy(e, me).wait_send()
        return carry

    lax.fori_loop(0, me, sent, 0)


def finish(flow, gains, attention, tail, vecs, weights, levels, heads, devices, mp, depth, ident):
    n, model = levels[0][0].shape
    width = heads * n
    group = 512 // n
    mix = heads * HD
    widths = [levels[1][i].shape[1] for i in (1, 3, 5, 7)] + [LANES]
    spans, total = [], 0
    for wide in widths:
        spans.append((total, total + wide))
        total += wide
    pieces = []
    for section, wide in enumerate(widths):
        pieces += [(section, low, low + LANES) for low in range(0, wide, LANES)]
    groups = []
    per = GROUP // LANES
    for index in range(0, len(pieces), per):
        merged = []
        for section, low, high in pieces[index : index + per]:
            if merged and merged[-1][0] == section:
                merged[-1] = (section, merged[-1][1], high)
            else:
                merged.append((section, low, high))
        wide = sum(high - low for _, low, high in merged)
        groups.append((wide, merged, (index // per) % 2))
    counts = [level[0].shape[0] for level in levels]
    rows = sum(counts)
    hidden = widths[1]
    many = len(groups)
    whole = [flow, gains, *attention, *tail, vecs]
    args = whole + [weights] + [item for level in levels for item in level]
    return pl.pallas_call(
        functools.partial(finish_kernel, n, heads, devices, mp, group, counts, spans, groups),
        out_shape=(
            jax.ShapeDtypeStruct(flow.shape, F32),
            jax.ShapeDtypeStruct((depth, mix), F32),
            jax.ShapeDtypeStruct((depth, HD), F32),
            jax.ShapeDtypeStruct((depth, HD), F32),
            jax.ShapeDtypeStruct((depth, mix), F32),
            jax.ShapeDtypeStruct((depth, hidden), F32),
            jax.ShapeDtypeStruct((depth, hidden), F32),
            jax.ShapeDtypeStruct((depth, hidden), F32),
            jax.ShapeDtypeStruct((depth, LANES), F32),
        ),
        in_specs=vmem(len(whole)) + [pl.BlockSpec(memory_space=pl.ANY)] * (len(args) - len(whole)),
        out_specs=tuple(vmem(9)),
        scratch_shapes=[
            pltpu.VMEM((2 * HD, width), BF),
            pltpu.VMEM((width, 2 * HD), BF),
            pltpu.VMEM((2 * HD, width), BF),
            pltpu.VMEM((2 * HD, width), F32),
            pltpu.VMEM((1, width), F32),
            pltpu.VMEM((devices, n, 2 * HD), BF),
            pltpu.VMEM((devices, n, 2 * HD), BF),
            pltpu.SemaphoreType.DMA((devices,)),
            pltpu.SemaphoreType.DMA((devices,)),
            pltpu.VMEM((model, mix + 2 * HD), BF),
            pltpu.SemaphoreType.DMA(()),
            *sum_scratch(mp, n, model),
            pltpu.VMEM((2, rows, model), BF),
            pltpu.VMEM((2, model, rows), BF),
            pltpu.VMEM((rows, spans[3][1]), BF),
            pltpu.VMEM((LANES, model), F32),
            pltpu.VMEM((SLOTS, 4, 4, 2, depth, GROUP), BF),
            pltpu.VMEM((many, 4, 4, depth, GROUP), BF),
            pltpu.VMEM((many, 2, 2, depth, GROUP), BF),
            pltpu.VMEM((many, 2, 4, depth, GROUP), BF),
            pltpu.VMEM((many, 3, depth, GROUP), BF),
            pltpu.SemaphoreType.DMA((len(levels), 8)),
            pltpu.SemaphoreType.DMA((many, 8)),
            pltpu.SemaphoreType.DMA((many, 8)),
        ],
        compiler_params=pltpu.CompilerParams(
            collective_id=ident, has_side_effects=True, vmem_limit_bytes=63 * 1024 * 1024
        ),
        name="finish",
    )(*args)


def rotary_tables(place):
    freq = jnp.exp(jnp.arange(HD // 2, dtype=F32) * (-2.0 * math.log(ROPE_BASE) / HD))
    angle = place.astype(F32)[:, None] * freq[None, :]
    cosine, sine = jnp.cos(angle), jnp.sin(angle)
    return (
        jnp.concatenate([cosine] * 4, axis=1),
        jnp.concatenate([-sine, sine, -sine, sine], axis=1),
    )


def local(
    tokens, depths, second_slot, third_slot, w_query, w_key, w_value, w_out, w_gate, w_up,
    w_down, norm_first, norm_second, router, cotangent,
):
    me = lax.axis_index("dp")
    devices, mp = lax.axis_size("dp"), lax.axis_size("mp")
    rows = tokens.shape[0]
    heads = w_query.shape[1] // HD
    depth = w_query.shape[0]
    home = rotary_tables(jnp.arange(rows, dtype=jnp.int32) + me * rows)

    def row(values):
        return values.reshape(1, -1)

    kept = advance(
        tokens, row(depths), row(second_slot), row(third_slot),
        (w_query, w_key, w_value, w_out.T, w_gate, w_up, w_down.T),
        (row(norm_first), row(norm_second), row(router)), home, heads, devices, mp, 0,
    )
    weights = kept["weights"].reshape(devices * depth, -1)
    gains = kept["gains"]
    back = retreat(cotangent, kept, weights, heads, devices, mp, 1)
    terms = []
    for level in range(3):
        terms.append(
            tuple(back.get(f"{base}_{level}", kept.get(f"{base}_{level}")) for base in (
                "second", "parts_grad", "grad_ffn", "hidden", "grad_attn", "mixed", "normed", "grad_qkv"
            )[: 8 if level else 7])
        )
    attention = [kept[f"{base}_0"] for base in ("place", "query", "packed", "mixed_t", "log")]
    flow, query_grad, key_grad, value_grad, out_grad, gate_grad, up_grad, down_grad, vec = finish(
        back["flow_out"], gains, (*attention, back["grad_mixed_0"], *home),
        (kept["rows_0"], back["middle_0"], back["logit_0"]), back["vecs"], weights, terms,
        heads, devices, mp, depth, 2,
    )
    return (
        kept["state"], flow, query_grad, key_grad, value_grad, out_grad.T, gate_grad, up_grad, down_grad.T,
        vec[:, 0], vec[:, 1], vec[:, 2],
    )


def solution(mesh):
    in_specs = (
        P("dp", None), P("dp"), P("dp"), P("dp"), P("dp", "mp"), P("dp", "mp"), P("dp", "mp"),
        P("mp", "dp"), P("dp", "mp"), P("dp", "mp"), P("mp", "dp"), P("dp"), P("dp"), P("dp"),
        P("dp", None),
    )
    out_specs = (
        P("dp", None), P("dp", None), P("dp", "mp"), P("dp", "mp"), P("dp", "mp"), P("mp", "dp"),
        P("dp", "mp"), P("dp", "mp"), P("mp", "dp"), P("dp"), P("dp"), P("dp"),
    )
    return jax.shard_map(local, mesh=mesh, in_specs=in_specs, out_specs=out_specs, check_vma=False)
```

```python
import functools
import math

import jax
import jax.numpy as jnp
from jax import lax
from jax.experimental import pallas as pl
from jax.experimental.pallas import tpu as pltpu
from jax.sharding import PartitionSpec as P

HD = 64
SECOND_SLOTS = 96
THIRD_SLOTS = 64
EPS = 1e-05
NEG = -1e30
ROPE_BASE = 10000.0
FAR = 1e9
BF = jnp.bfloat16
F32 = jnp.float32
MESH = pl.DeviceIdType.MESH

(K_ROWS, K_NORMED, K_ATTN, K_FFN, K_SECOND, K_PARTS, K_PACKED, K_QUERY, K_MIXED_T, K_LOG, K_MIXED, K_PLACE, K_PICK, K_COSINE, K_SINE, K_KEYS, K_STATE, K_WEIGHTS, K_GAINS, K_FLOW, K_FLOW_OUT, K_VECS, K_GRAD_QKV, K_GRAD_FFN, K_HIDDEN, K_PARTS_GRAD, K_GRAD_ATTN, K_GRAD_MIXED, K_MIDDLE, K_LOGIT, K_HEAD, K_TAIL, K_D, K_GU, K_O, K_QKV) = range(36)

LANES = 128
VMEM_LIMIT = 63 * 1024 * 1024


def dot_nn(left, right):
    return lax.dot_general(left, right, (((1,), (0,)), ((), ())), preferred_element_type=F32)


def dot_nt(left, right):
    return lax.dot_general(left, right, (((1,), (1,)), ((), ())), preferred_element_type=F32)


def dot_tn(left, right):
    return lax.dot_general(left, right, (((0,), (0,)), ((), ())), preferred_element_type=F32)


def unit_of(values):
    factor = lax.rsqrt(jnp.mean(values * values, axis=-1, keepdims=True) + EPS)
    return values * factor, factor


def unit_back(shaped, unit, factor):
    return factor * (shaped - unit * jnp.mean(shaped * unit, axis=-1, keepdims=True))


def sigmoid(values):
    return 1.0 / (1.0 + jnp.exp(-values))


def lanes_of(shape):
    return lax.broadcasted_iota(jnp.int32, shape, 1)


def swap_halves(tile):
    first = lax.rem(lanes_of(tile.shape), HD) < HD // 2
    return jnp.where(first, pltpu.roll(tile, LANES - HD // 2, 1), pltpu.roll(tile, HD // 2, 1))


def turn_back(part, cosine, sine, packed):
    if packed:
        left = lanes_of(part.shape) < HD
        cosine, sine = jnp.where(left, cosine, 1.0), jnp.where(left, sine, 0.0)
    return (part * cosine - swap_halves(part) * sine).astype(BF)


def tile_of(values, index):
    return values[:, index * LANES : (index + 1) * LANES]


def signal_all(group, me, axis):
    barrier = pltpu.get_barrier_semaphore()
    for k in range(1, group):
        pl.semaphore_signal(
            barrier, inc=1, device_id={axis: lax.rem(me + k, group)}, device_id_type=MESH
        )
    pl.semaphore_wait(barrier, group - 1)


PIECES = 2


class Sum:
    order = (2, 1, 3)

    def __init__(self, group, me, send, recv, full, sems):
        self.group, self.me, self.send, self.recv, self.full, self.sems = group, me, send, recv, full, sems
        self.wide = send.shape[-1]

    def remote(self, source, target, stage, k, piece):
        copy = pltpu.make_async_remote_copy(
            src_ref=source, dst_ref=target, send_sem=self.sems.at[stage, k - 1, piece],
            recv_sem=self.sems.at[stage + 1, k - 1, piece],
            device_id={"mp": lax.rem(self.me + k, self.group)}, device_id_type=MESH,
        )
        copy.start()
        return copy

    def start(self, make_piece):
        self.make, self.out, self.back = make_piece, [], []
        for piece in range(PIECES):
            copies = []
            for k in self.order:
                at = (k - 1, piece)
                self.send[at] = self.part(lax.rem(self.me + k, self.group), piece).astype(BF)
                copies.append(self.remote(self.send.at[at], self.recv.at[at], 0, k, piece))
            self.out.append(copies)

    def part(self, c, piece):
        start = c * (PIECES * self.wide) + piece * self.wide
        return self.make(pl.multiple_of(start, self.wide), self.wide)

    def middle(self):
        for piece in range(PIECES):
            total = self.part(self.me, piece).astype(BF).astype(F32)
            for k, copy in zip(self.order, self.out[piece]):
                copy.wait_recv()
                total = total + self.recv[k - 1, piece].astype(F32)
            self.full[self.me, piece] = total.astype(BF)
            where = self.full.at[self.me, piece]
            self.back.append([self.remote(where, where, 2, k, piece) for k in self.order])

    def finish(self):
        for copies in self.back:
            for copy in copies:
                copy.wait_recv()
        return jnp.concatenate(
            [self.full[c, piece] for c in range(self.group) for piece in range(PIECES)], axis=1
        )

    def drain(self):
        for copies in self.out + self.back:
            for copy in copies:
                copy.wait_send()


def vmem(count):
    return [pl.BlockSpec(memory_space=pltpu.VMEM)] * count


def sum_scratch(mp, n, model):
    wide = model // mp // PIECES
    return [
        pltpu.VMEM((mp - 1, PIECES, n, wide), BF),
        pltpu.VMEM((mp - 1, PIECES, n, wide), BF),
        pltpu.VMEM((mp, PIECES, n, wide), BF),
        pltpu.SemaphoreType.DMA((4, mp - 1, PIECES)),
    ]


def retreat_kernel(counts, heads, devices, mp, hidden, ins, names, inner, *refs):
    refs = list(refs)
    sources = {name: refs.pop(0) for name in ins}
    w_hbm = refs.pop(0)
    outs = {name: refs.pop(0) for name in names}
    held = {name: refs.pop(0) for name in ins}
    held.update({name: refs.pop(0) for name in names + inner})
    w_qkv, w_o, w_gu, w_d, fetch_sems, w_sems, keep_sems = [refs.pop(0) for _ in range(7)]
    query_t, grad_rows, grad_t, acc, delta = [refs.pop(0) for _ in range(5)]
    buffers = {level: [refs.pop(0) for _ in range(4)] for level in (1, 2)}
    sum_refs = {key: [refs.pop(0) for _ in range(4)] for key in ((K_HEAD, 2), (K_TAIL, 2), (K_HEAD, 1), (K_TAIL, 1))}
    me, mp_me = lax.axis_index("dp"), lax.axis_index("mp")
    model = w_o.shape[0]
    mix = heads * HD
    loads, keeps = {}, []

    def fetch(name):
        loads[name] = pltpu.make_async_copy(sources[name], held[name], fetch_sems.at[ins.index(name)])
        loads[name].start()

    def load(name, ref, start, index):
        loads[name] = pltpu.make_async_copy(w_hbm.at[:, start : start + ref.shape[1]], ref, w_sems.at[index])
        loads[name].start()

    def get(name):
        if name in loads:
            loads.pop(name).wait()
        return held[name]

    def need(name):
        if name in loads:
            loads.pop(name).wait()

    def keep(name):
        copy = pltpu.make_async_copy(held[name], outs[name], keep_sems.at[len(keeps)])
        copy.start()
        keeps.append(copy)

    base_o = mix + 2 * LANES
    for name in (K_FLOW, K_GAINS, (K_PICK, 2), (K_ROWS, 2), (K_ATTN, 2), (K_FFN, 2), (K_PARTS, 2)):
        fetch(name)
    load(K_D, w_d, base_o + mix + 2 * hidden, 0)
    load(K_GU, w_gu, base_o + mix, 1)
    load(K_O, w_o, base_o, 2)
    load(K_QKV, w_qkv, 0, 3)
    for name in ins:
        if name not in loads:
            fetch(name)

    barrier = pltpu.get_barrier_semaphore()

    def greet(k, carry):
        pl.semaphore_signal(
            barrier, inc=1, device_id={"dp": lax.rem(me + k, devices)}, device_id_type=MESH
        )
        return carry

    lax.fori_loop(1, devices, greet, 0)
    for k in range(1, mp):
        pl.semaphore_signal(
            barrier, inc=1, device_id={"mp": lax.rem(mp_me + k, mp)}, device_id_type=MESH
        )
    sums = {key: Sum(mp, mp_me, *items) for key, items in sum_refs.items()}
    vecs = held[K_VECS]
    vecs[...] = jnp.zeros(vecs.shape, F32)
    gate_of = {}

    def head(level):
        n = counts[level]
        name = lambda base: held[(base, level)]
        grad_update = get(K_FLOW)[...].astype(BF)
        if level:
            grad_update = dot_nn(get((K_PICK, level))[...], grad_update)
        grad_update = grad_update.astype(F32)
        rows_now = get((K_ROWS, level))[...].astype(F32)
        attn_now = get((K_ATTN, level))[...].astype(F32)
        gains = get(K_GAINS)
        gate = sigmoid(jnp.sum(rows_now * gains[2:3, :], axis=-1, keepdims=True))
        logit = jnp.sum(
            grad_update * (attn_now + get((K_FFN, level))[...].astype(F32)), axis=-1, keepdims=True
        )
        name(K_LOGIT)[...] = logit * gate * (1.0 - gate)
        grad_ffn = (gate * grad_update).astype(BF)
        name(K_GRAD_FFN)[...] = grad_ffn
        parts, parts_grad, hidden_out = get((K_PARTS, level)), name(K_PARTS_GRAD), name(K_HIDDEN)
        need(K_D)
        for t in range(hidden // LANES):
            cut = slice(t * LANES, (t + 1) * LANES)
            up_cut = slice(hidden + t * LANES, hidden + (t + 1) * LANES)
            if t % 2 == 0:
                both = dot_nn(grad_ffn, w_d[:, t * LANES : min((t + 2) * LANES, hidden)])
            grad_hidden = tile_of(both, t % 2)
            gate_part = parts[:, cut]
            up_part = parts[:, up_cut]
            sigma = sigmoid(gate_part)
            active = gate_part * sigma
            hidden_out[:, cut] = (active * up_part).astype(BF)
            parts_grad[:, cut] = (
                grad_hidden * up_part * sigma * (1.0 + gate_part * (1.0 - sigma))
            ).astype(BF)
            parts_grad[:, up_cut] = (grad_hidden * active).astype(BF)
        for base in (K_GRAD_FFN, K_HIDDEN, K_PARTS_GRAD, K_LOGIT):
            keep((base, level))
        return grad_update, rows_now, attn_now, gate

    def head_end(level, grad_update, rows_now, attn_now, gate):
        name = lambda base: held[(base, level)]
        gains = held[K_GAINS]
        need(K_GU)
        if level == 2:
            pl.semaphore_wait(barrier, devices - 1 + mp - 1)
        parts_now = name(K_PARTS_GRAD)[...]
        total = sums[(K_HEAD, level)]
        total.start(lambda start, wide: dot_nt(parts_now, w_gu[pl.ds(start, wide), :]))
        unit, factor = unit_of(rows_now + attn_now)
        total.middle()
        grad_second = total.finish().astype(F32)
        vecs[2 - level : 3 - level, :] = jnp.sum(grad_second * unit, axis=0, keepdims=True)
        grad_middle = unit_back(grad_second * gains[1:2, :], unit, factor)
        name(K_MIDDLE)[...] = grad_middle
        grad_attn = (gate * grad_update + grad_middle).astype(BF)
        name(K_GRAD_ATTN)[...] = grad_attn
        need(K_O)
        name(K_GRAD_MIXED)[...] = dot_nn(grad_attn, w_o[...]).astype(BF)
        keep((K_GRAD_ATTN, level))

    def attention(level):
        n = counts[level]
        group = 8
        width = heads * n
        send_buf, recv_buf, send_sems, recv_sems = buffers[level]
        query, packed = get((K_QUERY, level)), get((K_PACKED, level))
        mixed_t, log_total = get((K_MIXED_T, level)), get((K_LOG, level))
        keys, query_place = get((K_KEYS, level)), get((K_PLACE, level))
        cosine, sine = get((K_COSINE, level)), get((K_SINE, level))
        grad_mixed, grad_qkv = held[(K_GRAD_MIXED, level)], held[(K_GRAD_QKV, level)]
        left = lanes_of((n, LANES)) < HD
        for t in range(heads // 2):
            part = grad_mixed[:, t * LANES : (t + 1) * LANES].astype(F32)
            grad_rows[2 * t * n : (2 * t + 1) * n, :] = jnp.where(
                left, 0.0, pltpu.roll(part, HD, 1)
            ).astype(BF)
            grad_rows[(2 * t + 1) * n : (2 * t + 2) * n, :] = jnp.where(left, 0.0, part).astype(BF)
        query_t[:, :width] = query[...].T
        grad_t[:, :width] = grad_rows[:width, :].T
        delta[:, :width] = jnp.sum(grad_t[:, :width].astype(F32) * mixed_t[...], axis=0, keepdims=True)
        acc[:, :width] = jnp.zeros((2 * HD, width), F32)

        def send_copy(e, source_index):
            return pltpu.make_async_remote_copy(
                src_ref=send_buf.at[e], dst_ref=recv_buf.at[source_index],
                send_sem=send_sems.at[e], recv_sem=recv_sems.at[source_index],
                device_id={"dp": e}, device_id_type=MESH,
            )

        def one_block(b, carry):
            part = packed[pl.ds(b * group, group)].reshape(group * n, 2 * HD)
            scores = dot_nn(part, query_t[:, :width])
            place = keys[pl.ds(b * group, group)].reshape(group * n, LANES)
            place = jnp.concatenate([place] * (width // LANES), axis=1)
            scores = jnp.where(place <= query_place[...], scores, NEG)
            soft = jnp.exp(scores - log_total[...])
            grad_soft = dot_nn(part, grad_t[:, :width])
            grad_scores = (soft * (grad_soft - delta[:, :width])).astype(BF)
            grad_part = dot_nn(grad_scores, query[...]) + dot_nn(soft.astype(BF), grad_rows[:width, :])
            send_buf[pl.ds(b * group, group)] = grad_part.astype(BF).reshape(group, n, 2 * HD)
            acc[:, :width] += dot_tn(part, grad_scores)
            for g in range(group):
                e = b * group + g

                @pl.when(e < me)
                def _(e=e):
                    send_copy(e, me).start()

            return carry

        lax.fori_loop(0, me // group + 1, one_block, 0)
        grad_query = acc[:, :width].T * HD**-0.5
        for t in range(heads // 2):
            even = grad_query[2 * t * n : (2 * t + 1) * n, :]
            odd = grad_query[(2 * t + 1) * n : (2 * t + 2) * n, :]
            part = jnp.where(left, even, pltpu.roll(odd, HD, 1))
            grad_qkv[:, t * LANES : (t + 1) * LANES] = turn_back(part, cosine[...], sine[...], False)

        def add(e, carry):
            send_copy(me, e).wait_recv()
            return carry + recv_buf[e].astype(F32)

        part = lax.fori_loop(me + 1, devices, add, send_buf[me].astype(F32))
        grad_qkv[:, mix:] = turn_back(part, cosine[...], sine[...], True)

        def drain():
            def sent(e, carry):
                send_copy(e, me).wait_send()
                return carry

            lax.fori_loop(0, me, sent, 0)

        return drain

    def tail(level):
        gains, flow = held[K_GAINS], held[K_FLOW]
        grad_now = held[(K_GRAD_QKV, level)][...]
        need(K_QKV)
        total = sums[(K_TAIL, level)]
        total.start(lambda start, wide: dot_nt(grad_now, w_qkv[pl.ds(start, wide), :]))
        keep((K_GRAD_QKV, level))
        rows_now = held[(K_ROWS, level)][...].astype(F32)
        unit, factor = unit_of(rows_now)
        logit = held[(K_LOGIT, level)][...]
        vecs[7 - level : 8 - level, :] = jnp.sum(rows_now * logit, axis=0, keepdims=True)
        total.middle()
        grad_normed = total.finish().astype(F32)
        vecs[5 - level : 6 - level, :] = jnp.sum(grad_normed * unit, axis=0, keepdims=True)
        grad_rows_now = (
            unit_back(grad_normed * gains[0:1, :], unit, factor)
            + held[(K_MIDDLE, level)][...]
            + logit * gains[2:3, :]
        ).astype(BF)
        flow[...] = flow[...] + dot_tn(held[(K_PICK, level)][...], grad_rows_now)

    drains = []
    for level in (2, 1):
        head_end(level, *head(level))
        drains.append(attention(level))
        tail(level)
    held[K_FLOW_OUT][...] = held[K_FLOW][...]
    keep(K_FLOW_OUT)
    head(0)
    keep(K_VECS)
    for drain in drains:
        drain()
    for item in sums.values():
        item.drain()
    for copy in keeps:
        copy.wait()


def retreat(cotangent, kept, weights, heads, devices, mp, ident):
    counts = tuple(kept[(K_ROWS, level)].shape[0] for level in range(3))
    model = cotangent.shape[1]
    mix = heads * HD
    hidden = kept[(K_PARTS, 0)].shape[1] // 2
    ins = {K_FLOW: cotangent, K_GAINS: kept[K_GAINS]}
    inner = {}
    shapes = {K_FLOW_OUT: (cotangent.shape, F32), K_VECS: ((8, model), F32)}
    for level, n in enumerate(counts):
        for base in (K_ROWS, K_ATTN, K_FFN, K_PARTS):
            ins[(base, level)] = kept[(base, level)]
        if level:
            for base in (K_PICK, K_QUERY, K_PACKED, K_MIXED_T, K_LOG, K_KEYS, K_PLACE, K_COSINE, K_SINE):
                ins[(base, level)] = kept[(base, level)]
            shapes[(K_GRAD_QKV, level)] = ((n, mix + 2 * HD), BF)
            shapes[(K_GRAD_ATTN, level)] = ((n, model), BF)
            inner[(K_GRAD_MIXED, level)] = ((n, mix), BF)
            inner[(K_MIDDLE, level)] = ((n, model), F32)
        shapes[(K_GRAD_FFN, level)] = ((n, model), BF)
        shapes[(K_HIDDEN, level)] = ((n, hidden), BF)
        shapes[(K_PARTS_GRAD, level)] = ((n, 2 * hidden), BF)
        shapes[(K_LOGIT, level)] = ((n, 1), F32)
    names = tuple(shapes)
    most = heads * max(counts[1:])
    anywhere = pl.BlockSpec(memory_space=pl.ANY)
    outs = pl.pallas_call(
        functools.partial(retreat_kernel, counts, heads, devices, mp, hidden, tuple(ins), names, tuple(inner)),
        out_shape=tuple(jax.ShapeDtypeStruct(*shapes[name]) for name in names),
        in_specs=[anywhere] * (len(ins) + 1),
        out_specs=tuple([anywhere] * len(names)),
        scratch_shapes=[pltpu.VMEM(item.shape, item.dtype) for item in ins.values()]
        + [pltpu.VMEM(*shape) for shape in (*shapes.values(), *inner.values())]
        + [
            pltpu.VMEM((model, mix + 2 * HD), BF),
            pltpu.VMEM((model, mix), BF),
            pltpu.VMEM((model, 2 * hidden), BF),
            pltpu.VMEM((model, hidden), BF),
            pltpu.SemaphoreType.DMA((len(ins),)),
            pltpu.SemaphoreType.DMA((4,)),
            pltpu.SemaphoreType.DMA((len(names),)),
            pltpu.VMEM((2 * HD, most), BF),
            pltpu.VMEM((most, 2 * HD), BF),
            pltpu.VMEM((2 * HD, most), BF),
            pltpu.VMEM((2 * HD, most), F32),
            pltpu.VMEM((1, most), F32),
        ]
        + [
            item
            for level in (1, 2)
            for item in (
                pltpu.VMEM((devices, counts[level], 2 * HD), BF),
                pltpu.VMEM((devices, counts[level], 2 * HD), BF),
                pltpu.SemaphoreType.DMA((devices,)),
                pltpu.SemaphoreType.DMA((devices,)),
            )
        ]
        + [item for level in (2, 2, 1, 1) for item in sum_scratch(mp, counts[level], model)],
        compiler_params=pltpu.CompilerParams(
            collective_id=ident, has_side_effects=True, vmem_limit_bytes=VMEM_LIMIT
        ),
        name="retreat",
    )(*ins.values(), weights)
    return dict(zip(names, outs))


def plane(me):
    return me // 8, lax.rem(me // 2, 4), lax.rem(me, 2)


def peer(x, y, core):
    return {"dp": (lax.rem(x, 4) * 4 + lax.rem(y, 4)) * 2 + core}


def shifted(x, y, core, axis, k):
    return peer(x + k, y, core) if axis == 0 else peer(x, y + k, core)


def meet(me, partners):
    barrier = pltpu.get_barrier_semaphore()
    for device in partners:
        pl.semaphore_signal(barrier, inc=1, device_id=device, device_id_type=MESH)
    pl.semaphore_wait(barrier, len(partners))


def plane_partners(x, y, core):
    return (
        [peer(x, y, 1 - core)]
        + [shifted(x, y, core, 0, k) for k in (1, 2, 3)]
        + [shifted(x, y, core, 1, k) for k in (1, 2, 3)]
    )


class Spread:
    def __init__(self, groups, x, y, core, shard, full, send_sems, recv_sems):
        self.groups, self.x, self.y, self.core = groups, x, y, core
        self.shard, self.full = shard, full
        self.send_sems, self.recv_sems = send_sems, recv_sems
        self.started = []
        self.waits = [{} for _ in groups]

    def remote(self, g, index, source, target, device):
        copy = pltpu.make_async_remote_copy(
            src_ref=source, dst_ref=target, send_sem=self.send_sems.at[g, index],
            recv_sem=self.recv_sems.at[g, index], device_id=device, device_id_type=MESH,
        )
        copy.start()
        self.started.append(copy)
        return copy

    def line(self, axis, at, first, count, cut):
        if axis == 0:
            return self.full.at[pl.ds(first, count), at, self.core, :, cut]
        return self.full.at[at, pl.ds(first, count), self.core, :, cut]

    def one(self, g):
        low, high, axis = self.groups[g]
        cut = slice(low, high)
        self.waits[g][1] = [
            self.remote(
                g, k - 1, self.shard.at[:, cut], self.full.at[self.x, self.y, self.core, :, cut],
                shifted(self.x, self.y, self.core, axis, k),
            )
            for k in (2, 1, 3)
        ]

    def two(self, g):
        low, high, axis = self.groups[g]
        for copy in self.waits[g][1]:
            copy.wait_recv()
        mine = self.line(axis, self.y if axis == 0 else self.x, 0, 4, slice(low, high))
        self.waits[g][2] = [
            self.remote(g, 3 + i, mine, mine, shifted(self.x, self.y, self.core, 1 - axis, k))
            for i, k in enumerate((1, 3))
        ]

    def three(self, g):
        low, high, axis = self.groups[g]
        at = self.y if axis == 0 else self.x
        self.waits[g][3] = []
        for i, k in enumerate((1, 3)):
            self.waits[g][2][i].wait_recv()
            piece = self.line(axis, lax.rem(at + 4 - k, 4), 2 * i, 2, slice(low, high))
            self.waits[g][3].append(
                self.remote(g, 5 + i, piece, piece, shifted(self.x, self.y, self.core, 1 - axis, k))
            )

    def four(self, g):
        low, high, axis = self.groups[g]
        for copy in self.waits[g][3]:
            copy.wait_recv()
        mine = self.full.at[:, :, self.core, :, slice(low, high)]
        self.waits[g][4] = [self.remote(g, 7, mine, mine, peer(self.x, self.y, 1 - self.core))]

    def five(self, g):
        self.waits[g][4][0].wait_recv()

    def step(self, i):
        for back, work in ((0, self.one), (2, self.two), (4, self.three), (5, self.four), (6, self.five)):
            if 1 <= i - back < len(self.groups):
                work(i - back)

    def drain(self):
        for copy in self.started:
            copy.wait_send()


def advance_kernel(counts, heads, devices, mp, hidden, groups, names, *refs):
    refs = list(refs)
    (tokens, depths, second_slot, third_slot, w_query, w_key, w_value, w_out, w_gate, w_up, w_down,
     norm_first, norm_second, router, cosine_in, sine_in) = [refs.pop(0) for _ in range(16)]
    outs = {name: refs.pop(0) for name in names}
    held = {name: refs.pop(0) for name in names}
    shard, own_sem, send_sems, recv_sems, query_t, top, total, acc, hidden_v, keep_sems, kv_send, kv_recv = [
        refs.pop(0) for _ in range(12)
    ]
    sum_refs = refs
    me, mp_me = lax.axis_index("dp"), lax.axis_index("mp")
    x, y, core = plane(me)
    weights = held[K_WEIGHTS]
    rows, model = tokens.shape
    mix = heads * HD
    lanes = lanes_of((rows, LANES))
    left = lanes < HD
    keeps = []

    def keep(name):
        copy = pltpu.make_async_copy(held[name], outs[name], keep_sems.at[len(keeps)])
        copy.start()
        keeps.append(copy)

    barrier = pltpu.get_barrier_semaphore()

    def greet(k, carry):
        pl.semaphore_signal(
            barrier, inc=1, device_id={"dp": lax.rem(me + k, devices)}, device_id_type=MESH
        )
        return carry

    lax.fori_loop(1, devices, greet, 0)
    for k in range(1, mp):
        pl.semaphore_signal(
            barrier, inc=1, device_id={"mp": lax.rem(mp_me + k, mp)}, device_id_type=MESH
        )

    token = lanes_of((1, rows)).astype(F32)
    picks, marks, query_places = [None], [None], []
    query_places.append(
        (lax.rem(lanes_of((1, heads * rows)), rows) + me * rows).astype(F32)
    )
    held[(K_PLACE, 0)][...] = query_places[0]
    for level, slot, deep in ((1, second_slot, 2), (2, third_slot, 3)):
        count = counts[level]
        slots = lax.broadcasted_iota(jnp.int32, (count, rows), 0)
        active = (depths[...] >= deep) & (slot[...] >= 0)
        chosen = jnp.where(active, slot[...], -1) == slots
        pick = jnp.where(chosen, 1.0, 0.0).astype(BF)
        held[(K_PICK, level)][...] = pick
        picks.append(pick)
        marks.append(
            jnp.min(jnp.where(chosen, token, float(rows)), axis=1, keepdims=True)
        )
        sublane = lax.broadcasted_iota(jnp.int32, (16, rows), 0)
        probe = jnp.where(sublane == 0, token, 1.0).astype(BF)
        found = dot_nt(probe, jnp.concatenate([pick] * heads, axis=0))
        place = jnp.where(found[1:2, :] > 0.5, found[0:1, :] + (me * rows).astype(F32), FAR)
        held[(K_PLACE, level)][...] = place
        query_places.append(place)
        table = jnp.concatenate([cosine_in[...], sine_in[...]], axis=1)
        turned = lax.dot_general(
            pick.astype(F32), table, (((1,), (0,)), ((), ())),
            preferred_element_type=F32, precision=lax.Precision.HIGHEST,
        )
        held[(K_COSINE, level)][...] = turned[:, :LANES]
        held[(K_SINE, level)][...] = turned[:, LANES:]
    depth = w_query.shape[0]
    wide = jnp.zeros((1, LANES - depth), F32)
    gain_rows = jnp.concatenate(
        [jnp.concatenate([ref[...].astype(F32), wide], axis=1) for ref in (norm_first, norm_second, router)]
        + [jnp.zeros((LANES - 3, LANES), F32)],
        axis=0,
    )
    extra = gain_rows.T[:depth, :]
    rest = counts[1] - depth
    lane = lanes_of((depth, LANES))
    over = jnp.concatenate([marks[1][depth:, :], jnp.full((depth - rest, 1), float(rows), F32)], axis=0)
    extra = jnp.where(lane == 3, marks[1][:depth, :], extra)
    extra = jnp.where(lane == 4, over, extra)
    extra = jnp.where(lane == 5, marks[2], extra)
    pair = jnp.concatenate([w_key[...].astype(F32), w_value[...].astype(F32)], axis=1).astype(BF)
    start = 0
    for part in (
        w_query[...], pair, extra.astype(BF), w_out[...], w_gate[...], w_up[...], w_down[...],
    ):
        shard[:, start : start + part.shape[1]] = part
        start += part.shape[1]
    own = pltpu.make_async_copy(shard, weights.at[x, y, core], own_sem)
    own.start()
    spread = Spread(groups, x, y, core, shard, weights, send_sems, recv_sems)
    pl.semaphore_wait(barrier, devices - 1 + mp - 1)
    spread.one(0)
    own.wait()
    spread.step(1)
    spread.two(0)
    spread.step(2)
    spread.three(0)
    spread.four(0)
    spread.step(3)
    spread.five(0)
    upto = 4

    gains = held[K_GAINS]
    columns = weights[:, :, :, :, mix + LANES : mix + 2 * LANES].reshape(model, LANES).astype(F32)
    gains[...] = columns.T[: gains.shape[0], :]
    keep(K_GAINS)

    def key_places(e, carry):
        for level, lanes_at in ((1, (3, 4)), (2, (5,))):
            tile = weights[e // 8, lax.rem(e // 2, 4), lax.rem(e, 2), :, mix + LANES : mix + 2 * LANES].astype(F32)
            value = jnp.concatenate(
                [jnp.broadcast_to(tile[:, at : at + 1], (depth, LANES)) for at in lanes_at], axis=0
            )[: counts[level], :]
            held[(K_KEYS, level)][e] = jnp.where(
                value < rows, value + (e * rows).astype(F32), FAR
            )
        return carry

    lax.fori_loop(0, devices, key_places, 0)

    def kv_copy(level, e, source_index):
        packed = held[(K_PACKED, level)]
        return pltpu.make_async_remote_copy(
            src_ref=packed.at[me], dst_ref=packed.at[me],
            send_sem=kv_send.at[level, e], recv_sem=kv_recv.at[level, source_index],
            device_id={"dp": e}, device_id_type=MESH,
        )

    def project(level, now):
        n = counts[level]
        name = lambda base: held[(base, level)]
        name(K_ROWS)[...] = now
        unit, unused = unit_of(now.astype(F32))
        normed = (unit * gains[0:1, :]).astype(BF)
        name(K_NORMED)[...] = normed
        cosine, sine = (cosine_in[...], sine_in[...]) if level == 0 else (name(K_COSINE)[...], name(K_SINE)[...])
        here = left[:n]
        tiles = [None] * (heads // 2 + 1)
        for t in range(heads // 2, -1, -2):
            low = max(t - 1, 0)
            both = dot_nn(normed, weights[:, :, :, :, low * LANES : (t + 1) * LANES].reshape(model, (t + 1 - low) * LANES))
            for j in range(low, t + 1):
                part = tile_of(both, j - low)
                if j == heads // 2:
                    part = part * jnp.where(here, cosine, 1.0) + swap_halves(part) * jnp.where(here, sine, 0.0)
                    name(K_PACKED)[me] = part.astype(BF)

                    def send(k, carry):
                        kv_copy(level, devices - 1 - k, me).start()
                        return carry

                    lax.fori_loop(0, devices - 1 - me, send, 0)
                else:
                    tiles[j] = part * cosine + swap_halves(part) * sine

        def clear(e, carry):
            name(K_PACKED)[e] = jnp.zeros((n, 2 * HD), BF)
            return carry

        lax.fori_loop(me + 1, devices, clear, 0)
        for t in range(heads // 2):
            scaled = tiles[t].astype(BF).astype(F32) * HD**-0.5
            name(K_QUERY)[2 * t * n : (2 * t + 1) * n, :] = jnp.where(here, scaled, 0.0).astype(BF)
            name(K_QUERY)[(2 * t + 1) * n : (2 * t + 2) * n, :] = jnp.where(
                here, pltpu.roll(scaled, HD, 1), 0.0
            ).astype(BF)
        width = heads * n
        query_t[:, :width] = name(K_QUERY)[...].T
        top[:, :width] = jnp.full((1, width), NEG, F32)
        total[:, :width] = jnp.zeros((1, width), F32)
        acc[:, :width] = jnp.zeros((2 * HD, width), F32)
        for base in (K_ROWS, K_NORMED, K_QUERY):
            keep((base, level))

    def group_of(level):
        return (4, 8, 16)[level]

    def block(level, b):
        n, group = counts[level], group_of(level)
        width = heads * n
        for g in range(group):
            e = b * group + g

            @pl.when(e < me)
            def _(e=e):
                kv_copy(level, me, e).wait_recv()

        part = held[(K_PACKED, level)][pl.ds(b * group, group)].reshape(group * n, 2 * HD)
        scores = dot_nn(part, query_t[:, :width])
        if level:
            place = held[(K_KEYS, level)][pl.ds(b * group, group)].reshape(group * n, LANES)
        else:
            place = (lax.broadcasted_iota(jnp.int32, (group * n, LANES), 0) + b * (group * n)).astype(F32)
        place = jnp.concatenate([place] * (width // LANES), axis=1)
        scores = jnp.where(place <= held[(K_PLACE, level)][...], scores, NEG)
        before = top[:, :width]
        peak = jnp.maximum(before, jnp.max(scores, axis=0, keepdims=True))
        soft = jnp.exp(scores - peak)
        fade = jnp.exp(before - peak)
        total[:, :width] = total[:, :width] * fade + jnp.sum(soft, axis=0, keepdims=True)
        acc[:, :width] = acc[:, :width] * fade + dot_tn(part, soft.astype(BF))
        top[:, :width] = peak

    def mix_heads(level):
        n = counts[level]
        width = heads * n
        mixed_t = acc[:, :width] / total[:, :width]
        held[(K_MIXED_T, level)][...] = mixed_t
        held[(K_LOG, level)][...] = top[:, :width] + jnp.log(total[:, :width])
        mixed = mixed_t.T
        for t in range(heads // 2):
            even = mixed[2 * t * n : (2 * t + 1) * n, :]
            odd = mixed[(2 * t + 1) * n : (2 * t + 2) * n, :]
            held[(K_MIXED, level)][:, t * LANES : (t + 1) * LANES] = jnp.where(
                left[:n], pltpu.roll(even, HD, 1), odd
            ).astype(BF)
        for base in (K_MIXED_T, K_LOG, K_MIXED, K_PACKED):
            keep((base, level))

    sums = [Sum(mp, mp_me, *sum_refs[4 * i : 4 * i + 4]) for i in range(2 * len(counts))]
    chunk = model // mp
    base_o = mix + 2 * LANES
    base_gu = base_o + mix
    base_d = base_gu + 2 * hidden

    def rows_of(start, wide, low, high):
        return weights[start // chunk, pl.ds(lax.rem(start, chunk) // LANES, wide // LANES), :, :, low:high].reshape(
            wide, high - low
        )

    def feed(level, beside):
        name = lambda base: held[(base, level)]
        mixed_now = name(K_MIXED)[...]
        first, last = sums[2 * level], sums[2 * level + 1]
        first.start(lambda start, wide: dot_nt(mixed_now, rows_of(start, wide, base_o, base_gu)))
        beside(1)
        first.middle()
        beside(1)
        attn = first.finish()
        name(K_ATTN)[...] = attn
        level_rows = name(K_ROWS)[...].astype(F32)
        unit, unused = unit_of(level_rows + attn.astype(F32))
        second = (unit * gains[1:2, :]).astype(BF)
        name(K_SECOND)[...] = second
        beside(100)
        parts = name(K_PARTS)
        for t in range(2 * hidden // 256):
            low = base_gu + t * 256
            parts[:, t * 256 : (t + 1) * 256] = dot_nn(
                second, weights[:, :, :, :, low : low + 256].reshape(model, 256)
            )
        n = counts[level]
        for t in range(hidden // LANES):
            cut = slice(t * LANES, (t + 1) * LANES)
            gate_part = parts[:, cut]
            up_part = parts[:, hidden + t * LANES : hidden + (t + 1) * LANES]
            hidden_v[:n, cut] = (gate_part * sigmoid(gate_part) * up_part).astype(BF)
        hidden_now = hidden_v[:n, :]
        last.start(lambda start, wide: dot_nt(hidden_now, rows_of(start, wide, base_d, base_d + hidden)))
        for base in (K_ATTN, K_SECOND, K_PARTS):
            keep((base, level))
        gate = sigmoid(jnp.sum(level_rows * gains[2:3, :], axis=-1, keepdims=True))
        last.middle()
        ffn = last.finish()
        name(K_FFN)[...] = ffn
        keep((K_FFN, level))
        update = (gate * (attn.astype(F32) + ffn.astype(F32))).astype(BF)
        if level:
            update = dot_tn(held[(K_PICK, level)][...], update)
        held[K_STATE][...] = held[K_STATE][...] + update.astype(F32)

    steps = len(groups) + 6
    done = [upto]

    def beside(count):
        for _ in range(count):
            if done[0] < steps:
                spread.step(done[0])
                done[0] += 1

    project(0, tokens[...])
    held[K_STATE][...] = tokens[...].astype(F32)
    for name in ((K_PLACE, 0), (K_PICK, 1), (K_PICK, 2), (K_PLACE, 1), (K_PLACE, 2), (K_COSINE, 1), (K_SINE, 1), (K_COSINE, 2), (K_SINE, 2), (K_KEYS, 1), (K_KEYS, 2)):
        keep(name)
    for b in range(devices // group_of(0)):
        beside(1)

        @pl.when(b * group_of(0) <= me)
        def _(b=b):
            block(0, b)

    mix_heads(0)
    feed(0, beside)
    keep(K_WEIGHTS)
    for level in range(1, len(counts)):
        now = dot_nn(held[(K_PICK, level)][...], held[K_STATE][...].astype(BF)).astype(BF)
        project(level, now)

        def one_block(b, carry, level=level):
            block(level, b)
            return carry

        lax.fori_loop(0, me // group_of(level) + 1, one_block, 0)
        mix_heads(level)
        feed(level, lambda count: None)
    keep(K_STATE)
    spread.drain()
    for item in sums:
        item.drain()
    for level in range(len(counts)):

        def sent(e, carry, level=level):
            kv_copy(level, e, me).wait_send()
            return carry

        lax.fori_loop(me + 1, devices, sent, 0)
    for copy in keeps:
        copy.wait()


def advance(tokens, depths, second_slot, third_slot, matrices, vectors, tables, heads, devices, mp, ident):
    counts = (tokens.shape[0], SECOND_SLOTS, THIRD_SLOTS)
    rows, model = tokens.shape
    depth, mix = matrices[0].shape
    hidden = matrices[4].shape[1]
    total = 2 * mix + 2 * LANES + 3 * hidden
    cuts = [0, mix + 2 * LANES]
    while cuts[-1] < total:
        cuts.append(min(cuts[-1] + 512, total))
    if cuts[-1] - cuts[-2] < 256:
        cuts.pop(-2)
    groups = [(a, b, i % 2) for i, (a, b) in enumerate(zip(cuts[:-1], cuts[1:]))]
    shapes = {
        K_STATE: ((rows, model), F32),
        K_WEIGHTS: ((4, 4, 2, depth, total), BF),
        K_GAINS: ((8, model), F32),
    }
    for level, n in enumerate(counts):
        width = heads * n
        shapes[(K_PLACE, level)] = ((1, width), F32)
        if level:
            shapes[(K_PICK, level)] = ((n, rows), BF)
            shapes[(K_COSINE, level)] = ((n, LANES), F32)
            shapes[(K_SINE, level)] = ((n, LANES), F32)
            shapes[(K_KEYS, level)] = ((devices, n, LANES), F32)
        for base in (K_ROWS, K_NORMED, K_ATTN, K_FFN, K_SECOND):
            shapes[(base, level)] = ((n, model), BF)
        shapes[(K_PARTS, level)] = ((n, 2 * hidden), F32)
        shapes[(K_PACKED, level)] = ((devices, n, 2 * HD), BF)
        shapes[(K_QUERY, level)] = ((width, 2 * HD), BF)
        shapes[(K_MIXED_T, level)] = ((2 * HD, width), F32)
        shapes[(K_LOG, level)] = ((1, width), F32)
        shapes[(K_MIXED, level)] = ((n, mix), BF)
    names = tuple(shapes)
    args = (tokens, depths, second_slot, third_slot, *matrices, *vectors, *tables)
    width = heads * rows
    outs = pl.pallas_call(
        functools.partial(advance_kernel, counts, heads, devices, mp, hidden, groups, names),
        out_shape=tuple(jax.ShapeDtypeStruct(*shapes[name]) for name in names),
        in_specs=vmem(len(args)),
        out_specs=tuple([pl.BlockSpec(memory_space=pl.ANY)] * len(names)),
        scratch_shapes=[pltpu.VMEM(*shapes[name]) for name in names]
        + [
            pltpu.VMEM((depth, total), BF),
            pltpu.SemaphoreType.DMA(()),
            pltpu.SemaphoreType.DMA((len(groups), 8)),
            pltpu.SemaphoreType.DMA((len(groups), 8)),
            pltpu.VMEM((2 * HD, width), BF),
            pltpu.VMEM((1, width), F32),
            pltpu.VMEM((1, width), F32),
            pltpu.VMEM((2 * HD, width), F32),
            pltpu.VMEM((rows, hidden), BF),
            pltpu.SemaphoreType.DMA((len(names),)),
            pltpu.SemaphoreType.DMA((len(counts), devices)),
            pltpu.SemaphoreType.DMA((len(counts), devices)),
        ]
        + [item for n in counts for _ in range(2) for item in sum_scratch(mp, n, model)],
        compiler_params=pltpu.CompilerParams(
            collective_id=ident, has_side_effects=True, vmem_limit_bytes=VMEM_LIMIT
        ),
        name="advance",
    )(*args)
    return dict(zip(names, outs))


SLOTS = 6
CORE_SLOTS = 3
GROUP = 512


class Collect:
    def __init__(self, spans, groups, x, y, core, turned, rights, vectors, store, slots, core_recv, relay_recv, first_recv, mid, last_recv, send_sems, recv_sems, credit, turn):
        self.spans, self.groups = spans, groups
        self.x, self.y, self.core = x, y, core
        self.turned, self.rights, self.vectors, self.store, self.slots = turned, rights, vectors, store, slots
        self.core_recv, self.relay_recv, self.first_recv = core_recv, relay_recv, first_recv
        self.mid, self.last_recv, self.credit = mid, last_recv, credit
        self.send_sems, self.recv_sems = send_sems, recv_sems
        self.turn = turn
        self.waits = [{} for _ in groups]
        self.done = set()

    def remote(self, g, index, source, target, device):
        copy = pltpu.make_async_remote_copy(
            src_ref=source, dst_ref=target, send_sem=self.send_sems.at[g, index],
            recv_sem=self.recv_sems.at[g, index], device_id=device, device_id_type=MESH,
        )
        copy.start()
        return copy

    def held(self, slot, axis, at, first, count):
        if axis == 0:
            return self.slots.at[slot, at, pl.ds(first, count), self.core]
        return self.slots.at[slot, pl.ds(first, count), at, self.core]

    def zero(self, g):
        slot, waits = g % SLOTS, self.waits
        if g >= SLOTS:
            for stage in range(3):
                for copy in waits[g - SLOTS][stage]:
                    copy.wait_send()
        column = 0
        for section, low, high in self.groups[g][1]:
            wide = high - low
            if section < 4:
                if section not in self.done:
                    self.done.add(section)
                    self.turn(section)
                base = self.spans[section][0]

            def rows_of(m, carry, section=section, low=low, high=high, column=column, wide=wide):
                start = pl.multiple_of(m * 1024, 1024)
                if section < 4:
                    value = dot_nn(
                        self.turned[section % 2, pl.ds(start, 1024), :], self.rights[:, base + low : base + high]
                    )
                else:
                    few = self.vectors[:, pl.ds(start, 1024)]
                    value = jnp.concatenate([few, jnp.zeros((LANES - few.shape[0], 1024), F32)], axis=0).T
                self.slots[slot, pl.ds(m * 2, 2), :, :, :, column : column + wide] = (
                    value.astype(BF).reshape(2, 4, 2, 64, wide)
                )
                return carry

            lax.fori_loop(0, 2, rows_of, 0)
            column += wide
        if g >= CORE_SLOTS:
            pl.semaphore_wait(self.credit, 1)
        waits[g][0] = [
            self.remote(
                g, 0, self.slots.at[slot, :, :, 1 - self.core, :, :column],
                self.core_recv.at[g % CORE_SLOTS, :, :, :, :column], peer(self.x, self.y, 1 - self.core),
            )
        ]

    def first(self, g):
        slot, (width, _, axis) = g % SLOTS, self.groups[g]
        waits, slots = self.waits, self.slots
        waits[g][0][0].wait_recv()

        def add(i, carry):
            slots[slot, i, :, self.core, :, :width] = (
                slots[slot, i, :, self.core, :, :width] + self.core_recv[g % CORE_SLOTS, i, :, :, :width]
            )
            return carry

        lax.fori_loop(0, 4, add, 0)
        if g + CORE_SLOTS < len(self.groups):
            pl.semaphore_signal(
                self.credit, inc=1, device_id=peer(self.x, self.y, 1 - self.core), device_id_type=MESH
            )
        at = self.x if axis == 0 else self.y
        waits[g][1] = [
            self.remote(
                g, 1 + i, self.held(slot, axis, lax.rem(at + 2, 4), 2 * i, 2).at[:, :, :width],
                self.relay_recv.at[g, i, :, :, :width], shifted(self.x, self.y, self.core, axis, k),
            )
            for i, k in enumerate((1, 3))
        ]

    def second(self, g):
        slot, (width, _, axis) = g % SLOTS, self.groups[g]
        waits, slots = self.waits, self.slots
        at = self.x if axis == 0 else self.y
        waits[g][2] = []
        for i, k in enumerate((1, 3)):
            waits[g][1][i].wait_recv()
            there = lax.rem(at + k, 4)
            for j in range(2):
                b = 2 * i + j
                where = (slot, there, b, self.core) if axis == 0 else (slot, b, there, self.core)
                where = where + (slice(None), slice(0, width))
                slots[where] = slots[where] + self.relay_recv[g, i, j, :, :width]
            waits[g][2].append(
                self.remote(
                    g, 3 + i, self.held(slot, axis, there, 0, 4).at[:, :, :width],
                    self.first_recv.at[g, i, :, :, :width], shifted(self.x, self.y, self.core, axis, k),
                )
            )

    def third(self, g):
        slot, (width, _, axis) = g % SLOTS, self.groups[g]
        waits, slots = self.waits, self.slots
        at, other = (self.x, self.y) if axis == 0 else (self.y, self.x)
        for copy in waits[g][2]:
            copy.wait_recv()
        for b in range(4):
            where = (slot, at, b, self.core) if axis == 0 else (slot, b, at, self.core)
            self.mid[g, b, :, :width] = (
                slots[where + (slice(None), slice(0, width))].astype(F32)
                + self.first_recv[g, 0, b, :, :width].astype(F32)
                + self.first_recv[g, 1, b, :, :width].astype(F32)
            ).astype(BF)
        waits[g][3] = [
            self.remote(
                g, 4 + k, self.mid.at[g, lax.rem(other + k, 4), :, :width],
                self.last_recv.at[g, k - 1, :, :width],
                shifted(self.x, self.y, self.core, 1 - axis, k),
            )
            for k in (2, 1, 3)
        ]

    def fourth(self, g):
        width, pieces, axis = self.groups[g]
        other = self.y if axis == 0 else self.x
        value = self.mid[g, other, :, :width].astype(F32)
        for copy in self.waits[g][3]:
            copy.wait_recv()
        for k in range(3):
            value = value + self.last_recv[g, k, :, :width].astype(F32)
        column = 0
        for section, low, high in pieces:
            self.store(section, low, value[:, column : column + high - low])
            column += high - low

    def step(self, i, new=True):
        for back, work in ((0, self.zero), (1, self.first), (3, self.second), (5, self.third), (6, self.fourth)):
            if 0 <= i - back < len(self.groups) and (back or new):
                work(i - back)

    def drain(self):
        count = len(self.groups)
        for g in range(count):
            for stage in range(4):
                if stage == 3 or g >= count - SLOTS:
                    for copy in self.waits[g][stage]:
                        copy.wait_send()


def finish_kernel(n, heads, devices, mp, group, levels, spans, groups, *refs):
    refs = list(refs)
    flow, gains, query_place, query, packed, mixed_t, log_total, cosine, sine = [refs.pop(0) for _ in range(9)]
    rows_in, attn_in, logit, vecs = [refs.pop(0) for _ in range(4)]
    w_hbm = refs.pop(0)
    sources = [[refs.pop(0) if level or i not in (4, 7) else None for i in range(8)] for level in range(len(levels))]
    flow_out, q_out, k_out, v_out, out_out, gate_out, up_out, down_out, vec_out = [refs.pop(0) for _ in range(9)]
    query_t, grad_rows, grad_t, acc, delta, send_buf, recv_buf, kv_send, kv_recv = [refs.pop(0) for _ in range(9)]
    w_qkv, w_sem, w_gu, gu_sems, middle = [refs.pop(0) for _ in range(5)]
    sum_refs = [[refs.pop(0) for _ in range(4)] for _ in range(2)]
    (lefts, turned, rights, vectors, slots, core_recv, relay_recv, first_recv, mid, last_recv,
     loads, send_sems, recv_sems, credit) = refs
    me, mp_me = lax.axis_index("dp"), lax.axis_index("mp")
    x, y, core = plane(me)
    hidden = gate_out.shape[1]
    mix = q_out.shape[1]
    base_o = mix + 2 * LANES
    load_o = pltpu.make_async_copy(w_hbm.at[:, base_o : base_o + mix], w_qkv.at[:, :mix], w_sem)
    load_o.start()
    wide = w_gu.shape[1]
    pieces = [(mp_me + k, piece) for piece in range(PIECES) for k in Sum.order]
    pieces += [(mp_me, piece) for piece in range(PIECES)]
    gu_loads = []

    def load_gu():
        i = len(gu_loads)
        if i < len(pieces):
            start = pl.multiple_of((lax.rem(pieces[i][0], mp) * PIECES + pieces[i][1]) * wide, wide)
            copy = pltpu.make_async_copy(
                w_hbm.at[pl.ds(start, wide), base_o + mix : base_o + mix + 2 * hidden],
                w_gu.at[i % w_gu.shape[0]], gu_sems.at[i % w_gu.shape[0]],
            )
            copy.start()
            gu_loads.append(copy)

    for _ in range(w_gu.shape[0]):
        load_gu()
    fetches = [[] for _ in range(4)]

    def fetch(s, side):
        row = 0
        for level, count in enumerate(levels):
            low, high = spans[s]
            target = (lefts.at[s % 2, row : row + count], rights.at[row : row + count, low:high])[side]
            if sources[level][2 * s + side] is not None:
                copy = pltpu.make_async_copy(
                    sources[level][2 * s + side], target, loads.at[level, 2 * s + side]
                )
                copy.start()
                fetches[s].append(copy)
            row += count

    for s in range(4):
        if s < 2:
            fetch(s, 0)
        fetch(s, 1)

    barrier = pltpu.get_barrier_semaphore()

    def greet(k, carry):
        pl.semaphore_signal(
            barrier, inc=1, device_id={"dp": lax.rem(me + k, devices)}, device_id_type=MESH
        )
        return carry

    lax.fori_loop(1, devices, greet, 0)
    for k in range(1, mp):
        pl.semaphore_signal(
            barrier, inc=1, device_id={"mp": lax.rem(mp_me + k, mp)}, device_id_type=MESH
        )

    def turn(section):
        for copy in fetches[section]:
            copy.wait()
        turned[section % 2] = lefts[section % 2].T
        if section < 2:
            fetch(section + 2, 0)

    def store(section, low, value):
        high = low + value.shape[1]
        if section == 0:
            middle_cut = min(max(hidden - low, 0), high - low)
            if middle_cut:
                gate_out[:, low : low + middle_cut] = value[:, :middle_cut]
            if low + middle_cut < high:
                up_out[:, low + middle_cut - hidden : high - hidden] = value[:, middle_cut:]
        elif section == 1:
            down_out[:, low:high] = value
        elif section == 2:
            out_out[:, low:high] = value
        elif section == 3:
            if low < mix:
                q_out[:, low : min(high, mix)] = value[:, : min(high, mix) - low]
            if high > mix:
                k_out[...] = value[:, mix - low : mix - low + HD]
                v_out[...] = value[:, mix - low + HD :]
        else:
            vec_out[...] = value.T[: vec_out.shape[0], :]

    work = Collect(
        spans, groups, x, y, core, turned, rights, vectors, store, slots, core_recv, relay_recv,
        first_recv, mid, last_recv, send_sems, recv_sems, credit, turn,
    )
    pl.semaphore_wait(barrier, devices - 1 + mp - 1)
    for i in range(4):
        work.step(i)

    update = flow[...].astype(BF).astype(F32)
    level = rows_in[...].astype(F32)
    gate = sigmoid(jnp.sum(level * gains[2:3, :], axis=-1, keepdims=True))
    parts_now = rights[0:n, : 2 * hidden]
    used = []

    def gu_piece(start, size):
        i = len(used)
        used.append(i)
        gu_loads[i].wait()
        value = dot_nt(parts_now, w_gu[i % w_gu.shape[0]])
        load_gu()
        return value

    head = Sum(mp, mp_me, *sum_refs[0])
    head.start(gu_piece)
    work.step(4)
    head.middle()
    work.step(5)
    grad_second = head.finish().astype(F32)
    unit, factor = unit_of(level + attn_in[...].astype(F32))
    vectors[...] = jnp.zeros(vectors.shape, F32)
    vectors[1:2, :] = (
        jnp.sum(grad_second * unit, axis=0, keepdims=True) + vecs[0:1, :] + vecs[1:2, :]
    )
    middle[...] = unit_back(grad_second * gains[1:2, :], unit, factor)
    grad_attn = (gate * update + middle[...]).astype(BF)
    lefts[0, 0:n, :] = grad_attn
    load_o.wait()
    grad_mixed = dot_nn(grad_attn, w_qkv[:, :mix]).astype(BF).astype(F32)
    load_w = pltpu.make_async_copy(w_hbm.at[:, : w_qkv.shape[1]], w_qkv, w_sem)
    load_w.start()
    work.step(6)
    left = lanes_of((n, LANES)) < HD
    for t in range(heads // 2):
        part = grad_mixed[:, t * LANES : (t + 1) * LANES]
        grad_rows[2 * t * n : (2 * t + 1) * n, :] = jnp.where(
            left, 0.0, pltpu.roll(part, HD, 1)
        ).astype(BF)
        grad_rows[(2 * t + 1) * n : (2 * t + 2) * n, :] = jnp.where(left, 0.0, part).astype(BF)
    query_t[...] = query[...].T
    grad_t[...] = grad_rows[...].T
    delta[...] = jnp.sum(grad_t[...].astype(F32) * mixed_t[...], axis=0, keepdims=True)
    acc[...] = jnp.zeros(acc.shape, F32)
    width = heads * n

    def send_copy(e, source_index):
        return pltpu.make_async_remote_copy(
            src_ref=send_buf.at[e], dst_ref=recv_buf.at[source_index],
            send_sem=kv_send.at[e], recv_sem=kv_recv.at[source_index],
            device_id={"dp": e}, device_id_type=MESH,
        )

    def one_block(b):
        part = packed[b * group : (b + 1) * group].reshape(group * n, 2 * HD)
        scores = dot_nn(part, query_t[...])
        place = (lax.broadcasted_iota(jnp.int32, (group * n, LANES), 0) + b * (group * n)).astype(F32)
        place = jnp.concatenate([place] * (width // LANES), axis=1)
        scores = jnp.where(place <= query_place[...], scores, NEG)
        weights = jnp.exp(scores - log_total[...])
        grad_weights = dot_nn(part, grad_t[...])
        grad_scores = (weights * (grad_weights - delta[...])).astype(BF)
        grad_part = dot_nn(grad_scores, query[...]) + dot_nn(weights.astype(BF), grad_rows[...])
        send_buf[b * group : (b + 1) * group] = grad_part.astype(BF).reshape(group, n, 2 * HD)
        acc[...] += dot_tn(part, grad_scores)
        for e in range(b * group, (b + 1) * group):

            @pl.when(e < me)
            def _(e=e):
                send_copy(e, me).start()

    blocks = devices // group
    for b in range(blocks):
        if b == blocks // 2:
            work.step(7)

        @pl.when(b * group <= me)
        def _(b=b):
            one_block(b)

    work.step(8)
    grad_query = acc[...].T * HD**-0.5
    outs = []
    for t in range(heads // 2):
        even = grad_query[2 * t * n : (2 * t + 1) * n, :]
        odd = grad_query[(2 * t + 1) * n : (2 * t + 2) * n, :]
        outs.append(jnp.where(left, even, pltpu.roll(odd, HD, 1)))

    def add(e, carry):
        send_copy(me, e).wait_recv()
        return carry + recv_buf[e].astype(F32)

    outs.append(lax.fori_loop(me + 1, devices, add, send_buf[me].astype(F32)))
    low = spans[3][0]
    for t, part in enumerate(outs):
        rights[0:n, low + t * LANES : low + (t + 1) * LANES] = turn_back(
            part, cosine[...], sine[...], t == heads // 2
        )
    load_w.wait()
    grad_now = rights[0:n, low : spans[3][1]]

    def first_piece(start, wide):
        return dot_nt(grad_now, w_qkv[pl.ds(start, wide), :])

    total = Sum(mp, mp_me, *sum_refs[1])
    total.start(first_piece)
    work.step(9)
    total.middle()
    work.step(10)
    work.step(11, False)
    grad_normed = total.finish().astype(F32)
    unit, factor = unit_of(level)
    vectors[0:1, :] = jnp.sum(grad_normed * unit, axis=0, keepdims=True) + vecs[3:4, :] + vecs[4:5, :]
    vectors[2:3, :] = jnp.sum(level * logit[...], axis=0, keepdims=True) + vecs[5:6, :] + vecs[6:7, :]
    flow_out[...] = flow[...] + (
        unit_back(grad_normed * gains[0:1, :], unit, factor) + middle[...] + logit[...] * gains[2:3, :]
    ).astype(BF).astype(F32)
    work.zero(11)
    for i in range(12, len(groups) + 6):
        work.step(i)
    work.drain()
    head.drain()
    total.drain()

    def sent(e, carry):
        send_copy(e, me).wait_send()
        return carry

    lax.fori_loop(0, me, sent, 0)


def finish(flow, gains, attention, tail, vecs, weights, levels, heads, devices, mp, depth, ident):
    n, model = levels[0][0].shape
    width = heads * n
    group = 512 // n
    mix = heads * HD
    widths = [levels[1][i].shape[1] for i in (1, 3, 5, 7)] + [LANES]
    spans, total = [], 0
    for wide in widths:
        spans.append((total, total + wide))
        total += wide
    pieces = []
    for section, wide in enumerate(widths):
        pieces += [(section, low, low + LANES) for low in range(0, wide, LANES)]
    groups = []
    per = GROUP // LANES
    cuts = [*range(0, len(pieces) - 1, per), len(pieces) - 1, len(pieces)]
    for index, end in zip(cuts[:-1], cuts[1:]):
        merged = []
        for section, low, high in pieces[index:end]:
            if merged and merged[-1][0] == section:
                merged[-1] = (section, merged[-1][1], high)
            else:
                merged.append((section, low, high))
        wide = sum(high - low for _, low, high in merged)
        groups.append((wide, merged, len(groups) % 2))
    counts = [level[0].shape[0] for level in levels]
    rows = sum(counts)
    hidden = widths[1]
    many = len(groups)
    whole = [flow, gains, *attention, *tail, vecs]
    args = whole + [weights] + [item for level in levels for item in level if item is not None]
    return pl.pallas_call(
        functools.partial(finish_kernel, n, heads, devices, mp, group, counts, spans, groups),
        out_shape=(
            jax.ShapeDtypeStruct(flow.shape, F32),
            jax.ShapeDtypeStruct((depth, mix), F32),
            jax.ShapeDtypeStruct((depth, HD), F32),
            jax.ShapeDtypeStruct((depth, HD), F32),
            jax.ShapeDtypeStruct((depth, mix), F32),
            jax.ShapeDtypeStruct((depth, hidden), F32),
            jax.ShapeDtypeStruct((depth, hidden), F32),
            jax.ShapeDtypeStruct((depth, hidden), F32),
            jax.ShapeDtypeStruct((8, depth), F32),
        ),
        in_specs=vmem(len(whole)) + [pl.BlockSpec(memory_space=pl.ANY)] * (len(args) - len(whole)),
        out_specs=tuple(vmem(9)),
        scratch_shapes=[
            pltpu.VMEM((2 * HD, width), BF),
            pltpu.VMEM((width, 2 * HD), BF),
            pltpu.VMEM((2 * HD, width), BF),
            pltpu.VMEM((2 * HD, width), F32),
            pltpu.VMEM((1, width), F32),
            pltpu.VMEM((devices, n, 2 * HD), BF),
            pltpu.VMEM((devices, n, 2 * HD), BF),
            pltpu.SemaphoreType.DMA((devices,)),
            pltpu.SemaphoreType.DMA((devices,)),
            pltpu.VMEM((model, mix + 2 * HD), BF),
            pltpu.SemaphoreType.DMA(()),
            pltpu.VMEM((2, model // mp // PIECES, 2 * hidden), BF),
            pltpu.SemaphoreType.DMA((2,)),
            pltpu.VMEM((n, model), F32),
            *sum_scratch(mp, n, model),
            *sum_scratch(mp, n, model),
            pltpu.VMEM((2, rows, model), BF),
            pltpu.VMEM((2, model, rows), BF),
            pltpu.VMEM((rows, spans[3][1]), BF),
            pltpu.VMEM((8, model), F32),
            pltpu.VMEM((SLOTS, 4, 4, 2, depth, GROUP), BF),
            pltpu.VMEM((CORE_SLOTS, 4, 4, depth, GROUP), BF),
            pltpu.VMEM((many, 2, 2, depth, GROUP), BF),
            pltpu.VMEM((many, 2, 4, depth, GROUP), BF),
            pltpu.VMEM((many, 4, depth, GROUP), BF),
            pltpu.VMEM((many, 3, depth, GROUP), BF),
            pltpu.SemaphoreType.DMA((len(levels), 8)),
            pltpu.SemaphoreType.DMA((many, 8)),
            pltpu.SemaphoreType.DMA((many, 8)),
            pltpu.SemaphoreType.REGULAR,
        ],
        compiler_params=pltpu.CompilerParams(
            collective_id=ident, has_side_effects=True, vmem_limit_bytes=63 * 1024 * 1024
        ),
        name="finish",
    )(*args)


def hand_over_kernel(count, *refs):
    vectors, sources, targets = refs[0], refs[1 : 1 + count], refs[1 + count :]
    for source, target in zip(sources, targets):
        target[...] = source[...]
    for i, target in enumerate(targets[count:]):
        target[...] = vectors[i, :]


def hand_over(items, vectors):
    count = len(items)
    return pl.pallas_call(
        functools.partial(hand_over_kernel, count),
        out_shape=tuple(
            [jax.ShapeDtypeStruct(item.shape, F32) for item in items]
            + [jax.ShapeDtypeStruct(vectors.shape[1:], F32)] * 3
        ),
        in_specs=vmem(1 + count),
        out_specs=tuple(vmem(count + 3)),
        name="hand_over",
    )(vectors, *items)


def rotary_tables(place):
    freq = jnp.exp(jnp.arange(HD // 2, dtype=F32) * (-2.0 * math.log(ROPE_BASE) / HD))
    angle = place.astype(F32)[:, None] * freq[None, :]
    cosine, sine = jnp.cos(angle), jnp.sin(angle)
    return (
        jnp.concatenate([cosine] * 4, axis=1),
        jnp.concatenate([-sine, sine, -sine, sine], axis=1),
    )


def local(
    tokens, depths, second_slot, third_slot, w_query, w_key, w_value, w_out, w_gate, w_up,
    w_down, norm_first, norm_second, router, cotangent,
):
    me = lax.axis_index("dp")
    devices, mp = lax.axis_size("dp"), lax.axis_size("mp")
    rows = tokens.shape[0]
    heads = w_query.shape[1] // HD
    depth = w_query.shape[0]
    home = rotary_tables(jnp.arange(rows, dtype=jnp.int32) + me * rows)

    def row(values):
        return values.reshape(1, -1)

    kept = advance(
        tokens, row(depths), row(second_slot), row(third_slot),
        (w_query, w_key, w_value, w_out.T, w_gate, w_up, w_down.T),
        (row(norm_first), row(norm_second), row(router)), home, heads, devices, mp, 0,
    )
    weights = kept[K_WEIGHTS].reshape(devices * depth, -1)
    gains = kept[K_GAINS]
    back = retreat(cotangent, kept, weights, heads, devices, mp, 1)
    terms = []
    for level in range(3):
        terms.append(
            tuple(back.get((base, level), kept.get((base, level))) for base in (
                K_SECOND, K_PARTS_GRAD, K_GRAD_FFN, K_HIDDEN, K_GRAD_ATTN, K_MIXED, K_NORMED, K_GRAD_QKV
            ))
        )
    attention = [kept[(base, 0)] for base in (K_PLACE, K_QUERY, K_PACKED, K_MIXED_T, K_LOG)]
    results = finish(
        back[K_FLOW_OUT], gains, (*attention, *home),
        (kept[(K_ROWS, 0)], kept[(K_ATTN, 0)], back[(K_LOGIT, 0)]), back[K_VECS], weights, terms,
        heads, devices, mp, depth, 2,
    )
    (state, flow, query_grad, key_grad, value_grad, out_grad, gate_grad, up_grad, down_grad,
     first_grad, second_grad, router_grad) = hand_over((kept[K_STATE], *results[:-1]), results[-1])
    return (
        state, flow, query_grad, key_grad, value_grad, out_grad.T, gate_grad, up_grad, down_grad.T,
        first_grad, second_grad, router_grad,
    )


def solution(mesh):
    in_specs = (
        P("dp", None), P("dp"), P("dp"), P("dp"), P("dp", "mp"), P("dp", "mp"), P("dp", "mp"),
        P("mp", "dp"), P("dp", "mp"), P("dp", "mp"), P("mp", "dp"), P("dp"), P("dp"), P("dp"),
        P("dp", None),
    )
    out_specs = (
        P("dp", None), P("dp", None), P("dp", "mp"), P("dp", "mp"), P("dp", "mp"), P("mp", "dp"),
        P("dp", "mp"), P("dp", "mp"), P("mp", "dp"), P("dp"), P("dp"), P("dp"),
    )
    return jax.shard_map(local, mesh=mesh, in_specs=in_specs, out_specs=out_specs, check_vma=False)
```

```python
import functools
import math

import jax
import jax.numpy as jnp
from jax import lax
from jax.experimental import pallas as pl
from jax.experimental.pallas import tpu as pltpu
from jax.sharding import PartitionSpec as P

HD = 64
SECOND_SLOTS = 96
THIRD_SLOTS = 64
EPS = 1e-05
NEG = -1e30
ROPE_BASE = 10000.0
FAR = 1e9
BF = jnp.bfloat16
F32 = jnp.float32
MESH = pl.DeviceIdType.MESH

(K_ROWS, K_NORMED, K_ATTN, K_FFN, K_SECOND, K_PARTS, K_PACKED, K_QUERY, K_MIXED_T, K_LOG, K_MIXED, K_PLACE, K_PICK, K_COSINE, K_SINE, K_KEYS, K_STATE, K_WEIGHTS, K_GAINS, K_FLOW, K_FLOW_OUT, K_VECS, K_GRAD_QKV, K_GRAD_FFN, K_HIDDEN, K_PARTS_GRAD, K_GRAD_ATTN, K_GRAD_MIXED, K_MIDDLE, K_LOGIT, K_HEAD, K_TAIL, K_D, K_GU, K_O, K_QKV) = range(36)

LANES = 128
VMEM_LIMIT = 63 * 1024 * 1024


def dot_nn(left, right):
    return lax.dot_general(left, right, (((1,), (0,)), ((), ())), preferred_element_type=F32)


def dot_nt(left, right):
    return lax.dot_general(left, right, (((1,), (1,)), ((), ())), preferred_element_type=F32)


def dot_tn(left, right):
    return lax.dot_general(left, right, (((0,), (0,)), ((), ())), preferred_element_type=F32)


def unit_of(values):
    factor = lax.rsqrt(jnp.mean(values * values, axis=-1, keepdims=True) + EPS)
    return values * factor, factor


def unit_back(shaped, unit, factor):
    return factor * (shaped - unit * jnp.mean(shaped * unit, axis=-1, keepdims=True))


def sigmoid(values):
    return 1.0 / (1.0 + jnp.exp(-values))


def lanes_of(shape):
    return lax.broadcasted_iota(jnp.int32, shape, 1)


def swap_halves(tile):
    first = lax.rem(lanes_of(tile.shape), HD) < HD // 2
    return jnp.where(first, pltpu.roll(tile, LANES - HD // 2, 1), pltpu.roll(tile, HD // 2, 1))


def turn_back(part, cosine, sine, packed):
    if packed:
        left = lanes_of(part.shape) < HD
        cosine, sine = jnp.where(left, cosine, 1.0), jnp.where(left, sine, 0.0)
    return (part * cosine - swap_halves(part) * sine).astype(BF)


def tile_of(values, index):
    return values[:, index * LANES : (index + 1) * LANES]


def signal_all(group, me, axis):
    barrier = pltpu.get_barrier_semaphore()
    for k in range(1, group):
        pl.semaphore_signal(
            barrier, inc=1, device_id={axis: lax.rem(me + k, group)}, device_id_type=MESH
        )
    pl.semaphore_wait(barrier, group - 1)


PIECES = 2


class Sum:
    order = (2, 1, 3)

    def __init__(self, group, me, send, recv, full, sems):
        self.group, self.me, self.send, self.recv, self.full, self.sems = group, me, send, recv, full, sems
        self.wide = send.shape[-1]

    def remote(self, source, target, stage, k, piece):
        copy = pltpu.make_async_remote_copy(
            src_ref=source, dst_ref=target, send_sem=self.sems.at[stage, k - 1, piece],
            recv_sem=self.sems.at[stage + 1, k - 1, piece],
            device_id={"mp": lax.rem(self.me + k, self.group)}, device_id_type=MESH,
        )
        copy.start()
        return copy

    def start(self, make_piece):
        self.make, self.out, self.back = make_piece, [], []
        for piece in range(PIECES):
            copies = []
            for k in self.order:
                at = (k - 1, piece)
                self.send[at] = self.part(lax.rem(self.me + k, self.group), piece).astype(BF)
                copies.append(self.remote(self.send.at[at], self.recv.at[at], 0, k, piece))
            self.out.append(copies)

    def part(self, c, piece):
        start = c * (PIECES * self.wide) + piece * self.wide
        return self.make(pl.multiple_of(start, self.wide), self.wide)

    def middle(self):
        for piece in range(PIECES):
            total = self.part(self.me, piece).astype(BF).astype(F32)
            for k, copy in zip(self.order, self.out[piece]):
                copy.wait_recv()
                total = total + self.recv[k - 1, piece].astype(F32)
            self.full[self.me, piece] = total.astype(BF)
            where = self.full.at[self.me, piece]
            self.back.append([self.remote(where, where, 2, k, piece) for k in self.order])

    def finish(self):
        for copies in self.back:
            for copy in copies:
                copy.wait_recv()
        return jnp.concatenate(
            [self.full[c, piece] for c in range(self.group) for piece in range(PIECES)], axis=1
        )

    def drain(self):
        for copies in self.out + self.back:
            for copy in copies:
                copy.wait_send()


def vmem(count):
    return [pl.BlockSpec(memory_space=pltpu.VMEM)] * count


def sum_scratch(mp, n, model):
    wide = model // mp // PIECES
    return [
        pltpu.VMEM((mp - 1, PIECES, n, wide), BF),
        pltpu.VMEM((mp - 1, PIECES, n, wide), BF),
        pltpu.VMEM((mp, PIECES, n, wide), BF),
        pltpu.SemaphoreType.DMA((4, mp - 1, PIECES)),
    ]


def retreat_kernel(counts, heads, devices, mp, hidden, ins, names, inner, *refs):
    refs = list(refs)
    sources = {name: refs.pop(0) for name in ins}
    w_hbm = refs.pop(0)
    outs = {name: refs.pop(0) for name in names}
    held = {name: refs.pop(0) for name in ins}
    held.update({name: refs.pop(0) for name in names + inner})
    w_qkv, w_o, w_gu, w_d, fetch_sems, w_sems, keep_sems = [refs.pop(0) for _ in range(7)]
    query_t, grad_rows, grad_t, acc, delta = [refs.pop(0) for _ in range(5)]
    buffers = {level: [refs.pop(0) for _ in range(4)] for level in (1, 2)}
    sum_refs = {key: [refs.pop(0) for _ in range(4)] for key in ((K_HEAD, 2), (K_TAIL, 2), (K_HEAD, 1), (K_TAIL, 1))}
    me, mp_me = lax.axis_index("dp"), lax.axis_index("mp")
    model = w_o.shape[0]
    mix = heads * HD
    loads, keeps = {}, []

    def fetch(name):
        loads[name] = pltpu.make_async_copy(sources[name], held[name], fetch_sems.at[ins.index(name)])
        loads[name].start()

    def load(name, ref, start, index):
        loads[name] = pltpu.make_async_copy(w_hbm.at[:, start : start + ref.shape[1]], ref, w_sems.at[index])
        loads[name].start()

    def get(name):
        if name in loads:
            loads.pop(name).wait()
        return held[name]

    def need(name):
        if name in loads:
            loads.pop(name).wait()

    def keep(name):
        copy = pltpu.make_async_copy(held[name], outs[name], keep_sems.at[len(keeps)])
        copy.start()
        keeps.append(copy)

    base_o = mix + 2 * LANES
    for name in (K_FLOW, K_GAINS, (K_PICK, 2), (K_ROWS, 2), (K_ATTN, 2), (K_FFN, 2), (K_PARTS, 2)):
        fetch(name)
    load(K_D, w_d, base_o + mix + 2 * hidden, 0)
    load(K_GU, w_gu, base_o + mix, 1)
    load(K_O, w_o, base_o, 2)
    load(K_QKV, w_qkv, 0, 3)
    for name in ins:
        if name not in loads:
            fetch(name)

    barrier = pltpu.get_barrier_semaphore()

    def greet(k, carry):
        pl.semaphore_signal(
            barrier, inc=1, device_id={"dp": lax.rem(me + k, devices)}, device_id_type=MESH
        )
        return carry

    lax.fori_loop(1, devices, greet, 0)
    for k in range(1, mp):
        pl.semaphore_signal(
            barrier, inc=1, device_id={"mp": lax.rem(mp_me + k, mp)}, device_id_type=MESH
        )
    sums = {key: Sum(mp, mp_me, *items) for key, items in sum_refs.items()}
    vecs = held[K_VECS]
    vecs[...] = jnp.zeros(vecs.shape, F32)
    gate_of = {}

    def head(level):
        n = counts[level]
        name = lambda base: held[(base, level)]
        grad_update = get(K_FLOW)[...].astype(BF)
        if level:
            grad_update = dot_nn(get((K_PICK, level))[...], grad_update)
        grad_update = grad_update.astype(F32)
        rows_now = get((K_ROWS, level))[...].astype(F32)
        attn_now = get((K_ATTN, level))[...].astype(F32)
        gains = get(K_GAINS)
        gate = sigmoid(jnp.sum(rows_now * gains[2:3, :], axis=-1, keepdims=True))
        logit = jnp.sum(
            grad_update * (attn_now + get((K_FFN, level))[...].astype(F32)), axis=-1, keepdims=True
        )
        name(K_LOGIT)[...] = logit * gate * (1.0 - gate)
        grad_ffn = (gate * grad_update).astype(BF)
        name(K_GRAD_FFN)[...] = grad_ffn
        parts, parts_grad, hidden_out = get((K_PARTS, level)), name(K_PARTS_GRAD), name(K_HIDDEN)
        need(K_D)
        for t in range(hidden // LANES):
            cut = slice(t * LANES, (t + 1) * LANES)
            up_cut = slice(hidden + t * LANES, hidden + (t + 1) * LANES)
            if t % 2 == 0:
                both = dot_nn(grad_ffn, w_d[:, t * LANES : min((t + 2) * LANES, hidden)])
            grad_hidden = tile_of(both, t % 2)
            gate_part = parts[:, cut]
            up_part = parts[:, up_cut]
            sigma = sigmoid(gate_part)
            active = gate_part * sigma
            hidden_out[:, cut] = (active * up_part).astype(BF)
            parts_grad[:, cut] = (
                grad_hidden * up_part * sigma * (1.0 + gate_part * (1.0 - sigma))
            ).astype(BF)
            parts_grad[:, up_cut] = (grad_hidden * active).astype(BF)
        for base in (K_GRAD_FFN, K_HIDDEN, K_PARTS_GRAD, K_LOGIT):
            keep((base, level))
        return grad_update, rows_now, attn_now, gate

    def head_end(level, grad_update, rows_now, attn_now, gate):
        name = lambda base: held[(base, level)]
        gains = held[K_GAINS]
        need(K_GU)
        if level == 2:
            pl.semaphore_wait(barrier, devices - 1 + mp - 1)
        parts_now = name(K_PARTS_GRAD)[...]
        total = sums[(K_HEAD, level)]
        total.start(lambda start, wide: dot_nt(parts_now, w_gu[pl.ds(start, wide), :]))
        unit, factor = unit_of(rows_now + attn_now)
        total.middle()
        grad_second = total.finish().astype(F32)
        vecs[2 - level : 3 - level, :] = jnp.sum(grad_second * unit, axis=0, keepdims=True)
        grad_middle = unit_back(grad_second * gains[1:2, :], unit, factor)
        name(K_MIDDLE)[...] = grad_middle
        grad_attn = (gate * grad_update + grad_middle).astype(BF)
        name(K_GRAD_ATTN)[...] = grad_attn
        need(K_O)
        name(K_GRAD_MIXED)[...] = dot_nn(grad_attn, w_o[...]).astype(BF)
        keep((K_GRAD_ATTN, level))

    def attention(level):
        n = counts[level]
        group = 8
        width = heads * n
        send_buf, recv_buf, send_sems, recv_sems = buffers[level]
        query, packed = get((K_QUERY, level)), get((K_PACKED, level))
        mixed_t, log_total = get((K_MIXED_T, level)), get((K_LOG, level))
        keys, query_place = get((K_KEYS, level)), get((K_PLACE, level))
        cosine, sine = get((K_COSINE, level)), get((K_SINE, level))
        grad_mixed, grad_qkv = held[(K_GRAD_MIXED, level)], held[(K_GRAD_QKV, level)]
        left = lanes_of((n, LANES)) < HD
        for t in range(heads // 2):
            part = grad_mixed[:, t * LANES : (t + 1) * LANES].astype(F32)
            grad_rows[2 * t * n : (2 * t + 1) * n, :] = jnp.where(
                left, 0.0, pltpu.roll(part, HD, 1)
            ).astype(BF)
            grad_rows[(2 * t + 1) * n : (2 * t + 2) * n, :] = jnp.where(left, 0.0, part).astype(BF)
        query_t[:, :width] = query[...].T
        grad_t[:, :width] = grad_rows[:width, :].T
        delta[:, :width] = jnp.sum(grad_t[:, :width].astype(F32) * mixed_t[...], axis=0, keepdims=True)
        acc[:, :width] = jnp.zeros((2 * HD, width), F32)

        def send_copy(e, source_index):
            return pltpu.make_async_remote_copy(
                src_ref=send_buf.at[e], dst_ref=recv_buf.at[source_index],
                send_sem=send_sems.at[e], recv_sem=recv_sems.at[source_index],
                device_id={"dp": e}, device_id_type=MESH,
            )

        def one_block(b, carry):
            part = packed[pl.ds(b * group, group)].reshape(group * n, 2 * HD)
            scores = dot_nn(part, query_t[:, :width])
            place = keys[pl.ds(b * group, group)].reshape(group * n, LANES)
            place = jnp.concatenate([place] * (width // LANES), axis=1)
            scores = jnp.where(place <= query_place[...], scores, NEG)
            soft = jnp.exp(scores - log_total[...])
            grad_soft = dot_nn(part, grad_t[:, :width])
            grad_scores = (soft * (grad_soft - delta[:, :width])).astype(BF)
            grad_part = dot_nn(grad_scores, query[...]) + dot_nn(soft.astype(BF), grad_rows[:width, :])
            send_buf[pl.ds(b * group, group)] = grad_part.astype(BF).reshape(group, n, 2 * HD)
            acc[:, :width] += dot_tn(part, grad_scores)
            for g in range(group):
                e = b * group + g

                @pl.when(e < me)
                def _(e=e):
                    send_copy(e, me).start()

            return carry

        lax.fori_loop(0, me // group + 1, one_block, 0)
        grad_query = acc[:, :width].T * HD**-0.5
        for t in range(heads // 2):
            even = grad_query[2 * t * n : (2 * t + 1) * n, :]
            odd = grad_query[(2 * t + 1) * n : (2 * t + 2) * n, :]
            part = jnp.where(left, even, pltpu.roll(odd, HD, 1))
            grad_qkv[:, t * LANES : (t + 1) * LANES] = turn_back(part, cosine[...], sine[...], False)

        def add(e, carry):
            send_copy(me, e).wait_recv()
            return carry + recv_buf[e].astype(F32)

        part = lax.fori_loop(me + 1, devices, add, send_buf[me].astype(F32))
        grad_qkv[:, mix:] = turn_back(part, cosine[...], sine[...], True)

        def drain():
            def sent(e, carry):
                send_copy(e, me).wait_send()
                return carry

            lax.fori_loop(0, me, sent, 0)

        return drain

    def tail(level):
        gains, flow = held[K_GAINS], held[K_FLOW]
        grad_now = held[(K_GRAD_QKV, level)][...]
        need(K_QKV)
        total = sums[(K_TAIL, level)]
        total.start(lambda start, wide: dot_nt(grad_now, w_qkv[pl.ds(start, wide), :]))
        keep((K_GRAD_QKV, level))
        rows_now = held[(K_ROWS, level)][...].astype(F32)
        unit, factor = unit_of(rows_now)
        logit = held[(K_LOGIT, level)][...]
        vecs[7 - level : 8 - level, :] = jnp.sum(rows_now * logit, axis=0, keepdims=True)
        total.middle()
        grad_normed = total.finish().astype(F32)
        vecs[5 - level : 6 - level, :] = jnp.sum(grad_normed * unit, axis=0, keepdims=True)
        grad_rows_now = (
            unit_back(grad_normed * gains[0:1, :], unit, factor)
            + held[(K_MIDDLE, level)][...]
            + logit * gains[2:3, :]
        ).astype(BF)
        flow[...] = flow[...] + dot_tn(held[(K_PICK, level)][...], grad_rows_now)

    drains = []
    for level in (2, 1):
        head_end(level, *head(level))
        drains.append(attention(level))
        tail(level)
    held[K_FLOW_OUT][...] = held[K_FLOW][...]
    keep(K_FLOW_OUT)
    head(0)
    keep(K_VECS)
    for drain in drains:
        drain()
    for item in sums.values():
        item.drain()
    for copy in keeps:
        copy.wait()


def retreat(cotangent, kept, weights, heads, devices, mp, ident):
    counts = tuple(kept[(K_ROWS, level)].shape[0] for level in range(3))
    model = cotangent.shape[1]
    mix = heads * HD
    hidden = kept[(K_PARTS, 0)].shape[1] // 2
    ins = {K_FLOW: cotangent, K_GAINS: kept[K_GAINS]}
    inner = {}
    shapes = {K_FLOW_OUT: (cotangent.shape, F32), K_VECS: ((8, model), F32)}
    for level, n in enumerate(counts):
        for base in (K_ROWS, K_ATTN, K_FFN, K_PARTS):
            ins[(base, level)] = kept[(base, level)]
        if level:
            for base in (K_PICK, K_QUERY, K_PACKED, K_MIXED_T, K_LOG, K_KEYS, K_PLACE, K_COSINE, K_SINE):
                ins[(base, level)] = kept[(base, level)]
            shapes[(K_GRAD_QKV, level)] = ((n, mix + 2 * HD), BF)
            shapes[(K_GRAD_ATTN, level)] = ((n, model), BF)
            inner[(K_GRAD_MIXED, level)] = ((n, mix), BF)
            inner[(K_MIDDLE, level)] = ((n, model), F32)
        shapes[(K_GRAD_FFN, level)] = ((n, model), BF)
        shapes[(K_HIDDEN, level)] = ((n, hidden), BF)
        shapes[(K_PARTS_GRAD, level)] = ((n, 2 * hidden), BF)
        shapes[(K_LOGIT, level)] = ((n, 1), F32)
    names = tuple(shapes)
    most = heads * max(counts[1:])
    anywhere = pl.BlockSpec(memory_space=pl.ANY)
    outs = pl.pallas_call(
        functools.partial(retreat_kernel, counts, heads, devices, mp, hidden, tuple(ins), names, tuple(inner)),
        out_shape=tuple(jax.ShapeDtypeStruct(*shapes[name]) for name in names),
        in_specs=[anywhere] * (len(ins) + 1),
        out_specs=tuple([anywhere] * len(names)),
        scratch_shapes=[pltpu.VMEM(item.shape, item.dtype) for item in ins.values()]
        + [pltpu.VMEM(*shape) for shape in (*shapes.values(), *inner.values())]
        + [
            pltpu.VMEM((model, mix + 2 * HD), BF),
            pltpu.VMEM((model, mix), BF),
            pltpu.VMEM((model, 2 * hidden), BF),
            pltpu.VMEM((model, hidden), BF),
            pltpu.SemaphoreType.DMA((len(ins),)),
            pltpu.SemaphoreType.DMA((4,)),
            pltpu.SemaphoreType.DMA((len(names),)),
            pltpu.VMEM((2 * HD, most), BF),
            pltpu.VMEM((most, 2 * HD), BF),
            pltpu.VMEM((2 * HD, most), BF),
            pltpu.VMEM((2 * HD, most), F32),
            pltpu.VMEM((1, most), F32),
        ]
        + [
            item
            for level in (1, 2)
            for item in (
                pltpu.VMEM((devices, counts[level], 2 * HD), BF),
                pltpu.VMEM((devices, counts[level], 2 * HD), BF),
                pltpu.SemaphoreType.DMA((devices,)),
                pltpu.SemaphoreType.DMA((devices,)),
            )
        ]
        + [item for level in (2, 2, 1, 1) for item in sum_scratch(mp, counts[level], model)],
        compiler_params=pltpu.CompilerParams(
            collective_id=ident, has_side_effects=True, vmem_limit_bytes=VMEM_LIMIT
        ),
        name="retreat",
    )(*ins.values(), weights)
    return dict(zip(names, outs))


def plane(me):
    return me // 8, lax.rem(me // 2, 4), lax.rem(me, 2)


def peer(x, y, core):
    return {"dp": (lax.rem(x, 4) * 4 + lax.rem(y, 4)) * 2 + core}


def shifted(x, y, core, axis, k):
    return peer(x + k, y, core) if axis == 0 else peer(x, y + k, core)


def meet(me, partners):
    barrier = pltpu.get_barrier_semaphore()
    for device in partners:
        pl.semaphore_signal(barrier, inc=1, device_id=device, device_id_type=MESH)
    pl.semaphore_wait(barrier, len(partners))


def plane_partners(x, y, core):
    return (
        [peer(x, y, 1 - core)]
        + [shifted(x, y, core, 0, k) for k in (1, 2, 3)]
        + [shifted(x, y, core, 1, k) for k in (1, 2, 3)]
    )


class Spread:
    def __init__(self, groups, x, y, core, shard, full, pair, send_sems, recv_sems):
        self.x, self.y, self.core = x, y, core
        self.count = len(groups)
        self.items = [(shard.at[:, low:high], full, slice(low, high), axis) for low, high, axis in groups]
        self.items.append((pair.at[x, y, core], pair, slice(None), 0))
        self.send_sems, self.recv_sems = send_sems, recv_sems
        self.started = []
        self.waits = [{} for _ in self.items]

    def remote(self, g, index, source, target, device):
        copy = pltpu.make_async_remote_copy(
            src_ref=source, dst_ref=target, send_sem=self.send_sems.at[g, index],
            recv_sem=self.recv_sems.at[g, index], device_id=device, device_id_type=MESH,
        )
        copy.start()
        self.started.append(copy)
        return copy

    def line(self, g, at, first, count):
        _, full, cut, axis = self.items[g]
        if axis == 0:
            return full.at[pl.ds(first, count), at, self.core, :, cut]
        return full.at[at, pl.ds(first, count), self.core, :, cut]

    def one(self, g):
        own, full, cut, axis = self.items[g]
        self.waits[g][1] = [
            self.remote(
                g, k - 1, own, full.at[self.x, self.y, self.core, :, cut],
                shifted(self.x, self.y, self.core, axis, k),
            )
            for k in (2, 1, 3)
        ]

    def two(self, g):
        axis = self.items[g][-1]
        for copy in self.waits[g][1]:
            copy.wait_recv()
        mine = self.line(g, self.y if axis == 0 else self.x, 0, 4)
        self.waits[g][2] = [
            self.remote(g, 3 + i, mine, mine, shifted(self.x, self.y, self.core, 1 - axis, k))
            for i, k in enumerate((1, 3))
        ]

    def three(self, g):
        axis = self.items[g][-1]
        at = self.y if axis == 0 else self.x
        self.waits[g][3] = []
        for i, k in enumerate((1, 3)):
            self.waits[g][2][i].wait_recv()
            piece = self.line(g, lax.rem(at + 4 - k, 4), 2 * i, 2)
            self.waits[g][3].append(
                self.remote(g, 5 + i, piece, piece, shifted(self.x, self.y, self.core, 1 - axis, k))
            )

    def four(self, g):
        _, full, cut, _ = self.items[g]
        for copy in self.waits[g][3]:
            copy.wait_recv()
        mine = full.at[:, :, self.core, :, cut]
        self.waits[g][4] = [self.remote(g, 7, mine, mine, peer(self.x, self.y, 1 - self.core))]

    def five(self, g):
        self.waits[g][4][0].wait_recv()

    def run(self, *groups):
        for work, g in zip((self.two, self.one, self.three, self.four, self.five), groups):
            if g is not None and 0 <= g < self.count:
                work(g)

    def step(self, i):
        self.run(i, i + 3, i - 2, i - 4, i - 5)

    def drain(self):
        for copy in self.started:
            copy.wait_send()


def advance_kernel(counts, heads, devices, mp, hidden, groups, names, *refs):
    refs = list(refs)
    (tokens, depths, second_slot, third_slot, w_query, w_key, w_value, w_out, w_gate, w_up, w_down,
     norm_first, norm_second, router, cosine_in, sine_in) = [refs.pop(0) for _ in range(16)]
    outs = {name: refs.pop(0) for name in names}
    held = {name: refs.pop(0) for name in names}
    shard, own_sem, send_sems, recv_sems, query_t, top, total, acc, hidden_v, keep_sems, kv_send, kv_recv = [
        refs.pop(0) for _ in range(12)
    ]
    sum_refs = refs
    me, mp_me = lax.axis_index("dp"), lax.axis_index("mp")
    x, y, core = plane(me)
    weights = held[K_WEIGHTS]
    rows, model = tokens.shape
    mix = heads * HD
    lanes = lanes_of((rows, LANES))
    left = lanes < HD
    keeps = []

    def keep(name):
        copy = pltpu.make_async_copy(held[name], outs[name], keep_sems.at[len(keeps)])
        copy.start()
        keeps.append(copy)

    barrier = pltpu.get_barrier_semaphore()

    def greet(k, carry):
        pl.semaphore_signal(
            barrier, inc=1, device_id={"dp": lax.rem(me + k, devices)}, device_id_type=MESH
        )
        return carry

    lax.fori_loop(1, devices, greet, 0)
    for k in range(1, mp):
        pl.semaphore_signal(
            barrier, inc=1, device_id={"mp": lax.rem(mp_me + k, mp)}, device_id_type=MESH
        )

    token = lanes_of((1, rows)).astype(F32)
    picks, marks, query_places = [None], [None], []
    query_places.append(
        (lax.rem(lanes_of((1, heads * rows)), rows) + me * rows).astype(F32)
    )
    held[(K_PLACE, 0)][...] = query_places[0]
    for level, slot, deep in ((1, second_slot, 2), (2, third_slot, 3)):
        count = counts[level]
        slots = lax.broadcasted_iota(jnp.int32, (count, rows), 0)
        active = (depths[...] >= deep) & (slot[...] >= 0)
        chosen = jnp.where(active, slot[...], -1) == slots
        pick = jnp.where(chosen, 1.0, 0.0).astype(BF)
        held[(K_PICK, level)][...] = pick
        picks.append(pick)
        marks.append(
            jnp.min(jnp.where(chosen, token, float(rows)), axis=1, keepdims=True)
        )
    depth = w_query.shape[0]
    wide = jnp.zeros((1, LANES - depth), F32)
    gain_rows = jnp.concatenate(
        [jnp.concatenate([ref[...].astype(F32), wide], axis=1) for ref in (norm_first, norm_second, router)]
        + [jnp.zeros((LANES - 3, LANES), F32)],
        axis=0,
    )
    extra = gain_rows.T[:depth, :]
    rest = counts[1] - depth
    lane = lanes_of((depth, LANES))
    over = jnp.concatenate([marks[1][depth:, :], jnp.full((depth - rest, 1), float(rows), F32)], axis=0)
    extra = jnp.where(lane == 3, marks[1][:depth, :], extra)
    extra = jnp.where(lane == 4, over, extra)
    extra = jnp.where(lane == 5, marks[2], extra)
    pair = jnp.concatenate([w_key[...].astype(F32), w_value[...].astype(F32)], axis=1).astype(BF)
    start = 0
    for part in (
        w_query[...], pair, extra.astype(BF), w_out[...], w_gate[...], w_up[...], w_down[...],
    ):
        shard[:, start : start + part.shape[1]] = part
        start += part.shape[1]
    own = pltpu.make_async_copy(shard, weights.at[x, y, core], own_sem)
    own.start()
    spread = Spread(groups, x, y, core, shard, weights, held[K_PACKED, 0], send_sems, recv_sems)
    pl.semaphore_wait(barrier, devices - 1 + mp - 1)
    for g in range(3):
        spread.one(g)
    own.wait()
    for level, pick in ((1, picks[1]), (2, picks[2])):
        sublane = lax.broadcasted_iota(jnp.int32, (16, rows), 0)
        probe = jnp.where(sublane == 0, token, 1.0).astype(BF)
        found = dot_nt(probe, jnp.concatenate([pick] * heads, axis=0))
        place = jnp.where(found[1:2, :] > 0.5, found[0:1, :] + (me * rows).astype(F32), FAR)
        held[(K_PLACE, level)][...] = place
        query_places.append(place)
        table = jnp.concatenate([cosine_in[...], sine_in[...]], axis=1)
        turned = lax.dot_general(
            pick.astype(F32), table, (((1,), (0,)), ((), ())),
            preferred_element_type=F32, precision=lax.Precision.HIGHEST,
        )
        held[(K_COSINE, level)][...] = turned[:, :LANES]
        held[(K_SINE, level)][...] = turned[:, LANES:]
    spread.run(0, 3)
    spread.run(1, 4, 0)
    spread.run(2, 5, None, 0)
    spread.run(3, 6, 1, None, 0)

    gains = held[K_GAINS]
    columns = weights[:, :, :, :, mix + LANES : mix + 2 * LANES].reshape(model, LANES).astype(F32)
    gains[...] = columns.T[: gains.shape[0], :]
    keep(K_GAINS)

    def kv_copy(level, e, source_index):
        packed = held[(K_PACKED, level)]
        return pltpu.make_async_remote_copy(
            src_ref=packed.at[me], dst_ref=packed.at[me],
            send_sem=kv_send.at[level, e], recv_sem=kv_recv.at[level, source_index],
            device_id={"dp": e}, device_id_type=MESH,
        )

    def project(level, now):
        n = counts[level]
        name = lambda base: held[(base, level)]
        name(K_ROWS)[...] = now
        unit, unused = unit_of(now.astype(F32))
        normed = (unit * gains[0:1, :]).astype(BF)
        name(K_NORMED)[...] = normed
        cosine, sine = (cosine_in[...], sine_in[...]) if level == 0 else (name(K_COSINE)[...], name(K_SINE)[...])
        here = left[:n]
        tiles = [None] * (heads // 2 + 1)
        for t in range(heads // 2, -1, -2):
            low = max(t - 1, 0)
            both = dot_nn(normed, weights[:, :, :, :, low * LANES : (t + 1) * LANES].reshape(model, (t + 1 - low) * LANES))
            for j in range(low, t + 1):
                part = tile_of(both, j - low)
                if j == heads // 2:
                    part = part * jnp.where(here, cosine, 1.0) + swap_halves(part) * jnp.where(here, sine, 0.0)
                    if level == 0:
                        name(K_PACKED)[x, y, core] = part.astype(BF)
                        spread.one(spread.count)
                        continue
                    name(K_PACKED)[me] = part.astype(BF)

                    def send(k, carry):
                        kv_copy(level, devices - 1 - k, me).start()
                        return carry

                    lax.fori_loop(0, devices - 1 - me, send, 0)
                else:
                    tiles[j] = part * cosine + swap_halves(part) * sine

        def clear(e, carry):
            name(K_PACKED)[e] = jnp.zeros((n, 2 * HD), BF)
            return carry

        if level:
            lax.fori_loop(me + 1, devices, clear, 0)
        for t in range(heads // 2):
            scaled = tiles[t].astype(BF).astype(F32) * HD**-0.5
            name(K_QUERY)[2 * t * n : (2 * t + 1) * n, :] = jnp.where(here, scaled, 0.0).astype(BF)
            name(K_QUERY)[(2 * t + 1) * n : (2 * t + 2) * n, :] = jnp.where(
                here, pltpu.roll(scaled, HD, 1), 0.0
            ).astype(BF)
        width = heads * n
        query_t[:, :width] = name(K_QUERY)[...].T
        top[:, :width] = jnp.full((1, width), NEG, F32)
        total[:, :width] = jnp.zeros((1, width), F32)
        acc[:, :width] = jnp.zeros((2 * HD, width), F32)
        for base in (K_ROWS, K_NORMED, K_QUERY):
            keep((base, level))

    def group_of(level):
        return (4, 8, 16)[level]

    def block(level, b):
        n, group = counts[level], group_of(level)
        width = heads * n
        if level:
            for g in range(group):
                e = b * group + g

                @pl.when(e < me)
                def _(e=e):
                    kv_copy(level, me, e).wait_recv()

            part = held[K_PACKED, level][pl.ds(b * group, group)].reshape(group * n, 2 * HD)
        else:
            part = held[K_PACKED, level][b // 2, 2 * (b % 2) : 2 * (b % 2) + 2].reshape(group * n, 2 * HD)
        scores = dot_nn(part, query_t[:, :width])
        if level:
            place = held[(K_KEYS, level)][pl.ds(b * group, group)].reshape(group * n, LANES)
        else:
            place = (lax.broadcasted_iota(jnp.int32, (group * n, LANES), 0) + b * (group * n)).astype(F32)
        place = jnp.concatenate([place] * (width // LANES), axis=1)
        scores = jnp.where(place <= held[(K_PLACE, level)][...], scores, NEG)
        before = top[:, :width]
        peak = jnp.maximum(before, jnp.max(scores, axis=0, keepdims=True))
        soft = jnp.exp(scores - peak)
        fade = jnp.exp(before - peak)
        total[:, :width] = total[:, :width] * fade + jnp.sum(soft, axis=0, keepdims=True)
        acc[:, :width] = acc[:, :width] * fade + dot_tn(part, soft.astype(BF))
        top[:, :width] = peak

    def mix_heads(level):
        n = counts[level]
        width = heads * n
        mixed_t = acc[:, :width] / total[:, :width]
        held[(K_MIXED_T, level)][...] = mixed_t
        held[(K_LOG, level)][...] = top[:, :width] + jnp.log(total[:, :width])
        mixed = mixed_t.T
        for t in range(heads // 2):
            even = mixed[2 * t * n : (2 * t + 1) * n, :]
            odd = mixed[(2 * t + 1) * n : (2 * t + 2) * n, :]
            held[(K_MIXED, level)][:, t * LANES : (t + 1) * LANES] = jnp.where(
                left[:n], pltpu.roll(even, HD, 1), odd
            ).astype(BF)
        for base in (K_MIXED_T, K_LOG, K_MIXED, K_PACKED):
            keep((base, level))

    sums = [Sum(mp, mp_me, *sum_refs[4 * i : 4 * i + 4]) for i in range(2 * len(counts))]
    chunk = model // mp
    base_o = mix + 2 * LANES
    base_gu = base_o + mix
    base_d = base_gu + 2 * hidden

    def rows_of(start, wide, low, high):
        return weights[start // chunk, pl.ds(lax.rem(start, chunk) // LANES, wide // LANES), :, :, low:high].reshape(
            wide, high - low
        )

    def attn_sum(level):
        mixed_now = held[K_MIXED, level][...]
        total = sums[2 * level]
        total.start(lambda start, wide: dot_nt(mixed_now, rows_of(start, wide, base_o, base_gu)))
        return total

    def take_attn(level, total):
        attn = total.finish()
        held[K_ATTN, level][...] = attn
        rows_now = held[K_ROWS, level][...].astype(F32)
        unit, unused = unit_of(rows_now + attn.astype(F32))
        held[K_SECOND, level][...] = (unit * gains[1:2, :]).astype(BF)

    def widen(level):
        second, parts = held[K_SECOND, level][...], held[K_PARTS, level]
        for t in range(2 * hidden // 256):
            low = base_gu + t * 256
            parts[:, t * 256 : (t + 1) * 256] = dot_nn(
                second, weights[:, :, :, :, low : low + 256].reshape(model, 256)
            )
        n = counts[level]
        for t in range(hidden // LANES):
            cut = slice(t * LANES, (t + 1) * LANES)
            gate_part = parts[:, cut]
            up_part = parts[:, hidden + t * LANES : hidden + (t + 1) * LANES]
            hidden_v[:n, cut] = (gate_part * sigmoid(gate_part) * up_part).astype(BF)

    def narrow(level):
        hidden_now = hidden_v[: counts[level], :]
        total = sums[2 * level + 1]
        total.start(lambda start, wide: dot_nt(hidden_now, rows_of(start, wide, base_d, base_d + hidden)))
        for base in (K_ATTN, K_SECOND, K_PARTS):
            keep((base, level))
        rows_now = held[K_ROWS, level][...].astype(F32)
        gate = sigmoid(jnp.sum(rows_now * gains[2:3, :], axis=-1, keepdims=True))
        total.middle()
        ffn = total.finish()
        held[K_FFN, level][...] = ffn
        keep((K_FFN, level))
        update = (gate * (held[K_ATTN, level][...].astype(F32) + ffn.astype(F32))).astype(BF)
        if level:
            update = dot_tn(held[K_PICK, level][...], update)
        held[K_STATE][...] = held[K_STATE][...] + update.astype(F32)

    project(0, tokens[...])
    held[K_STATE][...] = tokens[...].astype(F32)
    for name in (
        (K_PLACE, 0), (K_PICK, 1), (K_PICK, 2), (K_PLACE, 1), (K_PLACE, 2), (K_COSINE, 1), (K_SINE, 1),
        (K_COSINE, 2), (K_SINE, 2),
    ):
        keep(name)
    spread.run(4, 7, 2)
    spread.two(spread.count)

    def key_places(e, carry):
        for level, lanes_at in ((1, (3, 4)), (2, (5,))):
            tile = weights[e // 8, lax.rem(e // 2, 4), lax.rem(e, 2), :, mix + LANES : mix + 2 * LANES].astype(F32)
            value = jnp.concatenate(
                [jnp.broadcast_to(tile[:, at : at + 1], (depth, LANES)) for at in lanes_at], axis=0
            )[: counts[level], :]
            held[(K_KEYS, level)][e] = jnp.where(
                value < rows, value + (e * rows).astype(F32), FAR
            )
        return carry

    lax.fori_loop(0, devices, key_places, 0)
    keep((K_KEYS, 1))
    keep((K_KEYS, 2))
    spread.run(5, 8, 3, 1)
    spread.three(spread.count)
    spread.step(6)
    spread.four(spread.count)
    spread.step(7)
    spread.five(spread.count)
    for b in range(devices // group_of(0)):

        @pl.when(b * group_of(0) <= me)
        def _(b=b):
            block(0, b)

        if b in (2, 5):
            spread.step(8 + b // 3)
    mix_heads(0)
    total_0 = attn_sum(0)
    spread.step(10)
    total_0.middle()
    spread.run(None, None, 9, 7, 6)
    spread.run(None, None, 10, 8, 7)
    take_attn(0, total_0)
    spread.run(None, None, None, 9, 8)
    widen(0)
    spread.run(None, None, None, 10, 9)
    spread.run(None, None, None, None, 10)
    narrow(0)
    keep(K_WEIGHTS)
    for level in range(1, len(counts)):
        now = dot_nn(held[K_PICK, level][...], held[K_STATE][...].astype(BF)).astype(BF)
        project(level, now)

        def one_block(b, carry, level=level):
            block(level, b)
            return carry

        lax.fori_loop(0, me // group_of(level) + 1, one_block, 0)
        mix_heads(level)
        attn_total = attn_sum(level)
        attn_total.middle()
        take_attn(level, attn_total)
        widen(level)
        narrow(level)
    keep(K_STATE)
    spread.drain()
    for item in sums:
        item.drain()
    for level in range(1, len(counts)):

        def sent(e, carry, level=level):
            kv_copy(level, e, me).wait_send()
            return carry

        lax.fori_loop(me + 1, devices, sent, 0)
    for copy in keeps:
        copy.wait()


def advance(tokens, depths, second_slot, third_slot, matrices, vectors, tables, heads, devices, mp, ident):
    counts = (tokens.shape[0], SECOND_SLOTS, THIRD_SLOTS)
    rows, model = tokens.shape
    depth, mix = matrices[0].shape
    hidden = matrices[4].shape[1]
    total = 2 * mix + 2 * LANES + 3 * hidden
    cuts = [0, *range(mix + 2 * LANES, total - 640, 512), total - 640, total - 256, total]
    groups = [(a, b, i % 2) for i, (a, b) in enumerate(zip(cuts[:-1], cuts[1:]))]
    shapes = {
        K_STATE: ((rows, model), F32),
        K_WEIGHTS: ((4, 4, 2, depth, total), BF),
        K_GAINS: ((8, model), F32),
    }
    for level, n in enumerate(counts):
        width = heads * n
        shapes[(K_PLACE, level)] = ((1, width), F32)
        if level:
            shapes[(K_PICK, level)] = ((n, rows), BF)
            shapes[(K_COSINE, level)] = ((n, LANES), F32)
            shapes[(K_SINE, level)] = ((n, LANES), F32)
            shapes[(K_KEYS, level)] = ((devices, n, LANES), F32)
        for base in (K_ROWS, K_NORMED, K_ATTN, K_FFN, K_SECOND):
            shapes[(base, level)] = ((n, model), BF)
        shapes[(K_PARTS, level)] = ((n, 2 * hidden), F32)
        shapes[K_PACKED, level] = (((devices,) if level else (4, 4, 2)) + (n, 2 * HD), BF)
        shapes[(K_QUERY, level)] = ((width, 2 * HD), BF)
        shapes[(K_MIXED_T, level)] = ((2 * HD, width), F32)
        shapes[(K_LOG, level)] = ((1, width), F32)
        shapes[(K_MIXED, level)] = ((n, mix), BF)
    names = tuple(shapes)
    args = (tokens, depths, second_slot, third_slot, *matrices, *vectors, *tables)
    width = heads * rows
    outs = pl.pallas_call(
        functools.partial(advance_kernel, counts, heads, devices, mp, hidden, groups, names),
        out_shape=tuple(jax.ShapeDtypeStruct(*shapes[name]) for name in names),
        in_specs=vmem(len(args)),
        out_specs=tuple([pl.BlockSpec(memory_space=pl.ANY)] * len(names)),
        scratch_shapes=[pltpu.VMEM(*shapes[name]) for name in names]
        + [
            pltpu.VMEM((depth, total), BF),
            pltpu.SemaphoreType.DMA(()),
            pltpu.SemaphoreType.DMA((len(groups) + 1, 8)),
            pltpu.SemaphoreType.DMA((len(groups) + 1, 8)),
            pltpu.VMEM((2 * HD, width), BF),
            pltpu.VMEM((1, width), F32),
            pltpu.VMEM((1, width), F32),
            pltpu.VMEM((2 * HD, width), F32),
            pltpu.VMEM((rows, hidden), BF),
            pltpu.SemaphoreType.DMA((len(names),)),
            pltpu.SemaphoreType.DMA((len(counts), devices)),
            pltpu.SemaphoreType.DMA((len(counts), devices)),
        ]
        + [item for n in counts for _ in range(2) for item in sum_scratch(mp, n, model)],
        compiler_params=pltpu.CompilerParams(
            collective_id=ident, has_side_effects=True, vmem_limit_bytes=VMEM_LIMIT
        ),
        name="advance",
    )(*args)
    kept = dict(zip(names, outs))
    kept[K_PACKED, 0] = kept[K_PACKED, 0].reshape(devices, rows, 2 * HD)
    return kept


SLOTS = 5
CORE_SLOTS = 3
GROUP = 512


class Collect:
    def __init__(self, spans, groups, x, y, core, turned, rights, vectors, store, slots, core_recv, relay_recv, first_recv, mid, last_recv, send_sems, recv_sems, credit, turn):
        self.spans, self.groups = spans, groups
        self.x, self.y, self.core = x, y, core
        self.turned, self.rights, self.vectors, self.store, self.slots = turned, rights, vectors, store, slots
        self.core_recv, self.relay_recv, self.first_recv = core_recv, relay_recv, first_recv
        self.mid, self.last_recv, self.credit = mid, last_recv, credit
        self.send_sems, self.recv_sems = send_sems, recv_sems
        self.turn = turn
        self.waits = [{} for _ in groups]
        self.done = set()

    def remote(self, g, index, source, target, device):
        copy = pltpu.make_async_remote_copy(
            src_ref=source, dst_ref=target, send_sem=self.send_sems.at[g, index],
            recv_sem=self.recv_sems.at[g, index], device_id=device, device_id_type=MESH,
        )
        copy.start()
        return copy

    def held(self, slot, axis, at, first, count):
        if axis == 0:
            return self.slots.at[slot, at, pl.ds(first, count), self.core]
        return self.slots.at[slot, pl.ds(first, count), at, self.core]

    def zero(self, g):
        slot, waits = g % SLOTS, self.waits
        if g >= SLOTS:
            for stage in range(3):
                for copy in waits[g - SLOTS][stage]:
                    copy.wait_send()
        column = 0
        for section, low, high in self.groups[g][1]:
            wide = high - low
            if section < 4:
                if section not in self.done:
                    self.done.add(section)
                    self.turn(section)
                base = self.spans[section][0]

            def rows_of(m, carry, section=section, low=low, high=high, column=column, wide=wide):
                start = pl.multiple_of(m * 1024, 1024)
                if section < 4:
                    value = dot_nn(
                        self.turned[section % 2, pl.ds(start, 1024), :], self.rights[:, base + low : base + high]
                    )
                else:
                    few = self.vectors[:, pl.ds(start, 1024)]
                    value = jnp.concatenate([few, jnp.zeros((LANES - few.shape[0], 1024), F32)], axis=0).T
                self.slots[slot, pl.ds(m * 2, 2), :, :, :, column : column + wide] = (
                    value.astype(BF).reshape(2, 4, 2, 64, wide)
                )
                return carry

            lax.fori_loop(0, 2, rows_of, 0)
            column += wide
        if g >= CORE_SLOTS:
            pl.semaphore_wait(self.credit, 1)
        waits[g][0] = [
            self.remote(
                g, 0, self.slots.at[slot, :, :, 1 - self.core, :, :column],
                self.core_recv.at[g % CORE_SLOTS, :, :, :, :column], peer(self.x, self.y, 1 - self.core),
            )
        ]

    def first(self, g):
        slot, (width, _, axis) = g % SLOTS, self.groups[g]
        waits, slots = self.waits, self.slots
        waits[g][0][0].wait_recv()

        def add(i, carry):
            slots[slot, i, :, self.core, :, :width] = (
                slots[slot, i, :, self.core, :, :width] + self.core_recv[g % CORE_SLOTS, i, :, :, :width]
            )
            return carry

        lax.fori_loop(0, 4, add, 0)
        if g + CORE_SLOTS < len(self.groups):
            pl.semaphore_signal(
                self.credit, inc=1, device_id=peer(self.x, self.y, 1 - self.core), device_id_type=MESH
            )
        at = self.x if axis == 0 else self.y
        waits[g][1] = [
            self.remote(
                g, 1 + i, self.held(slot, axis, lax.rem(at + 2, 4), 2 * i, 2).at[:, :, :width],
                self.relay_recv.at[g, i, :, :, :width], shifted(self.x, self.y, self.core, axis, k),
            )
            for i, k in enumerate((1, 3))
        ]

    def second(self, g):
        slot, (width, _, axis) = g % SLOTS, self.groups[g]
        waits, slots = self.waits, self.slots
        at = self.x if axis == 0 else self.y
        waits[g][2] = []
        for i, k in enumerate((1, 3)):
            waits[g][1][i].wait_recv()
            there = lax.rem(at + k, 4)
            for j in range(2):
                b = 2 * i + j
                where = (slot, there, b, self.core) if axis == 0 else (slot, b, there, self.core)
                where = where + (slice(None), slice(0, width))
                slots[where] = slots[where] + self.relay_recv[g, i, j, :, :width]
            waits[g][2].append(
                self.remote(
                    g, 3 + i, self.held(slot, axis, there, 0, 4).at[:, :, :width],
                    self.first_recv.at[g, i, :, :, :width], shifted(self.x, self.y, self.core, axis, k),
                )
            )

    def third(self, g):
        slot, (width, _, axis) = g % SLOTS, self.groups[g]
        waits, slots = self.waits, self.slots
        at, other = (self.x, self.y) if axis == 0 else (self.y, self.x)
        for copy in waits[g][2]:
            copy.wait_recv()
        for b in range(4):
            where = (slot, at, b, self.core) if axis == 0 else (slot, b, at, self.core)
            self.mid[g, b, :, :width] = (
                slots[where + (slice(None), slice(0, width))].astype(F32)
                + self.first_recv[g, 0, b, :, :width].astype(F32)
                + self.first_recv[g, 1, b, :, :width].astype(F32)
            ).astype(BF)
        waits[g][3] = [
            self.remote(
                g, 4 + k, self.mid.at[g, lax.rem(other + k, 4), :, :width],
                self.last_recv.at[g, k - 1, :, :width],
                shifted(self.x, self.y, self.core, 1 - axis, k),
            )
            for k in (2, 1, 3)
        ]

    def fourth(self, g):
        width, pieces, axis = self.groups[g]
        other = self.y if axis == 0 else self.x
        value = self.mid[g, other, :, :width].astype(F32)
        for copy in self.waits[g][3]:
            copy.wait_recv()
        for k in range(3):
            value = value + self.last_recv[g, k, :, :width].astype(F32)
        column = 0
        for section, low, high in pieces:
            self.store(section, low, value[:, column : column + high - low])
            column += high - low

    def run(self, *groups):
        for work, g in zip((self.zero, self.first, self.second, self.third, self.fourth), groups):
            if g is not None and 0 <= g < len(self.groups):
                work(g)

    def step(self, i):
        self.run(i, i - 1, i - 2, i - 4, i - 5)

    def drain(self):
        count = len(self.groups)
        for g in range(count):
            for stage in range(4):
                if stage == 3 or g >= count - SLOTS:
                    for copy in self.waits[g][stage]:
                        copy.wait_send()


def finish_kernel(n, heads, devices, mp, group, levels, spans, groups, *refs):
    refs = list(refs)
    flow, gains, query_place, query, packed, mixed_t, log_total, cosine, sine = [refs.pop(0) for _ in range(9)]
    rows_in, attn_in, logit, vecs = [refs.pop(0) for _ in range(4)]
    w_hbm = refs.pop(0)
    sources = [[refs.pop(0) if level or i not in (4, 7) else None for i in range(8)] for level in range(len(levels))]
    flow_out, q_out, k_out, v_out, out_out, gate_out, up_out, down_out, vec_out = [refs.pop(0) for _ in range(9)]
    query_t, grad_rows, grad_t, acc, delta, send_buf, recv_buf, kv_send, kv_recv = [refs.pop(0) for _ in range(9)]
    w_qkv, w_sem, w_gu, gu_sems, middle = [refs.pop(0) for _ in range(5)]
    sum_refs = [[refs.pop(0) for _ in range(4)] for _ in range(2)]
    (lefts, turned, rights, vectors, slots, core_recv, relay_recv, first_recv, mid, last_recv,
     loads, send_sems, recv_sems, credit) = refs
    me, mp_me = lax.axis_index("dp"), lax.axis_index("mp")
    x, y, core = plane(me)
    hidden = gate_out.shape[1]
    mix = q_out.shape[1]
    base_o = mix + 2 * LANES
    load_o = pltpu.make_async_copy(w_hbm.at[:, base_o : base_o + mix], w_qkv.at[:, :mix], w_sem)
    load_o.start()
    wide = w_gu.shape[1]
    pieces = [(mp_me + k, piece) for piece in range(PIECES) for k in Sum.order]
    pieces += [(mp_me, piece) for piece in range(PIECES)]
    gu_loads = []

    def load_gu():
        i = len(gu_loads)
        if i < len(pieces):
            start = pl.multiple_of((lax.rem(pieces[i][0], mp) * PIECES + pieces[i][1]) * wide, wide)
            copy = pltpu.make_async_copy(
                w_hbm.at[pl.ds(start, wide), base_o + mix : base_o + mix + 2 * hidden],
                w_gu.at[i % w_gu.shape[0]], gu_sems.at[i % w_gu.shape[0]],
            )
            copy.start()
            gu_loads.append(copy)

    for _ in range(w_gu.shape[0]):
        load_gu()
    fetches = [[] for _ in range(4)]

    def fetch(s, side):
        row = 0
        for level, count in enumerate(levels):
            low, high = spans[s]
            target = (lefts.at[s % 2, row : row + count], rights.at[row : row + count, low:high])[side]
            if sources[level][2 * s + side] is not None:
                copy = pltpu.make_async_copy(
                    sources[level][2 * s + side], target, loads.at[level, 2 * s + side]
                )
                copy.start()
                fetches[s].append(copy)
            row += count

    for s in range(4):
        if s < 2:
            fetch(s, 0)
        fetch(s, 1)

    barrier = pltpu.get_barrier_semaphore()

    def greet(k, carry):
        pl.semaphore_signal(
            barrier, inc=1, device_id={"dp": lax.rem(me + k, devices)}, device_id_type=MESH
        )
        return carry

    lax.fori_loop(1, devices, greet, 0)
    for k in range(1, mp):
        pl.semaphore_signal(
            barrier, inc=1, device_id={"mp": lax.rem(mp_me + k, mp)}, device_id_type=MESH
        )

    def turn(section):
        for copy in fetches[section]:
            copy.wait()
        turned[section % 2] = lefts[section % 2].T
        if section < 2:
            fetch(section + 2, 0)

    def store(section, low, value):
        high = low + value.shape[1]
        if section == 0:
            middle_cut = min(max(hidden - low, 0), high - low)
            if middle_cut:
                gate_out[:, low : low + middle_cut] = value[:, :middle_cut]
            if low + middle_cut < high:
                up_out[:, low + middle_cut - hidden : high - hidden] = value[:, middle_cut:]
        elif section == 1:
            down_out[:, low:high] = value
        elif section == 2:
            out_out[:, low:high] = value
        elif section == 3:
            if low < mix:
                q_out[:, low : min(high, mix)] = value[:, : min(high, mix) - low]
            if high > mix:
                k_out[...] = value[:, mix - low : mix - low + HD]
                v_out[...] = value[:, mix - low + HD :]
        else:
            vec_out[...] = value.T[: vec_out.shape[0], :]

    work = Collect(
        spans, groups, x, y, core, turned, rights, vectors, store, slots, core_recv, relay_recv,
        first_recv, mid, last_recv, send_sems, recv_sems, credit, turn,
    )
    pl.semaphore_wait(barrier, devices - 1 + mp - 1)
    work.step(0)

    update = flow[...].astype(BF).astype(F32)
    level = rows_in[...].astype(F32)
    gate = sigmoid(jnp.sum(level * gains[2:3, :], axis=-1, keepdims=True))
    parts_now = rights[0:n, : 2 * hidden]
    used = []

    def gu_piece(start, size):
        i = len(used)
        used.append(i)
        gu_loads[i].wait()
        value = dot_nt(parts_now, w_gu[i % w_gu.shape[0]])
        load_gu()
        return value

    head = Sum(mp, mp_me, *sum_refs[0])
    head.start(gu_piece)
    work.step(1)
    work.step(2)
    head.middle()
    work.step(3)
    grad_second = head.finish().astype(F32)
    unit, factor = unit_of(level + attn_in[...].astype(F32))
    vectors[...] = jnp.zeros(vectors.shape, F32)
    vectors[1:2, :] = (
        jnp.sum(grad_second * unit, axis=0, keepdims=True) + vecs[0:1, :] + vecs[1:2, :]
    )
    middle[...] = unit_back(grad_second * gains[1:2, :], unit, factor)
    grad_attn = (gate * update + middle[...]).astype(BF)
    lefts[0, 0:n, :] = grad_attn
    load_o.wait()
    grad_mixed = dot_nn(grad_attn, w_qkv[:, :mix]).astype(BF).astype(F32)
    load_w = pltpu.make_async_copy(w_hbm.at[:, : w_qkv.shape[1]], w_qkv, w_sem)
    load_w.start()
    work.step(4)
    left = lanes_of((n, LANES)) < HD
    for t in range(heads // 2):
        part = grad_mixed[:, t * LANES : (t + 1) * LANES]
        grad_rows[2 * t * n : (2 * t + 1) * n, :] = jnp.where(
            left, 0.0, pltpu.roll(part, HD, 1)
        ).astype(BF)
        grad_rows[(2 * t + 1) * n : (2 * t + 2) * n, :] = jnp.where(left, 0.0, part).astype(BF)
    query_t[...] = query[...].T
    grad_t[...] = grad_rows[...].T
    delta[...] = jnp.sum(grad_t[...].astype(F32) * mixed_t[...], axis=0, keepdims=True)
    acc[...] = jnp.zeros(acc.shape, F32)
    width = heads * n

    def send_copy(e, source_index):
        return pltpu.make_async_remote_copy(
            src_ref=send_buf.at[e], dst_ref=recv_buf.at[source_index],
            send_sem=kv_send.at[e], recv_sem=kv_recv.at[source_index],
            device_id={"dp": e}, device_id_type=MESH,
        )

    def one_block(b):
        part = packed[b * group : (b + 1) * group].reshape(group * n, 2 * HD)
        scores = dot_nn(part, query_t[...])
        place = (lax.broadcasted_iota(jnp.int32, (group * n, LANES), 0) + b * (group * n)).astype(F32)
        place = jnp.concatenate([place] * (width // LANES), axis=1)
        scores = jnp.where(place <= query_place[...], scores, NEG)
        weights = jnp.exp(scores - log_total[...])
        grad_weights = dot_nn(part, grad_t[...])
        grad_scores = (weights * (grad_weights - delta[...])).astype(BF)
        grad_part = dot_nn(grad_scores, query[...]) + dot_nn(weights.astype(BF), grad_rows[...])
        send_buf[b * group : (b + 1) * group] = grad_part.astype(BF).reshape(group, n, 2 * HD)
        acc[...] += dot_tn(part, grad_scores)
        for e in range(b * group, (b + 1) * group):

            @pl.when(e < me)
            def _(e=e):
                send_copy(e, me).start()

    blocks = devices // group
    for b in range(blocks):
        if b in (2, 4, 6):
            work.step(4 + b // 2)

        @pl.when(b * group <= me)
        def _(b=b):
            one_block(b)

    work.step(8)
    grad_query = acc[...].T * HD**-0.5
    low = spans[3][0]
    for t in range(heads // 2):
        even = grad_query[2 * t * n : (2 * t + 1) * n, :]
        odd = grad_query[(2 * t + 1) * n : (2 * t + 2) * n, :]
        part = jnp.where(left, even, pltpu.roll(odd, HD, 1))
        rights[0:n, low + t * LANES : low + (t + 1) * LANES] = turn_back(part, cosine[...], sine[...], False)
    work.step(9)

    def add(e, carry):
        send_copy(me, e).wait_recv()
        return carry + recv_buf[e].astype(F32)

    part = lax.fori_loop(me + 1, devices, add, send_buf[me].astype(F32))
    rights[0:n, low + mix : low + mix + LANES] = turn_back(part, cosine[...], sine[...], True)
    load_w.wait()
    grad_now = rights[0:n, low : spans[3][1]]

    def first_piece(start, wide):
        return dot_nt(grad_now, w_qkv[pl.ds(start, wide), :])

    total = Sum(mp, mp_me, *sum_refs[1])
    total.start(first_piece)
    work.step(10)
    total.middle()
    work.run(None, 10, 9, 7, 6)
    grad_normed = total.finish().astype(F32)
    unit, factor = unit_of(level)
    vectors[0:1, :] = jnp.sum(grad_normed * unit, axis=0, keepdims=True) + vecs[3:4, :] + vecs[4:5, :]
    vectors[2:3, :] = jnp.sum(level * logit[...], axis=0, keepdims=True) + vecs[5:6, :] + vecs[6:7, :]
    flow_out[...] = flow[...] + (
        unit_back(grad_normed * gains[0:1, :], unit, factor) + middle[...] + logit[...] * gains[2:3, :]
    ).astype(BF).astype(F32)
    work.run(11, None, 10, 8, 7)
    work.run(None, 11, None, 9, 8)
    work.run(None, None, 11, 10, 9)
    work.run(None, None, None, 11, 10)
    work.run(None, None, None, None, 11)
    work.drain()
    head.drain()
    total.drain()

    def sent(e, carry):
        send_copy(e, me).wait_send()
        return carry

    lax.fori_loop(0, me, sent, 0)


def finish(flow, gains, attention, tail, vecs, weights, levels, heads, devices, mp, depth, ident):
    n, model = levels[0][0].shape
    width = heads * n
    group = 512 // n
    mix = heads * HD
    widths = [levels[1][i].shape[1] for i in (1, 3, 5, 7)] + [LANES]
    spans, total = [], 0
    for wide in widths:
        spans.append((total, total + wide))
        total += wide
    pieces = []
    for section, wide in enumerate(widths):
        pieces += [(section, low, low + LANES) for low in range(0, wide, LANES)]
    groups = []
    per = GROUP // LANES
    cuts = [*range(0, len(pieces) - 1, per), len(pieces) - 1, len(pieces)]
    for index, end in zip(cuts[:-1], cuts[1:]):
        merged = []
        for section, low, high in pieces[index:end]:
            if merged and merged[-1][0] == section:
                merged[-1] = (section, merged[-1][1], high)
            else:
                merged.append((section, low, high))
        wide = sum(high - low for _, low, high in merged)
        groups.append((wide, merged, len(groups) % 2))
    counts = [level[0].shape[0] for level in levels]
    rows = sum(counts)
    hidden = widths[1]
    many = len(groups)
    whole = [flow, gains, *attention, *tail, vecs]
    args = whole + [weights] + [item for level in levels for item in level if item is not None]
    return pl.pallas_call(
        functools.partial(finish_kernel, n, heads, devices, mp, group, counts, spans, groups),
        out_shape=(
            jax.ShapeDtypeStruct(flow.shape, F32),
            jax.ShapeDtypeStruct((depth, mix), F32),
            jax.ShapeDtypeStruct((depth, HD), F32),
            jax.ShapeDtypeStruct((depth, HD), F32),
            jax.ShapeDtypeStruct((depth, mix), F32),
            jax.ShapeDtypeStruct((depth, hidden), F32),
            jax.ShapeDtypeStruct((depth, hidden), F32),
            jax.ShapeDtypeStruct((depth, hidden), F32),
            jax.ShapeDtypeStruct((8, depth), F32),
        ),
        in_specs=vmem(len(whole)) + [pl.BlockSpec(memory_space=pl.ANY)] * (len(args) - len(whole)),
        out_specs=tuple(vmem(9)),
        scratch_shapes=[
            pltpu.VMEM((2 * HD, width), BF),
            pltpu.VMEM((width, 2 * HD), BF),
            pltpu.VMEM((2 * HD, width), BF),
            pltpu.VMEM((2 * HD, width), F32),
            pltpu.VMEM((1, width), F32),
            pltpu.VMEM((devices, n, 2 * HD), BF),
            pltpu.VMEM((devices, n, 2 * HD), BF),
            pltpu.SemaphoreType.DMA((devices,)),
            pltpu.SemaphoreType.DMA((devices,)),
            pltpu.VMEM((model, mix + 2 * HD), BF),
            pltpu.SemaphoreType.DMA(()),
            pltpu.VMEM((3, model // mp // PIECES, 2 * hidden), BF),
            pltpu.SemaphoreType.DMA((3,)),
            pltpu.VMEM((n, model), F32),
            *sum_scratch(mp, n, model),
            *sum_scratch(mp, n, model),
            pltpu.VMEM((2, rows, model), BF),
            pltpu.VMEM((2, model, rows), BF),
            pltpu.VMEM((rows, spans[3][1]), BF),
            pltpu.VMEM((8, model), F32),
            pltpu.VMEM((SLOTS, 4, 4, 2, depth, GROUP), BF),
            pltpu.VMEM((CORE_SLOTS, 4, 4, depth, GROUP), BF),
            pltpu.VMEM((many, 2, 2, depth, GROUP), BF),
            pltpu.VMEM((many, 2, 4, depth, GROUP), BF),
            pltpu.VMEM((many, 4, depth, GROUP), BF),
            pltpu.VMEM((many, 3, depth, GROUP), BF),
            pltpu.SemaphoreType.DMA((len(levels), 8)),
            pltpu.SemaphoreType.DMA((many, 8)),
            pltpu.SemaphoreType.DMA((many, 8)),
            pltpu.SemaphoreType.REGULAR,
        ],
        compiler_params=pltpu.CompilerParams(
            collective_id=ident, has_side_effects=True, vmem_limit_bytes=63 * 1024 * 1024
        ),
        name="finish",
    )(*args)


def hand_over_kernel(count, *refs):
    vectors, sources, targets = refs[0], refs[1 : 1 + count], refs[1 + count :]
    for source, target in zip(sources, targets):
        target[...] = source[...]
    for i, target in enumerate(targets[count:]):
        target[...] = vectors[i, :]


def hand_over(items, vectors):
    count = len(items)
    return pl.pallas_call(
        functools.partial(hand_over_kernel, count),
        out_shape=tuple(
            [jax.ShapeDtypeStruct(item.shape, F32) for item in items]
            + [jax.ShapeDtypeStruct(vectors.shape[1:], F32)] * 3
        ),
        in_specs=vmem(1 + count),
        out_specs=tuple(vmem(count + 3)),
        name="hand_over",
    )(vectors, *items)


def rotary_tables(place):
    freq = jnp.exp(jnp.arange(HD // 2, dtype=F32) * (-2.0 * math.log(ROPE_BASE) / HD))
    angle = place.astype(F32)[:, None] * freq[None, :]
    cosine, sine = jnp.cos(angle), jnp.sin(angle)
    return (
        jnp.concatenate([cosine] * 4, axis=1),
        jnp.concatenate([-sine, sine, -sine, sine], axis=1),
    )


def local(
    tokens, depths, second_slot, third_slot, w_query, w_key, w_value, w_out, w_gate, w_up,
    w_down, norm_first, norm_second, router, cotangent,
):
    me = lax.axis_index("dp")
    devices, mp = lax.axis_size("dp"), lax.axis_size("mp")
    rows = tokens.shape[0]
    heads = w_query.shape[1] // HD
    depth = w_query.shape[0]
    home = rotary_tables(jnp.arange(rows, dtype=jnp.int32) + me * rows)

    def row(values):
        return values.reshape(1, -1)

    kept = advance(
        tokens, row(depths), row(second_slot), row(third_slot),
        (w_query, w_key, w_value, w_out.T, w_gate, w_up, w_down.T),
        (row(norm_first), row(norm_second), row(router)), home, heads, devices, mp, 0,
    )
    weights = kept[K_WEIGHTS].reshape(devices * depth, -1)
    gains = kept[K_GAINS]
    back = retreat(cotangent, kept, weights, heads, devices, mp, 1)
    terms = []
    for level in range(3):
        terms.append(
            tuple(back.get((base, level), kept.get((base, level))) for base in (
                K_SECOND, K_PARTS_GRAD, K_GRAD_FFN, K_HIDDEN, K_GRAD_ATTN, K_MIXED, K_NORMED, K_GRAD_QKV
            ))
        )
    attention = [kept[(base, 0)] for base in (K_PLACE, K_QUERY, K_PACKED, K_MIXED_T, K_LOG)]
    results = finish(
        back[K_FLOW_OUT], gains, (*attention, *home),
        (kept[(K_ROWS, 0)], kept[(K_ATTN, 0)], back[(K_LOGIT, 0)]), back[K_VECS], weights, terms,
        heads, devices, mp, depth, 2,
    )
    (state, flow, query_grad, key_grad, value_grad, out_grad, gate_grad, up_grad, down_grad,
     first_grad, second_grad, router_grad) = hand_over((kept[K_STATE], *results[:-1]), results[-1])
    return (
        state, flow, query_grad, key_grad, value_grad, out_grad.T, gate_grad, up_grad, down_grad.T,
        first_grad, second_grad, router_grad,
    )


def solution(mesh):
    in_specs = (
        P("dp", None), P("dp"), P("dp"), P("dp"), P("dp", "mp"), P("dp", "mp"), P("dp", "mp"),
        P("mp", "dp"), P("dp", "mp"), P("dp", "mp"), P("mp", "dp"), P("dp"), P("dp"), P("dp"),
        P("dp", None),
    )
    out_specs = (
        P("dp", None), P("dp", None), P("dp", "mp"), P("dp", "mp"), P("dp", "mp"), P("mp", "dp"),
        P("dp", "mp"), P("dp", "mp"), P("mp", "dp"), P("dp"), P("dp"), P("dp"),
    )
    return jax.shard_map(local, mesh=mesh, in_specs=in_specs, out_specs=out_specs, check_vma=False)
```

```python
import functools
import math

import jax
import jax.numpy as jnp
from jax import lax
from jax.experimental import pallas as pl
from jax.experimental.pallas import tpu as pltpu
from jax.sharding import PartitionSpec as P

HD = 64
SECOND_SLOTS = 96
THIRD_SLOTS = 64
EPS = 1e-05
NEG = -1e30
ROPE_BASE = 10000.0
FAR = 1e9
BF = jnp.bfloat16
F32 = jnp.float32
MESH = pl.DeviceIdType.MESH

(K_ROWS, K_NORMED, K_ATTN, K_FFN, K_SECOND, K_PARTS, K_PACKED, K_QUERY, K_MIXED_T, K_LOG, K_MIXED, K_PLACE, K_PICK, K_COSINE, K_SINE, K_KEYS, K_STATE, K_WEIGHTS, K_GAINS, K_FLOW, K_FLOW_OUT, K_VECS, K_GRAD_QKV, K_GRAD_FFN, K_HIDDEN, K_PARTS_GRAD, K_GRAD_ATTN, K_GRAD_MIXED, K_MIDDLE, K_LOGIT, K_HEAD, K_TAIL, K_D, K_GU, K_O, K_QKV) = range(36)

LANES = 128
VMEM_LIMIT = 63 * 1024 * 1024


def dot_nn(left, right):
    return lax.dot_general(left, right, (((1,), (0,)), ((), ())), preferred_element_type=F32)


def dot_nt(left, right):
    return lax.dot_general(left, right, (((1,), (1,)), ((), ())), preferred_element_type=F32)


def dot_tn(left, right):
    return lax.dot_general(left, right, (((0,), (0,)), ((), ())), preferred_element_type=F32)


def unit_of(values):
    factor = lax.rsqrt(jnp.mean(values * values, axis=-1, keepdims=True) + EPS)
    return values * factor, factor


def unit_back(shaped, unit, factor):
    return factor * (shaped - unit * jnp.mean(shaped * unit, axis=-1, keepdims=True))


def sigmoid(values):
    return 1.0 / (1.0 + jnp.exp(-values))


def lanes_of(shape):
    return lax.broadcasted_iota(jnp.int32, shape, 1)


def swap_halves(tile):
    first = lax.rem(lanes_of(tile.shape), HD) < HD // 2
    return jnp.where(first, pltpu.roll(tile, LANES - HD // 2, 1), pltpu.roll(tile, HD // 2, 1))


def turn_back(part, cosine, sine, packed):
    if packed:
        left = lanes_of(part.shape) < HD
        cosine, sine = jnp.where(left, cosine, 1.0), jnp.where(left, sine, 0.0)
    return (part * cosine - swap_halves(part) * sine).astype(BF)


def tile_of(values, index):
    return values[:, index * LANES : (index + 1) * LANES]


def signal_all(group, me, axis):
    barrier = pltpu.get_barrier_semaphore()
    for k in range(1, group):
        pl.semaphore_signal(
            barrier, inc=1, device_id={axis: lax.rem(me + k, group)}, device_id_type=MESH
        )
    pl.semaphore_wait(barrier, group - 1)


PIECES = 2


class Sum:
    order = (2, 1, 3)

    def __init__(self, group, me, send, recv, full, sems):
        self.group, self.me, self.send, self.recv, self.full, self.sems = group, me, send, recv, full, sems
        self.wide = send.shape[-1]

    def remote(self, source, target, stage, k, piece):
        copy = pltpu.make_async_remote_copy(
            src_ref=source, dst_ref=target, send_sem=self.sems.at[stage, k - 1, piece],
            recv_sem=self.sems.at[stage + 1, k - 1, piece],
            device_id={"mp": lax.rem(self.me + k, self.group)}, device_id_type=MESH,
        )
        copy.start()
        return copy

    def start(self, make_piece):
        self.make, self.out, self.back = make_piece, [], []
        for piece in range(PIECES):
            copies = []
            for k in self.order:
                at = (k - 1, piece)
                self.send[at] = self.part(lax.rem(self.me + k, self.group), piece).astype(BF)
                copies.append(self.remote(self.send.at[at], self.recv.at[at], 0, k, piece))
            self.out.append(copies)

    def part(self, c, piece):
        start = c * (PIECES * self.wide) + piece * self.wide
        return self.make(pl.multiple_of(start, self.wide), self.wide)

    def middle(self):
        for piece in range(PIECES):
            total = self.part(self.me, piece).astype(BF).astype(F32)
            for k, copy in zip(self.order, self.out[piece]):
                copy.wait_recv()
                total = total + self.recv[k - 1, piece].astype(F32)
            self.full[self.me, piece] = total.astype(BF)
            where = self.full.at[self.me, piece]
            self.back.append([self.remote(where, where, 2, k, piece) for k in self.order])

    def finish(self):
        for copies in self.back:
            for copy in copies:
                copy.wait_recv()
        return jnp.concatenate(
            [self.full[c, piece] for c in range(self.group) for piece in range(PIECES)], axis=1
        )

    def drain(self):
        for copies in self.out + self.back:
            for copy in copies:
                copy.wait_send()


def vmem(count):
    return [pl.BlockSpec(memory_space=pltpu.VMEM)] * count


def sum_scratch(mp, n, model):
    wide = model // mp // PIECES
    return [
        pltpu.VMEM((mp - 1, PIECES, n, wide), BF),
        pltpu.VMEM((mp - 1, PIECES, n, wide), BF),
        pltpu.VMEM((mp, PIECES, n, wide), BF),
        pltpu.SemaphoreType.DMA((4, mp - 1, PIECES)),
    ]


def retreat_kernel(counts, heads, devices, mp, hidden, ins, names, inner, *refs):
    refs = list(refs)
    sources = {name: refs.pop(0) for name in ins}
    w_hbm = refs.pop(0)
    outs = {name: refs.pop(0) for name in names}
    held = {name: refs.pop(0) for name in ins}
    held.update({name: refs.pop(0) for name in names + inner})
    w_qkv, w_o, w_gu, w_d, fetch_sems, w_sems, keep_sems = [refs.pop(0) for _ in range(7)]
    query_t, grad_rows, grad_t, acc, delta = [refs.pop(0) for _ in range(5)]
    buffers = {level: [refs.pop(0) for _ in range(4)] for level in (1, 2)}
    sum_refs = {key: [refs.pop(0) for _ in range(4)] for key in ((K_HEAD, 2), (K_TAIL, 2), (K_HEAD, 1), (K_TAIL, 1))}
    me, mp_me = lax.axis_index("dp"), lax.axis_index("mp")
    model = w_o.shape[0]
    mix = heads * HD
    loads, keeps = {}, []

    def fetch(name):
        loads[name] = pltpu.make_async_copy(sources[name], held[name], fetch_sems.at[ins.index(name)])
        loads[name].start()

    def load(name, ref, start, index):
        loads[name] = pltpu.make_async_copy(w_hbm.at[:, start : start + ref.shape[1]], ref, w_sems.at[index])
        loads[name].start()

    def get(name):
        if name in loads:
            loads.pop(name).wait()
        return held[name]

    def need(name):
        if name in loads:
            loads.pop(name).wait()

    def keep(name):
        copy = pltpu.make_async_copy(held[name], outs[name], keep_sems.at[len(keeps)])
        copy.start()
        keeps.append(copy)

    base_o = mix + 2 * LANES
    for name in (K_FLOW, K_GAINS, (K_PICK, 2), (K_ROWS, 2), (K_ATTN, 2), (K_FFN, 2), (K_PARTS, 2)):
        fetch(name)
    load(K_D, w_d, base_o + mix + 2 * hidden, 0)
    load(K_GU, w_gu, base_o + mix, 1)
    load(K_O, w_o, base_o, 2)
    load(K_QKV, w_qkv, 0, 3)
    for name in ins:
        if name not in loads:
            fetch(name)

    barrier = pltpu.get_barrier_semaphore()

    def greet(k, carry):
        pl.semaphore_signal(
            barrier, inc=1, device_id={"dp": lax.rem(me + k, devices)}, device_id_type=MESH
        )
        return carry

    lax.fori_loop(1, devices, greet, 0)
    for k in range(1, mp):
        pl.semaphore_signal(
            barrier, inc=1, device_id={"mp": lax.rem(mp_me + k, mp)}, device_id_type=MESH
        )
    sums = {key: Sum(mp, mp_me, *items) for key, items in sum_refs.items()}
    vecs = held[K_VECS]
    vecs[...] = jnp.zeros(vecs.shape, F32)
    gate_of = {}

    def head(level):
        n = counts[level]
        name = lambda base: held[(base, level)]
        grad_update = get(K_FLOW)[...].astype(BF)
        if level:
            grad_update = dot_nn(get((K_PICK, level))[...], grad_update)
        grad_update = grad_update.astype(F32)
        rows_now = get((K_ROWS, level))[...].astype(F32)
        attn_now = get((K_ATTN, level))[...].astype(F32)
        gains = get(K_GAINS)
        gate = sigmoid(jnp.sum(rows_now * gains[2:3, :], axis=-1, keepdims=True))
        logit = jnp.sum(
            grad_update * (attn_now + get((K_FFN, level))[...].astype(F32)), axis=-1, keepdims=True
        )
        name(K_LOGIT)[...] = logit * gate * (1.0 - gate)
        grad_ffn = (gate * grad_update).astype(BF)
        name(K_GRAD_FFN)[...] = grad_ffn
        parts, parts_grad, hidden_out = get((K_PARTS, level)), name(K_PARTS_GRAD), name(K_HIDDEN)
        need(K_D)
        for t in range(hidden // LANES):
            cut = slice(t * LANES, (t + 1) * LANES)
            up_cut = slice(hidden + t * LANES, hidden + (t + 1) * LANES)
            if t % 2 == 0:
                both = dot_nn(grad_ffn, w_d[:, t * LANES : min((t + 2) * LANES, hidden)])
            grad_hidden = tile_of(both, t % 2)
            gate_part = parts[:, cut]
            up_part = parts[:, up_cut]
            sigma = sigmoid(gate_part)
            active = gate_part * sigma
            hidden_out[:, cut] = (active * up_part).astype(BF)
            parts_grad[:, cut] = (
                grad_hidden * up_part * sigma * (1.0 + gate_part * (1.0 - sigma))
            ).astype(BF)
            parts_grad[:, up_cut] = (grad_hidden * active).astype(BF)
        for base in (K_GRAD_FFN, K_HIDDEN, K_PARTS_GRAD, K_LOGIT):
            keep((base, level))
        return grad_update, rows_now, attn_now, gate

    def head_end(level, grad_update, rows_now, attn_now, gate):
        name = lambda base: held[(base, level)]
        gains = held[K_GAINS]
        need(K_GU)
        if level == 2:
            pl.semaphore_wait(barrier, devices - 1 + mp - 1)
        parts_now = name(K_PARTS_GRAD)[...]
        total = sums[(K_HEAD, level)]
        total.start(lambda start, wide: dot_nt(parts_now, w_gu[pl.ds(start, wide), :]))
        unit, factor = unit_of(rows_now + attn_now)
        total.middle()
        grad_second = total.finish().astype(F32)
        vecs[2 - level : 3 - level, :] = jnp.sum(grad_second * unit, axis=0, keepdims=True)
        grad_middle = unit_back(grad_second * gains[1:2, :], unit, factor)
        name(K_MIDDLE)[...] = grad_middle
        grad_attn = (gate * grad_update + grad_middle).astype(BF)
        name(K_GRAD_ATTN)[...] = grad_attn
        need(K_O)
        name(K_GRAD_MIXED)[...] = dot_nn(grad_attn, w_o[...]).astype(BF)
        keep((K_GRAD_ATTN, level))

    def attention(level):
        n = counts[level]
        group = 8
        width = heads * n
        send_buf, recv_buf, send_sems, recv_sems = buffers[level]
        query, packed = get((K_QUERY, level)), get((K_PACKED, level))
        mixed_t, log_total = get((K_MIXED_T, level)), get((K_LOG, level))
        keys, query_place = get((K_KEYS, level)), get((K_PLACE, level))
        cosine, sine = get((K_COSINE, level)), get((K_SINE, level))
        grad_mixed, grad_qkv = held[(K_GRAD_MIXED, level)], held[(K_GRAD_QKV, level)]
        left = lanes_of((n, LANES)) < HD
        for t in range(heads // 2):
            part = grad_mixed[:, t * LANES : (t + 1) * LANES].astype(F32)
            grad_rows[2 * t * n : (2 * t + 1) * n, :] = jnp.where(
                left, 0.0, pltpu.roll(part, HD, 1)
            ).astype(BF)
            grad_rows[(2 * t + 1) * n : (2 * t + 2) * n, :] = jnp.where(left, 0.0, part).astype(BF)
        query_t[:, :width] = query[...].T
        grad_t[:, :width] = grad_rows[:width, :].T
        delta[:, :width] = jnp.sum(grad_t[:, :width].astype(F32) * mixed_t[...], axis=0, keepdims=True)
        acc[:, :width] = jnp.zeros((2 * HD, width), F32)

        def send_copy(e, source_index):
            return pltpu.make_async_remote_copy(
                src_ref=send_buf.at[e], dst_ref=recv_buf.at[source_index],
                send_sem=send_sems.at[e], recv_sem=recv_sems.at[source_index],
                device_id={"dp": e}, device_id_type=MESH,
            )

        def one_block(b, carry):
            part = packed[pl.ds(b * group, group)].reshape(group * n, 2 * HD)
            scores = dot_nn(part, query_t[:, :width])
            place = keys[pl.ds(b * group, group)].reshape(group * n, LANES)
            place = jnp.concatenate([place] * (width // LANES), axis=1)
            scores = jnp.where(place <= query_place[...], scores, NEG)
            soft = jnp.exp(scores - log_total[...])
            grad_soft = dot_nn(part, grad_t[:, :width])
            grad_scores = (soft * (grad_soft - delta[:, :width])).astype(BF)
            grad_part = dot_nn(grad_scores, query[...]) + dot_nn(soft.astype(BF), grad_rows[:width, :])
            send_buf[pl.ds(b * group, group)] = grad_part.astype(BF).reshape(group, n, 2 * HD)
            acc[:, :width] += dot_tn(part, grad_scores)
            for g in range(group):
                e = b * group + g

                @pl.when(e < me)
                def _(e=e):
                    send_copy(e, me).start()

            return carry

        lax.fori_loop(0, me // group + 1, one_block, 0)
        grad_query = acc[:, :width].T * HD**-0.5
        for t in range(heads // 2):
            even = grad_query[2 * t * n : (2 * t + 1) * n, :]
            odd = grad_query[(2 * t + 1) * n : (2 * t + 2) * n, :]
            part = jnp.where(left, even, pltpu.roll(odd, HD, 1))
            grad_qkv[:, t * LANES : (t + 1) * LANES] = turn_back(part, cosine[...], sine[...], False)

        def add(e, carry):
            send_copy(me, e).wait_recv()
            return carry + recv_buf[e].astype(F32)

        part = lax.fori_loop(me + 1, devices, add, send_buf[me].astype(F32))
        grad_qkv[:, mix:] = turn_back(part, cosine[...], sine[...], True)

        def drain():
            def sent(e, carry):
                send_copy(e, me).wait_send()
                return carry

            lax.fori_loop(0, me, sent, 0)

        return drain

    def tail(level):
        gains, flow = held[K_GAINS], held[K_FLOW]
        grad_now = held[(K_GRAD_QKV, level)][...]
        need(K_QKV)
        total = sums[(K_TAIL, level)]
        total.start(lambda start, wide: dot_nt(grad_now, w_qkv[pl.ds(start, wide), :]))
        keep((K_GRAD_QKV, level))
        rows_now = held[(K_ROWS, level)][...].astype(F32)
        unit, factor = unit_of(rows_now)
        logit = held[(K_LOGIT, level)][...]
        vecs[7 - level : 8 - level, :] = jnp.sum(rows_now * logit, axis=0, keepdims=True)
        total.middle()
        grad_normed = total.finish().astype(F32)
        vecs[5 - level : 6 - level, :] = jnp.sum(grad_normed * unit, axis=0, keepdims=True)
        grad_rows_now = (
            unit_back(grad_normed * gains[0:1, :], unit, factor)
            + held[(K_MIDDLE, level)][...]
            + logit * gains[2:3, :]
        ).astype(BF)
        flow[...] = flow[...] + dot_tn(held[(K_PICK, level)][...], grad_rows_now)

    drains = []
    for level in (2, 1):
        head_end(level, *head(level))
        drains.append(attention(level))
        tail(level)
    held[K_FLOW_OUT][...] = held[K_FLOW][...]
    keep(K_FLOW_OUT)
    head(0)
    keep(K_VECS)
    for drain in drains:
        drain()
    for item in sums.values():
        item.drain()
    for copy in keeps:
        copy.wait()


def retreat(cotangent, kept, weights, heads, devices, mp, ident):
    counts = tuple(kept[(K_ROWS, level)].shape[0] for level in range(3))
    model = cotangent.shape[1]
    mix = heads * HD
    hidden = kept[(K_PARTS, 0)].shape[1] // 2
    ins = {K_FLOW: cotangent, K_GAINS: kept[K_GAINS]}
    inner = {}
    shapes = {K_FLOW_OUT: (cotangent.shape, F32), K_VECS: ((8, model), F32)}
    for level, n in enumerate(counts):
        for base in (K_ROWS, K_ATTN, K_FFN, K_PARTS):
            ins[(base, level)] = kept[(base, level)]
        if level:
            for base in (K_PICK, K_QUERY, K_PACKED, K_MIXED_T, K_LOG, K_KEYS, K_PLACE, K_COSINE, K_SINE):
                ins[(base, level)] = kept[(base, level)]
            shapes[(K_GRAD_QKV, level)] = ((n, mix + 2 * HD), BF)
            shapes[(K_GRAD_ATTN, level)] = ((n, model), BF)
            inner[(K_GRAD_MIXED, level)] = ((n, mix), BF)
            inner[(K_MIDDLE, level)] = ((n, model), F32)
        shapes[(K_GRAD_FFN, level)] = ((n, model), BF)
        shapes[(K_HIDDEN, level)] = ((n, hidden), BF)
        shapes[(K_PARTS_GRAD, level)] = ((n, 2 * hidden), BF)
        shapes[(K_LOGIT, level)] = ((n, 1), F32)
    names = tuple(shapes)
    most = heads * max(counts[1:])
    anywhere = pl.BlockSpec(memory_space=pl.ANY)
    outs = pl.pallas_call(
        functools.partial(retreat_kernel, counts, heads, devices, mp, hidden, tuple(ins), names, tuple(inner)),
        out_shape=tuple(jax.ShapeDtypeStruct(*shapes[name]) for name in names),
        in_specs=[anywhere] * (len(ins) + 1),
        out_specs=tuple([anywhere] * len(names)),
        scratch_shapes=[pltpu.VMEM(item.shape, item.dtype) for item in ins.values()]
        + [pltpu.VMEM(*shape) for shape in (*shapes.values(), *inner.values())]
        + [
            pltpu.VMEM((model, mix + 2 * HD), BF),
            pltpu.VMEM((model, mix), BF),
            pltpu.VMEM((model, 2 * hidden), BF),
            pltpu.VMEM((model, hidden), BF),
            pltpu.SemaphoreType.DMA((len(ins),)),
            pltpu.SemaphoreType.DMA((4,)),
            pltpu.SemaphoreType.DMA((len(names),)),
            pltpu.VMEM((2 * HD, most), BF),
            pltpu.VMEM((most, 2 * HD), BF),
            pltpu.VMEM((2 * HD, most), BF),
            pltpu.VMEM((2 * HD, most), F32),
            pltpu.VMEM((1, most), F32),
        ]
        + [
            item
            for level in (1, 2)
            for item in (
                pltpu.VMEM((devices, counts[level], 2 * HD), BF),
                pltpu.VMEM((devices, counts[level], 2 * HD), BF),
                pltpu.SemaphoreType.DMA((devices,)),
                pltpu.SemaphoreType.DMA((devices,)),
            )
        ]
        + [item for level in (2, 2, 1, 1) for item in sum_scratch(mp, counts[level], model)],
        compiler_params=pltpu.CompilerParams(
            collective_id=ident, has_side_effects=True, vmem_limit_bytes=VMEM_LIMIT
        ),
        name="retreat",
    )(*ins.values(), weights)
    return dict(zip(names, outs))


def plane(me):
    return me // 8, lax.rem(me // 2, 4), lax.rem(me, 2)


def peer(x, y, core):
    return {"dp": (lax.rem(x, 4) * 4 + lax.rem(y, 4)) * 2 + core}


def shifted(x, y, core, axis, k):
    return peer(x + k, y, core) if axis == 0 else peer(x, y + k, core)


def meet(me, partners):
    barrier = pltpu.get_barrier_semaphore()
    for device in partners:
        pl.semaphore_signal(barrier, inc=1, device_id=device, device_id_type=MESH)
    pl.semaphore_wait(barrier, len(partners))


def plane_partners(x, y, core):
    return (
        [peer(x, y, 1 - core)]
        + [shifted(x, y, core, 0, k) for k in (1, 2, 3)]
        + [shifted(x, y, core, 1, k) for k in (1, 2, 3)]
    )


class Spread:
    def __init__(self, groups, x, y, core, shard, full, pair, send_sems, recv_sems):
        self.x, self.y, self.core = x, y, core
        self.count = len(groups)
        self.items = [(shard.at[:, low:high], full, slice(low, high), axis) for low, high, axis in groups]
        self.items.append((pair.at[x, y, core], pair, slice(None), 0))
        self.send_sems, self.recv_sems = send_sems, recv_sems
        self.started = []
        self.waits = [{} for _ in self.items]

    def remote(self, g, index, source, target, device):
        copy = pltpu.make_async_remote_copy(
            src_ref=source, dst_ref=target, send_sem=self.send_sems.at[g, index],
            recv_sem=self.recv_sems.at[g, index], device_id=device, device_id_type=MESH,
        )
        copy.start()
        self.started.append(copy)
        return copy

    def line(self, g, at, first, count):
        _, full, cut, axis = self.items[g]
        if axis == 0:
            return full.at[pl.ds(first, count), at, self.core, :, cut]
        return full.at[at, pl.ds(first, count), self.core, :, cut]

    def one(self, g):
        own, full, cut, axis = self.items[g]
        self.waits[g][1] = [
            self.remote(
                g, k - 1, own, full.at[self.x, self.y, self.core, :, cut],
                shifted(self.x, self.y, self.core, axis, k),
            )
            for k in (2, 1, 3)
        ]

    def two(self, g):
        axis = self.items[g][-1]
        for copy in self.waits[g][1]:
            copy.wait_recv()
        mine = self.line(g, self.y if axis == 0 else self.x, 0, 4)
        self.waits[g][2] = [
            self.remote(g, 3 + i, mine, mine, shifted(self.x, self.y, self.core, 1 - axis, k))
            for i, k in enumerate((1, 3))
        ]

    def three(self, g):
        axis = self.items[g][-1]
        at = self.y if axis == 0 else self.x
        self.waits[g][3] = []
        for i, k in enumerate((1, 3)):
            self.waits[g][2][i].wait_recv()
            piece = self.line(g, lax.rem(at + 4 - k, 4), 2 * i, 2)
            self.waits[g][3].append(
                self.remote(g, 5 + i, piece, piece, shifted(self.x, self.y, self.core, 1 - axis, k))
            )

    def four(self, g):
        _, full, cut, _ = self.items[g]
        for copy in self.waits[g][3]:
            copy.wait_recv()
        mine = full.at[:, :, self.core, :, cut]
        self.waits[g][4] = [self.remote(g, 7, mine, mine, peer(self.x, self.y, 1 - self.core))]

    def five(self, g):
        self.waits[g][4][0].wait_recv()

    def run(self, *groups):
        for work, g in zip((self.two, self.one, self.three, self.four, self.five), groups):
            if g is not None and 0 <= g < self.count:
                work(g)

    def step(self, i):
        self.run(i, i + 3, i - 2, i - 4, i - 5)

    def drain(self):
        for copy in self.started:
            copy.wait_send()


def advance_kernel(counts, heads, devices, mp, hidden, groups, names, *refs):
    refs = list(refs)
    (tokens, depths, second_slot, third_slot, w_query, w_key, w_value, w_out, w_gate, w_up, w_down,
     norm_first, norm_second, router, cosine_in, sine_in) = [refs.pop(0) for _ in range(16)]
    outs = {name: refs.pop(0) for name in names}
    held = {name: refs.pop(0) for name in names}
    shard, own_sem, send_sems, recv_sems, query_t, top, total, acc, hidden_v, keep_sems, kv_send, kv_recv = [
        refs.pop(0) for _ in range(12)
    ]
    sum_refs = refs
    me, mp_me = lax.axis_index("dp"), lax.axis_index("mp")
    x, y, core = plane(me)
    weights = held[K_WEIGHTS]
    rows, model = tokens.shape
    mix = heads * HD
    lanes = lanes_of((rows, LANES))
    left = lanes < HD
    keeps = []

    def keep(name):
        copy = pltpu.make_async_copy(held[name], outs[name], keep_sems.at[len(keeps)])
        copy.start()
        keeps.append(copy)

    barrier = pltpu.get_barrier_semaphore()

    def greet(k, carry):
        pl.semaphore_signal(
            barrier, inc=1, device_id={"dp": lax.rem(me + k, devices)}, device_id_type=MESH
        )
        return carry

    lax.fori_loop(1, devices, greet, 0)
    for k in range(1, mp):
        pl.semaphore_signal(
            barrier, inc=1, device_id={"mp": lax.rem(mp_me + k, mp)}, device_id_type=MESH
        )

    token = lanes_of((1, rows)).astype(F32)
    picks, marks, query_places = [None], [None], []
    query_places.append(
        (lax.rem(lanes_of((1, heads * rows)), rows) + me * rows).astype(F32)
    )
    held[(K_PLACE, 0)][...] = query_places[0]
    for level, slot, deep in ((1, second_slot, 2), (2, third_slot, 3)):
        count = counts[level]
        slots = lax.broadcasted_iota(jnp.int32, (count, rows), 0)
        active = (depths[...] >= deep) & (slot[...] >= 0)
        chosen = jnp.where(active, slot[...], -1) == slots
        pick = jnp.where(chosen, 1.0, 0.0).astype(BF)
        held[(K_PICK, level)][...] = pick
        picks.append(pick)
        marks.append(
            jnp.min(jnp.where(chosen, token, float(rows)), axis=1, keepdims=True)
        )
    depth = w_query.shape[0]
    wide = jnp.zeros((1, LANES - depth), F32)
    gain_rows = jnp.concatenate(
        [jnp.concatenate([ref[...].astype(F32), wide], axis=1) for ref in (norm_first, norm_second, router)]
        + [jnp.zeros((LANES - 3, LANES), F32)],
        axis=0,
    )
    extra = gain_rows.T[:depth, :]
    rest = counts[1] - depth
    lane = lanes_of((depth, LANES))
    over = jnp.concatenate([marks[1][depth:, :], jnp.full((depth - rest, 1), float(rows), F32)], axis=0)
    extra = jnp.where(lane == 3, marks[1][:depth, :], extra)
    extra = jnp.where(lane == 4, over, extra)
    extra = jnp.where(lane == 5, marks[2], extra)
    pair = jnp.concatenate([w_key[...].astype(F32), w_value[...].astype(F32)], axis=1).astype(BF)
    start = 0
    for part in (
        w_query[...], pair, extra.astype(BF), w_out[...], w_gate[...], w_up[...], w_down[...],
    ):
        shard[:, start : start + part.shape[1]] = part
        start += part.shape[1]
    own = pltpu.make_async_copy(shard, weights.at[x, y, core], own_sem)
    own.start()
    spread = Spread(groups, x, y, core, shard, weights, held[K_PACKED, 0], send_sems, recv_sems)
    pl.semaphore_wait(barrier, devices - 1 + mp - 1)
    for g in range(3):
        spread.one(g)
    own.wait()
    for level, pick in ((1, picks[1]), (2, picks[2])):
        sublane = lax.broadcasted_iota(jnp.int32, (16, rows), 0)
        probe = jnp.where(sublane == 0, token, 1.0).astype(BF)
        found = dot_nt(probe, jnp.concatenate([pick] * heads, axis=0))
        place = jnp.where(found[1:2, :] > 0.5, found[0:1, :] + (me * rows).astype(F32), FAR)
        held[(K_PLACE, level)][...] = place
        query_places.append(place)
        table = jnp.concatenate([cosine_in[...], sine_in[...]], axis=1)
        turned = lax.dot_general(
            pick.astype(F32), table, (((1,), (0,)), ((), ())),
            preferred_element_type=F32, precision=lax.Precision.HIGHEST,
        )
        held[(K_COSINE, level)][...] = turned[:, :LANES]
        held[(K_SINE, level)][...] = turned[:, LANES:]
    spread.run(0, 3)
    spread.run(1, 4, 0)
    spread.run(2, 5, None, 0)
    spread.run(3, 6, 1, None, 0)

    gains = held[K_GAINS]
    columns = weights[:, :, :, :, mix + LANES : mix + 2 * LANES].reshape(model, LANES).astype(F32)
    gains[...] = columns.T[: gains.shape[0], :]
    keep(K_GAINS)

    def kv_copy(level, e, source_index):
        packed = held[(K_PACKED, level)]
        return pltpu.make_async_remote_copy(
            src_ref=packed.at[me], dst_ref=packed.at[me],
            send_sem=kv_send.at[level, e], recv_sem=kv_recv.at[level, source_index],
            device_id={"dp": e}, device_id_type=MESH,
        )

    def project(level, now):
        n = counts[level]
        name = lambda base: held[(base, level)]
        name(K_ROWS)[...] = now
        unit, unused = unit_of(now.astype(F32))
        normed = (unit * gains[0:1, :]).astype(BF)
        name(K_NORMED)[...] = normed
        cosine, sine = (cosine_in[...], sine_in[...]) if level == 0 else (name(K_COSINE)[...], name(K_SINE)[...])
        here = left[:n]
        tiles = [None] * (heads // 2 + 1)
        for t in range(heads // 2, -1, -2):
            low = max(t - 1, 0)
            both = dot_nn(normed, weights[:, :, :, :, low * LANES : (t + 1) * LANES].reshape(model, (t + 1 - low) * LANES))
            for j in range(low, t + 1):
                part = tile_of(both, j - low)
                if j == heads // 2:
                    part = part * jnp.where(here, cosine, 1.0) + swap_halves(part) * jnp.where(here, sine, 0.0)
                    if level == 0:
                        name(K_PACKED)[x, y, core] = part.astype(BF)
                        spread.one(spread.count)
                        continue
                    name(K_PACKED)[me] = part.astype(BF)

                    def send(k, carry):
                        kv_copy(level, devices - 1 - k, me).start()
                        return carry

                    lax.fori_loop(0, devices - 1 - me, send, 0)
                else:
                    tiles[j] = part * cosine + swap_halves(part) * sine

        def clear(e, carry):
            name(K_PACKED)[e] = jnp.zeros((n, 2 * HD), BF)
            return carry

        if level:
            lax.fori_loop(me + 1, devices, clear, 0)
        for t in range(heads // 2):
            scaled = tiles[t].astype(BF).astype(F32) * HD**-0.5
            name(K_QUERY)[2 * t * n : (2 * t + 1) * n, :] = jnp.where(here, scaled, 0.0).astype(BF)
            name(K_QUERY)[(2 * t + 1) * n : (2 * t + 2) * n, :] = jnp.where(
                here, pltpu.roll(scaled, HD, 1), 0.0
            ).astype(BF)
        width = heads * n
        query_t[:, :width] = name(K_QUERY)[...].T
        top[:, :width] = jnp.full((1, width), NEG, F32)
        total[:, :width] = jnp.zeros((1, width), F32)
        acc[:, :width] = jnp.zeros((2 * HD, width), F32)
        for base in (K_ROWS, K_NORMED, K_QUERY):
            keep((base, level))

    def group_of(level):
        return (4, 8, 16)[level]

    def block(level, b):
        n, group = counts[level], group_of(level)
        width = heads * n
        if level:
            for g in range(group):
                e = b * group + g

                @pl.when(e < me)
                def _(e=e):
                    kv_copy(level, me, e).wait_recv()

            part = held[K_PACKED, level][pl.ds(b * group, group)].reshape(group * n, 2 * HD)
        else:
            part = held[K_PACKED, level][b // 2, 2 * (b % 2) : 2 * (b % 2) + 2].reshape(group * n, 2 * HD)
        scores = dot_nn(part, query_t[:, :width])
        if level:
            place = held[(K_KEYS, level)][pl.ds(b * group, group)].reshape(group * n, LANES)
        else:
            place = (lax.broadcasted_iota(jnp.int32, (group * n, LANES), 0) + b * (group * n)).astype(F32)
        place = jnp.concatenate([place] * (width // LANES), axis=1)
        scores = jnp.where(place <= held[(K_PLACE, level)][...], scores, NEG)
        before = top[:, :width]
        peak = jnp.maximum(before, jnp.max(scores, axis=0, keepdims=True))
        soft = jnp.exp(scores - peak)
        fade = jnp.exp(before - peak)
        total[:, :width] = total[:, :width] * fade + jnp.sum(soft, axis=0, keepdims=True)
        acc[:, :width] = acc[:, :width] * fade + dot_tn(part, soft.astype(BF))
        top[:, :width] = peak

    def mix_heads(level):
        n = counts[level]
        width = heads * n
        mixed_t = acc[:, :width] / total[:, :width]
        held[(K_MIXED_T, level)][...] = mixed_t
        held[(K_LOG, level)][...] = top[:, :width] + jnp.log(total[:, :width])
        mixed = mixed_t.T
        for t in range(heads // 2):
            even = mixed[2 * t * n : (2 * t + 1) * n, :]
            odd = mixed[(2 * t + 1) * n : (2 * t + 2) * n, :]
            held[(K_MIXED, level)][:, t * LANES : (t + 1) * LANES] = jnp.where(
                left[:n], pltpu.roll(even, HD, 1), odd
            ).astype(BF)
        for base in (K_MIXED_T, K_LOG, K_MIXED, K_PACKED):
            keep((base, level))

    sums = [Sum(mp, mp_me, *sum_refs[4 * i : 4 * i + 4]) for i in range(2 * len(counts))]
    chunk = model // mp
    base_o = mix + 2 * LANES
    base_gu = base_o + mix
    base_d = base_gu + 2 * hidden

    def rows_of(start, wide, low, high):
        return weights[start // chunk, pl.ds(lax.rem(start, chunk) // LANES, wide // LANES), :, :, low:high].reshape(
            wide, high - low
        )

    def attn_sum(level):
        mixed_now = held[K_MIXED, level][...]
        total = sums[2 * level]
        total.start(lambda start, wide: dot_nt(mixed_now, rows_of(start, wide, base_o, base_gu)))
        return total

    def take_attn(level, total):
        attn = total.finish()
        held[K_ATTN, level][...] = attn
        rows_now = held[K_ROWS, level][...].astype(F32)
        unit, unused = unit_of(rows_now + attn.astype(F32))
        held[K_SECOND, level][...] = (unit * gains[1:2, :]).astype(BF)

    def widen(level):
        second, parts = held[K_SECOND, level][...], held[K_PARTS, level]
        for t in range(2 * hidden // 256):
            low = base_gu + t * 256
            parts[:, t * 256 : (t + 1) * 256] = dot_nn(
                second, weights[:, :, :, :, low : low + 256].reshape(model, 256)
            )
        n = counts[level]
        for t in range(hidden // LANES):
            cut = slice(t * LANES, (t + 1) * LANES)
            gate_part = parts[:, cut]
            up_part = parts[:, hidden + t * LANES : hidden + (t + 1) * LANES]
            hidden_v[:n, cut] = (gate_part * sigmoid(gate_part) * up_part).astype(BF)

    def narrow(level):
        hidden_now = hidden_v[: counts[level], :]
        total = sums[2 * level + 1]
        total.start(lambda start, wide: dot_nt(hidden_now, rows_of(start, wide, base_d, base_d + hidden)))
        for base in (K_ATTN, K_SECOND, K_PARTS):
            keep((base, level))
        rows_now = held[K_ROWS, level][...].astype(F32)
        gate = sigmoid(jnp.sum(rows_now * gains[2:3, :], axis=-1, keepdims=True))
        total.middle()
        ffn = total.finish()
        held[K_FFN, level][...] = ffn
        keep((K_FFN, level))
        update = (gate * (held[K_ATTN, level][...].astype(F32) + ffn.astype(F32))).astype(BF)
        if level:
            update = dot_tn(held[K_PICK, level][...], update)
        held[K_STATE][...] = held[K_STATE][...] + update.astype(F32)

    project(0, tokens[...])
    held[K_STATE][...] = tokens[...].astype(F32)
    for name in (
        (K_PLACE, 0), (K_PICK, 1), (K_PICK, 2), (K_PLACE, 1), (K_PLACE, 2), (K_COSINE, 1), (K_SINE, 1),
        (K_COSINE, 2), (K_SINE, 2),
    ):
        keep(name)
    spread.run(4, 7, 2)
    spread.two(spread.count)

    def key_places(e, carry):
        for level, lanes_at in ((1, (3, 4)), (2, (5,))):
            tile = weights[e // 8, lax.rem(e // 2, 4), lax.rem(e, 2), :, mix + LANES : mix + 2 * LANES].astype(F32)
            value = jnp.concatenate(
                [jnp.broadcast_to(tile[:, at : at + 1], (depth, LANES)) for at in lanes_at], axis=0
            )[: counts[level], :]
            held[(K_KEYS, level)][e] = jnp.where(
                value < rows, value + (e * rows).astype(F32), FAR
            )
        return carry

    lax.fori_loop(0, devices, key_places, 0)
    keep((K_KEYS, 1))
    keep((K_KEYS, 2))
    spread.run(5, 8, 3, 1)
    spread.three(spread.count)
    spread.step(6)
    spread.four(spread.count)
    spread.step(7)
    spread.five(spread.count)
    for b in range(devices // group_of(0)):

        @pl.when(b * group_of(0) <= me)
        def _(b=b):
            block(0, b)

        if b in (2, 5):
            spread.step(8 + b // 3)
    mix_heads(0)
    total_0 = attn_sum(0)
    spread.step(10)
    total_0.middle()
    spread.run(None, None, 9, 7, 6)
    spread.run(None, None, 10, 8, 7)
    take_attn(0, total_0)
    spread.run(None, None, None, 9, 8)
    widen(0)
    spread.run(None, None, None, 10, 9)
    spread.run(None, None, None, None, 10)
    narrow(0)
    keep(K_WEIGHTS)
    for level in range(1, len(counts)):
        now = dot_nn(held[K_PICK, level][...], held[K_STATE][...].astype(BF)).astype(BF)
        project(level, now)

        def one_block(b, carry, level=level):
            block(level, b)
            return carry

        lax.fori_loop(0, me // group_of(level) + 1, one_block, 0)
        mix_heads(level)
        attn_total = attn_sum(level)
        attn_total.middle()
        take_attn(level, attn_total)
        widen(level)
        narrow(level)
    keep(K_STATE)
    spread.drain()
    for item in sums:
        item.drain()
    for level in range(1, len(counts)):

        def sent(e, carry, level=level):
            kv_copy(level, e, me).wait_send()
            return carry

        lax.fori_loop(me + 1, devices, sent, 0)
    for copy in keeps:
        copy.wait()


def advance(tokens, depths, second_slot, third_slot, matrices, vectors, tables, heads, devices, mp, ident):
    counts = (tokens.shape[0], SECOND_SLOTS, THIRD_SLOTS)
    rows, model = tokens.shape
    depth, mix = matrices[0].shape
    hidden = matrices[4].shape[1]
    total = 2 * mix + 2 * LANES + 3 * hidden
    cuts = [0, *range(mix + 2 * LANES, total - 640, 512), total - 640, total - 256, total]
    groups = [(a, b, i % 2) for i, (a, b) in enumerate(zip(cuts[:-1], cuts[1:]))]
    shapes = {
        K_STATE: ((rows, model), F32),
        K_WEIGHTS: ((4, 4, 2, depth, total), BF),
        K_GAINS: ((8, model), F32),
    }
    for level, n in enumerate(counts):
        width = heads * n
        shapes[(K_PLACE, level)] = ((1, width), F32)
        if level:
            shapes[(K_PICK, level)] = ((n, rows), BF)
            shapes[(K_COSINE, level)] = ((n, LANES), F32)
            shapes[(K_SINE, level)] = ((n, LANES), F32)
            shapes[(K_KEYS, level)] = ((devices, n, LANES), F32)
        for base in (K_ROWS, K_NORMED, K_ATTN, K_FFN, K_SECOND):
            shapes[(base, level)] = ((n, model), BF)
        shapes[(K_PARTS, level)] = ((n, 2 * hidden), F32)
        shapes[K_PACKED, level] = (((devices,) if level else (4, 4, 2)) + (n, 2 * HD), BF)
        shapes[(K_QUERY, level)] = ((width, 2 * HD), BF)
        shapes[(K_MIXED_T, level)] = ((2 * HD, width), F32)
        shapes[(K_LOG, level)] = ((1, width), F32)
        shapes[(K_MIXED, level)] = ((n, mix), BF)
    names = tuple(shapes)
    args = (tokens, depths, second_slot, third_slot, *matrices, *vectors, *tables)
    width = heads * rows
    outs = pl.pallas_call(
        functools.partial(advance_kernel, counts, heads, devices, mp, hidden, groups, names),
        out_shape=tuple(jax.ShapeDtypeStruct(*shapes[name]) for name in names),
        in_specs=vmem(len(args)),
        out_specs=tuple([pl.BlockSpec(memory_space=pl.ANY)] * len(names)),
        scratch_shapes=[pltpu.VMEM(*shapes[name]) for name in names]
        + [
            pltpu.VMEM((depth, total), BF),
            pltpu.SemaphoreType.DMA(()),
            pltpu.SemaphoreType.DMA((len(groups) + 1, 8)),
            pltpu.SemaphoreType.DMA((len(groups) + 1, 8)),
            pltpu.VMEM((2 * HD, width), BF),
            pltpu.VMEM((1, width), F32),
            pltpu.VMEM((1, width), F32),
            pltpu.VMEM((2 * HD, width), F32),
            pltpu.VMEM((rows, hidden), BF),
            pltpu.SemaphoreType.DMA((len(names),)),
            pltpu.SemaphoreType.DMA((len(counts), devices)),
            pltpu.SemaphoreType.DMA((len(counts), devices)),
        ]
        + [item for n in counts for _ in range(2) for item in sum_scratch(mp, n, model)],
        compiler_params=pltpu.CompilerParams(
            collective_id=ident, has_side_effects=True, vmem_limit_bytes=VMEM_LIMIT
        ),
        name="advance",
    )(*args)
    kept = dict(zip(names, outs))
    kept[K_PACKED, 0] = kept[K_PACKED, 0].reshape(devices, rows, 2 * HD)
    return kept


SLOTS = 5
CORE_SLOTS = 3
GROUP = 512


class Collect:
    def __init__(self, spans, groups, x, y, core, turned, rights, vectors, store, slots, core_recv, relay_recv, first_recv, mid, last_recv, send_sems, recv_sems, credit, turn):
        self.spans, self.groups = spans, groups
        self.x, self.y, self.core = x, y, core
        self.turned, self.rights, self.vectors, self.store, self.slots = turned, rights, vectors, store, slots
        self.core_recv, self.relay_recv, self.first_recv = core_recv, relay_recv, first_recv
        self.mid, self.last_recv, self.credit = mid, last_recv, credit
        self.send_sems, self.recv_sems = send_sems, recv_sems
        self.turn = turn
        self.waits = [{} for _ in groups]
        self.done = set()

    def remote(self, g, index, source, target, device):
        copy = pltpu.make_async_remote_copy(
            src_ref=source, dst_ref=target, send_sem=self.send_sems.at[g, index],
            recv_sem=self.recv_sems.at[g, index], device_id=device, device_id_type=MESH,
        )
        copy.start()
        return copy

    def held(self, slot, axis, at, first, count):
        if axis == 0:
            return self.slots.at[slot, at, pl.ds(first, count), self.core]
        return self.slots.at[slot, pl.ds(first, count), at, self.core]

    def zero(self, g):
        slot, waits = g % SLOTS, self.waits
        if g >= SLOTS:
            for stage in range(3):
                for copy in waits[g - SLOTS][stage]:
                    copy.wait_send()
        column = 0
        for section, low, high in self.groups[g][1]:
            wide = high - low
            if section < 4:
                if section not in self.done:
                    self.done.add(section)
                    self.turn(section)
                base = self.spans[section][0]

            def rows_of(m, carry, section=section, low=low, high=high, column=column, wide=wide):
                start = pl.multiple_of(m * 1024, 1024)
                if section < 4:
                    value = dot_nn(
                        self.turned[section % 2, pl.ds(start, 1024), :], self.rights[:, base + low : base + high]
                    )
                else:
                    few = self.vectors[:, pl.ds(start, 1024)]
                    value = jnp.concatenate([few, jnp.zeros((LANES - few.shape[0], 1024), F32)], axis=0).T
                self.slots[slot, pl.ds(m * 2, 2), :, :, :, column : column + wide] = (
                    value.astype(BF).reshape(2, 4, 2, 64, wide)
                )
                return carry

            lax.fori_loop(0, 2, rows_of, 0)
            column += wide
        if g >= CORE_SLOTS:
            pl.semaphore_wait(self.credit, 1)
        waits[g][0] = [
            self.remote(
                g, 0, self.slots.at[slot, :, :, 1 - self.core, :, :column],
                self.core_recv.at[g % CORE_SLOTS, :, :, :, :column], peer(self.x, self.y, 1 - self.core),
            )
        ]

    def first(self, g):
        slot, (width, _, axis) = g % SLOTS, self.groups[g]
        waits, slots = self.waits, self.slots
        waits[g][0][0].wait_recv()

        def add(i, carry):
            slots[slot, i, :, self.core, :, :width] = (
                slots[slot, i, :, self.core, :, :width] + self.core_recv[g % CORE_SLOTS, i, :, :, :width]
            )
            return carry

        lax.fori_loop(0, 4, add, 0)
        if g + CORE_SLOTS < len(self.groups):
            pl.semaphore_signal(
                self.credit, inc=1, device_id=peer(self.x, self.y, 1 - self.core), device_id_type=MESH
            )
        at = self.x if axis == 0 else self.y
        waits[g][1] = [
            self.remote(
                g, 1 + i, self.held(slot, axis, lax.rem(at + 2, 4), 2 * i, 2).at[:, :, :width],
                self.relay_recv.at[g, i, :, :, :width], shifted(self.x, self.y, self.core, axis, k),
            )
            for i, k in enumerate((1, 3))
        ]

    def second(self, g):
        slot, (width, _, axis) = g % SLOTS, self.groups[g]
        waits, slots = self.waits, self.slots
        at = self.x if axis == 0 else self.y
        waits[g][2] = []
        for i, k in enumerate((1, 3)):
            waits[g][1][i].wait_recv()
            there = lax.rem(at + k, 4)
            for j in range(2):
                b = 2 * i + j
                where = (slot, there, b, self.core) if axis == 0 else (slot, b, there, self.core)
                where = where + (slice(None), slice(0, width))
                slots[where] = slots[where] + self.relay_recv[g, i, j, :, :width]
            waits[g][2].append(
                self.remote(
                    g, 3 + i, self.held(slot, axis, there, 0, 4).at[:, :, :width],
                    self.first_recv.at[g, i, :, :, :width], shifted(self.x, self.y, self.core, axis, k),
                )
            )

    def third(self, g):
        slot, (width, _, axis) = g % SLOTS, self.groups[g]
        waits, slots = self.waits, self.slots
        at, other = (self.x, self.y) if axis == 0 else (self.y, self.x)
        for copy in waits[g][2]:
            copy.wait_recv()
        for b in range(4):
            where = (slot, at, b, self.core) if axis == 0 else (slot, b, at, self.core)
            self.mid[g, b, :, :width] = (
                slots[where + (slice(None), slice(0, width))].astype(F32)
                + self.first_recv[g, 0, b, :, :width].astype(F32)
                + self.first_recv[g, 1, b, :, :width].astype(F32)
            ).astype(BF)
        waits[g][3] = [
            self.remote(
                g, 4 + k, self.mid.at[g, lax.rem(other + k, 4), :, :width],
                self.last_recv.at[g, k - 1, :, :width],
                shifted(self.x, self.y, self.core, 1 - axis, k),
            )
            for k in (2, 1, 3)
        ]

    def fourth(self, g):
        width, pieces, axis = self.groups[g]
        other = self.y if axis == 0 else self.x
        value = self.mid[g, other, :, :width].astype(F32)
        for copy in self.waits[g][3]:
            copy.wait_recv()
        for k in range(3):
            value = value + self.last_recv[g, k, :, :width].astype(F32)
        column = 0
        for section, low, high in pieces:
            self.store(section, low, value[:, column : column + high - low])
            column += high - low

    def run(self, *groups):
        for work, g in zip((self.zero, self.first, self.second, self.third, self.fourth), groups):
            if g is not None and 0 <= g < len(self.groups):
                work(g)

    def step(self, i):
        self.run(i, i - 1, i - 2, i - 4, i - 5)

    def drain(self):
        count = len(self.groups)
        for g in range(count):
            for stage in range(4):
                if stage == 3 or g >= count - SLOTS:
                    for copy in self.waits[g][stage]:
                        copy.wait_send()


def finish_kernel(n, heads, devices, mp, group, levels, spans, groups, *refs):
    refs = list(refs)
    gains, query_place, log_total, cosine, sine, logit, vecs = [refs.pop(0) for _ in range(7)]
    large = [refs.pop(0) for _ in range(6)]
    w_hbm = refs.pop(0)
    sources = [[refs.pop(0) if level or i not in (4, 7) else None for i in range(8)] for level in range(len(levels))]
    flow_out, q_out, k_out, v_out, out_out, gate_out, up_out, down_out, vec_out = [refs.pop(0) for _ in range(9)]
    query_t, grad_rows, grad_t, acc, delta, send_buf, recv_buf, pair_buf, kv_send, kv_recv = [refs.pop(0) for _ in range(10)]
    w_qkv, w_sem, w_gu, gu_sems, middle = [refs.pop(0) for _ in range(5)]
    sum_refs = [[refs.pop(0) for _ in range(4)] for _ in range(2)]
    (lefts, turned, rights, vectors, slots, core_recv, relay_recv, first_recv, mid, last_recv,
     loads, send_sems, recv_sems, credit) = refs[:14]
    flow, rows_in, attn_in, query, mixed_t, packed = refs[14:20]
    large_copies = [
        pltpu.make_async_copy(source, target, refs[20].at[i])
        for i, (source, target) in enumerate(zip(large, refs[14:20]))
    ]
    me, mp_me = lax.axis_index("dp"), lax.axis_index("mp")
    x, y, core = plane(me)
    hidden = gate_out.shape[1]
    mix = q_out.shape[1]
    base_o = mix + 2 * LANES
    load_o = pltpu.make_async_copy(w_hbm.at[:, base_o : base_o + mix], w_qkv.at[:, :mix], w_sem)
    load_o.start()
    wide = w_gu.shape[1]
    pieces = [(mp_me + k, piece) for piece in range(PIECES) for k in Sum.order]
    pieces += [(mp_me, piece) for piece in range(PIECES)]
    gu_loads = []

    def load_gu():
        i = len(gu_loads)
        if i < len(pieces):
            start = pl.multiple_of((lax.rem(pieces[i][0], mp) * PIECES + pieces[i][1]) * wide, wide)
            copy = pltpu.make_async_copy(
                w_hbm.at[pl.ds(start, wide), base_o + mix : base_o + mix + 2 * hidden],
                w_gu.at[i % w_gu.shape[0]], gu_sems.at[i % w_gu.shape[0]],
            )
            copy.start()
            gu_loads.append(copy)

    for _ in range(w_gu.shape[0]):
        load_gu()
    fetches = [[] for _ in range(4)]

    def fetch(s, side):
        row = 0
        for level, count in enumerate(levels):
            low, high = spans[s]
            target = (lefts.at[s % 2, row : row + count], rights.at[row : row + count, low:high])[side]
            if sources[level][2 * s + side] is not None:
                copy = pltpu.make_async_copy(
                    sources[level][2 * s + side], target, loads.at[level, 2 * s + side]
                )
                copy.start()
                fetches[s].append(copy)
            row += count

    for s in range(4):
        if s < 2:
            fetch(s, 0)
        fetch(s, 1)
        if s == 0:
            for copy in large_copies:
                copy.start()

    barrier = pltpu.get_barrier_semaphore()

    def greet(k, carry):
        pl.semaphore_signal(
            barrier, inc=1, device_id={"dp": lax.rem(me + k, devices)}, device_id_type=MESH
        )
        return carry

    lax.fori_loop(1, devices, greet, 0)
    for k in range(1, mp):
        pl.semaphore_signal(
            barrier, inc=1, device_id={"mp": lax.rem(mp_me + k, mp)}, device_id_type=MESH
        )

    def turn(section):
        for copy in fetches[section]:
            copy.wait()
        turned[section % 2] = lefts[section % 2].T
        if section < 2:
            fetch(section + 2, 0)

    def store(section, low, value):
        high = low + value.shape[1]
        if section == 0:
            middle_cut = min(max(hidden - low, 0), high - low)
            if middle_cut:
                gate_out[:, low : low + middle_cut] = value[:, :middle_cut]
            if low + middle_cut < high:
                up_out[:, low + middle_cut - hidden : high - hidden] = value[:, middle_cut:]
        elif section == 1:
            down_out[:, low:high] = value
        elif section == 2:
            out_out[:, low:high] = value
        elif section == 3:
            if low < mix:
                q_out[:, low : min(high, mix)] = value[:, : min(high, mix) - low]
            if high > mix:
                k_out[...] = value[:, mix - low : mix - low + HD]
                v_out[...] = value[:, mix - low + HD :]
        else:
            vec_out[...] = value.T[: vec_out.shape[0], :]

    work = Collect(
        spans, groups, x, y, core, turned, rights, vectors, store, slots, core_recv, relay_recv,
        first_recv, mid, last_recv, send_sems, recv_sems, credit, turn,
    )
    pl.semaphore_wait(barrier, devices - 1 + mp - 1)
    work.step(0)

    for copy in large_copies[:3]:
        copy.wait()
    update = flow[...].astype(BF).astype(F32)
    level = rows_in[...].astype(F32)
    gate = sigmoid(jnp.sum(level * gains[2:3, :], axis=-1, keepdims=True))
    parts_now = rights[0:n, : 2 * hidden]
    used = []

    def gu_piece(start, size):
        i = len(used)
        used.append(i)
        gu_loads[i].wait()
        value = dot_nt(parts_now, w_gu[i % w_gu.shape[0]])
        load_gu()
        return value

    head = Sum(mp, mp_me, *sum_refs[0])
    head.start(gu_piece)
    work.step(1)
    work.step(2)
    head.middle()
    work.step(3)
    grad_second = head.finish().astype(F32)
    unit, factor = unit_of(level + attn_in[...].astype(F32))
    vectors[...] = jnp.zeros(vectors.shape, F32)
    vectors[1:2, :] = (
        jnp.sum(grad_second * unit, axis=0, keepdims=True) + vecs[0:1, :] + vecs[1:2, :]
    )
    middle[...] = unit_back(grad_second * gains[1:2, :], unit, factor)
    grad_attn = (gate * update + middle[...]).astype(BF)
    lefts[0, 0:n, :] = grad_attn
    load_o.wait()
    grad_mixed = dot_nn(grad_attn, w_qkv[:, :mix]).astype(BF).astype(F32)
    load_w = pltpu.make_async_copy(w_hbm.at[:, : w_qkv.shape[1]], w_qkv, w_sem)
    load_w.start()
    work.step(4)
    left = lanes_of((n, LANES)) < HD
    for t in range(heads // 2):
        part = grad_mixed[:, t * LANES : (t + 1) * LANES]
        grad_rows[2 * t * n : (2 * t + 1) * n, :] = jnp.where(
            left, 0.0, pltpu.roll(part, HD, 1)
        ).astype(BF)
        grad_rows[(2 * t + 1) * n : (2 * t + 2) * n, :] = jnp.where(left, 0.0, part).astype(BF)
    for copy in large_copies[3:]:
        copy.wait()
    query_t[...] = query[...].T
    grad_t[...] = grad_rows[...].T
    delta[...] = jnp.sum(grad_t[...].astype(F32) * mixed_t[...], axis=0, keepdims=True)
    acc[...] = jnp.zeros(acc.shape, F32)
    width = heads * n

    chips = devices // 2
    chip = me // 2

    def send_copy(there, source_index):
        return pltpu.make_async_remote_copy(
            src_ref=send_buf.at[there, core], dst_ref=recv_buf.at[source_index],
            send_sem=kv_send.at[there], recv_sem=kv_recv.at[source_index],
            device_id={"dp": 2 * there + core}, device_id_type=MESH,
        )

    def one_block(b):
        part = packed[b * group : (b + 1) * group].reshape(group * n, 2 * HD)
        scores = dot_nn(part, query_t[...])
        place = (lax.broadcasted_iota(jnp.int32, (group * n, LANES), 0) + b * (group * n)).astype(F32)
        place = jnp.concatenate([place] * (width // LANES), axis=1)
        scores = jnp.where(place <= query_place[...], scores, NEG)
        weights = jnp.exp(scores - log_total[...])
        grad_weights = dot_nn(part, grad_t[...])
        grad_scores = (weights * (grad_weights - delta[...])).astype(BF)
        grad_part = dot_nn(grad_scores, query[...]) + dot_nn(weights.astype(BF), grad_rows[...])
        send_buf[b * group // 2 : (b + 1) * group // 2] = grad_part.astype(BF).reshape(group // 2, 2, n, 2 * HD)
        acc[...] += dot_tn(part, grad_scores)

    blocks = devices // group
    for b in range(blocks):
        if b in (2, 4, 6):
            work.step(4 + b // 2)

        @pl.when(b * group <= me)
        def _(b=b):
            one_block(b)

    pair_copy = pltpu.make_async_remote_copy(
        src_ref=send_buf.at[:, 1 - core], dst_ref=pair_buf,
        send_sem=kv_send.at[chips], recv_sem=kv_recv.at[chips],
        device_id=peer(x, y, 1 - core), device_id_type=MESH,
    )
    pair_copy.start()
    work.step(8)
    pair_copy.wait_recv()

    def push(there, carry):
        send_buf[there, core] = send_buf[there, core] + pair_buf[there]
        send_copy(there, chip).start()
        return carry

    lax.fori_loop(0, chip, push, 0)
    grad_query = acc[...].T * HD**-0.5
    low = spans[3][0]
    for t in range(heads // 2):
        even = grad_query[2 * t * n : (2 * t + 1) * n, :]
        odd = grad_query[(2 * t + 1) * n : (2 * t + 2) * n, :]
        part = jnp.where(left, even, pltpu.roll(odd, HD, 1))
        rights[0:n, low + t * LANES : low + (t + 1) * LANES] = turn_back(part, cosine[...], sine[...], False)
    work.step(9)

    def add(there, carry):
        send_copy(chip, there).wait_recv()
        return carry + recv_buf[there].astype(F32)

    part = lax.fori_loop(
        chip + 1, chips, add, send_buf[chip, core].astype(F32) + pair_buf[chip].astype(F32)
    )
    rights[0:n, low + mix : low + mix + LANES] = turn_back(part, cosine[...], sine[...], True)
    load_w.wait()
    grad_now = rights[0:n, low : spans[3][1]]

    def first_piece(start, wide):
        return dot_nt(grad_now, w_qkv[pl.ds(start, wide), :])

    total = Sum(mp, mp_me, *sum_refs[1])
    total.start(first_piece)
    work.step(10)
    total.middle()
    work.run(None, 10, 9, 7, 6)
    grad_normed = total.finish().astype(F32)
    unit, factor = unit_of(level)
    vectors[0:1, :] = jnp.sum(grad_normed * unit, axis=0, keepdims=True) + vecs[3:4, :] + vecs[4:5, :]
    vectors[2:3, :] = jnp.sum(level * logit[...], axis=0, keepdims=True) + vecs[5:6, :] + vecs[6:7, :]
    flow_out[...] = flow[...] + (
        unit_back(grad_normed * gains[0:1, :], unit, factor) + middle[...] + logit[...] * gains[2:3, :]
    ).astype(BF).astype(F32)
    work.run(11, None, 10, 8, 7)
    work.run(None, 11, None, 9, 8)
    work.run(None, None, 11, 10, 9)
    work.run(None, None, None, 11, 10)
    work.run(None, None, None, None, 11)
    work.drain()
    head.drain()
    total.drain()

    pair_copy.wait_send()

    def sent(there, carry):
        send_copy(there, chip).wait_send()
        return carry

    lax.fori_loop(0, chip, sent, 0)


def finish(flow, gains, attention, tail, vecs, weights, levels, heads, devices, mp, depth, ident):
    n, model = levels[0][0].shape
    width = heads * n
    group = 512 // n
    mix = heads * HD
    widths = [levels[1][i].shape[1] for i in (1, 3, 5, 7)] + [LANES]
    spans, total = [], 0
    for wide in widths:
        spans.append((total, total + wide))
        total += wide
    pieces = []
    for section, wide in enumerate(widths):
        pieces += [(section, low, low + LANES) for low in range(0, wide, LANES)]
    groups = []
    per = GROUP // LANES
    cuts = [*range(0, len(pieces) - 1, per), len(pieces) - 1, len(pieces)]
    for index, end in zip(cuts[:-1], cuts[1:]):
        merged = []
        for section, low, high in pieces[index:end]:
            if merged and merged[-1][0] == section:
                merged[-1] = (section, merged[-1][1], high)
            else:
                merged.append((section, low, high))
        wide = sum(high - low for _, low, high in merged)
        groups.append((wide, merged, len(groups) % 2))
    counts = [level[0].shape[0] for level in levels]
    rows = sum(counts)
    hidden = widths[1]
    many = len(groups)
    query_place, query, packed, mixed_t, log_total, *tables = attention
    rows_in, attn_in, logit = tail
    whole = [gains, query_place, log_total, *tables, logit, vecs]
    large = [flow, rows_in, attn_in, query, mixed_t, packed]
    args = whole + large + [weights] + [item for level in levels for item in level if item is not None]
    return pl.pallas_call(
        functools.partial(finish_kernel, n, heads, devices, mp, group, counts, spans, groups),
        out_shape=(
            jax.ShapeDtypeStruct(flow.shape, F32),
            jax.ShapeDtypeStruct((depth, mix), F32),
            jax.ShapeDtypeStruct((depth, HD), F32),
            jax.ShapeDtypeStruct((depth, HD), F32),
            jax.ShapeDtypeStruct((depth, mix), F32),
            jax.ShapeDtypeStruct((depth, hidden), F32),
            jax.ShapeDtypeStruct((depth, hidden), F32),
            jax.ShapeDtypeStruct((depth, hidden), F32),
            jax.ShapeDtypeStruct((8, depth), F32),
        ),
        in_specs=vmem(len(whole)) + [pl.BlockSpec(memory_space=pl.ANY)] * (len(args) - len(whole)),
        out_specs=tuple(vmem(9)),
        scratch_shapes=[
            pltpu.VMEM((2 * HD, width), BF),
            pltpu.VMEM((width, 2 * HD), BF),
            pltpu.VMEM((2 * HD, width), BF),
            pltpu.VMEM((2 * HD, width), F32),
            pltpu.VMEM((1, width), F32),
            pltpu.VMEM((devices // 2, 2, n, 2 * HD), BF),
            pltpu.VMEM((devices // 2, n, 2 * HD), BF),
            pltpu.VMEM((devices // 2, n, 2 * HD), BF),
            pltpu.SemaphoreType.DMA((devices // 2 + 1,)),
            pltpu.SemaphoreType.DMA((devices // 2 + 1,)),
            pltpu.VMEM((model, mix + 2 * HD), BF),
            pltpu.SemaphoreType.DMA(()),
            pltpu.VMEM((3, model // mp // PIECES, 2 * hidden), BF),
            pltpu.SemaphoreType.DMA((3,)),
            pltpu.VMEM((n, model), F32),
            *sum_scratch(mp, n, model),
            *sum_scratch(mp, n, model),
            pltpu.VMEM((2, rows, model), BF),
            pltpu.VMEM((2, model, rows), BF),
            pltpu.VMEM((rows, spans[3][1]), BF),
            pltpu.VMEM((8, model), F32),
            pltpu.VMEM((SLOTS, 4, 4, 2, depth, GROUP), BF),
            pltpu.VMEM((CORE_SLOTS, 4, 4, depth, GROUP), BF),
            pltpu.VMEM((many, 2, 2, depth, GROUP), BF),
            pltpu.VMEM((many, 2, 4, depth, GROUP), BF),
            pltpu.VMEM((many, 4, depth, GROUP), BF),
            pltpu.VMEM((many, 3, depth, GROUP), BF),
            pltpu.SemaphoreType.DMA((len(levels), 8)),
            pltpu.SemaphoreType.DMA((many, 8)),
            pltpu.SemaphoreType.DMA((many, 8)),
            pltpu.SemaphoreType.REGULAR,
            *[pltpu.VMEM(item.shape, item.dtype) for item in large],
            pltpu.SemaphoreType.DMA((len(large),)),
        ],
        compiler_params=pltpu.CompilerParams(
            collective_id=ident, has_side_effects=True, vmem_limit_bytes=63 * 1024 * 1024
        ),
        name="finish",
    )(*args)


def hand_over_kernel(count, *refs):
    vectors, sources, targets = refs[0], refs[1 : 1 + count], refs[1 + count :]
    for source, target in zip(sources, targets):
        target[...] = source[...]
    for i, target in enumerate(targets[count:]):
        target[...] = vectors[i, :]


def hand_over(items, vectors):
    count = len(items)
    return pl.pallas_call(
        functools.partial(hand_over_kernel, count),
        out_shape=tuple(
            [jax.ShapeDtypeStruct(item.shape, F32) for item in items]
            + [jax.ShapeDtypeStruct(vectors.shape[1:], F32)] * 3
        ),
        in_specs=vmem(1 + count),
        out_specs=tuple(vmem(count + 3)),
        name="hand_over",
    )(vectors, *items)


def rotary_tables(place):
    freq = jnp.exp(jnp.arange(HD // 2, dtype=F32) * (-2.0 * math.log(ROPE_BASE) / HD))
    angle = place.astype(F32)[:, None] * freq[None, :]
    cosine, sine = jnp.cos(angle), jnp.sin(angle)
    return (
        jnp.concatenate([cosine] * 4, axis=1),
        jnp.concatenate([-sine, sine, -sine, sine], axis=1),
    )


def local(
    tokens, depths, second_slot, third_slot, w_query, w_key, w_value, w_out, w_gate, w_up,
    w_down, norm_first, norm_second, router, cotangent,
):
    me = lax.axis_index("dp")
    devices, mp = lax.axis_size("dp"), lax.axis_size("mp")
    rows = tokens.shape[0]
    heads = w_query.shape[1] // HD
    depth = w_query.shape[0]
    home = rotary_tables(jnp.arange(rows, dtype=jnp.int32) + me * rows)

    def row(values):
        return values.reshape(1, -1)

    kept = advance(
        tokens, row(depths), row(second_slot), row(third_slot),
        (w_query, w_key, w_value, w_out.T, w_gate, w_up, w_down.T),
        (row(norm_first), row(norm_second), row(router)), home, heads, devices, mp, 0,
    )
    weights = kept[K_WEIGHTS].reshape(devices * depth, -1)
    gains = kept[K_GAINS]
    back = retreat(cotangent, kept, weights, heads, devices, mp, 1)
    terms = []
    for level in range(3):
        terms.append(
            tuple(back.get((base, level), kept.get((base, level))) for base in (
                K_SECOND, K_PARTS_GRAD, K_GRAD_FFN, K_HIDDEN, K_GRAD_ATTN, K_MIXED, K_NORMED, K_GRAD_QKV
            ))
        )
    attention = [kept[(base, 0)] for base in (K_PLACE, K_QUERY, K_PACKED, K_MIXED_T, K_LOG)]
    results = finish(
        back[K_FLOW_OUT], gains, (*attention, *home),
        (kept[(K_ROWS, 0)], kept[(K_ATTN, 0)], back[(K_LOGIT, 0)]), back[K_VECS], weights, terms,
        heads, devices, mp, depth, 2,
    )
    (state, flow, query_grad, key_grad, value_grad, out_grad, gate_grad, up_grad, down_grad,
     first_grad, second_grad, router_grad) = hand_over((kept[K_STATE], *results[:-1]), results[-1])
    return (
        state, flow, query_grad, key_grad, value_grad, out_grad.T, gate_grad, up_grad, down_grad.T,
        first_grad, second_grad, router_grad,
    )


def solution(mesh):
    in_specs = (
        P("dp", None), P("dp"), P("dp"), P("dp"), P("dp", "mp"), P("dp", "mp"), P("dp", "mp"),
        P("mp", "dp"), P("dp", "mp"), P("dp", "mp"), P("mp", "dp"), P("dp"), P("dp"), P("dp"),
        P("dp", None),
    )
    out_specs = (
        P("dp", None), P("dp", None), P("dp", "mp"), P("dp", "mp"), P("dp", "mp"), P("mp", "dp"),
        P("dp", "mp"), P("dp", "mp"), P("mp", "dp"), P("dp"), P("dp"), P("dp"),
    )
    return jax.shard_map(local, mesh=mesh, in_specs=in_specs, out_specs=out_specs, check_vma=False)
```

```python
import functools
import math

import jax
import jax.numpy as jnp
from jax import lax
from jax.experimental import pallas as pl
from jax.experimental.pallas import tpu as pltpu
from jax.sharding import PartitionSpec as P

HD = 64
SECOND_SLOTS = 96
THIRD_SLOTS = 64
EPS = 1e-05
NEG = -1e30
ROPE_BASE = 10000.0
FAR = 1e9
BF = jnp.bfloat16
F32 = jnp.float32
MESH = pl.DeviceIdType.MESH

(K_ROWS, K_NORMED, K_ATTN, K_FFN, K_SECOND, K_PARTS, K_PACKED, K_QUERY, K_MIXED_T, K_LOG, K_MIXED, K_PLACE, K_PICK, K_COSINE, K_SINE, K_KEYS, K_STATE, K_WEIGHTS, K_GAINS, K_FLOW, K_FLOW_OUT, K_VECS, K_GRAD_QKV, K_GRAD_FFN, K_HIDDEN, K_PARTS_GRAD, K_GRAD_ATTN, K_GRAD_MIXED, K_MIDDLE, K_LOGIT, K_HEAD, K_TAIL, K_D, K_GU, K_O, K_QKV) = range(36)

LANES = 128
VMEM_LIMIT = 63 * 1024 * 1024


def dot_nn(left, right):
    return lax.dot_general(left, right, (((1,), (0,)), ((), ())), preferred_element_type=F32)


def dot_nt(left, right):
    return lax.dot_general(left, right, (((1,), (1,)), ((), ())), preferred_element_type=F32)


def dot_tn(left, right):
    return lax.dot_general(left, right, (((0,), (0,)), ((), ())), preferred_element_type=F32)


def unit_of(values):
    factor = lax.rsqrt(jnp.mean(values * values, axis=-1, keepdims=True) + EPS)
    return values * factor, factor


def unit_back(shaped, unit, factor):
    return factor * (shaped - unit * jnp.mean(shaped * unit, axis=-1, keepdims=True))


def sigmoid(values):
    return 1.0 / (1.0 + jnp.exp(-values))


def lanes_of(shape):
    return lax.broadcasted_iota(jnp.int32, shape, 1)


def swap_halves(tile):
    first = lax.rem(lanes_of(tile.shape), HD) < HD // 2
    return jnp.where(first, pltpu.roll(tile, LANES - HD // 2, 1), pltpu.roll(tile, HD // 2, 1))


def turn_back(part, cosine, sine, packed):
    if packed:
        left = lanes_of(part.shape) < HD
        cosine, sine = jnp.where(left, cosine, 1.0), jnp.where(left, sine, 0.0)
    return (part * cosine - swap_halves(part) * sine).astype(BF)


def tile_of(values, index):
    return values[:, index * LANES : (index + 1) * LANES]


def signal_all(group, me, axis):
    barrier = pltpu.get_barrier_semaphore()
    for k in range(1, group):
        pl.semaphore_signal(
            barrier, inc=1, device_id={axis: lax.rem(me + k, group)}, device_id_type=MESH
        )
    pl.semaphore_wait(barrier, group - 1)


PIECES = 2


class Sum:
    order = (2, 1, 3)

    def __init__(self, group, me, send, recv, full, sems):
        self.group, self.me, self.send, self.recv, self.full, self.sems = group, me, send, recv, full, sems
        self.wide = send.shape[-1]

    def remote(self, source, target, stage, k, piece):
        copy = pltpu.make_async_remote_copy(
            src_ref=source, dst_ref=target, send_sem=self.sems.at[stage, k - 1, piece],
            recv_sem=self.sems.at[stage + 1, k - 1, piece],
            device_id={"mp": lax.rem(self.me + k, self.group)}, device_id_type=MESH,
        )
        copy.start()
        return copy

    def start(self, make_piece):
        self.make, self.out, self.back = make_piece, [], []
        for piece in range(PIECES):
            copies = []
            for k in self.order:
                at = (k - 1, piece)
                self.send[at] = self.part(lax.rem(self.me + k, self.group), piece).astype(BF)
                copies.append(self.remote(self.send.at[at], self.recv.at[at], 0, k, piece))
            self.out.append(copies)

    def part(self, c, piece):
        start = c * (PIECES * self.wide) + piece * self.wide
        return self.make(pl.multiple_of(start, self.wide), self.wide)

    def middle(self):
        for piece in range(PIECES):
            total = self.part(self.me, piece).astype(BF).astype(F32)
            for k, copy in zip(self.order, self.out[piece]):
                copy.wait_recv()
                total = total + self.recv[k - 1, piece].astype(F32)
            self.full[self.me, piece] = total.astype(BF)
            where = self.full.at[self.me, piece]
            self.back.append([self.remote(where, where, 2, k, piece) for k in self.order])

    def finish(self):
        for copies in self.back:
            for copy in copies:
                copy.wait_recv()
        return jnp.concatenate(
            [self.full[c, piece] for c in range(self.group) for piece in range(PIECES)], axis=1
        )

    def drain(self):
        for copies in self.out + self.back:
            for copy in copies:
                copy.wait_send()


def vmem(count):
    return [pl.BlockSpec(memory_space=pltpu.VMEM)] * count


def sum_scratch(mp, n, model):
    wide = model // mp // PIECES
    return [
        pltpu.VMEM((mp - 1, PIECES, n, wide), BF),
        pltpu.VMEM((mp - 1, PIECES, n, wide), BF),
        pltpu.VMEM((mp, PIECES, n, wide), BF),
        pltpu.SemaphoreType.DMA((4, mp - 1, PIECES)),
    ]


def retreat_kernel(counts, heads, devices, mp, hidden, ins, names, inner, *refs):
    refs = list(refs)
    sources = {name: refs.pop(0) for name in ins}
    w_hbm = refs.pop(0)
    outs = {name: refs.pop(0) for name in names}
    held = {name: refs.pop(0) for name in ins}
    held.update({name: refs.pop(0) for name in names + inner})
    w_qkv, w_o, w_gu, w_d, fetch_sems, w_sems, keep_sems = [refs.pop(0) for _ in range(7)]
    query_t, grad_rows, grad_t, acc, delta = [refs.pop(0) for _ in range(5)]
    buffers = {level: [refs.pop(0) for _ in range(4)] for level in (1, 2)}
    sum_refs = {key: [refs.pop(0) for _ in range(4)] for key in ((K_HEAD, 2), (K_TAIL, 2), (K_HEAD, 1), (K_TAIL, 1))}
    me, mp_me = lax.axis_index("dp"), lax.axis_index("mp")
    model = w_o.shape[0]
    mix = heads * HD
    loads, keeps = {}, []

    def fetch(name):
        loads[name] = pltpu.make_async_copy(sources[name], held[name], fetch_sems.at[ins.index(name)])
        loads[name].start()

    def load(name, ref, start, index):
        loads[name] = pltpu.make_async_copy(w_hbm.at[:, start : start + ref.shape[1]], ref, w_sems.at[index])
        loads[name].start()

    def get(name):
        if name in loads:
            loads.pop(name).wait()
        return held[name]

    def need(name):
        if name in loads:
            loads.pop(name).wait()

    def keep(name):
        copy = pltpu.make_async_copy(held[name], outs[name], keep_sems.at[len(keeps)])
        copy.start()
        keeps.append(copy)

    barrier = pltpu.get_barrier_semaphore()

    def greet(k, carry):
        pl.semaphore_signal(
            barrier, inc=1, device_id={"dp": lax.rem(me + k, devices)}, device_id_type=MESH
        )
        return carry

    lax.fori_loop(1, devices, greet, 0)
    for k in range(1, mp):
        pl.semaphore_signal(
            barrier, inc=1, device_id={"mp": lax.rem(mp_me + k, mp)}, device_id_type=MESH
        )
    base_o = mix + 2 * LANES
    for name in (K_FLOW, K_GAINS, (K_PICK, 2), (K_ROWS, 2), (K_ATTN, 2), (K_FFN, 2), (K_PARTS, 2)):
        fetch(name)
    load(K_D, w_d, base_o + mix + 2 * hidden, 0)
    load(K_GU, w_gu, base_o + mix, 1)
    early = set(loads)

    def fetch_rest():
        load(K_O, w_o, base_o, 2)
        load(K_QKV, w_qkv, 0, 3)
        for name in ins:
            if name not in early:
                fetch(name)

    sums = {key: Sum(mp, mp_me, *items) for key, items in sum_refs.items()}
    vecs = held[K_VECS]
    vecs[...] = jnp.zeros(vecs.shape, F32)
    gate_of = {}

    def head(level):
        n = counts[level]
        name = lambda base: held[(base, level)]
        grad_update = get(K_FLOW)[...].astype(BF)
        if level:
            grad_update = dot_nn(get((K_PICK, level))[...], grad_update)
        grad_update = grad_update.astype(F32)
        rows_now = get((K_ROWS, level))[...].astype(F32)
        attn_now = get((K_ATTN, level))[...].astype(F32)
        gains = get(K_GAINS)
        gate = sigmoid(jnp.sum(rows_now * gains[2:3, :], axis=-1, keepdims=True))
        logit = jnp.sum(
            grad_update * (attn_now + get((K_FFN, level))[...].astype(F32)), axis=-1, keepdims=True
        )
        name(K_LOGIT)[...] = logit * gate * (1.0 - gate)
        grad_ffn = (gate * grad_update).astype(BF)
        name(K_GRAD_FFN)[...] = grad_ffn
        parts, parts_grad, hidden_out = get((K_PARTS, level)), name(K_PARTS_GRAD), name(K_HIDDEN)
        need(K_D)
        for t in range(hidden // LANES):
            cut = slice(t * LANES, (t + 1) * LANES)
            up_cut = slice(hidden + t * LANES, hidden + (t + 1) * LANES)
            if t % 2 == 0:
                both = dot_nn(grad_ffn, w_d[:, t * LANES : min((t + 2) * LANES, hidden)])
            grad_hidden = tile_of(both, t % 2)
            gate_part = parts[:, cut]
            up_part = parts[:, up_cut]
            sigma = sigmoid(gate_part)
            active = gate_part * sigma
            hidden_out[:, cut] = (active * up_part).astype(BF)
            parts_grad[:, cut] = (
                grad_hidden * up_part * sigma * (1.0 + gate_part * (1.0 - sigma))
            ).astype(BF)
            parts_grad[:, up_cut] = (grad_hidden * active).astype(BF)
        for base in (K_GRAD_FFN, K_HIDDEN, K_PARTS_GRAD, K_LOGIT):
            keep((base, level))
        return grad_update, rows_now, attn_now, gate

    def head_end(level, grad_update, rows_now, attn_now, gate):
        name = lambda base: held[(base, level)]
        gains = held[K_GAINS]
        need(K_GU)
        if level == 2:
            pl.semaphore_wait(barrier, devices - 1 + mp - 1)
        parts_now = name(K_PARTS_GRAD)[...]
        total = sums[(K_HEAD, level)]
        total.start(lambda start, wide: dot_nt(parts_now, w_gu[pl.ds(start, wide), :]))
        if level == 2:
            fetch_rest()
        unit, factor = unit_of(rows_now + attn_now)
        total.middle()
        grad_second = total.finish().astype(F32)
        vecs[2 - level : 3 - level, :] = jnp.sum(grad_second * unit, axis=0, keepdims=True)
        grad_middle = unit_back(grad_second * gains[1:2, :], unit, factor)
        name(K_MIDDLE)[...] = grad_middle
        grad_attn = (gate * grad_update + grad_middle).astype(BF)
        name(K_GRAD_ATTN)[...] = grad_attn
        need(K_O)
        name(K_GRAD_MIXED)[...] = dot_nn(grad_attn, w_o[...]).astype(BF)
        keep((K_GRAD_ATTN, level))

    def attention(level):
        n = counts[level]
        group = 8
        width = heads * n
        send_buf, recv_buf, send_sems, recv_sems = buffers[level]
        query, packed = get((K_QUERY, level)), get((K_PACKED, level))
        mixed_t, log_total = get((K_MIXED_T, level)), get((K_LOG, level))
        keys, query_place = get((K_KEYS, level)), get((K_PLACE, level))
        cosine, sine = get((K_COSINE, level)), get((K_SINE, level))
        grad_mixed, grad_qkv = held[(K_GRAD_MIXED, level)], held[(K_GRAD_QKV, level)]
        left = lanes_of((n, LANES)) < HD
        for t in range(heads // 2):
            part = grad_mixed[:, t * LANES : (t + 1) * LANES].astype(F32)
            grad_rows[2 * t * n : (2 * t + 1) * n, :] = jnp.where(
                left, 0.0, pltpu.roll(part, HD, 1)
            ).astype(BF)
            grad_rows[(2 * t + 1) * n : (2 * t + 2) * n, :] = jnp.where(left, 0.0, part).astype(BF)
        query_t[:, :width] = query[...].T
        grad_t[:, :width] = grad_rows[:width, :].T
        delta[:, :width] = jnp.sum(grad_t[:, :width].astype(F32) * mixed_t[...], axis=0, keepdims=True)
        acc[:, :width] = jnp.zeros((2 * HD, width), F32)

        def send_copy(e, source_index):
            return pltpu.make_async_remote_copy(
                src_ref=send_buf.at[e], dst_ref=recv_buf.at[source_index],
                send_sem=send_sems.at[e], recv_sem=recv_sems.at[source_index],
                device_id={"dp": e}, device_id_type=MESH,
            )

        def one_block(b, carry):
            part = packed[pl.ds(b * group, group)].reshape(group * n, 2 * HD)
            scores = dot_nn(part, query_t[:, :width])
            place = keys[pl.ds(b * group, group)].reshape(group * n, LANES)
            place = jnp.concatenate([place] * (width // LANES), axis=1)
            scores = jnp.where(place <= query_place[...], scores, NEG)
            soft = jnp.exp(scores - log_total[...])
            grad_soft = dot_nn(part, grad_t[:, :width])
            grad_scores = (soft * (grad_soft - delta[:, :width])).astype(BF)
            grad_part = dot_nn(grad_scores, query[...]) + dot_nn(soft.astype(BF), grad_rows[:width, :])
            send_buf[pl.ds(b * group, group)] = grad_part.astype(BF).reshape(group, n, 2 * HD)
            acc[:, :width] += dot_tn(part, grad_scores)
            for g in range(group):
                e = b * group + g

                @pl.when(e < me)
                def _(e=e):
                    send_copy(e, me).start()

            return carry

        lax.fori_loop(0, me // group + 1, one_block, 0)
        grad_query = acc[:, :width].T * HD**-0.5
        for t in range(heads // 2):
            even = grad_query[2 * t * n : (2 * t + 1) * n, :]
            odd = grad_query[(2 * t + 1) * n : (2 * t + 2) * n, :]
            part = jnp.where(left, even, pltpu.roll(odd, HD, 1))
            grad_qkv[:, t * LANES : (t + 1) * LANES] = turn_back(part, cosine[...], sine[...], False)

        def add(e, carry):
            send_copy(me, e).wait_recv()
            return carry + recv_buf[e].astype(F32)

        part = lax.fori_loop(me + 1, devices, add, send_buf[me].astype(F32))
        grad_qkv[:, mix:] = turn_back(part, cosine[...], sine[...], True)

        def drain():
            def sent(e, carry):
                send_copy(e, me).wait_send()
                return carry

            lax.fori_loop(0, me, sent, 0)

        return drain

    def tail(level):
        gains, flow = held[K_GAINS], held[K_FLOW]
        grad_now = held[(K_GRAD_QKV, level)][...]
        need(K_QKV)
        total = sums[(K_TAIL, level)]
        total.start(lambda start, wide: dot_nt(grad_now, w_qkv[pl.ds(start, wide), :]))
        keep((K_GRAD_QKV, level))
        rows_now = held[(K_ROWS, level)][...].astype(F32)
        unit, factor = unit_of(rows_now)
        logit = held[(K_LOGIT, level)][...]
        vecs[7 - level : 8 - level, :] = jnp.sum(rows_now * logit, axis=0, keepdims=True)
        total.middle()
        grad_normed = total.finish().astype(F32)
        vecs[5 - level : 6 - level, :] = jnp.sum(grad_normed * unit, axis=0, keepdims=True)
        grad_rows_now = (
            unit_back(grad_normed * gains[0:1, :], unit, factor)
            + held[(K_MIDDLE, level)][...]
            + logit * gains[2:3, :]
        ).astype(BF)
        flow[...] = flow[...] + dot_tn(held[(K_PICK, level)][...], grad_rows_now)

    drains = []
    for level in (2, 1):
        head_end(level, *head(level))
        drains.append(attention(level))
        tail(level)
    held[K_FLOW_OUT][...] = held[K_FLOW][...]
    keep(K_FLOW_OUT)
    head(0)
    keep(K_VECS)
    for drain in drains:
        drain()
    for item in sums.values():
        item.drain()
    for copy in keeps:
        copy.wait()


def retreat(cotangent, kept, weights, heads, devices, mp, ident):
    counts = tuple(kept[(K_ROWS, level)].shape[0] for level in range(3))
    model = cotangent.shape[1]
    mix = heads * HD
    hidden = kept[(K_PARTS, 0)].shape[1] // 2
    ins = {K_FLOW: cotangent, K_GAINS: kept[K_GAINS]}
    inner = {}
    shapes = {K_FLOW_OUT: (cotangent.shape, F32), K_VECS: ((8, model), F32)}
    for level, n in enumerate(counts):
        for base in (K_ROWS, K_ATTN, K_FFN, K_PARTS):
            ins[(base, level)] = kept[(base, level)]
        if level:
            for base in (K_PICK, K_QUERY, K_PACKED, K_MIXED_T, K_LOG, K_KEYS, K_PLACE, K_COSINE, K_SINE):
                ins[(base, level)] = kept[(base, level)]
            shapes[(K_GRAD_QKV, level)] = ((n, mix + 2 * HD), BF)
            shapes[(K_GRAD_ATTN, level)] = ((n, model), BF)
            inner[(K_GRAD_MIXED, level)] = ((n, mix), BF)
            inner[(K_MIDDLE, level)] = ((n, model), F32)
        shapes[(K_GRAD_FFN, level)] = ((n, model), BF)
        shapes[(K_HIDDEN, level)] = ((n, hidden), BF)
        shapes[(K_PARTS_GRAD, level)] = ((n, 2 * hidden), BF)
        shapes[(K_LOGIT, level)] = ((n, 1), F32)
    names = tuple(shapes)
    most = heads * max(counts[1:])
    anywhere = pl.BlockSpec(memory_space=pl.ANY)
    outs = pl.pallas_call(
        functools.partial(retreat_kernel, counts, heads, devices, mp, hidden, tuple(ins), names, tuple(inner)),
        out_shape=tuple(jax.ShapeDtypeStruct(*shapes[name]) for name in names),
        in_specs=[anywhere] * (len(ins) + 1),
        out_specs=tuple([anywhere] * len(names)),
        scratch_shapes=[pltpu.VMEM(item.shape, item.dtype) for item in ins.values()]
        + [pltpu.VMEM(*shape) for shape in (*shapes.values(), *inner.values())]
        + [
            pltpu.VMEM((model, mix + 2 * HD), BF),
            pltpu.VMEM((model, mix), BF),
            pltpu.VMEM((model, 2 * hidden), BF),
            pltpu.VMEM((model, hidden), BF),
            pltpu.SemaphoreType.DMA((len(ins),)),
            pltpu.SemaphoreType.DMA((4,)),
            pltpu.SemaphoreType.DMA((len(names),)),
            pltpu.VMEM((2 * HD, most), BF),
            pltpu.VMEM((most, 2 * HD), BF),
            pltpu.VMEM((2 * HD, most), BF),
            pltpu.VMEM((2 * HD, most), F32),
            pltpu.VMEM((1, most), F32),
        ]
        + [
            item
            for level in (1, 2)
            for item in (
                pltpu.VMEM((devices, counts[level], 2 * HD), BF),
                pltpu.VMEM((devices, counts[level], 2 * HD), BF),
                pltpu.SemaphoreType.DMA((devices,)),
                pltpu.SemaphoreType.DMA((devices,)),
            )
        ]
        + [item for level in (2, 2, 1, 1) for item in sum_scratch(mp, counts[level], model)],
        compiler_params=pltpu.CompilerParams(
            collective_id=ident, has_side_effects=True, vmem_limit_bytes=VMEM_LIMIT
        ),
        name="retreat",
    )(*ins.values(), weights)
    return dict(zip(names, outs))


def plane(me):
    return me // 8, lax.rem(me // 2, 4), lax.rem(me, 2)


def peer(x, y, core):
    return {"dp": (lax.rem(x, 4) * 4 + lax.rem(y, 4)) * 2 + core}


def shifted(x, y, core, axis, k):
    return peer(x + k, y, core) if axis == 0 else peer(x, y + k, core)


def meet(me, partners):
    barrier = pltpu.get_barrier_semaphore()
    for device in partners:
        pl.semaphore_signal(barrier, inc=1, device_id=device, device_id_type=MESH)
    pl.semaphore_wait(barrier, len(partners))


def plane_partners(x, y, core):
    return (
        [peer(x, y, 1 - core)]
        + [shifted(x, y, core, 0, k) for k in (1, 2, 3)]
        + [shifted(x, y, core, 1, k) for k in (1, 2, 3)]
    )


class Spread:
    def __init__(self, groups, x, y, core, shard, full, pair, send_sems, recv_sems):
        self.x, self.y, self.core = x, y, core
        self.count = len(groups)
        self.items = [(shard.at[:, low:high], full, slice(low, high), axis) for low, high, axis in groups]
        self.items.append((pair.at[x, y, core], pair, slice(None), 0))
        self.send_sems, self.recv_sems = send_sems, recv_sems
        self.started = []
        self.waits = [{} for _ in self.items]

    def remote(self, g, index, source, target, device):
        copy = pltpu.make_async_remote_copy(
            src_ref=source, dst_ref=target, send_sem=self.send_sems.at[g, index],
            recv_sem=self.recv_sems.at[g, index], device_id=device, device_id_type=MESH,
        )
        copy.start()
        self.started.append(copy)
        return copy

    def line(self, g, at, first, count):
        _, full, cut, axis = self.items[g]
        if axis == 0:
            return full.at[pl.ds(first, count), at, self.core, :, cut]
        return full.at[at, pl.ds(first, count), self.core, :, cut]

    def one(self, g):
        own, full, cut, axis = self.items[g]
        self.waits[g][1] = [
            self.remote(
                g, k - 1, own, full.at[self.x, self.y, self.core, :, cut],
                shifted(self.x, self.y, self.core, axis, k),
            )
            for k in (2, 1, 3)
        ]

    def two(self, g):
        axis = self.items[g][-1]
        for copy in self.waits[g][1]:
            copy.wait_recv()
        mine = self.line(g, self.y if axis == 0 else self.x, 0, 4)
        self.waits[g][2] = [
            self.remote(g, 3 + i, mine, mine, shifted(self.x, self.y, self.core, 1 - axis, k))
            for i, k in enumerate((1, 3))
        ]

    def three(self, g):
        axis = self.items[g][-1]
        at = self.y if axis == 0 else self.x
        self.waits[g][3] = []
        for i, k in enumerate((1, 3)):
            self.waits[g][2][i].wait_recv()
            piece = self.line(g, lax.rem(at + 4 - k, 4), 2 * i, 2)
            self.waits[g][3].append(
                self.remote(g, 5 + i, piece, piece, shifted(self.x, self.y, self.core, 1 - axis, k))
            )

    def four(self, g):
        _, full, cut, _ = self.items[g]
        for copy in self.waits[g][3]:
            copy.wait_recv()
        mine = full.at[:, :, self.core, :, cut]
        self.waits[g][4] = [self.remote(g, 7, mine, mine, peer(self.x, self.y, 1 - self.core))]

    def five(self, g):
        self.waits[g][4][0].wait_recv()

    def run(self, *groups):
        for work, g in zip((self.two, self.one, self.three, self.four, self.five), groups):
            if g is not None and 0 <= g < self.count:
                work(g)

    def step(self, i):
        self.run(i, i + 3, i - 2, i - 4, i - 5)

    def drain(self):
        for copy in self.started:
            copy.wait_send()


def advance_kernel(counts, heads, devices, mp, hidden, groups, names, *refs):
    refs = list(refs)
    (tokens, depths, second_slot, third_slot, w_query, w_key, w_value, w_out, w_gate, w_up, w_down,
     norm_first, norm_second, router, cosine_in, sine_in) = [refs.pop(0) for _ in range(16)]
    outs = {name: refs.pop(0) for name in names}
    held = {name: refs.pop(0) for name in names}
    shard, own_sem, send_sems, recv_sems, query_t, top, total, acc, hidden_v, keep_sems, kv_send, kv_recv = [
        refs.pop(0) for _ in range(12)
    ]
    sum_refs = refs
    me, mp_me = lax.axis_index("dp"), lax.axis_index("mp")
    x, y, core = plane(me)
    weights = held[K_WEIGHTS]
    rows, model = tokens.shape
    mix = heads * HD
    lanes = lanes_of((rows, LANES))
    left = lanes < HD
    keeps = []

    def keep(name):
        copy = pltpu.make_async_copy(held[name], outs[name], keep_sems.at[len(keeps)])
        copy.start()
        keeps.append(copy)

    barrier = pltpu.get_barrier_semaphore()

    def greet(k, carry):
        pl.semaphore_signal(
            barrier, inc=1, device_id={"dp": lax.rem(me + k, devices)}, device_id_type=MESH
        )
        return carry

    lax.fori_loop(1, devices, greet, 0)
    for k in range(1, mp):
        pl.semaphore_signal(
            barrier, inc=1, device_id={"mp": lax.rem(mp_me + k, mp)}, device_id_type=MESH
        )

    token = lanes_of((1, rows)).astype(F32)
    picks, marks, query_places = [None], [None], []
    query_places.append(
        (lax.rem(lanes_of((1, heads * rows)), rows) + me * rows).astype(F32)
    )
    held[(K_PLACE, 0)][...] = query_places[0]
    for level, slot, deep in ((1, second_slot, 2), (2, third_slot, 3)):
        count = counts[level]
        slots = lax.broadcasted_iota(jnp.int32, (count, rows), 0)
        active = (depths[...] >= deep) & (slot[...] >= 0)
        chosen = jnp.where(active, slot[...], -1) == slots
        pick = jnp.where(chosen, 1.0, 0.0).astype(BF)
        held[(K_PICK, level)][...] = pick
        picks.append(pick)
        marks.append(
            jnp.min(jnp.where(chosen, token, float(rows)), axis=1, keepdims=True)
        )
    depth = w_query.shape[0]
    wide = jnp.zeros((1, LANES - depth), F32)
    gain_rows = jnp.concatenate(
        [jnp.concatenate([ref[...].astype(F32), wide], axis=1) for ref in (norm_first, norm_second, router)]
        + [jnp.zeros((LANES - 3, LANES), F32)],
        axis=0,
    )
    extra = gain_rows.T[:depth, :]
    rest = counts[1] - depth
    lane = lanes_of((depth, LANES))
    over = jnp.concatenate([marks[1][depth:, :], jnp.full((depth - rest, 1), float(rows), F32)], axis=0)
    extra = jnp.where(lane == 3, marks[1][:depth, :], extra)
    extra = jnp.where(lane == 4, over, extra)
    extra = jnp.where(lane == 5, marks[2], extra)
    pair = jnp.concatenate([w_key[...].astype(F32), w_value[...].astype(F32)], axis=1).astype(BF)
    start = 0
    for part in (
        w_query[...], pair, extra.astype(BF), w_out[...], w_gate[...], w_up[...], w_down[...],
    ):
        shard[:, start : start + part.shape[1]] = part
        start += part.shape[1]
    own = pltpu.make_async_copy(shard, weights.at[x, y, core], own_sem)
    own.start()
    spread = Spread(groups, x, y, core, shard, weights, held[K_PACKED, 0], send_sems, recv_sems)
    pl.semaphore_wait(barrier, devices - 1 + mp - 1)
    for g in range(3):
        spread.one(g)
    own.wait()
    for level, pick in ((1, picks[1]), (2, picks[2])):
        sublane = lax.broadcasted_iota(jnp.int32, (16, rows), 0)
        probe = jnp.where(sublane == 0, token, 1.0).astype(BF)
        found = dot_nt(probe, jnp.concatenate([pick] * heads, axis=0))
        place = jnp.where(found[1:2, :] > 0.5, found[0:1, :] + (me * rows).astype(F32), FAR)
        held[(K_PLACE, level)][...] = place
        query_places.append(place)
        table = jnp.concatenate([cosine_in[...], sine_in[...]], axis=1)
        turned = lax.dot_general(
            pick.astype(F32), table, (((1,), (0,)), ((), ())),
            preferred_element_type=F32, precision=lax.Precision.HIGHEST,
        )
        held[(K_COSINE, level)][...] = turned[:, :LANES]
        held[(K_SINE, level)][...] = turned[:, LANES:]
    spread.run(0, 3)
    spread.run(1, 4, 0)
    spread.run(2, 5, None, 0)
    spread.run(3, 6, 1, None, 0)

    gains = held[K_GAINS]
    columns = weights[:, :, :, :, mix + LANES : mix + 2 * LANES].reshape(model, LANES).astype(F32)
    gains[...] = columns.T[: gains.shape[0], :]
    keep(K_GAINS)

    def kv_copy(level, e, source_index):
        packed = held[(K_PACKED, level)]
        return pltpu.make_async_remote_copy(
            src_ref=packed.at[me], dst_ref=packed.at[me],
            send_sem=kv_send.at[level, e], recv_sem=kv_recv.at[level, source_index],
            device_id={"dp": e}, device_id_type=MESH,
        )

    def project(level, now):
        n = counts[level]
        name = lambda base: held[(base, level)]
        name(K_ROWS)[...] = now
        unit, unused = unit_of(now.astype(F32))
        normed = (unit * gains[0:1, :]).astype(BF)
        name(K_NORMED)[...] = normed
        cosine, sine = (cosine_in[...], sine_in[...]) if level == 0 else (name(K_COSINE)[...], name(K_SINE)[...])
        here = left[:n]
        tiles = [None] * (heads // 2 + 1)
        for t in range(heads // 2, -1, -2):
            low = max(t - 1, 0)
            both = dot_nn(normed, weights[:, :, :, :, low * LANES : (t + 1) * LANES].reshape(model, (t + 1 - low) * LANES))
            for j in range(low, t + 1):
                part = tile_of(both, j - low)
                if j == heads // 2:
                    part = part * jnp.where(here, cosine, 1.0) + swap_halves(part) * jnp.where(here, sine, 0.0)
                    if level == 0:
                        name(K_PACKED)[x, y, core] = part.astype(BF)
                        spread.one(spread.count)
                        continue
                    name(K_PACKED)[me] = part.astype(BF)

                    def send(k, carry):
                        kv_copy(level, devices - 1 - k, me).start()
                        return carry

                    lax.fori_loop(0, devices - 1 - me, send, 0)
                else:
                    tiles[j] = part * cosine + swap_halves(part) * sine

        def clear(e, carry):
            name(K_PACKED)[e] = jnp.zeros((n, 2 * HD), BF)
            return carry

        if level:
            lax.fori_loop(me + 1, devices, clear, 0)
        for t in range(heads // 2):
            scaled = tiles[t].astype(BF).astype(F32) * HD**-0.5
            name(K_QUERY)[2 * t * n : (2 * t + 1) * n, :] = jnp.where(here, scaled, 0.0).astype(BF)
            name(K_QUERY)[(2 * t + 1) * n : (2 * t + 2) * n, :] = jnp.where(
                here, pltpu.roll(scaled, HD, 1), 0.0
            ).astype(BF)
        width = heads * n
        query_t[:, :width] = name(K_QUERY)[...].T
        top[:, :width] = jnp.full((1, width), NEG, F32)
        total[:, :width] = jnp.zeros((1, width), F32)
        acc[:, :width] = jnp.zeros((2 * HD, width), F32)
        for base in (K_ROWS, K_NORMED, K_QUERY):
            keep((base, level))

    def group_of(level):
        return (4, 8, 16)[level]

    def block(level, b):
        n, group = counts[level], group_of(level)
        width = heads * n
        if level:
            for g in range(group):
                e = b * group + g

                @pl.when(e < me)
                def _(e=e):
                    kv_copy(level, me, e).wait_recv()

            part = held[K_PACKED, level][pl.ds(b * group, group)].reshape(group * n, 2 * HD)
        else:
            part = held[K_PACKED, level][b // 2, 2 * (b % 2) : 2 * (b % 2) + 2].reshape(group * n, 2 * HD)
        scores = dot_nn(part, query_t[:, :width])
        if level:
            place = held[(K_KEYS, level)][pl.ds(b * group, group)].reshape(group * n, LANES)
        else:
            place = (lax.broadcasted_iota(jnp.int32, (group * n, LANES), 0) + b * (group * n)).astype(F32)
        place = jnp.concatenate([place] * (width // LANES), axis=1)
        scores = jnp.where(place <= held[(K_PLACE, level)][...], scores, NEG)
        before = top[:, :width]
        peak = jnp.maximum(before, jnp.max(scores, axis=0, keepdims=True))
        soft = jnp.exp(scores - peak)
        fade = jnp.exp(before - peak)
        total[:, :width] = total[:, :width] * fade + jnp.sum(soft, axis=0, keepdims=True)
        acc[:, :width] = acc[:, :width] * fade + dot_tn(part, soft.astype(BF))
        top[:, :width] = peak

    def mix_heads(level):
        n = counts[level]
        width = heads * n
        mixed_t = acc[:, :width] / total[:, :width]
        held[(K_MIXED_T, level)][...] = mixed_t
        held[(K_LOG, level)][...] = top[:, :width] + jnp.log(total[:, :width])
        mixed = mixed_t.T
        for t in range(heads // 2):
            even = mixed[2 * t * n : (2 * t + 1) * n, :]
            odd = mixed[(2 * t + 1) * n : (2 * t + 2) * n, :]
            held[(K_MIXED, level)][:, t * LANES : (t + 1) * LANES] = jnp.where(
                left[:n], pltpu.roll(even, HD, 1), odd
            ).astype(BF)
        for base in (K_MIXED_T, K_LOG, K_MIXED, K_PACKED):
            keep((base, level))

    sums = [Sum(mp, mp_me, *sum_refs[4 * i : 4 * i + 4]) for i in range(2 * len(counts))]
    chunk = model // mp
    base_o = mix + 2 * LANES
    base_gu = base_o + mix
    base_d = base_gu + 2 * hidden

    def rows_of(start, wide, low, high):
        return weights[start // chunk, pl.ds(lax.rem(start, chunk) // LANES, wide // LANES), :, :, low:high].reshape(
            wide, high - low
        )

    def attn_sum(level):
        mixed_now = held[K_MIXED, level][...]
        total = sums[2 * level]
        total.start(lambda start, wide: dot_nt(mixed_now, rows_of(start, wide, base_o, base_gu)))
        return total

    def take_attn(level, total):
        attn = total.finish()
        held[K_ATTN, level][...] = attn
        rows_now = held[K_ROWS, level][...].astype(F32)
        unit, unused = unit_of(rows_now + attn.astype(F32))
        held[K_SECOND, level][...] = (unit * gains[1:2, :]).astype(BF)

    def widen(level):
        second, parts = held[K_SECOND, level][...], held[K_PARTS, level]
        for t in range(2 * hidden // 256):
            low = base_gu + t * 256
            parts[:, t * 256 : (t + 1) * 256] = dot_nn(
                second, weights[:, :, :, :, low : low + 256].reshape(model, 256)
            )
        n = counts[level]
        for t in range(hidden // LANES):
            cut = slice(t * LANES, (t + 1) * LANES)
            gate_part = parts[:, cut]
            up_part = parts[:, hidden + t * LANES : hidden + (t + 1) * LANES]
            hidden_v[:n, cut] = (gate_part * sigmoid(gate_part) * up_part).astype(BF)

    def narrow(level):
        hidden_now = hidden_v[: counts[level], :]
        total = sums[2 * level + 1]
        total.start(lambda start, wide: dot_nt(hidden_now, rows_of(start, wide, base_d, base_d + hidden)))
        for base in (K_ATTN, K_SECOND, K_PARTS):
            keep((base, level))
        rows_now = held[K_ROWS, level][...].astype(F32)
        gate = sigmoid(jnp.sum(rows_now * gains[2:3, :], axis=-1, keepdims=True))
        total.middle()
        ffn = total.finish()
        held[K_FFN, level][...] = ffn
        keep((K_FFN, level))
        update = (gate * (held[K_ATTN, level][...].astype(F32) + ffn.astype(F32))).astype(BF)
        if level:
            update = dot_tn(held[K_PICK, level][...], update)
        held[K_STATE][...] = held[K_STATE][...] + update.astype(F32)

    project(0, tokens[...])
    held[K_STATE][...] = tokens[...].astype(F32)
    for name in (
        (K_PLACE, 0), (K_PICK, 1), (K_PICK, 2), (K_PLACE, 1), (K_PLACE, 2), (K_COSINE, 1), (K_SINE, 1),
        (K_COSINE, 2), (K_SINE, 2),
    ):
        keep(name)
    spread.run(4, 7, 2)
    spread.two(spread.count)

    def key_places(e, carry):
        for level, lanes_at in ((1, (3, 4)), (2, (5,))):
            tile = weights[e // 8, lax.rem(e // 2, 4), lax.rem(e, 2), :, mix + LANES : mix + 2 * LANES].astype(F32)
            value = jnp.concatenate(
                [jnp.broadcast_to(tile[:, at : at + 1], (depth, LANES)) for at in lanes_at], axis=0
            )[: counts[level], :]
            held[(K_KEYS, level)][e] = jnp.where(
                value < rows, value + (e * rows).astype(F32), FAR
            )
        return carry

    lax.fori_loop(0, devices, key_places, 0)
    keep((K_KEYS, 1))
    keep((K_KEYS, 2))
    spread.run(5, 8, 3, 1)
    spread.three(spread.count)
    spread.step(6)
    spread.four(spread.count)
    spread.step(7)
    spread.five(spread.count)
    for b in range(devices // group_of(0)):

        @pl.when(b * group_of(0) <= me)
        def _(b=b):
            block(0, b)

        if b in (2, 5):
            spread.step(8 + b // 3)
    mix_heads(0)
    total_0 = attn_sum(0)
    spread.step(10)
    total_0.middle()
    spread.run(None, None, 9, 7, 6)
    spread.run(None, None, 10, 8, 7)
    take_attn(0, total_0)
    spread.run(None, None, None, 9, 8)
    widen(0)
    spread.run(None, None, None, 10, 9)
    spread.run(None, None, None, None, 10)
    narrow(0)
    keep(K_WEIGHTS)
    for level in range(1, len(counts)):
        now = dot_nn(held[K_PICK, level][...], held[K_STATE][...].astype(BF)).astype(BF)
        project(level, now)

        def one_block(b, carry, level=level):
            block(level, b)
            return carry

        lax.fori_loop(0, me // group_of(level) + 1, one_block, 0)
        mix_heads(level)
        attn_total = attn_sum(level)
        attn_total.middle()
        take_attn(level, attn_total)
        widen(level)
        narrow(level)
    keep(K_STATE)
    spread.drain()
    for item in sums:
        item.drain()
    for level in range(1, len(counts)):

        def sent(e, carry, level=level):
            kv_copy(level, e, me).wait_send()
            return carry

        lax.fori_loop(me + 1, devices, sent, 0)
    for copy in keeps:
        copy.wait()


def advance(tokens, depths, second_slot, third_slot, matrices, vectors, tables, heads, devices, mp, ident):
    counts = (tokens.shape[0], SECOND_SLOTS, THIRD_SLOTS)
    rows, model = tokens.shape
    depth, mix = matrices[0].shape
    hidden = matrices[4].shape[1]
    total = 2 * mix + 2 * LANES + 3 * hidden
    cuts = [0, *range(mix + 2 * LANES, total - 640, 512), total - 640, total - 256, total]
    groups = [(a, b, i % 2) for i, (a, b) in enumerate(zip(cuts[:-1], cuts[1:]))]
    shapes = {
        K_STATE: ((rows, model), F32),
        K_WEIGHTS: ((4, 4, 2, depth, total), BF),
        K_GAINS: ((8, model), F32),
    }
    for level, n in enumerate(counts):
        width = heads * n
        shapes[(K_PLACE, level)] = ((1, width), F32)
        if level:
            shapes[(K_PICK, level)] = ((n, rows), BF)
            shapes[(K_COSINE, level)] = ((n, LANES), F32)
            shapes[(K_SINE, level)] = ((n, LANES), F32)
            shapes[(K_KEYS, level)] = ((devices, n, LANES), F32)
        for base in (K_ROWS, K_NORMED, K_ATTN, K_FFN, K_SECOND):
            shapes[(base, level)] = ((n, model), BF)
        shapes[(K_PARTS, level)] = ((n, 2 * hidden), F32)
        shapes[K_PACKED, level] = (((devices,) if level else (4, 4, 2)) + (n, 2 * HD), BF)
        shapes[(K_QUERY, level)] = ((width, 2 * HD), BF)
        shapes[(K_MIXED_T, level)] = ((2 * HD, width), F32)
        shapes[(K_LOG, level)] = ((1, width), F32)
        shapes[(K_MIXED, level)] = ((n, mix), BF)
    names = tuple(shapes)
    args = (tokens, depths, second_slot, third_slot, *matrices, *vectors, *tables)
    width = heads * rows
    outs = pl.pallas_call(
        functools.partial(advance_kernel, counts, heads, devices, mp, hidden, groups, names),
        out_shape=tuple(jax.ShapeDtypeStruct(*shapes[name]) for name in names),
        in_specs=vmem(len(args)),
        out_specs=tuple([pl.BlockSpec(memory_space=pl.ANY)] * len(names)),
        scratch_shapes=[pltpu.VMEM(*shapes[name]) for name in names]
        + [
            pltpu.VMEM((depth, total), BF),
            pltpu.SemaphoreType.DMA(()),
            pltpu.SemaphoreType.DMA((len(groups) + 1, 8)),
            pltpu.SemaphoreType.DMA((len(groups) + 1, 8)),
            pltpu.VMEM((2 * HD, width), BF),
            pltpu.VMEM((1, width), F32),
            pltpu.VMEM((1, width), F32),
            pltpu.VMEM((2 * HD, width), F32),
            pltpu.VMEM((rows, hidden), BF),
            pltpu.SemaphoreType.DMA((len(names),)),
            pltpu.SemaphoreType.DMA((len(counts), devices)),
            pltpu.SemaphoreType.DMA((len(counts), devices)),
        ]
        + [item for n in counts for _ in range(2) for item in sum_scratch(mp, n, model)],
        compiler_params=pltpu.CompilerParams(
            collective_id=ident, has_side_effects=True, vmem_limit_bytes=VMEM_LIMIT
        ),
        name="advance",
    )(*args)
    kept = dict(zip(names, outs))
    kept[K_PACKED, 0] = kept[K_PACKED, 0].reshape(devices, rows, 2 * HD)
    return kept


SLOTS = 5
CORE_SLOTS = 3
GROUP = 512


class Collect:
    def __init__(self, spans, groups, x, y, core, turned, rights, vectors, store, slots, core_recv, relay_recv, first_recv, mid, last_recv, send_sems, recv_sems, credit, turn):
        self.spans, self.groups = spans, groups
        self.x, self.y, self.core = x, y, core
        self.turned, self.rights, self.vectors, self.store, self.slots = turned, rights, vectors, store, slots
        self.core_recv, self.relay_recv, self.first_recv = core_recv, relay_recv, first_recv
        self.mid, self.last_recv, self.credit = mid, last_recv, credit
        self.send_sems, self.recv_sems = send_sems, recv_sems
        self.turn = turn
        self.waits = [{} for _ in groups]
        self.done = set()

    def remote(self, g, index, source, target, device):
        copy = pltpu.make_async_remote_copy(
            src_ref=source, dst_ref=target, send_sem=self.send_sems.at[g, index],
            recv_sem=self.recv_sems.at[g, index], device_id=device, device_id_type=MESH,
        )
        copy.start()
        return copy

    def held(self, slot, axis, at, first, count):
        if axis == 0:
            return self.slots.at[slot, at, pl.ds(first, count), self.core]
        return self.slots.at[slot, pl.ds(first, count), at, self.core]

    def zero(self, g):
        slot, waits = g % SLOTS, self.waits
        if g >= SLOTS:
            for stage in range(3):
                for copy in waits[g - SLOTS][stage]:
                    copy.wait_send()
        column = 0
        for section, low, high in self.groups[g][1]:
            wide = high - low
            if section < 4:
                if section not in self.done:
                    self.done.add(section)
                    self.turn(section)
                base = self.spans[section][0]

            def rows_of(m, carry, section=section, low=low, high=high, column=column, wide=wide):
                start = pl.multiple_of(m * 1024, 1024)
                if section < 4:
                    value = dot_nn(
                        self.turned[section % 2, pl.ds(start, 1024), :], self.rights[:, base + low : base + high]
                    )
                else:
                    few = self.vectors[:, pl.ds(start, 1024)]
                    value = jnp.concatenate([few, jnp.zeros((LANES - few.shape[0], 1024), F32)], axis=0).T
                self.slots[slot, pl.ds(m * 2, 2), :, :, :, column : column + wide] = (
                    value.astype(BF).reshape(2, 4, 2, 64, wide)
                )
                return carry

            lax.fori_loop(0, 2, rows_of, 0)
            column += wide
        if g >= CORE_SLOTS:
            pl.semaphore_wait(self.credit, 1)
        waits[g][0] = [
            self.remote(
                g, 0, self.slots.at[slot, :, :, 1 - self.core, :, :column],
                self.core_recv.at[g % CORE_SLOTS, :, :, :, :column], peer(self.x, self.y, 1 - self.core),
            )
        ]

    def first(self, g):
        slot, (width, _, axis) = g % SLOTS, self.groups[g]
        waits, slots = self.waits, self.slots
        waits[g][0][0].wait_recv()

        def add(i, carry):
            slots[slot, i, :, self.core, :, :width] = (
                slots[slot, i, :, self.core, :, :width] + self.core_recv[g % CORE_SLOTS, i, :, :, :width]
            )
            return carry

        lax.fori_loop(0, 4, add, 0)
        if g + CORE_SLOTS < len(self.groups):
            pl.semaphore_signal(
                self.credit, inc=1, device_id=peer(self.x, self.y, 1 - self.core), device_id_type=MESH
            )
        at = self.x if axis == 0 else self.y
        waits[g][1] = [
            self.remote(
                g, 1 + i, self.held(slot, axis, lax.rem(at + 2, 4), 2 * i, 2).at[:, :, :width],
                self.relay_recv.at[g, i, :, :, :width], shifted(self.x, self.y, self.core, axis, k),
            )
            for i, k in enumerate((1, 3))
        ]

    def second(self, g):
        slot, (width, _, axis) = g % SLOTS, self.groups[g]
        waits, slots = self.waits, self.slots
        at = self.x if axis == 0 else self.y
        waits[g][2] = []
        for i, k in enumerate((1, 3)):
            waits[g][1][i].wait_recv()
            there = lax.rem(at + k, 4)
            for j in range(2):
                b = 2 * i + j
                where = (slot, there, b, self.core) if axis == 0 else (slot, b, there, self.core)
                where = where + (slice(None), slice(0, width))
                slots[where] = slots[where] + self.relay_recv[g, i, j, :, :width]
            waits[g][2].append(
                self.remote(
                    g, 3 + i, self.held(slot, axis, there, 0, 4).at[:, :, :width],
                    self.first_recv.at[g, i, :, :, :width], shifted(self.x, self.y, self.core, axis, k),
                )
            )

    def third(self, g):
        slot, (width, _, axis) = g % SLOTS, self.groups[g]
        waits, slots = self.waits, self.slots
        at, other = (self.x, self.y) if axis == 0 else (self.y, self.x)
        for copy in waits[g][2]:
            copy.wait_recv()
        for b in range(4):
            where = (slot, at, b, self.core) if axis == 0 else (slot, b, at, self.core)
            self.mid[g, b, :, :width] = (
                slots[where + (slice(None), slice(0, width))].astype(F32)
                + self.first_recv[g, 0, b, :, :width].astype(F32)
                + self.first_recv[g, 1, b, :, :width].astype(F32)
            ).astype(BF)
        waits[g][3] = [
            self.remote(
                g, 4 + k, self.mid.at[g, lax.rem(other + k, 4), :, :width],
                self.last_recv.at[g, k - 1, :, :width],
                shifted(self.x, self.y, self.core, 1 - axis, k),
            )
            for k in (2, 1, 3)
        ]

    def fourth(self, g):
        width, pieces, axis = self.groups[g]
        other = self.y if axis == 0 else self.x
        value = self.mid[g, other, :, :width].astype(F32)
        for copy in self.waits[g][3]:
            copy.wait_recv()
        for k in range(3):
            value = value + self.last_recv[g, k, :, :width].astype(F32)
        column = 0
        for section, low, high in pieces:
            self.store(section, low, value[:, column : column + high - low])
            column += high - low

    def run(self, *groups):
        for work, g in zip((self.zero, self.first, self.second, self.third, self.fourth), groups):
            if g is not None and 0 <= g < len(self.groups):
                work(g)

    def step(self, i):
        self.run(i, i - 1, i - 2, i - 4, i - 5)

    def drain(self):
        count = len(self.groups)
        for g in range(count):
            for stage in range(4):
                if stage == 3 or g >= count - SLOTS:
                    for copy in self.waits[g][stage]:
                        copy.wait_send()


def finish_kernel(n, heads, devices, mp, group, levels, spans, groups, *refs):
    refs = list(refs)
    gains, query_place, log_total, cosine, sine, logit, vecs = [refs.pop(0) for _ in range(7)]
    large = [refs.pop(0) for _ in range(6)]
    w_hbm = refs.pop(0)
    sources = [[refs.pop(0) if level or i not in (4, 7) else None for i in range(8)] for level in range(len(levels))]
    flow_out, q_out, k_out, v_out, out_out, gate_out, up_out, down_out, vec_out = [refs.pop(0) for _ in range(9)]
    query_t, grad_rows, grad_t, acc, delta, send_buf, recv_buf, pair_buf, kv_send, kv_recv = [refs.pop(0) for _ in range(10)]
    w_qkv, w_sem, w_gu, gu_sems, middle = [refs.pop(0) for _ in range(5)]
    sum_refs = [[refs.pop(0) for _ in range(4)] for _ in range(2)]
    (lefts, turned, rights, vectors, slots, core_recv, relay_recv, first_recv, mid, last_recv,
     loads, send_sems, recv_sems, credit) = refs[:14]
    flow, rows_in, attn_in, query, mixed_t, packed = refs[14:20]
    large_copies = [
        pltpu.make_async_copy(source, target, refs[20].at[i])
        for i, (source, target) in enumerate(zip(large, refs[14:20]))
    ]
    me, mp_me = lax.axis_index("dp"), lax.axis_index("mp")
    x, y, core = plane(me)
    barrier = pltpu.get_barrier_semaphore()

    def greet(k, carry):
        pl.semaphore_signal(
            barrier, inc=1, device_id={"dp": lax.rem(me + k, devices)}, device_id_type=MESH
        )
        return carry

    lax.fori_loop(1, devices, greet, 0)
    for k in range(1, mp):
        pl.semaphore_signal(
            barrier, inc=1, device_id={"mp": lax.rem(mp_me + k, mp)}, device_id_type=MESH
        )

    hidden = gate_out.shape[1]
    mix = q_out.shape[1]
    base_o = mix + 2 * LANES
    load_o = pltpu.make_async_copy(w_hbm.at[:, base_o : base_o + mix], w_qkv.at[:, :mix], w_sem)
    load_o.start()
    wide = w_gu.shape[1]
    pieces = [(mp_me + k, piece) for piece in range(PIECES) for k in Sum.order]
    pieces += [(mp_me, piece) for piece in range(PIECES)]
    gu_loads = []

    def load_gu():
        i = len(gu_loads)
        if i < len(pieces):
            start = pl.multiple_of((lax.rem(pieces[i][0], mp) * PIECES + pieces[i][1]) * wide, wide)
            copy = pltpu.make_async_copy(
                w_hbm.at[pl.ds(start, wide), base_o + mix : base_o + mix + 2 * hidden],
                w_gu.at[i % w_gu.shape[0]], gu_sems.at[i % w_gu.shape[0]],
            )
            copy.start()
            gu_loads.append(copy)

    for _ in range(w_gu.shape[0]):
        load_gu()
    fetches = [[] for _ in range(4)]

    def fetch(s, side):
        row = 0
        for level, count in enumerate(levels):
            low, high = spans[s]
            target = (lefts.at[s % 2, row : row + count], rights.at[row : row + count, low:high])[side]
            if sources[level][2 * s + side] is not None:
                copy = pltpu.make_async_copy(
                    sources[level][2 * s + side], target, loads.at[level, 2 * s + side]
                )
                copy.start()
                fetches[s].append(copy)
            row += count

    fetch(0, 0)
    fetch(0, 1)
    for copy in large_copies:
        copy.start()

    def turn(section):
        for copy in fetches[section]:
            copy.wait()
        turned[section % 2] = lefts[section % 2].T
        if section < 2:
            fetch(section + 2, 0)

    def store(section, low, value):
        high = low + value.shape[1]
        if section == 0:
            middle_cut = min(max(hidden - low, 0), high - low)
            if middle_cut:
                gate_out[:, low : low + middle_cut] = value[:, :middle_cut]
            if low + middle_cut < high:
                up_out[:, low + middle_cut - hidden : high - hidden] = value[:, middle_cut:]
        elif section == 1:
            down_out[:, low:high] = value
        elif section == 2:
            out_out[:, low:high] = value
        elif section == 3:
            if low < mix:
                q_out[:, low : min(high, mix)] = value[:, : min(high, mix) - low]
            if high > mix:
                k_out[...] = value[:, mix - low : mix - low + HD]
                v_out[...] = value[:, mix - low + HD :]
        else:
            vec_out[...] = value.T[: vec_out.shape[0], :]

    work = Collect(
        spans, groups, x, y, core, turned, rights, vectors, store, slots, core_recv, relay_recv,
        first_recv, mid, last_recv, send_sems, recv_sems, credit, turn,
    )
    pl.semaphore_wait(barrier, devices - 1 + mp - 1)
    work.step(0)
    fetch(1, 0)
    for s in range(1, 4):
        fetch(s, 1)

    for copy in large_copies[:3]:
        copy.wait()
    update = flow[...].astype(BF).astype(F32)
    level = rows_in[...].astype(F32)
    gate = sigmoid(jnp.sum(level * gains[2:3, :], axis=-1, keepdims=True))
    parts_now = rights[0:n, : 2 * hidden]
    used = []

    def gu_piece(start, size):
        i = len(used)
        used.append(i)
        gu_loads[i].wait()
        value = dot_nt(parts_now, w_gu[i % w_gu.shape[0]])
        load_gu()
        return value

    head = Sum(mp, mp_me, *sum_refs[0])
    head.start(gu_piece)
    work.step(1)
    work.step(2)
    head.middle()
    work.step(3)
    grad_second = head.finish().astype(F32)
    unit, factor = unit_of(level + attn_in[...].astype(F32))
    vectors[...] = jnp.zeros(vectors.shape, F32)
    vectors[1:2, :] = (
        jnp.sum(grad_second * unit, axis=0, keepdims=True) + vecs[0:1, :] + vecs[1:2, :]
    )
    middle[...] = unit_back(grad_second * gains[1:2, :], unit, factor)
    grad_attn = (gate * update + middle[...]).astype(BF)
    lefts[0, 0:n, :] = grad_attn
    load_o.wait()
    grad_mixed = dot_nn(grad_attn, w_qkv[:, :mix]).astype(BF).astype(F32)
    load_w = pltpu.make_async_copy(w_hbm.at[:, : w_qkv.shape[1]], w_qkv, w_sem)
    load_w.start()
    work.step(4)
    left = lanes_of((n, LANES)) < HD
    for t in range(heads // 2):
        part = grad_mixed[:, t * LANES : (t + 1) * LANES]
        grad_rows[2 * t * n : (2 * t + 1) * n, :] = jnp.where(
            left, 0.0, pltpu.roll(part, HD, 1)
        ).astype(BF)
        grad_rows[(2 * t + 1) * n : (2 * t + 2) * n, :] = jnp.where(left, 0.0, part).astype(BF)
    for copy in large_copies[3:]:
        copy.wait()
    query_t[...] = query[...].T
    grad_t[...] = grad_rows[...].T
    delta[...] = jnp.sum(grad_t[...].astype(F32) * mixed_t[...], axis=0, keepdims=True)
    acc[...] = jnp.zeros(acc.shape, F32)
    width = heads * n

    chips = devices // 2
    chip = me // 2

    def send_copy(there, source_index):
        return pltpu.make_async_remote_copy(
            src_ref=send_buf.at[there, core], dst_ref=recv_buf.at[source_index],
            send_sem=kv_send.at[there], recv_sem=kv_recv.at[source_index],
            device_id={"dp": 2 * there + core}, device_id_type=MESH,
        )

    def one_block(b):
        part = packed[b * group : (b + 1) * group].reshape(group * n, 2 * HD)
        scores = dot_nn(part, query_t[...])
        place = (lax.broadcasted_iota(jnp.int32, (group * n, LANES), 0) + b * (group * n)).astype(F32)
        place = jnp.concatenate([place] * (width // LANES), axis=1)
        scores = jnp.where(place <= query_place[...], scores, NEG)
        weights = jnp.exp(scores - log_total[...])
        grad_weights = dot_nn(part, grad_t[...])
        grad_scores = (weights * (grad_weights - delta[...])).astype(BF)
        grad_part = dot_nn(grad_scores, query[...]) + dot_nn(weights.astype(BF), grad_rows[...])
        send_buf[b * group // 2 : (b + 1) * group // 2] = grad_part.astype(BF).reshape(group // 2, 2, n, 2 * HD)
        acc[...] += dot_tn(part, grad_scores)

    blocks = devices // group
    for b in range(blocks):
        if b in (2, 4, 6):
            work.step(4 + b // 2)

        @pl.when(b * group <= me)
        def _(b=b):
            one_block(b)

    pair_copy = pltpu.make_async_remote_copy(
        src_ref=send_buf.at[:, 1 - core], dst_ref=pair_buf,
        send_sem=kv_send.at[chips], recv_sem=kv_recv.at[chips],
        device_id=peer(x, y, 1 - core), device_id_type=MESH,
    )
    pair_copy.start()
    work.step(8)
    pair_copy.wait_recv()

    def push(there, carry):
        send_buf[there, core] = send_buf[there, core] + pair_buf[there]
        send_copy(there, chip).start()
        return carry

    lax.fori_loop(0, chip, push, 0)
    grad_query = acc[...].T * HD**-0.5
    low = spans[3][0]
    for t in range(heads // 2):
        even = grad_query[2 * t * n : (2 * t + 1) * n, :]
        odd = grad_query[(2 * t + 1) * n : (2 * t + 2) * n, :]
        part = jnp.where(left, even, pltpu.roll(odd, HD, 1))
        rights[0:n, low + t * LANES : low + (t + 1) * LANES] = turn_back(part, cosine[...], sine[...], False)
    work.step(9)

    def add(there, carry):
        send_copy(chip, there).wait_recv()
        return carry + recv_buf[there].astype(F32)

    part = lax.fori_loop(
        chip + 1, chips, add, send_buf[chip, core].astype(F32) + pair_buf[chip].astype(F32)
    )
    rights[0:n, low + mix : low + mix + LANES] = turn_back(part, cosine[...], sine[...], True)
    load_w.wait()
    grad_now = rights[0:n, low : spans[3][1]]

    def first_piece(start, wide):
        return dot_nt(grad_now, w_qkv[pl.ds(start, wide), :])

    total = Sum(mp, mp_me, *sum_refs[1])
    total.start(first_piece)
    work.step(10)
    total.middle()
    work.run(None, 10, 9, 7, 6)
    grad_normed = total.finish().astype(F32)
    unit, factor = unit_of(level)
    vectors[0:1, :] = jnp.sum(grad_normed * unit, axis=0, keepdims=True) + vecs[3:4, :] + vecs[4:5, :]
    vectors[2:3, :] = jnp.sum(level * logit[...], axis=0, keepdims=True) + vecs[5:6, :] + vecs[6:7, :]
    flow_out[...] = flow[...] + (
        unit_back(grad_normed * gains[0:1, :], unit, factor) + middle[...] + logit[...] * gains[2:3, :]
    ).astype(BF).astype(F32)
    work.run(11, None, 10, 8, 7)
    work.run(None, 11, None, 9, 8)
    work.run(None, None, 11, 10, 9)
    work.run(None, None, None, 11, 10)
    work.run(None, None, None, None, 11)
    work.drain()
    head.drain()
    total.drain()

    pair_copy.wait_send()

    def sent(there, carry):
        send_copy(there, chip).wait_send()
        return carry

    lax.fori_loop(0, chip, sent, 0)


def finish(flow, gains, attention, tail, vecs, weights, levels, heads, devices, mp, depth, ident):
    n, model = levels[0][0].shape
    width = heads * n
    group = 512 // n
    mix = heads * HD
    widths = [levels[1][i].shape[1] for i in (1, 3, 5, 7)] + [LANES]
    spans, total = [], 0
    for wide in widths:
        spans.append((total, total + wide))
        total += wide
    pieces = []
    for section, wide in enumerate(widths):
        pieces += [(section, low, low + LANES) for low in range(0, wide, LANES)]
    groups = []
    per = GROUP // LANES
    cuts = [*range(0, len(pieces) - 1, per), len(pieces) - 1, len(pieces)]
    for index, end in zip(cuts[:-1], cuts[1:]):
        merged = []
        for section, low, high in pieces[index:end]:
            if merged and merged[-1][0] == section:
                merged[-1] = (section, merged[-1][1], high)
            else:
                merged.append((section, low, high))
        wide = sum(high - low for _, low, high in merged)
        groups.append((wide, merged, len(groups) % 2))
    counts = [level[0].shape[0] for level in levels]
    rows = sum(counts)
    hidden = widths[1]
    many = len(groups)
    query_place, query, packed, mixed_t, log_total, *tables = attention
    rows_in, attn_in, logit = tail
    whole = [gains, query_place, log_total, *tables, logit, vecs]
    large = [flow, rows_in, attn_in, query, mixed_t, packed]
    args = whole + large + [weights] + [item for level in levels for item in level if item is not None]
    return pl.pallas_call(
        functools.partial(finish_kernel, n, heads, devices, mp, group, counts, spans, groups),
        out_shape=(
            jax.ShapeDtypeStruct(flow.shape, F32),
            jax.ShapeDtypeStruct((depth, mix), F32),
            jax.ShapeDtypeStruct((depth, HD), F32),
            jax.ShapeDtypeStruct((depth, HD), F32),
            jax.ShapeDtypeStruct((depth, mix), F32),
            jax.ShapeDtypeStruct((depth, hidden), F32),
            jax.ShapeDtypeStruct((depth, hidden), F32),
            jax.ShapeDtypeStruct((depth, hidden), F32),
            jax.ShapeDtypeStruct((8, depth), F32),
        ),
        in_specs=vmem(len(whole)) + [pl.BlockSpec(memory_space=pl.ANY)] * (len(args) - len(whole)),
        out_specs=tuple(vmem(9)),
        scratch_shapes=[
            pltpu.VMEM((2 * HD, width), BF),
            pltpu.VMEM((width, 2 * HD), BF),
            pltpu.VMEM((2 * HD, width), BF),
            pltpu.VMEM((2 * HD, width), F32),
            pltpu.VMEM((1, width), F32),
            pltpu.VMEM((devices // 2, 2, n, 2 * HD), BF),
            pltpu.VMEM((devices // 2, n, 2 * HD), BF),
            pltpu.VMEM((devices // 2, n, 2 * HD), BF),
            pltpu.SemaphoreType.DMA((devices // 2 + 1,)),
            pltpu.SemaphoreType.DMA((devices // 2 + 1,)),
            pltpu.VMEM((model, mix + 2 * HD), BF),
            pltpu.SemaphoreType.DMA(()),
            pltpu.VMEM((3, model // mp // PIECES, 2 * hidden), BF),
            pltpu.SemaphoreType.DMA((3,)),
            pltpu.VMEM((n, model), F32),
            *sum_scratch(mp, n, model),
            *sum_scratch(mp, n, model),
            pltpu.VMEM((2, rows, model), BF),
            pltpu.VMEM((2, model, rows), BF),
            pltpu.VMEM((rows, spans[3][1]), BF),
            pltpu.VMEM((8, model), F32),
            pltpu.VMEM((SLOTS, 4, 4, 2, depth, GROUP), BF),
            pltpu.VMEM((CORE_SLOTS, 4, 4, depth, GROUP), BF),
            pltpu.VMEM((many, 2, 2, depth, GROUP), BF),
            pltpu.VMEM((many, 2, 4, depth, GROUP), BF),
            pltpu.VMEM((many, 4, depth, GROUP), BF),
            pltpu.VMEM((many, 3, depth, GROUP), BF),
            pltpu.SemaphoreType.DMA((len(levels), 8)),
            pltpu.SemaphoreType.DMA((many, 8)),
            pltpu.SemaphoreType.DMA((many, 8)),
            pltpu.SemaphoreType.REGULAR,
            *[pltpu.VMEM(item.shape, item.dtype) for item in large],
            pltpu.SemaphoreType.DMA((len(large),)),
        ],
        compiler_params=pltpu.CompilerParams(
            collective_id=ident, has_side_effects=True, vmem_limit_bytes=63 * 1024 * 1024
        ),
        name="finish",
    )(*args)


def hand_over_kernel(count, *refs):
    vectors, sources, targets = refs[0], refs[1 : 1 + count], refs[1 + count :]
    for source, target in zip(sources, targets):
        target[...] = source[...]
    for i, target in enumerate(targets[count:]):
        target[...] = vectors[i, :]


def hand_over(items, vectors):
    count = len(items)
    return pl.pallas_call(
        functools.partial(hand_over_kernel, count),
        out_shape=tuple(
            [jax.ShapeDtypeStruct(item.shape, F32) for item in items]
            + [jax.ShapeDtypeStruct(vectors.shape[1:], F32)] * 3
        ),
        in_specs=vmem(1 + count),
        out_specs=tuple(vmem(count + 3)),
        name="hand_over",
    )(vectors, *items)


def rotary_tables(place):
    freq = jnp.exp(jnp.arange(HD // 2, dtype=F32) * (-2.0 * math.log(ROPE_BASE) / HD))
    angle = place.astype(F32)[:, None] * freq[None, :]
    cosine, sine = jnp.cos(angle), jnp.sin(angle)
    return (
        jnp.concatenate([cosine] * 4, axis=1),
        jnp.concatenate([-sine, sine, -sine, sine], axis=1),
    )


def local(
    tokens, depths, second_slot, third_slot, w_query, w_key, w_value, w_out, w_gate, w_up,
    w_down, norm_first, norm_second, router, cotangent,
):
    me = lax.axis_index("dp")
    devices, mp = lax.axis_size("dp"), lax.axis_size("mp")
    rows = tokens.shape[0]
    heads = w_query.shape[1] // HD
    depth = w_query.shape[0]
    home = rotary_tables(jnp.arange(rows, dtype=jnp.int32) + me * rows)

    def row(values):
        return values.reshape(1, -1)

    kept = advance(
        tokens, row(depths), row(second_slot), row(third_slot),
        (w_query, w_key, w_value, w_out.T, w_gate, w_up, w_down.T),
        (row(norm_first), row(norm_second), row(router)), home, heads, devices, mp, 0,
    )
    weights = kept[K_WEIGHTS].reshape(devices * depth, -1)
    gains = kept[K_GAINS]
    back = retreat(cotangent, kept, weights, heads, devices, mp, 1)
    terms = []
    for level in range(3):
        terms.append(
            tuple(back.get((base, level), kept.get((base, level))) for base in (
                K_SECOND, K_PARTS_GRAD, K_GRAD_FFN, K_HIDDEN, K_GRAD_ATTN, K_MIXED, K_NORMED, K_GRAD_QKV
            ))
        )
    attention = [kept[(base, 0)] for base in (K_PLACE, K_QUERY, K_PACKED, K_MIXED_T, K_LOG)]
    results = finish(
        back[K_FLOW_OUT], gains, (*attention, *home),
        (kept[(K_ROWS, 0)], kept[(K_ATTN, 0)], back[(K_LOGIT, 0)]), back[K_VECS], weights, terms,
        heads, devices, mp, depth, 2,
    )
    (state, flow, query_grad, key_grad, value_grad, out_grad, gate_grad, up_grad, down_grad,
     first_grad, second_grad, router_grad) = hand_over((kept[K_STATE], *results[:-1]), results[-1])
    return (
        state, flow, query_grad, key_grad, value_grad, out_grad.T, gate_grad, up_grad, down_grad.T,
        first_grad, second_grad, router_grad,
    )


def solution(mesh):
    in_specs = (
        P("dp", None), P("dp"), P("dp"), P("dp"), P("dp", "mp"), P("dp", "mp"), P("dp", "mp"),
        P("mp", "dp"), P("dp", "mp"), P("dp", "mp"), P("mp", "dp"), P("dp"), P("dp"), P("dp"),
        P("dp", None),
    )
    out_specs = (
        P("dp", None), P("dp", None), P("dp", "mp"), P("dp", "mp"), P("dp", "mp"), P("mp", "dp"),
        P("dp", "mp"), P("dp", "mp"), P("mp", "dp"), P("dp"), P("dp"), P("dp"),
    )
    return jax.shard_map(local, mesh=mesh, in_specs=in_specs, out_specs=out_specs, check_vma=False)
```
